32 devices in a mesh: dp: 16 (over z, x, core), fsdp: 2 (over y).
Axes of the slice: x: 2, y: 2, z: 4, core: 2. Of those that a mesh axis runs over, the one named last changes fastest.
Arguments:
- decoder_in: float32 [2, 512, 768], P('fsdp', 'dp'), may hold values from -6 to 6
- memory: bfloat16 [2, 6688, 768], P('fsdp', 'dp'), may hold values from -6 to 6
- res_group: int32 [2, 16], P('fsdp'), may hold values from 0 to 1, as said below
- prefix_len: int32 [2, 16], P('fsdp', 'dp'), may hold values from 1 to 32, as said below
- self_gain: bfloat16 [768], P('fsdp'), may hold values from 0.5 to 1.5
- self_qkv: bfloat16 [768, 2304], P('fsdp'), may hold values from -0.3125 to 0.3125
- self_out: bfloat16 [768, 768], P('fsdp'), may hold values from -0.4375 to 0.4375
- cross_gain: bfloat16 [768], P('fsdp'), may hold values from 0.5 to 1.5
- cross_query: bfloat16 [768, 768], P('fsdp'), may hold values from -0.3125 to 0.3125
- cross_kv: bfloat16 [768, 1536], P('fsdp'), may hold values from -0.3125 to 0.3125
- cross_out: bfloat16 [768, 768], P('fsdp'), may hold values from -0.875 to 0.875
- ffn_gain: bfloat16 [768], P('fsdp'), may hold values from 0.5 to 1.5
- ffn_in: bfloat16 [768, 3072], P('fsdp'), may hold values from -0.21875 to 0.21875
- ffn_out: bfloat16 [3072, 768], P('fsdp'), may hold values from -0.109375 to 0.109375
- cotangent: float32 [2, 512, 768], P('fsdp', 'dp'), may hold values from -6 to 6
Outputs:
- decoder_out: float32 [2, 512, 768], P('fsdp', 'dp')
- decoder_grad: float32 [2, 512, 768], P('fsdp', 'dp')
- memory_grad: float32 [2, 6688, 768], P('fsdp', 'dp')
- self_gain_grad: float32 [768], P('fsdp')
- self_qkv_grad: float32 [768, 2304], P('fsdp')
- self_out_grad: float32 [768, 768], P('fsdp')
- cross_gain_grad: float32 [768], P('fsdp')
- cross_query_grad: float32 [768, 768], P('fsdp')
- cross_kv_grad: float32 [768, 1536], P('fsdp')
- cross_out_grad: float32 [768, 768], P('fsdp')
- ffn_gain_grad: float32 [768], P('fsdp')
- ffn_in_grad: float32 [768, 3072], P('fsdp')
- ffn_out_grad: float32 [3072, 768], P('fsdp')
The draws below stay inside these ranges and needn't reach their ends.
Inputs may be any that keep to these rules, and one draw needn't show every extreme that they name: In every column exactly half of the 16 examples have res_group 1. `prefix_len`: some example has 32 prefix tokens and some has 1.
All inputs are finite; a program needn't handle non-finite values.
Results may differ from the reference program's by a relative error of at most 0.03.
The reference program's roundings to bfloat16 on the way count: a program that leaves them out, or rounds other values in their place, can miss the bound.
Values may be sent and summed in bfloat16 or wider, within the bound.
A program may use at most 192 MiB of HBM per device.

```python
import jax
import jax.numpy as jnp
from jax import lax

D = 768
HEADS = 12
HEAD_DIM = 64
FF = 3072
SUFFIX = 32
PATCH_S = 196
PATCH_L = 576
PREFIX = 32
COLUMNS = 2
EX_COL = 16
DEC_ROWS = 512
SLOT_S = 228
SLOT_L = 608
MEM_COL = 6688


def draw_res_group(key, part):
    key = jax.random.fold_in(key, 11)
    keys = jax.random.split(key, COLUMNS)
    base = (jnp.arange(EX_COL) % 2).astype(jnp.int32)
    return jax.vmap(lambda column_key: jax.random.permutation(column_key, base))(keys).astype(jnp.int32)


def draw_prefix_len(key, part):
    key = jax.random.fold_in(key, 23)
    first, second = jax.random.split(key)
    total = COLUMNS * EX_COL
    lengths = jax.random.randint(first, (total,), 1, PREFIX + 1)
    spot = jax.random.randint(second, (), 0, total)
    places = jnp.arange(total)
    lengths = jnp.where(places == spot, PREFIX, lengths)
    lengths = jnp.where(places == (spot + 1) % total, 1, lengths)
    return lengths.reshape(COLUMNS, EX_COL).astype(jnp.int32)


def shard_levels(rng, dims, shards, least, high):
    level = 1.0
    for axis_at, parts in shards:
        steps = jax.random.uniform(jax.random.fold_in(jax.random.fold_in(rng, 6), axis_at), (parts,), jnp.float32, least / len(shards), high / len(shards))
        level = level * jnp.repeat(jnp.exp(steps), dims[axis_at] // parts).reshape((-1,) + (1,) * (len(dims) - 1 - axis_at))
    return level


def bell_draw(key, dims, spread, reach, cuts=(), kind=jnp.bfloat16):
    values = spread * jax.random.normal(key, dims, jnp.float32)
    if cuts:
        values = values * shard_levels(key, dims, cuts, -0.22, 0.18)
    return jnp.clip(values, -reach, reach).astype(kind)


def setup_inputs(seed: int = 0) -> dict:
    splits = jax.random.split(jax.random.key(seed), 16)
    decoder_in = bell_draw(splits[0], (COLUMNS, DEC_ROWS, D), 1.0, 6.0, ((0, 2), (1, 16)), jnp.float32)
    memory = bell_draw(splits[1], (COLUMNS, MEM_COL, D), 1.0, 6.0, ((0, 2), (1, 16)))
    res_group = draw_res_group(jax.random.fold_in(splits[15], 71), 0)
    prefix_len = draw_prefix_len(jax.random.fold_in(splits[15], 71), 0)
    self_gain = jnp.clip(1.0 + 0.1 * jax.random.normal(splits[4], (D,), jnp.float32), 0.5, 1.5).astype(jnp.bfloat16)
    self_qkv = bell_draw(splits[5], (D, 3 * D), (D // 2) ** -0.5, 0.3125, ((0, 2),))
    self_out = bell_draw(splits[6], (D, D), (D // 4) ** -0.5, 0.4375, ((0, 2),))
    cross_gain = jnp.clip(1.0 + 0.1 * jax.random.normal(splits[7], (D,), jnp.float32), 0.5, 1.5).astype(jnp.bfloat16)
    cross_query = bell_draw(splits[8], (D, D), (D // 2) ** -0.5, 0.3125, ((0, 2),))
    cross_kv = bell_draw(splits[9], (D, 2 * D), (D // 2) ** -0.5, 0.3125, ((0, 2),))
    cross_out = bell_draw(splits[10], (D, D), (D // 16) ** -0.5, 0.875, ((0, 2),))
    ffn_gain = jnp.clip(1.0 + 0.1 * jax.random.normal(splits[11], (D,), jnp.float32), 0.5, 1.5).astype(jnp.bfloat16)
    ffn_in = bell_draw(splits[12], (D, FF), D ** -0.5, 0.21875, ((0, 2),))
    ffn_out = bell_draw(splits[13], (FF, D), FF ** -0.5, 0.109375, ((0, 2),))
    cotangent = bell_draw(splits[14], (COLUMNS, DEC_ROWS, D), 1.0, 6.0, ((0, 2), (1, 16)), jnp.float32)
    return dict(decoder_in=decoder_in, memory=memory, res_group=res_group, prefix_len=prefix_len, self_gain=self_gain, self_qkv=self_qkv, self_out=self_out, cross_gain=cross_gain, cross_query=cross_query, cross_kv=cross_kv, cross_out=cross_out, ffn_gain=ffn_gain, ffn_in=ffn_in, ffn_out=ffn_out, cotangent=cotangent)


@jax.custom_vjp
def low(v):
    return lax.optimization_barrier(v.astype(jnp.bfloat16)).astype(jnp.float32)

@jax.custom_vjp
def low_back(v):
    return v

def low_keep(v):
    return (low(v), None)

def low_pass(kept, grad):
    return (grad,)

def back_keep(v):
    return (v, None)

def back_low(kept, grad):
    return (low(grad),)
low.defvjp(low_keep, low_pass)
low_back.defvjp(back_keep, back_low)
norm_eps = 1e-06

def layer_norm(value, gain):
    mean = lax.optimization_barrier(jnp.mean(value, axis=-1, keepdims=True))
    centred = value - mean
    variance = lax.optimization_barrier(jnp.mean(centred * centred, axis=-1, keepdims=True))
    return centred * lax.rsqrt(variance + norm_eps) * gain

def matmul(left, right):
    return jnp.dot(left, right, precision=lax.Precision.HIGHEST)

def attend(query, keys, values, allowed, scale):
    scores = low_back(jnp.einsum('eqhd,ekhd->ehqk', query, keys, precision=lax.Precision.HIGHEST) * scale)
    scores = jnp.where(allowed[:, None], scores, -1e+30)
    top = lax.optimization_barrier(jnp.max(scores, axis=-1, keepdims=True))
    weights = jnp.exp(scores - top)
    probs = low(weights / lax.optimization_barrier(jnp.sum(weights, axis=-1, keepdims=True)))
    return jnp.einsum('ehqk,ekhd->eqhd', probs, values, precision=lax.Precision.HIGHEST)

def window_layout(res_group, prefix_len):
    small = 1 - res_group
    small_count = lax.optimization_barrier(jnp.sum(small, axis=-1, keepdims=True))
    small_before = jnp.cumsum(small, axis=-1) - small
    large_before = jnp.cumsum(res_group, axis=-1) - res_group
    offset = jnp.where(res_group == 1, SLOT_S * small_count + SLOT_L * large_before, SLOT_S * small_before).astype(jnp.int32)
    start = jnp.minimum(offset, MEM_COL - SLOT_L).astype(jnp.int32)
    valid = (jnp.where(res_group == 1, PATCH_L, PATCH_S) + prefix_len).astype(jnp.int32)
    return (offset, start, valid)

def take_windows(table, starts):
    return jax.vmap(lambda begin: lax.dynamic_slice_in_dim(table, begin.astype(jnp.int32), SLOT_L, 0))(starts)

def forward(decoder_in, memory, offset, start, valid, params):
    self_gain, self_qkv, self_out, cross_gain, cross_query, cross_kv, cross_out, ffn_gain, ffn_in, ffn_out = params
    examples = COLUMNS * EX_COL
    scale = HEAD_DIM ** (-0.5)
    row_index = lax.broadcasted_iota(jnp.int32, (SUFFIX, SUFFIX), 0)
    col_index = lax.broadcasted_iota(jnp.int32, (SUFFIX, SUFFIX), 1)
    causal = (row_index >= col_index)[None]
    resid = decoder_in.reshape(examples, SUFFIX, D)
    normed_one = low(layer_norm(resid, self_gain))
    packed = low(low_back(matmul(normed_one, self_qkv))).reshape(examples, SUFFIX, 3, HEADS, HEAD_DIM)
    self_mixed = attend(packed[:, :, 0], packed[:, :, 1], packed[:, :, 2], causal, scale)
    self_mixed = low(low_back(self_mixed)).reshape(examples, SUFFIX, D)
    after_self = resid + low_back(matmul(self_mixed, self_out))
    normed_two = low(layer_norm(after_self, cross_gain))
    query = low(low_back(matmul(normed_two, cross_query))).reshape(examples, SUFFIX, HEADS, HEAD_DIM)
    memory_kv = low(low_back(matmul(memory, cross_kv)))
    windows = jax.vmap(take_windows)(memory_kv, start).reshape(examples, SLOT_L, 2, HEADS, HEAD_DIM)
    positions = start[..., None] + jnp.arange(SLOT_L, dtype=jnp.int32)
    allowed = (positions >= offset[..., None]) & (positions < (offset + valid)[..., None])
    allowed = allowed.reshape(examples, 1, SLOT_L)
    cross_mixed = attend(query, windows[:, :, 0], windows[:, :, 1], allowed, scale)
    cross_mixed = low(low_back(cross_mixed)).reshape(examples, SUFFIX, D)
    after_cross = after_self + low_back(matmul(cross_mixed, cross_out))
    normed_three = low(layer_norm(after_cross, ffn_gain))
    up = low_back(matmul(normed_three, ffn_in))
    act = low(jax.nn.gelu(up, approximate=True))
    result = after_cross + low_back(matmul(act, ffn_out))
    return result.reshape(COLUMNS, EX_COL * SUFFIX, D)

def reference(decoder_in, memory, res_group, prefix_len, self_gain, self_qkv, self_out, cross_gain, cross_query, cross_kv, cross_out, ffn_gain, ffn_in, ffn_out, cotangent):
    offset, start, valid = window_layout(res_group, prefix_len)
    params = (self_gain.astype(jnp.float32), self_qkv.astype(jnp.float32), self_out.astype(jnp.float32), cross_gain.astype(jnp.float32), cross_query.astype(jnp.float32), cross_kv.astype(jnp.float32), cross_out.astype(jnp.float32), ffn_gain.astype(jnp.float32), ffn_in.astype(jnp.float32), ffn_out.astype(jnp.float32))

    def run(rows, table, params):
        return forward(rows, table, offset, start, valid, params)
    result, pullback = jax.vjp(run, decoder_in, memory.astype(jnp.float32), params)
    rows_grad, table_grad, grads = pullback(cotangent)
    return (result, rows_grad, table_grad, grads[0], grads[1], grads[2], grads[3], grads[4], grads[5], grads[6], grads[7], grads[8], grads[9])
```

```python
from functools import partial

import jax
import jax.numpy as jnp
from jax import lax
from jax.experimental import pallas as pl
from jax.experimental.pallas import tpu as pltpu
from jax.sharding import PartitionSpec as P

D = 768
HEADS = 12
HEAD_DIM = 64
SUFFIX = 32
PATCH_S = 196
PATCH_L = 576
SLOT_S = 228
SLOT_L = 608
RING = 4
SIDE = 2
CORES = 2
norm_eps = 1e-06
MESH = pl.DeviceIdType.MESH
F32 = jnp.float32
BF16 = jnp.bfloat16
NONE = -1e30


def mm(left, right):
    return jnp.dot(left, right, preferred_element_type=F32)


def mm_nt(left, right):
    return lax.dot_general(left, right, (((1,), (1,)), ((), ())), preferred_element_type=F32)


def mm_tn(left, right):
    return lax.dot_general(left, right, (((0,), (0,)), ((), ())), preferred_element_type=F32)


def normed(value):
    mean = jnp.mean(value, axis=-1, keepdims=True)
    centred = value - mean
    variance = jnp.mean(centred * centred, axis=-1, keepdims=True)
    scale = lax.rsqrt(variance + norm_eps)
    return centred * scale, scale


def norm_back(grad, hat, scale, gain):
    inner = grad * gain
    mean_one = jnp.mean(inner, axis=-1, keepdims=True)
    mean_two = jnp.mean(inner * hat, axis=-1, keepdims=True)
    gain_grad = jnp.sum(grad * hat, axis=0, keepdims=True)
    return scale * (inner - mean_one - hat * mean_two), gain_grad


def gelu_parts(up):
    inner = 0.7978845608 * (up + 0.044715 * up * up * up)
    tanh = jnp.tanh(inner)
    slope = 0.7978845608 * (1.0 + 3.0 * 0.044715 * up * up)
    value = 0.5 * up * (1.0 + tanh)
    grad = 0.5 * (1.0 + tanh) + 0.5 * up * (1.0 - tanh * tanh) * slope
    return value, grad


class Gather:
    def __init__(self, place, view, width, sems, at):
        self.z, self.x, self.c, self.f = place
        self.view = view
        half = (width // 256) * 128
        self.halves = ((0, half), (half, width - half))
        self.send, self.recv = sems
        self.at = at
        self.sent = []

    def dev(self, z, x, c):
        return (z * (SIDE * CORES) + x * CORES + c, self.f)

    def copy(self, block, half, target, into):
        z, x, c = block
        ref = self.view(z, x, c, self.halves[half] if half is not None else None)
        return pltpu.make_async_remote_copy(
            src_ref=ref,
            dst_ref=ref,
            send_sem=self.send.at[self.at, len(self.sent)],
            recv_sem=self.recv.at[self.at, into],
            device_id=self.dev(*target),
            device_id_type=MESH,
        )

    def go(self, block, half, target, into):
        item = self.copy(block, half, target, into)
        item.start()
        self.sent.append(item)

    def wait(self, block, half, into):
        z, x, c = block
        ref = self.view(z, x, c, self.halves[half] if half is not None else None)
        pltpu.make_async_remote_copy(
            src_ref=ref,
            dst_ref=ref,
            send_sem=self.send.at[self.at, 0],
            recv_sem=self.recv.at[self.at, into],
            device_id=self.dev(self.z, 1 - self.x, self.c),
            device_id_type=MESH,
        ).wait_recv()

    def names(self):
        z, x, c = self.z, self.x, self.c
        up, down, far = lax.rem(z + 1, RING), lax.rem(z + 3, RING), lax.rem(z + 2, RING)
        return z, x, c, up, down, far

    def step_one(self):
        z, x, c, up, down, far = self.names()
        own = (z, x, c)
        self.go(own, None, (z, 1 - x, c), 0)
        self.go(own, None, (up, x, c), 1)
        self.go(own, None, (down, x, c), 2)
        self.go(own, None, (z, x, 1 - c), 8)

    def step_two(self):
        z, x, c, up, down, far = self.names()
        mate = (z, x, 1 - c)
        self.wait((z, 1 - x, c), None, 0)
        self.go((z, 1 - x, c), None, (up, x, c), 5)
        self.go((z, 1 - x, c), None, (down, x, c), 6)
        self.go((z, 1 - x, c), None, mate, 9)
        self.wait((down, x, c), None, 1)
        self.go((down, x, c), 0, (up, x, c), 3)
        self.go((down, x, c), None, mate, 10)
        self.wait((up, x, c), None, 2)
        self.go((up, x, c), 1, (down, x, c), 4)
        self.go((up, x, c), None, mate, 11)

    def step_three(self):
        z, x, c, up, down, far = self.names()
        mate = (z, x, 1 - c)
        self.wait((far, x, c), 0, 3)
        self.wait((far, x, c), 1, 4)
        self.go((far, x, c), None, (z, 1 - x, c), 7)
        self.go((far, x, c), None, mate, 12)
        self.wait((down, 1 - x, c), None, 5)
        self.go((down, 1 - x, c), None, mate, 13)
        self.wait((up, 1 - x, c), None, 6)
        self.go((up, 1 - x, c), None, mate, 14)

    def step_four(self):
        z, x, c, up, down, far = self.names()
        mate = (z, x, 1 - c)
        self.wait((far, 1 - x, c), None, 7)
        self.go((far, 1 - x, c), None, mate, 15)
        o = 1 - c
        self.wait((z, x, o), None, 8)
        self.wait((z, 1 - x, o), None, 9)
        self.wait((down, x, o), None, 10)
        self.wait((up, x, o), None, 11)
        self.wait((far, x, o), None, 12)
        self.wait((down, 1 - x, o), None, 13)
        self.wait((up, 1 - x, o), None, 14)
        self.wait((far, 1 - x, o), None, 15)

    def finish(self):
        for item in self.sent:
            item.wait_send()


class Pieces:
    def __init__(self, count, own_rows):
        self.half = count // 2
        self.edge = self.half * SLOT_S
        self.rows = own_rows
        self.count = count

    def start(self, rank):
        return jnp.where(
            rank < self.half, SLOT_S * rank, self.edge + SLOT_L * (rank - self.half)
        )

    def size(self, rank):
        return jnp.where(rank < self.half, SLOT_S, SLOT_L)

    def rank_of(self, row):
        return jnp.where(
            row < self.edge,
            lax.div(row, SLOT_S),
            self.half + lax.div(jnp.maximum(row - self.edge, 0), SLOT_L),
        )

    def first_rank(self, device):
        return self.rank_of(device * self.rows)

    def last_rank(self, device):
        return self.rank_of(device * self.rows + self.rows - 1)

    def first_device(self, rank):
        return lax.div(self.start(rank), self.rows)

    def last_device(self, rank):
        return lax.div(self.start(rank) + self.size(rank) - 1, self.rows)


SLOTS = 3
LANE_QKV, LANE_SO, LANE_CQ, LANE_CKV, LANE_CO, LANE_FI, LANE_FO = 0, 2304, 3072, 3840, 5376, 6144, 9216
UNITS = 16
KV_UNITS = (5, 6)
TOKEN_UNITS = tuple(u for u in range(UNITS) if u not in KV_UNITS)
GROUPS = ((0, 2304), (2304, 3072), (5376, 6912))


def layer_kernel(
    ranks,
    columns,
    x_ref, cot_ref, mem_ref, res_ref, pre_ref, gains_ref,
    qkv_ref, so_ref, cq_ref, ckv_ref, co_ref, fi_ref, fo_ref,
    out_ref, grad_ref, memgrad_ref, gain_out_ref, weights_out_ref,
    wb, gb, rb, sb, xb, cb, ob, gainb, memp, kvb, kvg, kp, kr, kc, cp,
    cqb, qbuf, osend, ostat_send, obuf, ostat, dob, dstat_b, dobuf, dstat, dqsend, dqbuf, gmine, gpeer,
    load_sem, gsend, grecv, ysend, yrecv, psend, precv, usend, urecv, ksend, krecv,
):
    me = lax.axis_index("dp")
    f = lax.axis_index("fsdp")
    z = lax.div(me, SIDE * CORES)
    x = lax.rem(lax.div(me, CORES), SIDE)
    c = lax.rem(me, CORES)
    chip = lax.div(me, CORES)
    chips = ranks // CORES
    place = (z, x, c, f)
    half_rows = D // columns
    slab = half_rows // chips
    own_rows = mem_ref.shape[0]
    padded = memp.shape[0]
    lay = Pieces(ranks, own_rows)
    other = 1 - f
    everyone = ranks * columns
    lin = f * ranks + me

    loads = []

    def load(src, lane, width):
        item = pltpu.make_async_copy(
            src, wb.at[pl.ds(pl.multiple_of(f * half_rows, 128), half_rows), pl.ds(lane, width)],
            load_sem.at[len(loads)],
        )
        item.start()
        loads.append(item)

    load(qkv_ref, LANE_QKV, 2304)
    load(so_ref, LANE_SO, 768)
    load(cq_ref, LANE_CQ, 768)
    load(ckv_ref, LANE_CKV, 1536)
    load(co_ref, LANE_CO, 768)
    load(fi_ref, LANE_FI, 3072)
    for j in range(4):
        load(fo_ref.at[pl.ds(j * half_rows, half_rows)], LANE_FO + 768 * j, 768)

    for s in range(SLOTS):
        qbuf[s] = jnp.zeros_like(qbuf[s])
        obuf[s] = jnp.zeros_like(obuf[s])
        ostat[s, 0] = jnp.full_like(ostat[s, 0], NONE)
        ostat[s, 1] = jnp.zeros_like(ostat[s, 1])
        dobuf[s] = jnp.zeros_like(dobuf[s])
        dstat[s] = jnp.zeros_like(dstat[s])
        dqbuf[s] = jnp.zeros_like(dqbuf[s])

    xb[me, 0:SUFFIX] = x_ref[...]
    xb[me, SUFFIX : SUFFIX + 8] = jnp.full((8, D), pre_ref[0, 0].astype(F32), F32)
    cb[me] = cot_ref[...]
    gainb[f] = gains_ref[...]

    barrier = pltpu.get_barrier_semaphore()

    def greet(i, carry):
        to = lax.rem(lin + i, everyone)
        pl.semaphore_signal(
            barrier, inc=1, device_id=(lax.rem(to, ranks), lax.div(to, ranks)), device_id_type=MESH
        )
        return carry

    lax.fori_loop(1, everyone, greet, 0)
    pl.semaphore_wait(barrier, everyone - 1)

    y_items = []

    def push_y(ref, at):
        item = pltpu.make_async_remote_copy(
            src_ref=ref, dst_ref=ref, send_sem=ysend.at[at], recv_sem=yrecv.at[at],
            device_id=(me, other), device_id_type=MESH,
        )
        item.start()
        y_items.append(item)
        return item

    def slab_view(first, width, mine):
        half = width // CORES
        rows_from = f if mine else other

        def view(zz, xx, cc, part):
            low, size = part if part is not None else (0, half)
            row = pl.multiple_of(rows_from * half_rows + (zz * SIDE + xx) * slab, 16)
            lane = pl.multiple_of(first + cc * half + low, 128)
            return wb.at[pl.ds(row, slab), pl.ds(lane, size)]

        return view

    sems = (gsend, grecv)
    ag_x = Gather(place, lambda zz, xx, cc, part: xb.at[zz * 4 + xx * 2 + cc] if part is None else xb.at[zz * 4 + xx * 2 + cc, :, pl.ds(*part)], D, sems, 0)
    ag_w = [
        Gather(place, slab_view(first, width, False), width // CORES, sems, 1 + n)
        for n, (first, width) in enumerate(GROUPS)
    ]
    ag_c = Gather(place, lambda zz, xx, cc, part: cb.at[zz * 4 + xx * 2 + cc] if part is None else cb.at[zz * 4 + xx * 2 + cc, :, pl.ds(*part)], D, sems, 4)

    ag_x.step_one()
    gain_item = push_y(gainb.at[f], 3)
    y_w = []
    waits = ((0,), (1, 2, 3), tuple(range(4, 10)))
    for n, (first, width) in enumerate(GROUPS):
        for i in waits[n]:
            loads[i].wait()
        y_w.append(push_y(slab_view(first, width, True)(z, x, c, None), n))
    ag_x.step_two()
    y_w[0].wait_recv()
    ag_w[0].step_one()
    ag_x.step_three()
    ag_w[0].step_two()
    ag_x.step_four()
    y_w[1].wait_recv()
    ag_w[1].step_one()
    ag_w[0].step_three()
    ag_c.step_one()
    ag_w[1].step_two()
    gain_item.wait_recv()

    memp[0:own_rows] = mem_ref[...]
    memp[own_rows:padded] = jnp.zeros((padded - own_rows, D), BF16)

    def example_of(rank):
        small = jnp.int32(0)
        large = jnp.int32(0)
        found = jnp.int32(0)
        for i in range(ranks):
            group = res_ref[0, i]
            where = jnp.where(group == 1, lay.half + large, small)
            found = jnp.where(where == rank, i, found)
            large = large + group
            small = small + (1 - group)
        return found

    def rank_of_example(example):
        before_large = jnp.int32(0)
        mine = jnp.int32(0)
        for i in range(ranks):
            group = res_ref[0, i]
            before_large = before_large + jnp.where(i < example, group, 0)
            mine = jnp.where(i == example, group, mine)
        return jnp.where(mine == 1, lay.half + before_large, example - before_large)

    gain = [jnp.concatenate([gainb[i, n : n + 1] for i in range(columns)], axis=1) for n in range(3)]

    mine = example_of(me)
    resid = xb[mine, 0:SUFFIX]
    hat_one, rs_one = normed(resid)
    n1 = (hat_one * gain[0]).astype(BF16)

    ag_w[0].step_four()

    lanes = lax.broadcasted_iota(jnp.int32, (1, 256), 1)
    head_f32 = [(lax.div(lanes, HEAD_DIM) == h).astype(F32) for h in range(4)]
    head_b16 = [m.astype(BF16) for m in head_f32]

    def stack(value):
        return jnp.concatenate([value * m for m in head_b16], axis=0)

    def unstack(value):
        rows = value.shape[0] // 4
        total = value[0:rows] * head_f32[0]
        for h in range(1, 4):
            total = total + value[h * rows : (h + 1) * rows] * head_f32[h]
        return total

    q = (mm(n1, wb[:, 0:768])).astype(BF16)
    k = (mm(n1, wb[:, 768:1536])).astype(BF16)
    v = (mm(n1, wb[:, 1536:2304])).astype(BF16)
    scale = HEAD_DIM**-0.5
    qs = (q.astype(F32) * scale).astype(BF16)
    row_at = lax.broadcasted_iota(jnp.int32, (SUFFIX, SUFFIX), 0)
    col_at = lax.broadcasted_iota(jnp.int32, (SUFFIX, SUFFIX), 1)
    causal = jnp.concatenate([(row_at >= col_at).astype(F32)] * 4, axis=0) > 0.0
    self_p = []
    mixed = []
    for g in range(3):
        sl = slice(256 * g, 256 * g + 256)
        s = mm_nt(stack(qs[:, sl]), k[:, sl])
        s = jnp.where(causal, s, NONE)
        e = jnp.exp(s - jnp.max(s, axis=-1, keepdims=True))
        p = e / jnp.sum(e, axis=-1, keepdims=True)
        self_p.append(p)
        mixed.append(unstack(mm(p.astype(BF16), v[:, sl])))
    sm = jnp.concatenate(mixed, axis=1).astype(BF16)

    ag_w[1].step_three()
    ag_w[1].step_four()
    y_w[2].wait_recv()
    ag_w[2].step_one()
    ag_c.step_two()

    after_self = resid + mm(sm, wb[:, LANE_SO : LANE_SO + 768])
    hat_two, rs_two = normed(after_self)
    n2 = (hat_two * gain[1]).astype(BF16)
    cq = mm(n2, wb[:, LANE_CQ : LANE_CQ + 768]).astype(BF16)
    cqb[...] = cq

    my_first, my_last = lay.first_device(me), lay.last_device(me)
    held_first, held_last = lay.first_rank(me), lay.last_rank(me)

    def to_holders(pairs):
        for i in range(SLOTS):
            target = my_first + i
            slot = me - lay.first_rank(target)
            there = target <= my_last

            @pl.when(there & (target == me))
            def _():
                for src, dst, at in pairs:
                    dst[slot] = src[...]

            @pl.when(there & (target != me))
            def _():
                for src, dst, at in pairs:
                    pltpu.make_async_remote_copy(
                        src_ref=src, dst_ref=dst.at[slot], send_sem=psend.at[at, i],
                        recv_sem=precv.at[at, slot], device_id=(target, f), device_id_type=MESH,
                    ).start()

    def to_holders_sent(pairs):
        for i in range(SLOTS):
            target = my_first + i

            @pl.when((target <= my_last) & (target != me))
            def _():
                for src, dst, at in pairs:
                    pltpu.make_async_remote_copy(
                        src_ref=src, dst_ref=dst.at[0], send_sem=psend.at[at, i],
                        recv_sem=precv.at[at, 0], device_id=(target, f), device_id_type=MESH,
                    ).wait_send()

    def at_holders(pairs):
        for s in range(SLOTS):
            rank = held_first + s

            @pl.when((rank <= held_last) & (rank != me))
            def _():
                for src, dst, at in pairs:
                    pltpu.make_async_remote_copy(
                        src_ref=src, dst_ref=dst.at[s], send_sem=psend.at[at, 0],
                        recv_sem=precv.at[at, s], device_id=(rank, f), device_id_type=MESH,
                    ).wait_recv()

    def to_owners(pairs):
        for s in range(SLOTS):
            rank = held_first + s
            index = me - lay.first_device(rank)
            there = rank <= held_last

            @pl.when(there & (rank == me))
            def _():
                for src, dst, at in pairs:
                    dst[index] = src[s]

            @pl.when(there & (rank != me))
            def _():
                for src, dst, at in pairs:
                    pltpu.make_async_remote_copy(
                        src_ref=src.at[s], dst_ref=dst.at[index], send_sem=psend.at[at, s],
                        recv_sem=precv.at[at, index], device_id=(rank, f), device_id_type=MESH,
                    ).start()

    def to_owners_sent(pairs):
        for s in range(SLOTS):
            rank = held_first + s

            @pl.when((rank <= held_last) & (rank != me))
            def _():
                for src, dst, at in pairs:
                    pltpu.make_async_remote_copy(
                        src_ref=src.at[s], dst_ref=dst.at[0], send_sem=psend.at[at, s],
                        recv_sem=precv.at[at, 0], device_id=(rank, f), device_id_type=MESH,
                    ).wait_send()

    def at_owners(pairs):
        for i in range(SLOTS):
            target = my_first + i

            @pl.when((target <= my_last) & (target != me))
            def _():
                for src, dst, at in pairs:
                    pltpu.make_async_remote_copy(
                        src_ref=src.at[0], dst_ref=dst.at[i], send_sem=psend.at[at, 0],
                        recv_sem=precv.at[at, i], device_id=(target, f), device_id_type=MESH,
                    ).wait_recv()

    q_pairs = [(cqb, qbuf, 0)]
    o_pairs = [(osend, obuf, 1), (ostat_send, ostat, 2)]
    d_pairs = [(dob, dobuf, 3), (dstat_b, dstat, 4)]
    dq_pairs = [(dqsend, dqbuf, 5)]

    to_holders(q_pairs)

    def kv_step(i, carry):
        lane = pl.multiple_of(i * 256, 256)
        kvb[:, pl.ds(lane, 256)] = mm(memp[...], wb[:, pl.ds(LANE_CKV + lane, 256)]).astype(BF16)
        return carry

    lax.fori_loop(0, 6, kv_step, 0)

    lane_f = lax.broadcasted_iota(jnp.int32, (SUFFIX, padded), 1).astype(F32)
    allowed = []
    for s in range(SLOTS):
        rank = held_first + s
        ok = rank <= held_last
        example = example_of(jnp.minimum(rank, ranks - 1))
        prefix = xb[example, SUFFIX : SUFFIX + 8, 0:128][0:1, 0:1]
        low = (lay.start(rank) - me * own_rows).astype(F32)
        patches = jnp.where(rank < lay.half, PATCH_S, PATCH_L).astype(F32)
        high = jnp.minimum(low + patches + prefix, jnp.float32(own_rows))
        high = jnp.where(ok, high, jnp.float32(-1.0))
        allowed.append(((lane_f >= low) & (lane_f < high)).astype(F32))
    allowed = jnp.concatenate(allowed * 4, axis=0) > 0.0

    at_holders(q_pairs)
    to_holders_sent(q_pairs)
    qh = jnp.concatenate([qbuf[s] for s in range(SLOTS)], axis=0)
    qh = (qh.astype(F32) * scale).astype(BF16)
    lane_c = lax.broadcasted_iota(jnp.int32, (SUFFIX, 128), 1)
    top_c = [jnp.zeros((SUFFIX, 128), F32) for _ in range(SLOTS)]
    sum_c = [jnp.zeros((SUFFIX, 128), F32) for _ in range(SLOTS)]
    for g in range(3):
        sl = slice(256 * g, 256 * g + 256)
        s = mm_nt(stack(qh[:, sl]), kvb[:, sl])
        s = jnp.where(allowed, s, NONE)
        top = jnp.max(s, axis=-1, keepdims=True)
        e = jnp.where(allowed, jnp.exp(s - top), 0.0)
        total = jnp.sum(e, axis=-1, keepdims=True)
        o = mm(e.astype(BF16), kvb[:, 768 + 256 * g : 1024 + 256 * g])
        o = o * jnp.where(total > 0.0, 1.0 / jnp.where(total > 0.0, total, 1.0), 0.0)
        o = unstack(o).astype(BF16)
        for n in range(SLOTS):
            osend[n, :, sl] = o[n * SUFFIX : (n + 1) * SUFFIX]
            for h in range(4):
                at = h * SLOTS * SUFFIX + n * SUFFIX
                hit = lane_c == 4 * g + h
                top_c[n] = jnp.where(hit, top[at : at + SUFFIX], top_c[n])
                sum_c[n] = jnp.where(hit, total[at : at + SUFFIX], sum_c[n])
    for n in range(SLOTS):
        ostat_send[n, 0] = top_c[n]
        ostat_send[n, 1] = sum_c[n]
    to_owners(o_pairs)

    ag_w[2].step_two()
    ag_c.step_three()

    at_owners(o_pairs)
    to_owners_sent(o_pairs)

    def expand(compact):
        low = lane_c < HEAD_DIM
        return jnp.concatenate(
            [jnp.where(low, compact[:, 2 * t : 2 * t + 1], compact[:, 2 * t + 1 : 2 * t + 2]) for t in range(6)],
            axis=1,
        )

    tops = [ostat[i, 0] for i in range(SLOTS)]
    top_all = jnp.maximum(jnp.maximum(tops[0], tops[1]), tops[2])
    shares = [ostat[i, 1] * jnp.exp(tops[i] - top_all) for i in range(SLOTS)]
    whole = shares[0] + shares[1] + shares[2]
    whole = jnp.where(whole > 0.0, whole, 1.0)
    lse = top_all + jnp.log(whole)
    cross = jnp.zeros((SUFFIX, D), F32)
    for i in range(SLOTS):
        cross = cross + expand(shares[i] / whole) * obuf[i].astype(F32)
    cm = cross.astype(BF16)

    ag_c.step_four()
    ag_w[2].step_three()
    ag_w[2].step_four()

    after_cross = after_self + mm(cm, wb[:, LANE_CO : LANE_CO + 768])
    hat_three, rs_three = normed(after_cross)
    n3 = (hat_three * gain[2]).astype(BF16)

    cot = cb[mine]
    out_low = cot.astype(BF16)
    acts, up_grads = [], []
    hidden_grad = [mm_nt(out_low, wb[:, LANE_FO + 768 * j : LANE_FO + 768 * (j + 1)]) for j in range(4)]

    def by_hidden(j):
        parts = []
        for t in range(768 // half_rows):
            at = 768 * j + t * half_rows
            col, unit = at // (4 * half_rows), (at % (4 * half_rows)) // half_rows
            parts.append(hidden_grad[unit][:, col * half_rows : (col + 1) * half_rows])
        return jnp.concatenate(parts, axis=1)

    n3_grad = jnp.zeros((SUFFIX, D), F32)
    for j in range(4):
        weight = wb[:, LANE_FI + 768 * j : LANE_FI + 768 * (j + 1)]
        value, slope = gelu_parts(mm(n3, weight))
        acts.append(value.astype(BF16))
        ug = (by_hidden(j) * slope).astype(BF16)
        up_grads.append(ug)
        n3_grad = n3_grad + mm_nt(ug, weight)
    act = jnp.concatenate(acts, axis=1)

    def act_unit(j):
        return [act[:, i * 4 * half_rows + j * half_rows : i * 4 * half_rows + (j + 1) * half_rows] for i in range(columns)]

    part, ffn_gain_grad = norm_back(n3_grad, hat_three, rs_three, gain[2])
    cross_res = cot + part
    cross_low = cross_res.astype(BF16)
    d_mixed = mm_nt(cross_low, wb[:, LANE_CO : LANE_CO + 768]).astype(BF16)
    dob[...] = d_mixed
    prod = d_mixed.astype(F32) * cross
    delta = jnp.zeros((SUFFIX, 128), F32)
    for t in range(6):
        tile = prod[:, 128 * t : 128 * (t + 1)]
        left = jnp.sum(jnp.where(lane_c < HEAD_DIM, tile, 0.0), axis=-1, keepdims=True)
        right = jnp.sum(jnp.where(lane_c < HEAD_DIM, 0.0, tile), axis=-1, keepdims=True)
        delta = jnp.where(lane_c == 2 * t, left, delta)
        delta = jnp.where(lane_c == 2 * t + 1, right, delta)
    dstat_b[0] = lse
    dstat_b[1] = delta
    to_holders(d_pairs)

    down = jnp.zeros((SUFFIX, D), F32)
    for j in range(4):
        down = down + mm(
            jnp.concatenate(act_unit(j), axis=1), wb[:, LANE_FO + 768 * j : LANE_FO + 768 * (j + 1)]
        )
    ob[me, 0:SUFFIX] = after_cross + down

    def unit_device(u):
        return 2 * u + 1 if u < 8 else 2 * (u - 8)

    unit_items = []

    def push_unit(u, left_parts, right):
        to = unit_device(u)
        for col in range(columns):
            at = u * columns + col
            sb[at, :, 0:half_rows] = left_parts[col]
            sb[at, :, half_rows : half_rows + D] = right
            self_hit = (me == to) & (f == col)
            row = pl.multiple_of(lin * SUFFIX, SUFFIX)

            @pl.when(self_hit)
            def _():
                rb[pl.ds(row, SUFFIX)] = sb[at]

            @pl.when(jnp.logical_not(self_hit))
            def _():
                pltpu.make_async_remote_copy(
                    src_ref=sb.at[at], dst_ref=rb.at[pl.ds(row, SUFFIX)], send_sem=usend.at[at],
                    recv_sem=urecv.at[lin], device_id=(to, col), device_id_type=MESH,
                ).start()

            unit_items.append((at, to, col))

    def halves(value):
        return [value[:, i * half_rows : (i + 1) * half_rows] for i in range(columns)]

    for j in range(4):
        push_unit(8 + j, halves(n3), up_grads[j])
        push_unit(12 + j, act_unit(j), out_low)
    push_unit(7, halves(cm), cross_low)

    at_holders(d_pairs)
    to_holders_sent(d_pairs)

    doh = jnp.concatenate([dobuf[s] for s in range(SLOTS)], axis=0)
    for g in range(3):
        sl = slice(256 * g, 256 * g + 256)
        kg = kvb[:, sl]
        vg = kvb[:, 768 + 256 * g : 1024 + 256 * g]
        q4 = stack(qh[:, sl])
        do4 = stack(doh[:, sl])
        lse_col = jnp.concatenate([dstat[n, 0][:, 4 * g + h : 4 * g + h + 1] for h in range(4) for n in range(SLOTS)], axis=0)
        del_col = jnp.concatenate([dstat[n, 1][:, 4 * g + h : 4 * g + h + 1] for h in range(4) for n in range(SLOTS)], axis=0)
        s = mm_nt(q4, kg)
        p = jnp.where(allowed, jnp.exp(jnp.where(allowed, s - lse_col, 0.0)), 0.0)
        dp = mm_nt(do4, vg)
        ds = (p * (dp - del_col)).astype(BF16)
        kvg[:, 768 + 256 * g : 1024 + 256 * g] = mm_tn(p.astype(BF16), do4).astype(BF16)
        kvg[:, sl] = mm_tn(ds, q4).astype(BF16)
        dq = unstack(mm(ds, kg)) * scale
        for n in range(SLOTS):
            dqsend[n, :, sl] = dq[n * SUFFIX : (n + 1) * SUFFIX]
    to_owners(dq_pairs)

    def kp_step(i, carry):
        lane = pl.multiple_of(i * 256, 256)
        kp[:, pl.ds(lane, 256)] = mm_tn(memp[...], kvg[:, pl.ds(lane, 256)]).astype(BF16)
        return carry

    lax.fori_loop(0, 6, kp_step, 0)
    mate = (z * 4 + x * 2 + (1 - c), f)
    kr_item = pltpu.make_async_remote_copy(
        src_ref=kp.at[pl.ds(pl.multiple_of((1 - c) * half_rows, 128), half_rows)], dst_ref=kr,
        send_sem=ksend.at[2 * chips], recv_sem=krecv.at[2 * chips], device_id=mate, device_id_type=MESH,
    )
    kr_item.start()

    at_owners(dq_pairs)
    to_owners_sent(dq_pairs)
    cqg = (dqbuf[0] + dqbuf[1] + dqbuf[2]).astype(BF16)
    n2_grad = mm_nt(cqg, wb[:, LANE_CQ : LANE_CQ + 768])
    part, cross_gain_grad = norm_back(n2_grad, hat_two, rs_two, gain[1])
    self_res = cross_res + part
    self_low = self_res.astype(BF16)
    push_unit(4, halves(n2), cqg)
    push_unit(3, halves(sm), self_low)
    dmix = mm_nt(self_low, wb[:, LANE_SO : LANE_SO + 768]).astype(BF16)
    dqs, dks, dvs = [], [], []
    for g in range(3):
        sl = slice(256 * g, 256 * g + 256)
        q4 = stack(qs[:, sl])
        do4 = stack(dmix[:, sl])
        p = self_p[g]
        dp = mm_nt(do4, v[:, sl])
        ds = (p * (dp - jnp.sum(p * dp, axis=-1, keepdims=True))).astype(BF16)
        dvs.append(mm_tn(p.astype(BF16), do4))
        dks.append(mm_tn(ds, q4))
        dqs.append(unstack(mm(ds, k[:, sl])) * scale)
    packed_grad = [jnp.concatenate(parts, axis=1).astype(BF16) for parts in (dqs, dks, dvs)]
    n1_grad = jnp.zeros((SUFFIX, D), F32)
    for j in range(3):
        push_unit(j, halves(n1), packed_grad[j])
    for j in range(3):
        n1_grad = n1_grad + mm_nt(packed_grad[j], wb[:, 768 * j : 768 * (j + 1)])
    part, self_gain_grad = norm_back(n1_grad, hat_one, rs_one, gain[0])
    ob[me, SUFFIX : 2 * SUFFIX] = self_res + part
    gmine[...] = jnp.concatenate(
        [self_gain_grad, cross_gain_grad, ffn_gain_grad, jnp.zeros((5, D), F32)], axis=0
    )
    g_item = pltpu.make_async_remote_copy(
        src_ref=gmine, dst_ref=gpeer, send_sem=ysend.at[4], recv_sem=yrecv.at[4],
        device_id=(me, other), device_id_type=MESH,
    )
    g_item.start()

    kr_item.wait_recv()
    kc[...] = (
        kp[pl.ds(pl.multiple_of(c * half_rows, 128), half_rows)].astype(F32) + kr[...].astype(F32)
    ).astype(BF16)
    k_items = []
    for t in range(chips):
        for j in range(CORES):
            at = t * CORES + j
            self_hit = (f == c) & (chip == t) & (c == j)
            src = kc.at[pl.ds(t * slab, slab), pl.ds(j * D, D)]
            slot = f * chips + chip

            @pl.when(self_hit)
            def _():
                cp[slot] = kc[pl.ds(t * slab, slab), pl.ds(j * D, D)]

            @pl.when(jnp.logical_not(self_hit))
            def _():
                pltpu.make_async_remote_copy(
                    src_ref=src, dst_ref=cp.at[slot], send_sem=ksend.at[at], recv_sem=krecv.at[slot],
                    device_id=(t * CORES + j, c), device_id_type=MESH,
                ).start()

            k_items.append((at, src, self_hit))

    g_item.wait_recv()
    ob[me, 2 * SUFFIX : 2 * SUFFIX + 8] = gmine[...] + gpeer[...]
    ag_o = Gather(place, lambda zz, xx, cc, part: ob.at[zz * 4 + xx * 2 + cc] if part is None else ob.at[zz * 4 + xx * 2 + cc, :, pl.ds(*part)], D, sems, 5)
    ag_o.step_one()

    unit = jnp.where(c == 1, chip, chip + 8)
    has_unit = (unit != KV_UNITS[0]) & (unit != KV_UNITS[1])

    def unit_lane(zz, xx, cc):
        n = zz * SIDE + xx
        u = jnp.where(cc == 1, n, n + 8)
        spare = (u == KV_UNITS[0]) | (u == KV_UNITS[1])
        return jnp.where(spare, UNITS + u - KV_UNITS[0], u) * D

    @pl.when(has_unit)
    def _():
        def take(i, carry):
            @pl.when(i != lin)
            def _():
                pltpu.make_async_remote_copy(
                    src_ref=sb.at[0], dst_ref=rb.at[pl.ds(pl.multiple_of(i * SUFFIX, SUFFIX), SUFFIX)],
                    send_sem=usend.at[0], recv_sem=urecv.at[i], device_id=mate, device_id_type=MESH,
                ).wait_recv()
            return carry

        lax.fori_loop(0, everyone, take, 0)

        def sum_step(i, carry):
            lane = pl.multiple_of(i * 256, 256)
            total = mm_tn(rb[:, 0:half_rows], rb[:, pl.ds(half_rows + lane, 256)])
            gb[:, pl.ds(pl.multiple_of(unit_lane(z, x, c) + lane, 256), 256)] = total.astype(BF16)
            return carry

        lax.fori_loop(0, 3, sum_step, 0)

    @pl.when(jnp.logical_not(has_unit))
    def _():
        gb[:, pl.ds(pl.multiple_of(unit_lane(z, x, c), 256), D)] = jnp.zeros((half_rows, D), BF16)

    def unit_view(zz, xx, cc, part):
        low, size = part if part is not None else (0, D)
        return gb.at[:, pl.ds(pl.multiple_of(unit_lane(zz, xx, cc) + low, 128), size)]

    ag_g = Gather(place, unit_view, D, sems, 6)
    ag_g.step_one()

    def take_k(i, carry):
        @pl.when((i != f * chips + chip) | (c != f))
        def _():
            pltpu.make_async_remote_copy(
                src_ref=kc.at[pl.ds(0, slab), pl.ds(0, D)], dst_ref=cp.at[i], send_sem=ksend.at[0],
                recv_sem=krecv.at[i], device_id=mate, device_id_type=MESH,
            ).wait_recv()
        return carry

    lax.fori_loop(0, 2 * chips, take_k, 0)
    total = cp[0].astype(F32)
    for i in range(1, 2 * chips):
        total = total + cp[i].astype(F32)
    k_lane = pl.multiple_of(LANE_CKV + c * D, 128)
    gb[pl.ds(pl.multiple_of(chip * slab, 16), slab), pl.ds(k_lane, D)] = total.astype(BF16)

    def kv_view(zz, xx, cc, part):
        low, size = part if part is not None else (0, D)
        row = pl.multiple_of((zz * SIDE + xx) * slab, 16)
        return gb.at[pl.ds(row, slab), pl.ds(pl.multiple_of(LANE_CKV + cc * D + low, 128), size)]

    ag_k = Gather(place, kv_view, D, sems, 7)
    ag_k.step_one()
    ag_o.step_two()
    ag_k.step_two()
    ag_o.step_three()
    ag_k.step_three()
    ag_o.step_four()
    ag_k.step_four()
    ag_g.step_two()

    def mg_step(i, carry):
        row = pl.multiple_of(i * 128, 128)
        memgrad_ref[pl.ds(row, 128)] = mm_nt(kvg[pl.ds(row, 128)], wb[:, LANE_CKV : LANE_CKV + 2 * D])
        return carry

    full = own_rows // 128
    lax.fori_loop(0, full, mg_step, 0)
    if own_rows % 128:
        tail = mm_nt(kvg[full * 128 : (full + 1) * 128], wb[:, LANE_CKV : LANE_CKV + 2 * D])
        memgrad_ref[full * 128 : own_rows] = tail[0 : own_rows - full * 128]

    mine_rank = rank_of_example(me)
    out_ref[...] = ob[mine_rank, 0:SUFFIX]
    grad_ref[...] = ob[mine_rank, SUFFIX : 2 * SUFFIX]
    gains_all = ob[0, 2 * SUFFIX : 2 * SUFFIX + 8]
    for i in range(1, ranks):
        gains_all = gains_all + ob[i, 2 * SUFFIX : 2 * SUFFIX + 8]
    own_gain = gains_all[:, 0:half_rows]
    for i in range(1, columns):
        own_gain = jnp.where(f == i, gains_all[:, i * half_rows : (i + 1) * half_rows], own_gain)
    gain_out_ref[...] = own_gain

    ag_g.step_three()
    ag_g.step_four()
    done = pltpu.make_async_copy(gb.at[:, pl.ds(0, UNITS * D)], weights_out_ref, load_sem.at[0])
    done.start()

    for at, to, col in unit_items:
        @pl.when(jnp.logical_not((me == to) & (f == col)))
        def _():
            pltpu.make_async_remote_copy(
                src_ref=sb.at[at], dst_ref=rb.at[pl.ds(0, SUFFIX)], send_sem=usend.at[at],
                recv_sem=urecv.at[0], device_id=(to, col), device_id_type=MESH,
            ).wait_send()
    for at, src, self_hit in k_items:
        @pl.when(jnp.logical_not(self_hit))
        def _():
            pltpu.make_async_remote_copy(
                src_ref=src, dst_ref=cp.at[0], send_sem=ksend.at[at], recv_sem=krecv.at[0],
                device_id=mate, device_id_type=MESH,
            ).wait_send()
    kr_item.wait_send()
    for item in y_items + [g_item]:
        item.wait_send()
    for item in [ag_x, *ag_w, ag_c, ag_o, ag_g, ag_k]:
        item.finish()
    done.wait()


def fused_body(
    ranks, columns,
    decoder_in, memory, res_group, prefix_len, self_gain, self_qkv, self_out, cross_gain, cross_query,
    cross_kv, cross_out, ffn_gain, ffn_in, ffn_out, cotangent,
):
    half_rows = D // columns
    chips = ranks // CORES
    slab = half_rows // chips
    own_rows = memory.shape[1]
    padded = -(-own_rows // 128) * 128
    everyone = ranks * columns
    gains = jnp.stack([self_gain, cross_gain, ffn_gain]).astype(F32)
    gains = jnp.pad(gains, ((0, 5), (0, 0)))
    vm = pl.BlockSpec(memory_space=pltpu.VMEM)
    sm = pl.BlockSpec(memory_space=pltpu.SMEM)
    hbm = pl.BlockSpec(memory_space=pl.ANY)
    dma = pltpu.SemaphoreType.DMA
    scratch = [
        pltpu.VMEM((D, UNITS * D), BF16),
        pltpu.VMEM((half_rows, (UNITS + 2) * D), BF16),
        pltpu.VMEM((everyone * SUFFIX, half_rows + D), BF16),
        pltpu.VMEM((UNITS * columns, SUFFIX, half_rows + D), BF16),
        pltpu.VMEM((ranks, SUFFIX + 8, D), F32),
        pltpu.VMEM((ranks, SUFFIX, D), F32),
        pltpu.VMEM((ranks, 2 * SUFFIX + 8, D), F32),
        pltpu.VMEM((columns, 8, half_rows), F32),
        pltpu.VMEM((padded, D), BF16),
        pltpu.VMEM((padded, 2 * D), BF16),
        pltpu.VMEM((padded, 2 * D), BF16),
        pltpu.VMEM((D, 2 * D), BF16),
        pltpu.VMEM((half_rows, 2 * D), BF16),
        pltpu.VMEM((half_rows, 2 * D), BF16),
        pltpu.VMEM((columns * chips, slab, D), BF16),
        pltpu.VMEM((SUFFIX, D), BF16),
        pltpu.VMEM((SLOTS, SUFFIX, D), BF16),
        pltpu.VMEM((SLOTS, SUFFIX, D), BF16),
        pltpu.VMEM((SLOTS, 2, SUFFIX, 128), F32),
        pltpu.VMEM((SLOTS, SUFFIX, D), BF16),
        pltpu.VMEM((SLOTS, 2, SUFFIX, 128), F32),
        pltpu.VMEM((SUFFIX, D), BF16),
        pltpu.VMEM((2, SUFFIX, 128), F32),
        pltpu.VMEM((SLOTS, SUFFIX, D), BF16),
        pltpu.VMEM((SLOTS, 2, SUFFIX, 128), F32),
        pltpu.VMEM((SLOTS, SUFFIX, D), F32),
        pltpu.VMEM((SLOTS, SUFFIX, D), F32),
        pltpu.VMEM((8, D), F32),
        pltpu.VMEM((8, D), F32),
        dma((10,)),
        dma((8, 16)),
        dma((8, 16)),
        dma((5,)),
        dma((5,)),
        dma((6, SLOTS)),
        dma((6, SLOTS)),
        dma((UNITS * columns,)),
        dma((everyone,)),
        dma((2 * chips + 1,)),
        dma((2 * chips + 1,)),
    ]
    out, grad, memgrad, gain_grads, weight_grads = pl.pallas_call(
        partial(layer_kernel, ranks, columns),
        out_shape=(
            jax.ShapeDtypeStruct((SUFFIX, D), F32),
            jax.ShapeDtypeStruct((SUFFIX, D), F32),
            jax.ShapeDtypeStruct((own_rows, D), F32),
            jax.ShapeDtypeStruct((8, half_rows), F32),
            jax.ShapeDtypeStruct((half_rows, UNITS * D), BF16),
        ),
        in_specs=[vm, vm, vm, sm, sm, vm] + [hbm] * 7,
        out_specs=(vm, vm, vm, vm, hbm),
        scratch_shapes=scratch,
        compiler_params=pltpu.CompilerParams(
            collective_id=0, has_side_effects=True, vmem_limit_bytes=62 * 2**20
        ),
        name="layer",
    )(
        decoder_in[0], cotangent[0], memory[0], res_group, prefix_len, gains,
        self_qkv, self_out, cross_query, cross_kv, cross_out, ffn_in, ffn_out,
    )

    def lanes(low, width):
        return weight_grads[:, low : low + width].astype(F32)

    ffn_out_grad = jnp.concatenate([lanes(LANE_FO + D * j, D) for j in range(4)], axis=0)
    return (
        out[None], grad[None], memgrad[None],
        gain_grads[0], lanes(LANE_QKV, 3 * D), lanes(LANE_SO, D),
        gain_grads[1], lanes(LANE_CQ, D), lanes(LANE_CKV, 2 * D), lanes(LANE_CO, D),
        gain_grads[2], lanes(LANE_FI, 4 * D), ffn_out_grad,
    )


def layer_norm(value, gain):
    mean = jnp.mean(value, axis=-1, keepdims=True)
    centred = value - mean
    variance = jnp.mean(centred * centred, axis=-1, keepdims=True)
    return centred * lax.rsqrt(variance + norm_eps) * gain


def product(left, right):
    return jnp.dot(left, right, preferred_element_type=jnp.float32)


def outer_sum(left, right):
    flat_left = left.reshape(-1, left.shape[-1])
    flat_right = right.reshape(-1, right.shape[-1])
    return lax.dot_general(
        flat_left, flat_right, (((0,), (0,)), ((), ())), preferred_element_type=jnp.float32
    )


def back_product(grad, weight):
    return lax.dot_general(
        grad, weight, (((grad.ndim - 1,), (1,)), ((), ())), preferred_element_type=jnp.float32
    )


def attend(query, keys, values, allowed, scale):
    scores = jnp.einsum("eqhd,ekhd->ehqk", query, keys, preferred_element_type=jnp.float32) * scale
    scores = jnp.where(allowed[:, None], scores, -1e30)
    top = jnp.max(scores, axis=-1, keepdims=True)
    weights = jnp.exp(scores - top)
    probs = weights / jnp.sum(weights, axis=-1, keepdims=True)
    mixed = jnp.einsum(
        "ehqk,ekhd->eqhd", probs.astype(jnp.bfloat16), values, preferred_element_type=jnp.float32
    )
    return (mixed.astype(jnp.bfloat16), probs)


def attend_back(grad_mixed, query, keys, values, probs, scale):
    probs_low = probs.astype(jnp.bfloat16)
    grad_values = jnp.einsum(
        "ehqk,eqhd->ekhd", probs_low, grad_mixed, preferred_element_type=jnp.float32
    )
    grad_probs = jnp.einsum(
        "eqhd,ekhd->ehqk", grad_mixed, values, preferred_element_type=jnp.float32
    )
    grad_scores = probs * (grad_probs - jnp.sum(probs * grad_probs, axis=-1, keepdims=True))
    grad_low = grad_scores.astype(jnp.bfloat16)
    grad_query = (
        jnp.einsum("ehqk,ekhd->eqhd", grad_low, keys, preferred_element_type=jnp.float32) * scale
    )
    grad_keys = (
        jnp.einsum("ehqk,eqhd->ekhd", grad_low, query, preferred_element_type=jnp.float32) * scale
    )
    return (grad_query, grad_keys, grad_values)


def window_layout(res_group, mem_col):
    small = 1 - res_group
    small_count = jnp.sum(small, axis=-1, keepdims=True)
    small_before = jnp.cumsum(small, axis=-1) - small
    large_before = jnp.cumsum(res_group, axis=-1) - res_group
    offset = jnp.where(
        res_group == 1, SLOT_S * small_count + SLOT_L * large_before, SLOT_S * small_before
    )
    start = jnp.minimum(offset, mem_col - SLOT_L)
    return (offset, start)


def take_windows(column, starts):
    return jax.vmap(lambda begin: lax.dynamic_slice_in_dim(column, begin, SLOT_L, 0))(starts)


def forward(decoder_rows, windows, cross_allowed, weights):
    (
        self_gain,
        self_qkv,
        self_out,
        cross_gain,
        cross_query,
        cross_kv,
        cross_out,
        ffn_gain,
        ffn_in,
        ffn_out,
    ) = weights
    count = decoder_rows.shape[0] // SUFFIX
    scale = HEAD_DIM ** (-0.5)
    row_index = lax.broadcasted_iota(jnp.int32, (SUFFIX, SUFFIX), 0)
    col_index = lax.broadcasted_iota(jnp.int32, (SUFFIX, SUFFIX), 1)
    causal = (row_index >= col_index)[None]
    resid = decoder_rows.reshape(count, SUFFIX, D)
    normed_one = layer_norm(resid, self_gain.astype(jnp.float32)).astype(jnp.bfloat16)
    packed = product(normed_one, self_qkv).astype(jnp.bfloat16)
    heads = packed.reshape(count, SUFFIX, 3, HEADS, HEAD_DIM)
    self_mixed, self_probs = attend(heads[:, :, 0], heads[:, :, 1], heads[:, :, 2], causal, scale)
    self_mixed = self_mixed.reshape(count, SUFFIX, D)
    after_self = resid + product(self_mixed, self_out)
    normed_two = layer_norm(after_self, cross_gain.astype(jnp.float32)).astype(jnp.bfloat16)
    cross_q = product(normed_two, cross_query).astype(jnp.bfloat16)
    window_kv = product(windows, cross_kv).astype(jnp.bfloat16)
    query_heads = cross_q.reshape(count, SUFFIX, HEADS, HEAD_DIM)
    kv_heads = window_kv.reshape(count, SLOT_L, 2, HEADS, HEAD_DIM)
    cross_mixed, cross_probs = attend(
        query_heads, kv_heads[:, :, 0], kv_heads[:, :, 1], cross_allowed, scale
    )
    cross_mixed = cross_mixed.reshape(count, SUFFIX, D)
    after_cross = after_self + product(cross_mixed, cross_out)
    normed_three = layer_norm(after_cross, ffn_gain.astype(jnp.float32)).astype(jnp.bfloat16)
    up = product(normed_three, ffn_in)
    act = jax.nn.gelu(up, approximate=True).astype(jnp.bfloat16)
    result = after_cross + product(act, ffn_out)
    return (
        resid,
        normed_one,
        packed,
        self_probs,
        self_mixed,
        after_self,
        normed_two,
        cross_q,
        window_kv,
        cross_probs,
        cross_mixed,
        after_cross,
        normed_three,
        up,
        act,
        result,
    )


def backward(grad_out, saved, weights):
    (
        self_gain,
        self_qkv,
        self_out,
        cross_gain,
        cross_query,
        cross_kv,
        cross_out,
        ffn_gain,
        ffn_in,
        ffn_out,
    ) = weights
    (
        resid,
        normed_one,
        packed,
        self_probs,
        self_mixed,
        after_self,
        normed_two,
        cross_q,
        window_kv,
        cross_probs,
        cross_mixed,
        after_cross,
        normed_three,
        up,
        act,
        result,
    ) = saved
    count = resid.shape[0]
    scale = HEAD_DIM ** (-0.5)
    grad_out = grad_out.reshape(count, SUFFIX, D)
    out_low = grad_out.astype(jnp.bfloat16)
    ffn_out_grad = outer_sum(act, out_low)
    act_grad = back_product(out_low, ffn_out)
    gelu_value, gelu_back = jax.vjp(partial(jax.nn.gelu, approximate=True), up)
    up_grad = gelu_back(act_grad)[0].astype(jnp.bfloat16)
    ffn_in_grad = outer_sum(normed_three, up_grad)
    normed_three_grad = back_product(up_grad, ffn_in)
    norm_value, norm_back = jax.vjp(layer_norm, after_cross, ffn_gain.astype(jnp.float32))
    resid_part, ffn_gain_grad = norm_back(normed_three_grad)
    cross_res_grad = grad_out + resid_part
    cross_low = cross_res_grad.astype(jnp.bfloat16)
    cross_out_grad = outer_sum(cross_mixed, cross_low)
    mixed_grad = (
        back_product(cross_low, cross_out)
        .astype(jnp.bfloat16)
        .reshape(count, SUFFIX, HEADS, HEAD_DIM)
    )
    query_heads = cross_q.reshape(count, SUFFIX, HEADS, HEAD_DIM)
    kv_heads = window_kv.reshape(count, SLOT_L, 2, HEADS, HEAD_DIM)
    query_grad, keys_grad, values_grad = attend_back(
        mixed_grad, query_heads, kv_heads[:, :, 0], kv_heads[:, :, 1], cross_probs, scale
    )
    cross_q_grad = query_grad.reshape(count, SUFFIX, D).astype(jnp.bfloat16)
    window_kv_grad = (
        jnp.stack((keys_grad, values_grad), axis=2)
        .reshape(count, SLOT_L, 2 * D)
        .astype(jnp.bfloat16)
    )
    cross_query_grad = outer_sum(normed_two, cross_q_grad)
    normed_two_grad = back_product(cross_q_grad, cross_query)
    norm_value, norm_back = jax.vjp(layer_norm, after_self, cross_gain.astype(jnp.float32))
    resid_part, cross_gain_grad = norm_back(normed_two_grad)
    self_res_grad = cross_res_grad + resid_part
    self_low = self_res_grad.astype(jnp.bfloat16)
    self_out_grad = outer_sum(self_mixed, self_low)
    mixed_grad = (
        back_product(self_low, self_out)
        .astype(jnp.bfloat16)
        .reshape(count, SUFFIX, HEADS, HEAD_DIM)
    )
    heads = packed.reshape(count, SUFFIX, 3, HEADS, HEAD_DIM)
    query_grad, keys_grad, values_grad = attend_back(
        mixed_grad, heads[:, :, 0], heads[:, :, 1], heads[:, :, 2], self_probs, scale
    )
    packed_grad = (
        jnp.stack((query_grad, keys_grad, values_grad), axis=2)
        .reshape(count, SUFFIX, 3 * D)
        .astype(jnp.bfloat16)
    )
    self_qkv_grad = outer_sum(normed_one, packed_grad)
    normed_one_grad = back_product(packed_grad, self_qkv)
    norm_value, norm_back = jax.vjp(layer_norm, resid, self_gain.astype(jnp.float32))
    resid_part, self_gain_grad = norm_back(normed_one_grad)
    decoder_grad = self_res_grad + resid_part
    weight_grads = (
        self_gain_grad,
        self_qkv_grad,
        self_out_grad,
        cross_gain_grad,
        cross_query_grad,
        cross_out_grad,
        ffn_gain_grad,
        ffn_in_grad,
        ffn_out_grad,
    )
    return (decoder_grad, window_kv_grad, weight_grads)


def make_placer(all_starts, lowest, own_rows):

    def place(total, piece, begin):

        def add_one(item, acc):
            relative = all_starts[item] - lowest
            inside = ((relative > -SLOT_L) & (relative < own_rows)).astype(jnp.float32)
            spot = jnp.clip(relative + SLOT_L, 0, own_rows + SLOT_L)
            current = lax.dynamic_slice_in_dim(acc, spot, SLOT_L, 0)
            added = current + piece[item].astype(jnp.float32) * inside
            return lax.dynamic_update_slice_in_dim(acc, added, spot, 0)

        return lax.fori_loop(0, piece.shape[0], add_one, total)

    return place


def body(
    decoder_in,
    memory,
    res_group,
    prefix_len,
    self_gain,
    self_qkv,
    self_out,
    cross_gain,
    cross_query,
    cross_kv,
    cross_out,
    ffn_gain,
    ffn_in,
    ffn_out,
    cotangent,
):
    count = prefix_len.shape[1]
    own_rows = memory.shape[1]
    mem_col = own_rows * lax.axis_size("dp")
    offset, start = window_layout(res_group, mem_col)
    all_starts = start[0]
    first = lax.axis_index("dp") * count
    own_offset = lax.dynamic_slice_in_dim(offset[0], first, count)
    own_start = lax.dynamic_slice_in_dim(all_starts, first, count)
    own_group = lax.dynamic_slice_in_dim(res_group[0], first, count)
    valid = jnp.where(own_group == 1, PATCH_L, PATCH_S) + prefix_len[0]
    positions = own_start[:, None] + jnp.arange(SLOT_L, dtype=jnp.int32)[None]
    cross_allowed = (
        (positions >= own_offset[:, None]) & (positions < (own_offset + valid)[:, None])
    )[:, None]
    weights = (
        lax.all_gather(self_gain, "fsdp", axis=0, tiled=True),
        lax.all_gather(self_qkv, "fsdp", axis=0, tiled=True),
        lax.all_gather(self_out, "fsdp", axis=0, tiled=True),
        lax.all_gather(cross_gain, "fsdp", axis=0, tiled=True),
        lax.all_gather(cross_query, "fsdp", axis=0, tiled=True),
        lax.all_gather(cross_kv, "fsdp", axis=0, tiled=True),
        lax.all_gather(cross_out, "fsdp", axis=0, tiled=True),
        lax.all_gather(ffn_gain, "fsdp", axis=0, tiled=True),
        lax.all_gather(ffn_in, "fsdp", axis=0, tiled=True),
        lax.all_gather(ffn_out, "fsdp", axis=0, tiled=True),
    )
    column = lax.all_gather(memory[0], "dp", axis=0, tiled=True)
    windows = take_windows(column, own_start)
    saved = forward(decoder_in[0], windows, cross_allowed, weights)
    decoder_out = saved[-1]
    weights = (
        lax.all_gather(self_gain, "fsdp", axis=0, tiled=True),
        lax.all_gather(self_qkv, "fsdp", axis=0, tiled=True),
        lax.all_gather(self_out, "fsdp", axis=0, tiled=True),
        lax.all_gather(cross_gain, "fsdp", axis=0, tiled=True),
        lax.all_gather(cross_query, "fsdp", axis=0, tiled=True),
        lax.all_gather(cross_kv, "fsdp", axis=0, tiled=True),
        lax.all_gather(cross_out, "fsdp", axis=0, tiled=True),
        lax.all_gather(ffn_gain, "fsdp", axis=0, tiled=True),
        lax.all_gather(ffn_in, "fsdp", axis=0, tiled=True),
        lax.all_gather(ffn_out, "fsdp", axis=0, tiled=True),
    )
    column = lax.all_gather(memory[0], "dp", axis=0, tiled=True)
    windows = take_windows(column, own_start)
    saved = forward(decoder_in[0], windows, cross_allowed, weights)
    whole_kv = weights[5]
    decoder_grad, window_kv_grad, local_grads = backward(cotangent[0], saved, weights)
    lowest = lax.axis_index("dp") * own_rows
    place = make_placer(all_starts, lowest, own_rows)
    empty = jnp.zeros((own_rows + 2 * SLOT_L, 2 * D), jnp.float32)
    summed = place(empty, lax.all_gather(window_kv_grad, "dp", axis=0, tiled=True), jnp.int32(0))
    own_kv_grad = summed[SLOT_L : SLOT_L + own_rows].astype(jnp.bfloat16)
    memory_grad = back_product(own_kv_grad, whole_kv)
    cross_kv_part = outer_sum(memory[0], own_kv_grad)
    grads = (
        local_grads[0],
        local_grads[1],
        local_grads[2],
        local_grads[3],
        local_grads[4],
        cross_kv_part,
        local_grads[5],
        local_grads[6],
        local_grads[7],
        local_grads[8],
    )
    shards = (
        lax.psum_scatter(
            grads[0].astype(jnp.bfloat16), "fsdp", scatter_dimension=0, tiled=True
        ).astype(jnp.float32),
        lax.psum_scatter(
            grads[1].astype(jnp.bfloat16), "fsdp", scatter_dimension=0, tiled=True
        ).astype(jnp.float32),
        lax.psum_scatter(
            grads[2].astype(jnp.bfloat16), "fsdp", scatter_dimension=0, tiled=True
        ).astype(jnp.float32),
        lax.psum_scatter(
            grads[3].astype(jnp.bfloat16), "fsdp", scatter_dimension=0, tiled=True
        ).astype(jnp.float32),
        lax.psum_scatter(
            grads[4].astype(jnp.bfloat16), "fsdp", scatter_dimension=0, tiled=True
        ).astype(jnp.float32),
        lax.psum_scatter(
            grads[5].astype(jnp.bfloat16), "fsdp", scatter_dimension=0, tiled=True
        ).astype(jnp.float32),
        lax.psum_scatter(
            grads[6].astype(jnp.bfloat16), "fsdp", scatter_dimension=0, tiled=True
        ).astype(jnp.float32),
        lax.psum_scatter(
            grads[7].astype(jnp.bfloat16), "fsdp", scatter_dimension=0, tiled=True
        ).astype(jnp.float32),
        lax.psum_scatter(
            grads[8].astype(jnp.bfloat16), "fsdp", scatter_dimension=0, tiled=True
        ).astype(jnp.float32),
        lax.psum_scatter(
            grads[9].astype(jnp.bfloat16), "fsdp", scatter_dimension=0, tiled=True
        ).astype(jnp.float32),
    )
    totals = (
        lax.psum(shards[0].astype(jnp.bfloat16), "dp").astype(jnp.float32),
        lax.psum(shards[1].astype(jnp.bfloat16), "dp").astype(jnp.float32),
        lax.psum(shards[2].astype(jnp.bfloat16), "dp").astype(jnp.float32),
        lax.psum(shards[3].astype(jnp.bfloat16), "dp").astype(jnp.float32),
        lax.psum(shards[4].astype(jnp.bfloat16), "dp").astype(jnp.float32),
        lax.psum(shards[5].astype(jnp.bfloat16), "dp").astype(jnp.float32),
        lax.psum(shards[6].astype(jnp.bfloat16), "dp").astype(jnp.float32),
        lax.psum(shards[7].astype(jnp.bfloat16), "dp").astype(jnp.float32),
        lax.psum(shards[8].astype(jnp.bfloat16), "dp").astype(jnp.float32),
        lax.psum(shards[9].astype(jnp.bfloat16), "dp").astype(jnp.float32),
    )
    return (
        decoder_out,
        decoder_grad,
        memory_grad[None],
        totals[0],
        totals[1],
        totals[2],
        totals[3],
        totals[4],
        totals[5],
        totals[6],
        totals[7],
        totals[8],
        totals[9],
    )


def choose(mesh):
    ranks, columns = mesh.shape["dp"], mesh.shape["fsdp"]
    slabs = (D // columns) % (16 * (ranks // CORES)) == 0
    if slabs and columns == 2 and ranks == RING * SIDE * CORES:
        return partial(fused_body, ranks, columns)
    return body


def solution(mesh):
    placed = (
        P("fsdp", "dp", None),
        P("fsdp", "dp", None),
        P("fsdp", None),
        P("fsdp", "dp"),
        P("fsdp"),
        P("fsdp", None),
        P("fsdp", None),
        P("fsdp"),
        P("fsdp", None),
        P("fsdp", None),
        P("fsdp", None),
        P("fsdp"),
        P("fsdp", None),
        P("fsdp", None),
        P("fsdp", "dp", None),
    )
    return jax.shard_map(
        choose(mesh),
        mesh=mesh,
        in_specs=placed,
        out_specs=(
            P("fsdp", "dp", None),
            P("fsdp", "dp", None),
            P("fsdp", "dp", None),
            P("fsdp"),
            P("fsdp", None),
            P("fsdp", None),
            P("fsdp"),
            P("fsdp", None),
            P("fsdp", None),
            P("fsdp", None),
            P("fsdp"),
            P("fsdp", None),
            P("fsdp", None),
        ),
        check_vma=False,
    )
```

```python
from functools import partial

import jax
import jax.numpy as jnp
from jax import lax
from jax.experimental import pallas as pl
from jax.experimental.pallas import tpu as pltpu
from jax.sharding import PartitionSpec as P

D = 768
HEADS = 12
HEAD_DIM = 64
SUFFIX = 32
PATCH_S = 196
PATCH_L = 576
SLOT_S = 228
SLOT_L = 608
RING = 4
SIDE = 2
CORES = 2
norm_eps = 1e-06
MESH = pl.DeviceIdType.MESH
F32 = jnp.float32
BF16 = jnp.bfloat16
NONE = -1e30


def mm(left, right):
    return jnp.dot(left, right, preferred_element_type=F32)


def mm_nt(left, right):
    return lax.dot_general(left, right, (((1,), (1,)), ((), ())), preferred_element_type=F32)


def mm_tn(left, right):
    return lax.dot_general(left, right, (((0,), (0,)), ((), ())), preferred_element_type=F32)


def normed(value):
    mean = jnp.mean(value, axis=-1, keepdims=True)
    centred = value - mean
    variance = jnp.mean(centred * centred, axis=-1, keepdims=True)
    scale = lax.rsqrt(variance + norm_eps)
    return centred * scale, scale


def norm_back(grad, hat, scale, gain):
    inner = grad * gain
    mean_one = jnp.mean(inner, axis=-1, keepdims=True)
    mean_two = jnp.mean(inner * hat, axis=-1, keepdims=True)
    gain_grad = jnp.sum(grad * hat, axis=0, keepdims=True)
    return scale * (inner - mean_one - hat * mean_two), gain_grad


def gelu_parts(up):
    inner = 0.7978845608 * (up + 0.044715 * up * up * up)
    tanh = jnp.tanh(inner)
    slope = 0.7978845608 * (1.0 + 3.0 * 0.044715 * up * up)
    value = 0.5 * up * (1.0 + tanh)
    grad = 0.5 * (1.0 + tanh) + 0.5 * up * (1.0 - tanh * tanh) * slope
    return value, grad


class Relay:
    def __init__(self, place, view, sems, at, has=None):
        self.z, self.x, self.c, self.f = place
        self.view = view
        self.send, self.recv = sems
        self.at = at
        self.has = has
        self.sent = []
        self.own = (self.z, self.x, self.c)
        self.side = (self.z, 1 - self.x, self.c)
        self.up = (lax.rem(self.z + 1, RING), self.x, self.c)
        self.down = (lax.rem(self.z + 3, RING), self.x, self.c)
        self.far = (lax.rem(self.z + 2, RING), self.x, self.c)
        self.up_side = (self.up[0], 1 - self.x, self.c)
        self.down_side = (self.down[0], 1 - self.x, self.c)
        self.far_side = (self.far[0], 1 - self.x, self.c)
        self.mate = (self.z, self.x, 1 - self.c)

    def when(self, block, act):
        if self.has is None:
            act()
        else:
            pl.when(self.has(*block))(act)

    def copy(self, block, part, target, into, index):
        ref = self.view(*block, part)
        z, x, c = target
        return pltpu.make_async_remote_copy(
            src_ref=ref,
            dst_ref=ref,
            send_sem=self.send.at[self.at, index],
            recv_sem=self.recv.at[self.at, into],
            device_id=(z * (SIDE * CORES) + x * CORES + c, self.f),
            device_id_type=MESH,
        )

    def go(self, block, target, into, part=None):
        item = self.copy(block, part, target, into, len(self.sent))
        self.when(block, item.start)
        self.sent.append((block, item))

    def wait(self, block, into, part=None):
        self.when(block, self.copy(block, part, self.side, into, 0).wait_recv)

    def finish(self):
        for block, item in self.sent:
            self.when(block, item.wait_send)


class Gather(Relay):
    def __init__(self, place, view, width, sems, at, has=None):
        super().__init__(place, view, sems, at, has)
        half = (width // 256) * 128
        self.parts = ((0, half), (half, width - half))

    def step_one(self):
        self.go(self.own, self.up, 1)
        self.go(self.own, self.down, 2)
        self.go(self.own, self.side, 0)
        self.go(self.own, self.mate, 8)

    def step_two(self):
        low, high = self.parts
        self.wait(self.down, 1)
        self.go(self.down, self.up, 3, low)
        self.wait(self.up, 2)
        self.go(self.up, self.down, 4, high)
        self.wait(self.side, 0)
        self.go(self.side, self.up, 5)
        self.go(self.side, self.down, 6)
        self.go(self.down, self.mate, 10)
        self.go(self.up, self.mate, 11)
        self.go(self.side, self.mate, 9)

    def step_three(self):
        low, high = self.parts
        self.wait(self.far, 3, low)
        self.wait(self.far, 4, high)
        self.go(self.far, self.side, 7)
        self.go(self.far, self.mate, 12)
        self.wait(self.down_side, 5)
        self.go(self.down_side, self.mate, 13)
        self.wait(self.up_side, 6)
        self.go(self.up_side, self.mate, 14)

    def step_four(self):
        self.wait(self.far_side, 7)
        self.go(self.far_side, self.mate, 15)

    def step_five(self):
        z, x, c = self.mate
        order = (self.own, self.side, self.down, self.up, self.far, self.down_side, self.up_side, self.far_side)
        for n, block in enumerate(order):
            self.wait((block[0], block[1], c), 8 + n)


class Spread(Relay):
    def __init__(self, place, theirs, mine, sems, at):
        super().__init__(place, theirs, sems, at)
        self.mine = mine
        self.columns_item = []

    def push(self):
        z, x, c = self.own
        for n, block in enumerate((self.own, self.far)):
            ref = self.mine(*block, None)
            item = pltpu.make_async_remote_copy(
                src_ref=ref, dst_ref=ref, send_sem=self.send.at[self.at, 14 + n], recv_sem=self.recv.at[self.at, 14 + n],
                device_id=(z * (SIDE * CORES) + x * CORES + c, 1 - self.f), device_id_type=MESH,
            )
            item.start()
            self.columns_item.append(item)

    def step_one(self):
        self.wait(self.own, 14)
        self.go(self.own, self.side, 0)
        self.go(self.own, self.up, 1)
        self.go(self.own, self.down, 2)
        self.go(self.own, self.mate, 6)
        self.wait(self.far, 15)
        self.go(self.far, self.side, 3)
        self.go(self.far, self.mate, 7)

    def step_two(self):
        self.wait(self.side, 0)
        self.go(self.side, self.up, 4)
        self.go(self.side, self.down, 5)
        self.go(self.side, self.mate, 8)
        self.wait(self.down, 1)
        self.go(self.down, self.mate, 9)
        self.wait(self.up, 2)
        self.go(self.up, self.mate, 10)

    def step_three(self):
        self.wait(self.far_side, 3)
        self.go(self.far_side, self.mate, 11)
        self.wait(self.down_side, 4)
        self.go(self.down_side, self.mate, 12)
        self.wait(self.up_side, 5)
        self.go(self.up_side, self.mate, 13)

    def step_four(self):
        c = self.mate[2]
        order = (self.own, self.far, self.side, self.down, self.up, self.far_side, self.down_side, self.up_side)
        for n, block in enumerate(order):
            self.wait((block[0], block[1], c), 6 + n)

    def finish(self):
        super().finish()
        for item in self.columns_item:
            item.wait_send()


class Pieces:
    def __init__(self, count, own_rows):
        self.half = count // 2
        self.edge = self.half * SLOT_S
        self.rows = own_rows
        self.count = count

    def start(self, rank):
        return jnp.where(
            rank < self.half, SLOT_S * rank, self.edge + SLOT_L * (rank - self.half)
        )

    def size(self, rank):
        return jnp.where(rank < self.half, SLOT_S, SLOT_L)

    def rank_of(self, row):
        return jnp.where(
            row < self.edge,
            lax.div(row, SLOT_S),
            self.half + lax.div(jnp.maximum(row - self.edge, 0), SLOT_L),
        )

    def first_rank(self, device):
        return self.rank_of(device * self.rows)

    def last_rank(self, device):
        return self.rank_of(device * self.rows + self.rows - 1)

    def first_device(self, rank):
        return lax.div(self.start(rank), self.rows)

    def last_device(self, rank):
        return lax.div(self.start(rank) + self.size(rank) - 1, self.rows)


SLOTS = 3
UNITS = 16
LANE_QKV, LANE_SO, LANE_CQ, LANE_CKV, LANE_CO, LANE_FI, LANE_FO = 0, 2304, 3072, 3840, 5376, 6144, 9216
CHUNKS = ((0, 2304), (2304, 1536), (3840, 1536), (5376, 2304), (7680, 2304), (9984, 2304))
LOADS_BY_CHUNK = ((0,), (1, 2), (3,), (4, 5), (6,), (7, 8, 9))
PIECE = 384
HALF_UNITS = 6


def layer_kernel(
    ranks,
    columns,
    x_ref, cot_ref, mem_ref, res_ref, pre_ref, gains_ref,
    qkv_ref, so_ref, cq_ref, ckv_ref, co_ref, fi_ref, fo_ref,
    out_ref, grad_ref, memgrad_ref, gain_out_ref, weights_out_ref,
    wb, gb, rb, sb, xb, cb, nb, olr, ob, tb, pb, gainb, memp, kvb, kvg, kp, kr, kc, ky, cp,
    hb, fg, fsend, frecv, ug, usend_b, urecv_b,
    cqb, qbuf, osend, ostat_send, obuf, ostat, dob, dstat_b, dobuf, dstat, dqsend, dqbuf, gmine, gpeer,
    load_sem, wsend, wrecv, gsend, grecv, bsend, brecv, ysend, yrecv, psend, precv, usend, urecv, ksend, krecv,
):
    me = lax.axis_index("dp")
    f = lax.axis_index("fsdp")
    z = lax.div(me, SIDE * CORES)
    x = lax.rem(lax.div(me, CORES), SIDE)
    c = lax.rem(me, CORES)
    chip = lax.div(me, CORES)
    chips = ranks // CORES
    place = (z, x, c, f)
    half_rows = D // columns
    slab = half_rows // chips
    own_rows = mem_ref.shape[0]
    padded = memp.shape[0]
    lay = Pieces(ranks, own_rows)
    other = 1 - f
    everyone = ranks * columns
    lin = f * ranks + me

    loads = []

    def load(src, lane, width):
        item = pltpu.make_async_copy(
            src, wb.at[pl.ds(pl.multiple_of(f * half_rows, 128), half_rows), pl.ds(lane, width)],
            load_sem.at[len(loads)],
        )
        item.start()
        loads.append(item)

    load(qkv_ref, LANE_QKV, 3 * D)
    load(so_ref, LANE_SO, D)
    load(cq_ref, LANE_CQ, D)
    load(ckv_ref, LANE_CKV, 2 * D)
    load(co_ref, LANE_CO, D)
    load(fi_ref, LANE_FI, 4 * D)
    for j in range(4):
        load(fo_ref.at[pl.ds(j * half_rows, half_rows)], LANE_FO + D * j, D)

    for s in range(SLOTS):
        qbuf[s] = jnp.zeros_like(qbuf[s])
        obuf[s] = jnp.zeros_like(obuf[s])
        ostat[s, 0] = jnp.full_like(ostat[s, 0], NONE)
        ostat[s, 1] = jnp.zeros_like(ostat[s, 1])
        dobuf[s] = jnp.zeros_like(dobuf[s])
        dstat[s] = jnp.zeros_like(dstat[s])
        dqbuf[s] = jnp.zeros_like(dqbuf[s])

    def rows_of(device):
        return pl.ds(pl.multiple_of(device * SUFFIX, SUFFIX), SUFFIX)

    xb[me] = x_ref[...]
    cb[me] = cot_ref[...].astype(BF16)
    pb[me] = jnp.full((8, 128), pre_ref[0, 0].astype(F32), F32)
    gainb[f] = gains_ref[...]

    barrier = pltpu.get_barrier_semaphore()

    def greet(i, carry):
        to = lax.rem(me + i, ranks)
        pl.semaphore_signal(barrier, inc=1, device_id=(to, f), device_id_type=MESH)
        return carry

    lax.fori_loop(1, ranks, greet, 0)
    pl.semaphore_signal(barrier, inc=1, device_id=(me, other), device_id_type=MESH)
    pl.semaphore_wait(barrier, ranks)

    y_items = []

    def push_y(src, dst, at):
        item = pltpu.make_async_remote_copy(
            src_ref=src, dst_ref=dst, send_sem=ysend.at[at], recv_sem=yrecv.at[at],
            device_id=(me, other), device_id_type=MESH,
        )
        item.start()
        y_items.append(item)
        return item

    class Tell:
        def __init__(self, ref, at):
            self.ref, self.at = ref, at

        def copy(self, source, index, to):
            return pltpu.make_async_remote_copy(
                src_ref=self.ref.at[source], dst_ref=self.ref.at[source], send_sem=bsend.at[self.at, index],
                recv_sem=brecv.at[self.at, source], device_id=(to, f), device_id_type=MESH,
            )

        def start(self):
            def one(i, carry):
                self.copy(me, i, lax.rem(me + i, ranks)).start()
                return carry

            lax.fori_loop(1, ranks, one, 0)

        def wait(self):
            def one(i, carry):
                source = lax.rem(me + i, ranks)
                self.copy(source, i, source).wait_recv()
                return carry

            lax.fori_loop(1, ranks, one, 0)

        def finish(self):
            def one(i, carry):
                self.copy(me, i, lax.rem(me + i, ranks)).wait_send()
                return carry

            lax.fori_loop(1, ranks, one, 0)

    def slab_view(first, width, rows_from):
        half = width // CORES

        def view(zz, xx, cc, part):
            row = pl.multiple_of(rows_from * half_rows + (zz * SIDE + xx) * slab, 16)
            lane = pl.multiple_of(first + cc * half, 128)
            return wb.at[pl.ds(row, slab), pl.ds(lane, half)]

        return view

    def block_view(ref):
        def view(zz, xx, cc, part):
            row = ref.at[zz * (SIDE * CORES) + xx * CORES + cc]
            return row if part is None else row.at[:, pl.ds(*part)]

        return view

    def token_view(ref):
        def view(zz, xx, cc, part):
            rows = rows_of(zz * (SIDE * CORES) + xx * CORES + cc)
            return ref.at[rows] if part is None else ref.at[rows, pl.ds(*part)]

        return view

    sems = (gsend, grecv)
    ag_x = Gather(place, block_view(xb), D, sems, 0)
    ag_c = Gather(place, block_view(cb), D, sems, 1)
    ag_n = Gather(place, token_view(nb), D, sems, 2)
    tell_p = Tell(pb, 0)
    spread = [
        Spread(place, slab_view(first, width, other), slab_view(first, width, f), (wsend, wrecv), n)
        for n, (first, width) in enumerate(CHUNKS)
    ]

    def push_chunk(n):
        for i in LOADS_BY_CHUNK[n]:
            loads[i].wait()
        spread[n].push()

    ag_x.step_one()
    push_chunk(0)
    gain_item = push_y(gainb.at[f], gainb.at[f], 0)
    tell_p.start()
    push_chunk(1)
    ag_x.step_two()
    spread[0].step_one()
    push_chunk(2)
    ag_x.step_three()
    spread[0].step_two()
    ag_x.step_four()
    spread[1].step_one()
    push_chunk(3)
    spread[0].step_three()
    ag_x.step_five()
    spread[1].step_two()
    spread[2].step_one()
    push_chunk(4)
    gain_item.wait_recv()

    memp[0:own_rows] = mem_ref[...]
    memp[own_rows:padded] = jnp.zeros((padded - own_rows, D), BF16)

    positions = []
    before_large = jnp.int32(0)
    mine_rank = jnp.int32(0)
    for i in range(ranks):
        group = res_ref[0, i]
        spot = jnp.where(group == 1, lay.half + before_large, i - before_large)
        positions.append(spot)
        mine_rank = jnp.where(me == i, spot, mine_rank)
        before_large = before_large + group

    def example_of(rank):
        found = jnp.int32(0)
        for i in range(ranks):
            found = jnp.where(positions[i] == rank, i, found)
        return found

    gain = [jnp.concatenate([gainb[i, n : n + 1] for i in range(columns)], axis=1) for n in range(3)]

    mine = example_of(me)
    resid = xb[mine]
    hat_one, rs_one = normed(resid)
    n1 = (hat_one * gain[0]).astype(BF16)

    lanes = lax.broadcasted_iota(jnp.int32, (1, 256), 1)
    head_f32 = [(lax.div(lanes, HEAD_DIM) == h).astype(F32) for h in range(4)]
    head_b16 = [m.astype(BF16) for m in head_f32]

    def stack(value):
        return jnp.concatenate([value * m for m in head_b16], axis=0)

    def unstack(value):
        rows = value.shape[0] // 4
        total = value[0:rows] * head_f32[0]
        for h in range(1, 4):
            total = total + value[h * rows : (h + 1) * rows] * head_f32[h]
        return total

    spread[0].step_four()
    q = mm(n1, wb[:, 0:D]).astype(BF16)
    k = mm(n1, wb[:, D : 2 * D]).astype(BF16)
    v = mm(n1, wb[:, 2 * D : 3 * D]).astype(BF16)
    spread[1].step_three()
    spread[2].step_two()
    spread[3].step_one()
    push_chunk(5)
    scale = HEAD_DIM**-0.5
    qs = (q.astype(F32) * scale).astype(BF16)
    row_at = lax.broadcasted_iota(jnp.int32, (SUFFIX, SUFFIX), 0)
    col_at = lax.broadcasted_iota(jnp.int32, (SUFFIX, SUFFIX), 1)
    causal = jnp.concatenate([(row_at >= col_at).astype(F32)] * 4, axis=0) > 0.0
    self_p = []
    mixed = []
    for g in range(3):
        sl = slice(256 * g, 256 * g + 256)
        s = mm_nt(stack(qs[:, sl]), k[:, sl])
        s = jnp.where(causal, s, NONE)
        e = jnp.exp(s - jnp.max(s, axis=-1, keepdims=True))
        p = e / jnp.sum(e, axis=-1, keepdims=True)
        self_p.append(p)
        mixed.append(unstack(mm(p.astype(BF16), v[:, sl])))
    sm = jnp.concatenate(mixed, axis=1).astype(BF16)

    spread[1].step_four()
    after_self = resid + mm(sm, wb[:, LANE_SO : LANE_SO + D])
    hat_two, rs_two = normed(after_self)
    n2 = (hat_two * gain[1]).astype(BF16)
    cq = mm(n2, wb[:, LANE_CQ : LANE_CQ + D]).astype(BF16)
    cqb[...] = cq

    my_first, my_last = lay.first_device(me), lay.last_device(me)
    held_first, held_last = lay.first_rank(me), lay.last_rank(me)

    def piece_copy(src, dst, at, sent, landed, target):
        return pltpu.make_async_remote_copy(
            src_ref=src, dst_ref=dst, send_sem=psend.at[at, sent], recv_sem=precv.at[at, landed],
            device_id=(target, f), device_id_type=MESH,
        )

    def to_holders(pairs):
        for i in range(SLOTS):
            target = my_first + i
            slot = me - lay.first_rank(target)
            there = target <= my_last

            @pl.when(there & (target == me))
            def _():
                for src, dst, at in pairs:
                    dst[slot] = src[...]

            @pl.when(there & (target != me))
            def _():
                for src, dst, at in pairs:
                    piece_copy(src, dst.at[slot], at, i, slot, target).start()

    def to_holders_sent(pairs):
        for i in range(SLOTS):
            target = my_first + i

            @pl.when((target <= my_last) & (target != me))
            def _():
                for src, dst, at in pairs:
                    piece_copy(src, dst.at[0], at, i, 0, target).wait_send()

    def at_holders(pairs):
        for s in range(SLOTS):
            rank = held_first + s

            @pl.when((rank <= held_last) & (rank != me))
            def _():
                for src, dst, at in pairs:
                    piece_copy(src, dst.at[s], at, 0, s, rank).wait_recv()

    def to_owners(pairs):
        for s in range(SLOTS):
            rank = held_first + s
            index = me - lay.first_device(rank)
            there = rank <= held_last

            @pl.when(there & (rank == me))
            def _():
                for src, dst, at in pairs:
                    dst[index] = src[s]

            @pl.when(there & (rank != me))
            def _():
                for src, dst, at in pairs:
                    piece_copy(src.at[s], dst.at[index], at, s, index, rank).start()

    def to_owners_sent(pairs):
        for s in range(SLOTS):
            rank = held_first + s

            @pl.when((rank <= held_last) & (rank != me))
            def _():
                for src, dst, at in pairs:
                    piece_copy(src.at[s], dst.at[0], at, s, 0, rank).wait_send()

    def at_owners(pairs):
        for i in range(SLOTS):
            target = my_first + i

            @pl.when((target <= my_last) & (target != me))
            def _():
                for src, dst, at in pairs:
                    piece_copy(src.at[0], dst.at[i], at, 0, i, target).wait_recv()

    q_pairs = [(cqb, qbuf, 0)]
    o_pairs = [(osend, obuf, 1), (ostat_send, ostat, 2)]
    d_pairs = [(dob, dobuf, 3), (dstat_b, dstat, 4)]
    dq_pairs = [(dqsend, dqbuf, 5)]

    to_holders(q_pairs)

    spread[2].step_three()
    spread[3].step_two()
    spread[4].step_one()
    spread[2].step_four()

    def kv_step(i, carry):
        lane = pl.multiple_of(i * 256, 256)
        kvb[:, pl.ds(lane, 256)] = mm(memp[...], wb[:, pl.ds(LANE_CKV + lane, 256)]).astype(BF16)
        return carry

    lax.fori_loop(0, 6, kv_step, 0)

    tell_p.wait()
    lane_f = lax.broadcasted_iota(jnp.int32, (SUFFIX, padded), 1).astype(F32)
    allowed = []
    for s in range(SLOTS):
        rank = held_first + s
        ok = rank <= held_last
        example = example_of(jnp.minimum(rank, ranks - 1))
        prefix = pb[example][0:1, 0:1]
        low = (lay.start(rank) - me * own_rows).astype(F32)
        patches = jnp.where(rank < lay.half, PATCH_S, PATCH_L).astype(F32)
        high = jnp.minimum(low + patches + prefix, jnp.float32(own_rows))
        high = jnp.where(ok, high, jnp.float32(-1.0))
        allowed.append(((lane_f >= low) & (lane_f < high)).astype(F32))
    allowed = jnp.concatenate(allowed * 4, axis=0) > 0.0

    at_holders(q_pairs)
    qh = jnp.concatenate([qbuf[s] for s in range(SLOTS)], axis=0)
    qh = (qh.astype(F32) * scale).astype(BF16)
    lane_c = lax.broadcasted_iota(jnp.int32, (SUFFIX, 128), 1)
    top_c = [jnp.zeros((SUFFIX, 128), F32) for _ in range(SLOTS)]
    sum_c = [jnp.zeros((SUFFIX, 128), F32) for _ in range(SLOTS)]
    for g in range(3):
        sl = slice(256 * g, 256 * g + 256)
        s = mm_nt(stack(qh[:, sl]), kvb[:, sl])
        s = jnp.where(allowed, s, NONE)
        top = jnp.max(s, axis=-1, keepdims=True)
        e = jnp.where(allowed, jnp.exp(s - top), 0.0)
        total = jnp.sum(e, axis=-1, keepdims=True)
        o = mm(e.astype(BF16), kvb[:, D + 256 * g : D + 256 * g + 256])
        o = o * jnp.where(total > 0.0, 1.0 / jnp.where(total > 0.0, total, 1.0), 0.0)
        o = unstack(o).astype(BF16)
        for n in range(SLOTS):
            osend[n, :, sl] = o[n * SUFFIX : (n + 1) * SUFFIX]
            for h in range(4):
                at = h * SLOTS * SUFFIX + n * SUFFIX
                hit = lane_c == 4 * g + h
                top_c[n] = jnp.where(hit, top[at : at + SUFFIX], top_c[n])
                sum_c[n] = jnp.where(hit, total[at : at + SUFFIX], sum_c[n])
    for n in range(SLOTS):
        ostat_send[n, 0] = top_c[n]
        ostat_send[n, 1] = sum_c[n]
    to_owners(o_pairs)

    spread[3].step_three()
    spread[4].step_two()
    spread[5].step_one()
    ag_c.step_one()
    spread[3].step_four()
    at_owners(o_pairs)

    def expand(compact):
        low = lane_c < HEAD_DIM
        return jnp.concatenate(
            [jnp.where(low, compact[:, 2 * t : 2 * t + 1], compact[:, 2 * t + 1 : 2 * t + 2]) for t in range(6)],
            axis=1,
        )

    tops = [ostat[i, 0] for i in range(SLOTS)]
    top_all = jnp.maximum(jnp.maximum(tops[0], tops[1]), tops[2])
    shares = [ostat[i, 1] * jnp.exp(tops[i] - top_all) for i in range(SLOTS)]
    whole = shares[0] + shares[1] + shares[2]
    whole = jnp.where(whole > 0.0, whole, 1.0)
    lse = top_all + jnp.log(whole)
    cross = jnp.zeros((SUFFIX, D), F32)
    for i in range(SLOTS):
        cross = cross + expand(shares[i] / whole) * obuf[i].astype(F32)
    cm = cross.astype(BF16)

    after_cross = after_self + mm(cm, wb[:, LANE_CO : LANE_CO + D])
    hat_three, rs_three = normed(after_cross)
    n3 = (hat_three * gain[2]).astype(BF16)
    nb[rows_of(me)] = n3
    ag_n.step_one()

    spread[4].step_three()
    spread[5].step_two()
    ag_c.step_two()
    spread[4].step_four()
    spread[5].step_three()
    ag_c.step_three()
    ag_n.step_two()
    ag_c.step_four()
    ag_c.step_five()
    spread[5].step_four()

    out_low = cb[mine]
    cot = out_low.astype(F32)
    acts, up_grads = [], []
    hidden_grad = [mm_nt(out_low, wb[:, LANE_FO + D * j : LANE_FO + D * (j + 1)]) for j in range(4)]

    def by_hidden(j):
        parts = []
        for t in range(D // half_rows):
            at = D * j + t * half_rows
            col, unit = at // (4 * half_rows), (at % (4 * half_rows)) // half_rows
            parts.append(hidden_grad[unit][:, col * half_rows : (col + 1) * half_rows])
        return jnp.concatenate(parts, axis=1)

    n3_grad = jnp.zeros((SUFFIX, D), F32)
    for j in range(4):
        weight = wb[:, LANE_FI + D * j : LANE_FI + D * (j + 1)]
        value, slope = gelu_parts(mm(n3, weight))
        acts.append(value.astype(BF16))
        part = (by_hidden(j) * slope).astype(BF16)
        n3_grad = n3_grad + mm_nt(part, weight)
    act = jnp.concatenate(acts, axis=1)

    part, ffn_gain_grad = norm_back(n3_grad, hat_three, rs_three, gain[2])
    cross_res = cot + part
    cross_low = cross_res.astype(BF16)
    d_mixed = mm_nt(cross_low, wb[:, LANE_CO : LANE_CO + D]).astype(BF16)
    dob[...] = d_mixed
    prod = d_mixed.astype(F32) * cross
    delta = jnp.zeros((SUFFIX, 128), F32)
    for t in range(6):
        tile = prod[:, 128 * t : 128 * (t + 1)]
        left = jnp.sum(jnp.where(lane_c < HEAD_DIM, tile, 0.0), axis=-1, keepdims=True)
        right = jnp.sum(jnp.where(lane_c < HEAD_DIM, 0.0, tile), axis=-1, keepdims=True)
        delta = jnp.where(lane_c == 2 * t, left, delta)
        delta = jnp.where(lane_c == 2 * t + 1, right, delta)
    dstat_b[0] = lse
    dstat_b[1] = delta
    to_holders(d_pairs)
    ag_n.step_three()

    down = jnp.zeros((SUFFIX, D), F32)
    for j in range(4):
        lhs = jnp.concatenate(
            [act[:, i * 4 * half_rows + j * half_rows : i * 4 * half_rows + (j + 1) * half_rows] for i in range(columns)],
            axis=1,
        )
        down = down + mm(lhs, wb[:, LANE_FO + D * j : LANE_FO + D * (j + 1)])
    ob[me, 0:SUFFIX] = (after_cross + down).astype(BF16)

    def unit_device(h):
        return CORES * h if h < HALF_UNITS else CORES * (h - HALF_UNITS) + 1

    unit_items = []

    def push_unit(h, left, right):
        to = unit_device(h)
        sb[h, :, 0:D] = left
        sb[h, :, D : D + PIECE] = right

        @pl.when(me == to)
        def _():
            rb[rows_of(me)] = sb[h]

        @pl.when(me != to)
        def _():
            pltpu.make_async_remote_copy(
                src_ref=sb.at[h], dst_ref=rb.at[rows_of(me)], send_sem=usend.at[h],
                recv_sem=urecv.at[me], device_id=(to, f), device_id_type=MESH,
            ).start()

        unit_items.append((h, to))

    ag_n.step_four()
    push_unit(HALF_UNITS + 4, cm, cross_low[:, 0:PIECE])
    push_unit(HALF_UNITS + 5, cm, cross_low[:, PIECE:])

    for r in range(ranks):
        olr[r * SUFFIX : (r + 1) * SUFFIX] = cb[example_of(r)]

    at_holders(d_pairs)

    doh = jnp.concatenate([dobuf[s] for s in range(SLOTS)], axis=0)
    for g in range(3):
        sl = slice(256 * g, 256 * g + 256)
        kg = kvb[:, sl]
        vg = kvb[:, D + 256 * g : D + 256 * g + 256]
        q4 = stack(qh[:, sl])
        do4 = stack(doh[:, sl])
        lse_col = jnp.concatenate([dstat[n, 0][:, 4 * g + h : 4 * g + h + 1] for h in range(4) for n in range(SLOTS)], axis=0)
        del_col = jnp.concatenate([dstat[n, 1][:, 4 * g + h : 4 * g + h + 1] for h in range(4) for n in range(SLOTS)], axis=0)
        s = mm_nt(q4, kg)
        p = jnp.where(allowed, jnp.exp(jnp.where(allowed, s - lse_col, 0.0)), 0.0)
        dp = mm_nt(do4, vg)
        ds = (p * (dp - del_col)).astype(BF16)
        kvg[:, D + 256 * g : D + 256 * g + 256] = mm_tn(p.astype(BF16), do4).astype(BF16)
        kvg[:, sl] = mm_tn(ds, q4).astype(BF16)
        dq = unstack(mm(ds, kg)) * scale
        for n in range(SLOTS):
            dqsend[n, :, sl] = dq[n * SUFFIX : (n + 1) * SUFFIX]
    to_owners(dq_pairs)

    ag_n.step_five()
    rows_step = 128
    steps = ranks * SUFFIX // rows_step

    @pl.when(c == 0)
    def _():
        lane = pl.multiple_of(LANE_FI + PIECE * chip, 128)
        row = pl.multiple_of(lax.div(chip, 4) * half_rows, 128)
        lane_o = pl.multiple_of(LANE_FO + D * lax.rem(chip, 4), 128)

        def one(i, carry):
            at = pl.ds(pl.multiple_of(i * rows_step, rows_step), rows_step)
            value, slope = gelu_parts(mm(nb[at], wb[:, pl.ds(lane, PIECE)]))
            back = mm_nt(olr[at], wb[pl.ds(row, half_rows), pl.ds(lane_o, D)])
            hb[0, at] = (back * slope).astype(BF16)
            return carry

        lax.fori_loop(0, steps, one, 0)
        for col in range(columns):
            fg[col] = mm_tn(nb[:, col * half_rows : (col + 1) * half_rows], hb[0])

    @pl.when(c == 1)
    def _():
        side = pl.ds(pl.multiple_of(PIECE * lax.div(chip, 4), 128), PIECE)

        def one(i, carry):
            at = pl.ds(pl.multiple_of(i * rows_step, rows_step), rows_step)
            for col in range(columns):
                lane = pl.multiple_of(LANE_FI + col * 4 * half_rows + PIECE * lax.rem(chip, 4), 128)
                value, slope = gelu_parts(mm(nb[at], wb[:, pl.ds(lane, PIECE)]))
                hb[col, at] = value.astype(BF16)
            return carry

        lax.fori_loop(0, steps, one, 0)
        for col in range(columns):
            fg[col] = mm_tn(hb[col], olr[:, side])

    fsend[...] = fg[other].astype(BF16)
    f_item = push_y(fsend, frecv, 1)

    at_owners(dq_pairs)
    cqg = (dqbuf[0] + dqbuf[1] + dqbuf[2]).astype(BF16)
    n2_grad = mm_nt(cqg, wb[:, LANE_CQ : LANE_CQ + D])
    part, cross_gain_grad = norm_back(n2_grad, hat_two, rs_two, gain[1])
    self_res = cross_res + part
    self_low = self_res.astype(BF16)
    dmix = mm_nt(self_low, wb[:, LANE_SO : LANE_SO + D]).astype(BF16)
    dqs, dks, dvs = [], [], []
    for g in range(3):
        sl = slice(256 * g, 256 * g + 256)
        q4 = stack(qs[:, sl])
        do4 = stack(dmix[:, sl])
        p = self_p[g]
        dp = mm_nt(do4, v[:, sl])
        ds = (p * (dp - jnp.sum(p * dp, axis=-1, keepdims=True))).astype(BF16)
        dvs.append(mm_tn(p.astype(BF16), do4))
        dks.append(mm_tn(ds, q4))
        dqs.append(unstack(mm(ds, k[:, sl])) * scale)
    packed_grad = [jnp.concatenate(parts, axis=1).astype(BF16) for parts in (dqs, dks, dvs)]
    for h in range(HALF_UNITS):
        push_unit(h, n1, packed_grad[h // 2][:, (h % 2) * PIECE : (h % 2 + 1) * PIECE])
    for h in range(2):
        push_unit(HALF_UNITS + 2 + h, n2, cqg[:, h * PIECE : (h + 1) * PIECE])
        push_unit(HALF_UNITS + h, sm, self_low[:, h * PIECE : (h + 1) * PIECE])

    f_item.wait_recv()
    f_lane = jnp.where(
        c == 0, LANE_FI + PIECE * chip, LANE_FO + D * lax.rem(chip, 4) + PIECE * lax.div(chip, 4)
    )
    gb[:, pl.ds(pl.multiple_of(f_lane, 128), PIECE)] = (fg[f] + frecv[...].astype(F32)).astype(BF16)

    def gb_view(lane_of):
        def view(zz, xx, cc, part):
            low, size = part if part is not None else (0, PIECE)
            return gb.at[:, pl.ds(pl.multiple_of(lane_of(zz * SIDE + xx, cc) + low, 128), size)]

        return view

    ag_f = Gather(
        place,
        gb_view(lambda n, cc: jnp.where(cc == 0, LANE_FI + PIECE * n, LANE_FO + D * lax.rem(n, 4) + PIECE * lax.div(n, 4))),
        PIECE, sems, 3,
    )
    ag_f.step_one()

    n1_grad = jnp.zeros((SUFFIX, D), F32)
    for j in range(3):
        n1_grad = n1_grad + mm_nt(packed_grad[j], wb[:, D * j : D * (j + 1)])
    part, self_gain_grad = norm_back(n1_grad, hat_one, rs_one, gain[0])
    ob[me, SUFFIX : 2 * SUFFIX] = (self_res + part).astype(BF16)
    gmine[...] = jnp.concatenate(
        [self_gain_grad, cross_gain_grad, ffn_gain_grad, jnp.zeros((5, D), F32)], axis=0
    )
    g_item = push_y(gmine, gpeer, 2)

    def kp_step(i, carry):
        lane = pl.multiple_of(i * 256, 256)
        kp[:, pl.ds(lane, 256)] = mm_tn(memp[...], kvg[:, pl.ds(lane, 256)]).astype(BF16)
        return carry

    lax.fori_loop(0, 6, kp_step, 0)
    mate = (z * (SIDE * CORES) + x * CORES + (1 - c), f)
    kr_item = pltpu.make_async_remote_copy(
        src_ref=kp.at[pl.ds(pl.multiple_of((1 - c) * half_rows, 128), half_rows)], dst_ref=kr,
        send_sem=ksend.at[2 * chips], recv_sem=krecv.at[chips], device_id=mate, device_id_type=MESH,
    )
    kr_item.start()

    ag_f.step_two()

    has_unit = chip < HALF_UNITS

    def unit_lane(n, cc):
        kind = lax.div(n, 2)
        base = jnp.where(kind == 0, LANE_SO, jnp.where(kind == 1, LANE_CQ, LANE_CO))
        return jnp.where(cc == 0, PIECE * n, base + PIECE * lax.rem(n, 2))

    u_items = []

    def unit_sum(pred, at):
        @pl.when(pred)
        def _():
            def take(i, carry):
                @pl.when(i != me)
                def _():
                    pltpu.make_async_remote_copy(
                        src_ref=sb.at[0], dst_ref=rb.at[rows_of(i)], send_sem=usend.at[0],
                        recv_sem=urecv.at[i], device_id=mate, device_id_type=MESH,
                    ).wait_recv()

                return carry

            lax.fori_loop(0, ranks, take, 0)
            for col in range(columns):
                ug[col] = mm_tn(rb[:, col * half_rows : (col + 1) * half_rows], rb[:, D : D + PIECE])
            usend_b[...] = ug[other].astype(BF16)
            pltpu.make_async_remote_copy(
                src_ref=usend_b, dst_ref=urecv_b, send_sem=ysend.at[at], recv_sem=yrecv.at[at],
                device_id=(me, other), device_id_type=MESH,
            ).start()

    def unit_join(pred, at):
        @pl.when(pred)
        def _():
            item = pltpu.make_async_remote_copy(
                src_ref=usend_b, dst_ref=urecv_b, send_sem=ysend.at[at], recv_sem=yrecv.at[at],
                device_id=(me, other), device_id_type=MESH,
            )
            item.wait_recv()
            gb[:, pl.ds(pl.multiple_of(unit_lane(chip, c), 128), PIECE)] = (
                ug[f] + urecv_b[...].astype(F32)
            ).astype(BF16)
            item.wait_send()

    def has_block(zz, xx, cc):
        return zz * SIDE + xx < HALF_UNITS

    ag_u = Gather(place, gb_view(unit_lane), PIECE, sems, 4, has_block)
    unit_sum(has_unit, 3)

    kr_item.wait_recv()
    kc[...] = (
        kp[pl.ds(pl.multiple_of(c * half_rows, 128), half_rows)].astype(F32) + kr[...].astype(F32)
    ).astype(BF16)
    ky_item = pltpu.make_async_remote_copy(
        src_ref=kc, dst_ref=ky, send_sem=ksend.at[2 * chips + 1], recv_sem=krecv.at[chips + 1],
        device_id=(me, other), device_id_type=MESH,
    )

    @pl.when(c != f)
    def _():
        ky_item.start()

    unit_join(has_unit, 3)
    ag_u.step_one()
    ag_f.step_three()
    k_items = []

    def k_copy(t, j, src):
        return pltpu.make_async_remote_copy(
            src_ref=src, dst_ref=cp.at[chip], send_sem=ksend.at[t * CORES + j], recv_sem=krecv.at[chip],
            device_id=(t * CORES + j, f), device_id_type=MESH,
        )

    @pl.when(c == f)
    def _():
        ky_item.wait_recv()
        kc[...] = (kc[...].astype(F32) + ky[...].astype(F32)).astype(BF16)

    for t in range(chips):
        for j in range(CORES):
            src = kc.at[pl.ds(t * slab, slab), pl.ds(j * D, D)]
            here = (chip == t) & (c == j)

            @pl.when((c == f) & here)
            def _():
                cp[chip] = kc[t * slab : (t + 1) * slab, j * D : (j + 1) * D]

            @pl.when((c == f) & jnp.logical_not(here))
            def _():
                k_copy(t, j, src).start()

            k_items.append((t, j, src, here))

    g_item.wait_recv()
    tb[me] = gmine[...] + gpeer[...]
    tell_g = Tell(tb, 1)
    tell_g.start()
    ag_o = Gather(place, block_view(ob), D, sems, 5)
    ag_o.step_one()
    ag_u.step_two()
    ag_f.step_four()

    def take_k(i, carry):
        @pl.when((i != chip) | (c != f))
        def _():
            pltpu.make_async_remote_copy(
                src_ref=kc.at[pl.ds(0, slab), pl.ds(0, D)], dst_ref=cp.at[i], send_sem=ksend.at[0],
                recv_sem=krecv.at[i], device_id=mate, device_id_type=MESH,
            ).wait_recv()

        return carry

    lax.fori_loop(0, chips, take_k, 0)
    total = cp[0].astype(F32)
    for i in range(1, chips):
        total = total + cp[i].astype(F32)
    k_lane = pl.multiple_of(LANE_CKV + c * D, 128)
    gb[pl.ds(pl.multiple_of(chip * slab, 16), slab), pl.ds(k_lane, D)] = total.astype(BF16)

    def kv_view(zz, xx, cc, part):
        low, size = part if part is not None else (0, D)
        row = pl.multiple_of((zz * SIDE + xx) * slab, 16)
        return gb.at[pl.ds(row, slab), pl.ds(pl.multiple_of(LANE_CKV + cc * D + low, 128), size)]

    ag_k = Gather(place, kv_view, D, sems, 6)
    ag_k.step_one()
    ag_u.step_three()
    ag_o.step_two()
    ag_k.step_two()

    def mg_step(i, carry):
        row = pl.multiple_of(i * 128, 128)
        memgrad_ref[pl.ds(row, 128)] = mm_nt(kvg[pl.ds(row, 128)], wb[:, LANE_CKV : LANE_CKV + 2 * D])
        return carry

    full = own_rows // 128
    lax.fori_loop(0, full, mg_step, 0)
    if own_rows % 128:
        tail = mm_nt(kvg[full * 128 : (full + 1) * 128], wb[:, LANE_CKV : LANE_CKV + 2 * D])
        memgrad_ref[full * 128 : own_rows] = tail[0 : own_rows - full * 128]

    ag_u.step_four()
    ag_o.step_three()
    ag_k.step_three()
    ag_o.step_four()
    ag_k.step_four()
    tell_g.wait()
    gains_all = tb[0]
    for i in range(1, ranks):
        gains_all = gains_all + tb[i]
    own_gain = gains_all[:, 0:half_rows]
    for i in range(1, columns):
        own_gain = jnp.where(f == i, gains_all[:, i * half_rows : (i + 1) * half_rows], own_gain)
    gain_out_ref[...] = own_gain
    ag_f.step_five()
    ag_o.step_five()
    out_ref[...] = ob[mine_rank, 0:SUFFIX].astype(F32)
    grad_ref[...] = ob[mine_rank, SUFFIX : 2 * SUFFIX].astype(F32)
    ag_k.step_five()
    ag_u.step_five()
    done = pltpu.make_async_copy(gb, weights_out_ref, load_sem.at[0])
    done.start()

    to_holders_sent(q_pairs)
    to_owners_sent(o_pairs)
    to_holders_sent(d_pairs)
    to_owners_sent(dq_pairs)
    for h, to in unit_items:
        @pl.when(me != to)
        def _():
            pltpu.make_async_remote_copy(
                src_ref=sb.at[h], dst_ref=rb.at[rows_of(me)], send_sem=usend.at[h],
                recv_sem=urecv.at[0], device_id=(to, f), device_id_type=MESH,
            ).wait_send()
    for t, j, src, here in k_items:
        @pl.when((c == f) & jnp.logical_not(here))
        def _():
            k_copy(t, j, src).wait_send()
    kr_item.wait_send()

    @pl.when(c != f)
    def _():
        ky_item.wait_send()

    for item in y_items:
        item.wait_send()
    tell_p.finish()
    tell_g.finish()
    for item in [ag_x, *spread, ag_c, ag_n, ag_f, ag_u, ag_o, ag_k]:
        item.finish()
    done.wait()


def fused_body(
    ranks, columns,
    decoder_in, memory, res_group, prefix_len, self_gain, self_qkv, self_out, cross_gain, cross_query,
    cross_kv, cross_out, ffn_gain, ffn_in, ffn_out, cotangent,
):
    half_rows = D // columns
    chips = ranks // CORES
    slab = half_rows // chips
    own_rows = memory.shape[1]
    padded = -(-own_rows // 128) * 128
    tokens = ranks * SUFFIX
    gains = jnp.stack([self_gain, cross_gain, ffn_gain]).astype(F32)
    gains = jnp.pad(gains, ((0, 5), (0, 0)))
    vm = pl.BlockSpec(memory_space=pltpu.VMEM)
    sm = pl.BlockSpec(memory_space=pltpu.SMEM)
    hbm = pl.BlockSpec(memory_space=pl.ANY)
    dma = pltpu.SemaphoreType.DMA
    scratch = [
        pltpu.VMEM((D, UNITS * D), BF16),
        pltpu.VMEM((half_rows, UNITS * D), BF16),
        pltpu.VMEM((tokens, D + PIECE), BF16),
        pltpu.VMEM((2 * HALF_UNITS, SUFFIX, D + PIECE), BF16),
        pltpu.VMEM((ranks, SUFFIX, D), F32),
        pltpu.VMEM((ranks, SUFFIX, D), BF16),
        pltpu.VMEM((tokens, D), BF16),
        pltpu.VMEM((tokens, D), BF16),
        pltpu.VMEM((ranks, 2 * SUFFIX, D), BF16),
        pltpu.VMEM((ranks, 8, D), F32),
        pltpu.VMEM((ranks, 8, 128), F32),
        pltpu.VMEM((columns, 8, half_rows), F32),
        pltpu.VMEM((padded, D), BF16),
        pltpu.VMEM((padded, 2 * D), BF16),
        pltpu.VMEM((padded, 2 * D), BF16),
        pltpu.VMEM((D, 2 * D), BF16),
        pltpu.VMEM((half_rows, 2 * D), BF16),
        pltpu.VMEM((half_rows, 2 * D), BF16),
        pltpu.VMEM((half_rows, 2 * D), BF16),
        pltpu.VMEM((chips, slab, D), BF16),
        pltpu.VMEM((columns, tokens, PIECE), BF16),
        pltpu.VMEM((columns, half_rows, PIECE), F32),
        pltpu.VMEM((half_rows, PIECE), BF16),
        pltpu.VMEM((half_rows, PIECE), BF16),
        pltpu.VMEM((columns, half_rows, PIECE), F32),
        pltpu.VMEM((half_rows, PIECE), BF16),
        pltpu.VMEM((half_rows, PIECE), BF16),
        pltpu.VMEM((SUFFIX, D), BF16),
        pltpu.VMEM((SLOTS, SUFFIX, D), BF16),
        pltpu.VMEM((SLOTS, SUFFIX, D), BF16),
        pltpu.VMEM((SLOTS, 2, SUFFIX, 128), F32),
        pltpu.VMEM((SLOTS, SUFFIX, D), BF16),
        pltpu.VMEM((SLOTS, 2, SUFFIX, 128), F32),
        pltpu.VMEM((SUFFIX, D), BF16),
        pltpu.VMEM((2, SUFFIX, 128), F32),
        pltpu.VMEM((SLOTS, SUFFIX, D), BF16),
        pltpu.VMEM((SLOTS, 2, SUFFIX, 128), F32),
        pltpu.VMEM((SLOTS, SUFFIX, D), F32),
        pltpu.VMEM((SLOTS, SUFFIX, D), F32),
        pltpu.VMEM((8, D), F32),
        pltpu.VMEM((8, D), F32),
        dma((10,)),
        dma((len(CHUNKS), 16)),
        dma((len(CHUNKS), 16)),
        dma((7, 16)),
        dma((7, 16)),
        dma((2, ranks)),
        dma((2, ranks)),
        dma((4,)),
        dma((4,)),
        dma((6, SLOTS)),
        dma((6, SLOTS)),
        dma((2 * HALF_UNITS,)),
        dma((ranks,)),
        dma((2 * chips + 2,)),
        dma((chips + 2,)),
    ]
    out, grad, memgrad, gain_grads, weight_grads = pl.pallas_call(
        partial(layer_kernel, ranks, columns),
        out_shape=(
            jax.ShapeDtypeStruct((SUFFIX, D), F32),
            jax.ShapeDtypeStruct((SUFFIX, D), F32),
            jax.ShapeDtypeStruct((own_rows, D), F32),
            jax.ShapeDtypeStruct((8, half_rows), F32),
            jax.ShapeDtypeStruct((half_rows, UNITS * D), BF16),
        ),
        in_specs=[vm, vm, vm, sm, sm, vm] + [hbm] * 7,
        out_specs=(vm, vm, vm, vm, hbm),
        scratch_shapes=scratch,
        compiler_params=pltpu.CompilerParams(
            collective_id=0, has_side_effects=True, vmem_limit_bytes=62 * 2**20
        ),
        name="layer",
    )(
        decoder_in[0], cotangent[0], memory[0], res_group, prefix_len, gains,
        self_qkv, self_out, cross_query, cross_kv, cross_out, ffn_in, ffn_out,
    )

    def lanes(low, width):
        return weight_grads[:, low : low + width].astype(F32)

    ffn_out_grad = jnp.concatenate([lanes(LANE_FO + D * j, D) for j in range(4)], axis=0)
    return (
        out[None], grad[None], memgrad[None],
        gain_grads[0], lanes(LANE_QKV, 3 * D), lanes(LANE_SO, D),
        gain_grads[1], lanes(LANE_CQ, D), lanes(LANE_CKV, 2 * D), lanes(LANE_CO, D),
        gain_grads[2], lanes(LANE_FI, 4 * D), ffn_out_grad,
    )


def layer_norm(value, gain):
    mean = jnp.mean(value, axis=-1, keepdims=True)
    centred = value - mean
    variance = jnp.mean(centred * centred, axis=-1, keepdims=True)
    return centred * lax.rsqrt(variance + norm_eps) * gain


def product(left, right):
    return jnp.dot(left, right, preferred_element_type=jnp.float32)


def outer_sum(left, right):
    flat_left = left.reshape(-1, left.shape[-1])
    flat_right = right.reshape(-1, right.shape[-1])
    return lax.dot_general(
        flat_left, flat_right, (((0,), (0,)), ((), ())), preferred_element_type=jnp.float32
    )


def back_product(grad, weight):
    return lax.dot_general(
        grad, weight, (((grad.ndim - 1,), (1,)), ((), ())), preferred_element_type=jnp.float32
    )


def attend(query, keys, values, allowed, scale):
    scores = jnp.einsum("eqhd,ekhd->ehqk", query, keys, preferred_element_type=jnp.float32) * scale
    scores = jnp.where(allowed[:, None], scores, -1e30)
    top = jnp.max(scores, axis=-1, keepdims=True)
    weights = jnp.exp(scores - top)
    probs = weights / jnp.sum(weights, axis=-1, keepdims=True)
    mixed = jnp.einsum(
        "ehqk,ekhd->eqhd", probs.astype(jnp.bfloat16), values, preferred_element_type=jnp.float32
    )
    return (mixed.astype(jnp.bfloat16), probs)


def attend_back(grad_mixed, query, keys, values, probs, scale):
    probs_low = probs.astype(jnp.bfloat16)
    grad_values = jnp.einsum(
        "ehqk,eqhd->ekhd", probs_low, grad_mixed, preferred_element_type=jnp.float32
    )
    grad_probs = jnp.einsum(
        "eqhd,ekhd->ehqk", grad_mixed, values, preferred_element_type=jnp.float32
    )
    grad_scores = probs * (grad_probs - jnp.sum(probs * grad_probs, axis=-1, keepdims=True))
    grad_low = grad_scores.astype(jnp.bfloat16)
    grad_query = (
        jnp.einsum("ehqk,ekhd->eqhd", grad_low, keys, preferred_element_type=jnp.float32) * scale
    )
    grad_keys = (
        jnp.einsum("ehqk,eqhd->ekhd", grad_low, query, preferred_element_type=jnp.float32) * scale
    )
    return (grad_query, grad_keys, grad_values)


def window_layout(res_group, mem_col):
    small = 1 - res_group
    small_count = jnp.sum(small, axis=-1, keepdims=True)
    small_before = jnp.cumsum(small, axis=-1) - small
    large_before = jnp.cumsum(res_group, axis=-1) - res_group
    offset = jnp.where(
        res_group == 1, SLOT_S * small_count + SLOT_L * large_before, SLOT_S * small_before
    )
    start = jnp.minimum(offset, mem_col - SLOT_L)
    return (offset, start)


def take_windows(column, starts):
    return jax.vmap(lambda begin: lax.dynamic_slice_in_dim(column, begin, SLOT_L, 0))(starts)


def forward(decoder_rows, windows, cross_allowed, weights):
    (
        self_gain,
        self_qkv,
        self_out,
        cross_gain,
        cross_query,
        cross_kv,
        cross_out,
        ffn_gain,
        ffn_in,
        ffn_out,
    ) = weights
    count = decoder_rows.shape[0] // SUFFIX
    scale = HEAD_DIM ** (-0.5)
    row_index = lax.broadcasted_iota(jnp.int32, (SUFFIX, SUFFIX), 0)
    col_index = lax.broadcasted_iota(jnp.int32, (SUFFIX, SUFFIX), 1)
    causal = (row_index >= col_index)[None]
    resid = decoder_rows.reshape(count, SUFFIX, D)
    normed_one = layer_norm(resid, self_gain.astype(jnp.float32)).astype(jnp.bfloat16)
    packed = product(normed_one, self_qkv).astype(jnp.bfloat16)
    heads = packed.reshape(count, SUFFIX, 3, HEADS, HEAD_DIM)
    self_mixed, self_probs = attend(heads[:, :, 0], heads[:, :, 1], heads[:, :, 2], causal, scale)
    self_mixed = self_mixed.reshape(count, SUFFIX, D)
    after_self = resid + product(self_mixed, self_out)
    normed_two = layer_norm(after_self, cross_gain.astype(jnp.float32)).astype(jnp.bfloat16)
    cross_q = product(normed_two, cross_query).astype(jnp.bfloat16)
    window_kv = product(windows, cross_kv).astype(jnp.bfloat16)
    query_heads = cross_q.reshape(count, SUFFIX, HEADS, HEAD_DIM)
    kv_heads = window_kv.reshape(count, SLOT_L, 2, HEADS, HEAD_DIM)
    cross_mixed, cross_probs = attend(
        query_heads, kv_heads[:, :, 0], kv_heads[:, :, 1], cross_allowed, scale
    )
    cross_mixed = cross_mixed.reshape(count, SUFFIX, D)
    after_cross = after_self + product(cross_mixed, cross_out)
    normed_three = layer_norm(after_cross, ffn_gain.astype(jnp.float32)).astype(jnp.bfloat16)
    up = product(normed_three, ffn_in)
    act = jax.nn.gelu(up, approximate=True).astype(jnp.bfloat16)
    result = after_cross + product(act, ffn_out)
    return (
        resid,
        normed_one,
        packed,
        self_probs,
        self_mixed,
        after_self,
        normed_two,
        cross_q,
        window_kv,
        cross_probs,
        cross_mixed,
        after_cross,
        normed_three,
        up,
        act,
        result,
    )


def backward(grad_out, saved, weights):
    (
        self_gain,
        self_qkv,
        self_out,
        cross_gain,
        cross_query,
        cross_kv,
        cross_out,
        ffn_gain,
        ffn_in,
        ffn_out,
    ) = weights
    (
        resid,
        normed_one,
        packed,
        self_probs,
        self_mixed,
        after_self,
        normed_two,
        cross_q,
        window_kv,
        cross_probs,
        cross_mixed,
        after_cross,
        normed_three,
        up,
        act,
        result,
    ) = saved
    count = resid.shape[0]
    scale = HEAD_DIM ** (-0.5)
    grad_out = grad_out.reshape(count, SUFFIX, D)
    out_low = grad_out.astype(jnp.bfloat16)
    ffn_out_grad = outer_sum(act, out_low)
    act_grad = back_product(out_low, ffn_out)
    gelu_value, gelu_back = jax.vjp(partial(jax.nn.gelu, approximate=True), up)
    up_grad = gelu_back(act_grad)[0].astype(jnp.bfloat16)
    ffn_in_grad = outer_sum(normed_three, up_grad)
    normed_three_grad = back_product(up_grad, ffn_in)
    norm_value, norm_back = jax.vjp(layer_norm, after_cross, ffn_gain.astype(jnp.float32))
    resid_part, ffn_gain_grad = norm_back(normed_three_grad)
    cross_res_grad = grad_out + resid_part
    cross_low = cross_res_grad.astype(jnp.bfloat16)
    cross_out_grad = outer_sum(cross_mixed, cross_low)
    mixed_grad = (
        back_product(cross_low, cross_out)
        .astype(jnp.bfloat16)
        .reshape(count, SUFFIX, HEADS, HEAD_DIM)
    )
    query_heads = cross_q.reshape(count, SUFFIX, HEADS, HEAD_DIM)
    kv_heads = window_kv.reshape(count, SLOT_L, 2, HEADS, HEAD_DIM)
    query_grad, keys_grad, values_grad = attend_back(
        mixed_grad, query_heads, kv_heads[:, :, 0], kv_heads[:, :, 1], cross_probs, scale
    )
    cross_q_grad = query_grad.reshape(count, SUFFIX, D).astype(jnp.bfloat16)
    window_kv_grad = (
        jnp.stack((keys_grad, values_grad), axis=2)
        .reshape(count, SLOT_L, 2 * D)
        .astype(jnp.bfloat16)
    )
    cross_query_grad = outer_sum(normed_two, cross_q_grad)
    normed_two_grad = back_product(cross_q_grad, cross_query)
    norm_value, norm_back = jax.vjp(layer_norm, after_self, cross_gain.astype(jnp.float32))
    resid_part, cross_gain_grad = norm_back(normed_two_grad)
    self_res_grad = cross_res_grad + resid_part
    self_low = self_res_grad.astype(jnp.bfloat16)
    self_out_grad = outer_sum(self_mixed, self_low)
    mixed_grad = (
        back_product(self_low, self_out)
        .astype(jnp.bfloat16)
        .reshape(count, SUFFIX, HEADS, HEAD_DIM)
    )
    heads = packed.reshape(count, SUFFIX, 3, HEADS, HEAD_DIM)
    query_grad, keys_grad, values_grad = attend_back(
        mixed_grad, heads[:, :, 0], heads[:, :, 1], heads[:, :, 2], self_probs, scale
    )
    packed_grad = (
        jnp.stack((query_grad, keys_grad, values_grad), axis=2)
        .reshape(count, SUFFIX, 3 * D)
        .astype(jnp.bfloat16)
    )
    self_qkv_grad = outer_sum(normed_one, packed_grad)
    normed_one_grad = back_product(packed_grad, self_qkv)
    norm_value, norm_back = jax.vjp(layer_norm, resid, self_gain.astype(jnp.float32))
    resid_part, self_gain_grad = norm_back(normed_one_grad)
    decoder_grad = self_res_grad + resid_part
    weight_grads = (
        self_gain_grad,
        self_qkv_grad,
        self_out_grad,
        cross_gain_grad,
        cross_query_grad,
        cross_out_grad,
        ffn_gain_grad,
        ffn_in_grad,
        ffn_out_grad,
    )
    return (decoder_grad, window_kv_grad, weight_grads)


def make_placer(all_starts, lowest, own_rows):

    def place(total, piece, begin):

        def add_one(item, acc):
            relative = all_starts[item] - lowest
            inside = ((relative > -SLOT_L) & (relative < own_rows)).astype(jnp.float32)
            spot = jnp.clip(relative + SLOT_L, 0, own_rows + SLOT_L)
            current = lax.dynamic_slice_in_dim(acc, spot, SLOT_L, 0)
            added = current + piece[item].astype(jnp.float32) * inside
            return lax.dynamic_update_slice_in_dim(acc, added, spot, 0)

        return lax.fori_loop(0, piece.shape[0], add_one, total)

    return place


def body(
    decoder_in,
    memory,
    res_group,
    prefix_len,
    self_gain,
    self_qkv,
    self_out,
    cross_gain,
    cross_query,
    cross_kv,
    cross_out,
    ffn_gain,
    ffn_in,
    ffn_out,
    cotangent,
):
    count = prefix_len.shape[1]
    own_rows = memory.shape[1]
    mem_col = own_rows * lax.axis_size("dp")
    offset, start = window_layout(res_group, mem_col)
    all_starts = start[0]
    first = lax.axis_index("dp") * count
    own_offset = lax.dynamic_slice_in_dim(offset[0], first, count)
    own_start = lax.dynamic_slice_in_dim(all_starts, first, count)
    own_group = lax.dynamic_slice_in_dim(res_group[0], first, count)
    valid = jnp.where(own_group == 1, PATCH_L, PATCH_S) + prefix_len[0]
    positions = own_start[:, None] + jnp.arange(SLOT_L, dtype=jnp.int32)[None]
    cross_allowed = (
        (positions >= own_offset[:, None]) & (positions < (own_offset + valid)[:, None])
    )[:, None]
    weights = (
        lax.all_gather(self_gain, "fsdp", axis=0, tiled=True),
        lax.all_gather(self_qkv, "fsdp", axis=0, tiled=True),
        lax.all_gather(self_out, "fsdp", axis=0, tiled=True),
        lax.all_gather(cross_gain, "fsdp", axis=0, tiled=True),
        lax.all_gather(cross_query, "fsdp", axis=0, tiled=True),
        lax.all_gather(cross_kv, "fsdp", axis=0, tiled=True),
        lax.all_gather(cross_out, "fsdp", axis=0, tiled=True),
        lax.all_gather(ffn_gain, "fsdp", axis=0, tiled=True),
        lax.all_gather(ffn_in, "fsdp", axis=0, tiled=True),
        lax.all_gather(ffn_out, "fsdp", axis=0, tiled=True),
    )
    column = lax.all_gather(memory[0], "dp", axis=0, tiled=True)
    windows = take_windows(column, own_start)
    saved = forward(decoder_in[0], windows, cross_allowed, weights)
    decoder_out = saved[-1]
    weights = (
        lax.all_gather(self_gain, "fsdp", axis=0, tiled=True),
        lax.all_gather(self_qkv, "fsdp", axis=0, tiled=True),
        lax.all_gather(self_out, "fsdp", axis=0, tiled=True),
        lax.all_gather(cross_gain, "fsdp", axis=0, tiled=True),
        lax.all_gather(cross_query, "fsdp", axis=0, tiled=True),
        lax.all_gather(cross_kv, "fsdp", axis=0, tiled=True),
        lax.all_gather(cross_out, "fsdp", axis=0, tiled=True),
        lax.all_gather(ffn_gain, "fsdp", axis=0, tiled=True),
        lax.all_gather(ffn_in, "fsdp", axis=0, tiled=True),
        lax.all_gather(ffn_out, "fsdp", axis=0, tiled=True),
    )
    column = lax.all_gather(memory[0], "dp", axis=0, tiled=True)
    windows = take_windows(column, own_start)
    saved = forward(decoder_in[0], windows, cross_allowed, weights)
    whole_kv = weights[5]
    decoder_grad, window_kv_grad, local_grads = backward(cotangent[0], saved, weights)
    lowest = lax.axis_index("dp") * own_rows
    place = make_placer(all_starts, lowest, own_rows)
    empty = jnp.zeros((own_rows + 2 * SLOT_L, 2 * D), jnp.float32)
    summed = place(empty, lax.all_gather(window_kv_grad, "dp", axis=0, tiled=True), jnp.int32(0))
    own_kv_grad = summed[SLOT_L : SLOT_L + own_rows].astype(jnp.bfloat16)
    memory_grad = back_product(own_kv_grad, whole_kv)
    cross_kv_part = outer_sum(memory[0], own_kv_grad)
    grads = (
        local_grads[0],
        local_grads[1],
        local_grads[2],
        local_grads[3],
        local_grads[4],
        cross_kv_part,
        local_grads[5],
        local_grads[6],
        local_grads[7],
        local_grads[8],
    )
    shards = (
        lax.psum_scatter(
            grads[0].astype(jnp.bfloat16), "fsdp", scatter_dimension=0, tiled=True
        ).astype(jnp.float32),
        lax.psum_scatter(
            grads[1].astype(jnp.bfloat16), "fsdp", scatter_dimension=0, tiled=True
        ).astype(jnp.float32),
        lax.psum_scatter(
            grads[2].astype(jnp.bfloat16), "fsdp", scatter_dimension=0, tiled=True
        ).astype(jnp.float32),
        lax.psum_scatter(
            grads[3].astype(jnp.bfloat16), "fsdp", scatter_dimension=0, tiled=True
        ).astype(jnp.float32),
        lax.psum_scatter(
            grads[4].astype(jnp.bfloat16), "fsdp", scatter_dimension=0, tiled=True
        ).astype(jnp.float32),
        lax.psum_scatter(
            grads[5].astype(jnp.bfloat16), "fsdp", scatter_dimension=0, tiled=True
        ).astype(jnp.float32),
        lax.psum_scatter(
            grads[6].astype(jnp.bfloat16), "fsdp", scatter_dimension=0, tiled=True
        ).astype(jnp.float32),
        lax.psum_scatter(
            grads[7].astype(jnp.bfloat16), "fsdp", scatter_dimension=0, tiled=True
        ).astype(jnp.float32),
        lax.psum_scatter(
            grads[8].astype(jnp.bfloat16), "fsdp", scatter_dimension=0, tiled=True
        ).astype(jnp.float32),
        lax.psum_scatter(
            grads[9].astype(jnp.bfloat16), "fsdp", scatter_dimension=0, tiled=True
        ).astype(jnp.float32),
    )
    totals = (
        lax.psum(shards[0].astype(jnp.bfloat16), "dp").astype(jnp.float32),
        lax.psum(shards[1].astype(jnp.bfloat16), "dp").astype(jnp.float32),
        lax.psum(shards[2].astype(jnp.bfloat16), "dp").astype(jnp.float32),
        lax.psum(shards[3].astype(jnp.bfloat16), "dp").astype(jnp.float32),
        lax.psum(shards[4].astype(jnp.bfloat16), "dp").astype(jnp.float32),
        lax.psum(shards[5].astype(jnp.bfloat16), "dp").astype(jnp.float32),
        lax.psum(shards[6].astype(jnp.bfloat16), "dp").astype(jnp.float32),
        lax.psum(shards[7].astype(jnp.bfloat16), "dp").astype(jnp.float32),
        lax.psum(shards[8].astype(jnp.bfloat16), "dp").astype(jnp.float32),
        lax.psum(shards[9].astype(jnp.bfloat16), "dp").astype(jnp.float32),
    )
    return (
        decoder_out,
        decoder_grad,
        memory_grad[None],
        totals[0],
        totals[1],
        totals[2],
        totals[3],
        totals[4],
        totals[5],
        totals[6],
        totals[7],
        totals[8],
        totals[9],
    )


def choose(mesh):
    ranks, columns = mesh.shape["dp"], mesh.shape["fsdp"]
    slabs = (D // columns) % (16 * (ranks // CORES)) == 0
    if slabs and columns == 2 and ranks == RING * SIDE * CORES:
        return partial(fused_body, ranks, columns)
    return body


def solution(mesh):
    placed = (
        P("fsdp", "dp", None),
        P("fsdp", "dp", None),
        P("fsdp", None),
        P("fsdp", "dp"),
        P("fsdp"),
        P("fsdp", None),
        P("fsdp", None),
        P("fsdp"),
        P("fsdp", None),
        P("fsdp", None),
        P("fsdp", None),
        P("fsdp"),
        P("fsdp", None),
        P("fsdp", None),
        P("fsdp", "dp", None),
    )
    return jax.shard_map(
        choose(mesh),
        mesh=mesh,
        in_specs=placed,
        out_specs=(
            P("fsdp", "dp", None),
            P("fsdp", "dp", None),
            P("fsdp", "dp", None),
            P("fsdp"),
            P("fsdp", None),
            P("fsdp", None),
            P("fsdp"),
            P("fsdp", None),
            P("fsdp", None),
            P("fsdp", None),
            P("fsdp"),
            P("fsdp", None),
            P("fsdp", None),
        ),
        check_vma=False,
    )
```

```python
from functools import partial

import jax
import jax.numpy as jnp
from jax import lax
from jax.experimental import pallas as pl
from jax.experimental.pallas import tpu as pltpu
from jax.sharding import PartitionSpec as P

D = 768
HEADS = 12
HEAD_DIM = 64
SUFFIX = 32
PATCH_S = 196
PATCH_L = 576
SLOT_S = 228
SLOT_L = 608
RING = 4
SIDE = 2
CORES = 2
norm_eps = 1e-06
MESH = pl.DeviceIdType.MESH
F32 = jnp.float32
BF16 = jnp.bfloat16
NONE = -1e30


def mm(left, right):
    return jnp.dot(left, right, preferred_element_type=F32)


def mm_nt(left, right):
    return lax.dot_general(left, right, (((1,), (1,)), ((), ())), preferred_element_type=F32)


def mm_tn(left, right):
    return lax.dot_general(left, right, (((0,), (0,)), ((), ())), preferred_element_type=F32)


def normed(value):
    mean = jnp.mean(value, axis=-1, keepdims=True)
    centred = value - mean
    variance = jnp.mean(centred * centred, axis=-1, keepdims=True)
    scale = lax.rsqrt(variance + norm_eps)
    return centred * scale, scale


def norm_back(grad, hat, scale, gain):
    inner = grad * gain
    mean_one = jnp.mean(inner, axis=-1, keepdims=True)
    mean_two = jnp.mean(inner * hat, axis=-1, keepdims=True)
    gain_grad = jnp.sum(grad * hat, axis=0, keepdims=True)
    return scale * (inner - mean_one - hat * mean_two), gain_grad


def gelu_parts(up):
    inner = 0.7978845608 * (up + 0.044715 * up * up * up)
    tanh = jnp.tanh(inner)
    slope = 0.7978845608 * (1.0 + 3.0 * 0.044715 * up * up)
    value = 0.5 * up * (1.0 + tanh)
    grad = 0.5 * (1.0 + tanh) + 0.5 * up * (1.0 - tanh * tanh) * slope
    return value, grad


class Gather:
    def __init__(self, place, view, sems, at, has=None):
        self.z, self.x, self.c, self.f = place
        self.view = view
        self.send, self.recv = sems
        self.at = at
        self.has = has
        self.sent = []

    def copy(self, block, target, into, index):
        ref = self.view(*block)
        z, x, c = target
        return pltpu.make_async_remote_copy(
            src_ref=ref,
            dst_ref=ref,
            send_sem=self.send.at[self.at, index],
            recv_sem=self.recv.at[self.at, into],
            device_id=(z * (SIDE * CORES) + x * CORES + c, self.f),
            device_id_type=MESH,
        )

    def place_at(self, k):
        return lax.rem(self.z + k + RING, RING)

    def holds(self, block, cond):
        return cond if self.has is None else cond & self.has(*block)

    def go(self, block, target, into, cond):
        item = self.copy(block, target, into, len(self.sent))
        cond = self.holds(block, cond)
        pl.when(cond)(item.start)
        self.sent.append((cond, item))

    def wait(self, block, into, cond):
        pl.when(self.holds(block, cond))(self.copy(block, (self.z, 1 - self.x, self.c), into, 0).wait_recv)

    def line(self, block, up, down, cond):
        z, x, c = self.z, self.x, self.c
        at = block[0]
        if up:
            self.go(block, (self.place_at(1), x, c), at, cond & (z < RING - 1))
        if down:
            self.go(block, (self.place_at(-1), x, c), at, cond & (z > 0))

    def spread(self, block, cond):
        z, x, c = self.z, self.x, self.c
        self.go(block, (z, 1 - x, c), RING + block[0], cond)
        self.go(block, (z, x, 1 - c), 2 * RING + block[0], cond)

    def step_one(self):
        own = (self.z, self.x, self.c)
        self.line(own, True, True, self.z >= 0)
        self.spread(own, self.z >= 0)

    def arrive(self, k):
        low, high = (self.place_at(-k), self.x, self.c), (self.place_at(k), self.x, self.c)
        self.wait(low, low[0], self.z >= k)
        self.line(low, True, False, self.z >= k)
        self.wait(high, high[0], self.z < RING - k)
        self.line(high, False, True, self.z < RING - k)
        self.spread(low, self.z >= k)
        self.spread(high, self.z < RING - k)

    def side(self, k):
        z, x, c = self.z, self.x, self.c
        for at, cond in ((self.place_at(-k), z >= k), (self.place_at(k), z < RING - k))[: 1 if k == 0 else 2]:
            block = (at, 1 - x, c)
            self.wait(block, RING + at, cond)
            self.go(block, (z, x, 1 - c), 3 * RING + at, cond)

    def step_two(self):
        self.arrive(1)
        self.side(0)

    def step_three(self):
        self.arrive(2)
        self.side(1)

    def step_four(self):
        self.arrive(3)
        self.side(2)

    def step_five(self):
        self.side(3)
        always = self.z >= 0
        for at in range(RING):
            self.wait((at, self.x, 1 - self.c), 2 * RING + at, always)
            self.wait((at, 1 - self.x, 1 - self.c), 3 * RING + at, always)

    def finish(self):
        for cond, item in self.sent:
            pl.when(cond)(item.wait_send)


class Spread(Gather):
    def __init__(self, place, theirs, mine, sems, at):
        super().__init__(place, theirs, sems, at)
        self.mine = mine
        self.pushed = []

    def push(self):
        z, x, c = self.z, self.x, self.c
        for n, block in enumerate(((z, x, c), (z, 1 - x, c))):
            ref = self.mine(*block)
            item = pltpu.make_async_remote_copy(
                src_ref=ref, dst_ref=ref, send_sem=self.send.at[self.at, 28 + n], recv_sem=self.recv.at[self.at, 16 + n],
                device_id=(z * (SIDE * CORES) + x * CORES + c, 1 - self.f), device_id_type=MESH,
            )
            item.start()
            self.pushed.append(item)

    def step_one(self):
        z, x, c = self.z, self.x, self.c
        always = z >= 0
        own, side = (z, x, c), (z, 1 - x, c)
        self.wait(own, 16, always)
        self.line(own, True, True, always)
        self.go(own, (z, x, 1 - c), 2 * RING + z, always)
        self.wait(side, 17, always)
        self.go(side, (z, x, 1 - c), 3 * RING + z, always)

    def step_two(self):
        self.arrive(1)

    def finish(self):
        super().finish()
        for item in self.pushed:
            item.wait_send()


class Pieces:
    def __init__(self, count, own_rows):
        self.half = count // 2
        self.edge = self.half * SLOT_S
        self.rows = own_rows
        self.count = count

    def start(self, rank):
        return jnp.where(
            rank < self.half, SLOT_S * rank, self.edge + SLOT_L * (rank - self.half)
        )

    def size(self, rank):
        return jnp.where(rank < self.half, SLOT_S, SLOT_L)

    def rank_of(self, row):
        return jnp.where(
            row < self.edge,
            lax.div(row, SLOT_S),
            self.half + lax.div(jnp.maximum(row - self.edge, 0), SLOT_L),
        )

    def first_rank(self, device):
        return self.rank_of(device * self.rows)

    def last_rank(self, device):
        return self.rank_of(device * self.rows + self.rows - 1)

    def first_device(self, rank):
        return lax.div(self.start(rank), self.rows)

    def last_device(self, rank):
        return lax.div(self.start(rank) + self.size(rank) - 1, self.rows)


SLOTS = 3
UNITS = 16
LANE_QKV, LANE_SO, LANE_CQ, LANE_CKV, LANE_CO, LANE_FI, LANE_FO = 0, 2304, 3072, 3840, 5376, 6144, 9216
CHUNKS = ((0, 2304), (2304, 1536), (3840, 1536), (5376, 2304), (7680, 2304), (9984, 2304))
LOADS_BY_CHUNK = ((0,), (1, 2), (3,), (4, 5), (6,), (7, 8, 9))
PIECE = 384
HALF_UNITS = 6


def layer_kernel(
    ranks,
    columns,
    x_ref, cot_ref, mem_ref, res_ref, pre_ref, gains_ref,
    qkv_ref, so_ref, cq_ref, ckv_ref, co_ref, fi_ref, fo_ref,
    out_ref, grad_ref, memgrad_ref, gain_out_ref, weights_out_ref,
    wb, gb, rb, sb, xb, cb, nb, olr, ob, tb, pb, gainb, memp, kvb, kvg, kp, kr, kc, ky, cp,
    kx, ks, hb, ab, ug, usend_b, urecv_b,
    cqb, qbuf, osend, ostat_send, obuf, ostat, dob, dstat_b, dobuf, dstat, dqsend, dqbuf, gmine, gpeer,
    load_sem, wsend, wrecv, gsend, grecv, bsend, brecv, asend, arecv, fsend, frecv, ysend, yrecv, psend, precv, usend, urecv,
    ksend, krecv,
):
    me = lax.axis_index("dp")
    f = lax.axis_index("fsdp")
    z = lax.div(me, SIDE * CORES)
    x = lax.rem(lax.div(me, CORES), SIDE)
    c = lax.rem(me, CORES)
    chip = lax.div(me, CORES)
    chips = ranks // CORES
    place = (z, x, c, f)
    half_rows = D // columns
    slab = half_rows // chips
    own_rows = mem_ref.shape[0]
    padded = memp.shape[0]
    lay = Pieces(ranks, own_rows)
    other = 1 - f
    mate = (z * (SIDE * CORES) + x * CORES + (1 - c), f)
    everyone = ranks * columns
    lin = f * ranks + me

    loads = []

    def load(src, lane, width):
        item = pltpu.make_async_copy(
            src, wb.at[pl.ds(pl.multiple_of(f * half_rows, 128), half_rows), pl.ds(lane, width)],
            load_sem.at[len(loads)],
        )
        item.start()
        loads.append(item)

    load(qkv_ref, LANE_QKV, 3 * D)
    load(so_ref, LANE_SO, D)
    load(cq_ref, LANE_CQ, D)
    load(ckv_ref, LANE_CKV, 2 * D)
    load(co_ref, LANE_CO, D)
    load(fi_ref, LANE_FI, 4 * D)
    for j in range(4):
        load(fo_ref.at[pl.ds(j * half_rows, half_rows)], LANE_FO + D * j, D)

    for s in range(SLOTS):
        qbuf[s] = jnp.zeros_like(qbuf[s])
        obuf[s] = jnp.zeros_like(obuf[s])
        ostat[s, 0] = jnp.full_like(ostat[s, 0], NONE)
        ostat[s, 1] = jnp.zeros_like(ostat[s, 1])
        dobuf[s] = jnp.zeros_like(dobuf[s])
        dstat[s] = jnp.zeros_like(dstat[s])
        dqbuf[s] = jnp.zeros_like(dqbuf[s])

    def rows_of(device):
        return pl.ds(pl.multiple_of(device * SUFFIX, SUFFIX), SUFFIX)

    xb[me] = x_ref[...]
    cb[me] = cot_ref[...].astype(BF16)
    pb[me] = jnp.full((8, 128), pre_ref[0, 0].astype(F32), F32)
    gainb[f] = gains_ref[...]

    barrier = pltpu.get_barrier_semaphore()

    def greet(i, carry):
        to = lax.rem(me + i, ranks)
        pl.semaphore_signal(barrier, inc=1, device_id=(to, f), device_id_type=MESH)
        return carry

    lax.fori_loop(1, ranks, greet, 0)
    pl.semaphore_signal(barrier, inc=1, device_id=(me, other), device_id_type=MESH)
    pl.semaphore_wait(barrier, ranks)

    y_items = []

    def push_y(src, dst, at):
        item = pltpu.make_async_remote_copy(
            src_ref=src, dst_ref=dst, send_sem=ysend.at[at], recv_sem=yrecv.at[at],
            device_id=(me, other), device_id_type=MESH,
        )
        item.start()
        y_items.append(item)
        return item

    class Tell:
        def __init__(self, ref, at):
            self.ref, self.at = ref, at

        def copy(self, source, index, to):
            return pltpu.make_async_remote_copy(
                src_ref=self.ref.at[source], dst_ref=self.ref.at[source], send_sem=bsend.at[self.at, index],
                recv_sem=brecv.at[self.at, source], device_id=(to, f), device_id_type=MESH,
            )

        def start(self):
            def one(i, carry):
                self.copy(me, i, lax.rem(me + i, ranks)).start()
                return carry

            lax.fori_loop(1, ranks, one, 0)

        def wait(self):
            def one(i, carry):
                source = lax.rem(me + i, ranks)
                self.copy(source, i, source).wait_recv()
                return carry

            lax.fori_loop(1, ranks, one, 0)

        def finish(self):
            def one(i, carry):
                self.copy(me, i, lax.rem(me + i, ranks)).wait_send()
                return carry

            lax.fori_loop(1, ranks, one, 0)

    def slab_view(first, width, rows_from):
        half = width // CORES

        def view(zz, xx, cc):
            row = pl.multiple_of(rows_from * half_rows + (zz * SIDE + xx) * slab, 16)
            lane = pl.multiple_of(first + cc * half, 128)
            return wb.at[pl.ds(row, slab), pl.ds(lane, half)]

        return view

    def block_view(ref):
        def view(zz, xx, cc):
            return ref.at[zz * (SIDE * CORES) + xx * CORES + cc]

        return view

    def token_rows(col, cc, at):
        return pl.ds(pl.multiple_of(((col * CORES + cc) * chips + at) * SUFFIX, SUFFIX), SUFFIX)

    def token_view(ref):
        def view(zz, xx, cc):
            return ref.at[token_rows(f, cc, zz * SIDE + xx)]

        return view

    plane = pl.ds(pl.multiple_of((f * CORES + c) * chips * SUFFIX, SUFFIX), chips * SUFFIX)
    plane_in = pl.ds(pl.multiple_of((other * CORES + c) * chips * SUFFIX, SUFFIX), chips * SUFFIX)
    plane_mate = pl.ds(pl.multiple_of((other * CORES + 1 - c) * chips * SUFFIX, SUFFIX), chips * SUFFIX)

    class Across:
        def __init__(self, ref, at):
            self.ref, self.at = ref, at

        def copy(self, rows, n, to):
            ref = self.ref.at[rows]
            return pltpu.make_async_remote_copy(
                src_ref=ref, dst_ref=ref, send_sem=asend.at[self.at, n], recv_sem=arecv.at[self.at, n],
                device_id=to, device_id_type=MESH,
            )

        def start(self):
            self.copy(plane, 0, (me, other)).start()

        def relay(self):
            self.copy(plane_in, 0, (me, other)).wait_recv()
            self.copy(plane_in, 1, mate).start()

        def wait(self):
            self.copy(plane_mate, 1, mate).wait_recv()

        def finish(self):
            self.copy(plane, 0, (me, other)).wait_send()
            self.copy(plane_in, 1, mate).wait_send()

    sems = (gsend, grecv)
    ag_x = Gather(place, block_view(xb), sems, 0)
    ag_c = Gather(place, block_view(cb), sems, 1)
    ag_n = Gather(place, token_view(nb), sems, 2)
    tell_p = Tell(pb, 0)
    spread = [
        Spread(place, slab_view(first, width, other), slab_view(first, width, f), (wsend, wrecv), n)
        for n, (first, width) in enumerate(CHUNKS)
    ]

    def push_chunk(n):
        for i in LOADS_BY_CHUNK[n]:
            loads[i].wait()
        spread[n].push()

    ag_x.step_one()
    push_chunk(0)
    gain_item = push_y(gainb.at[f], gainb.at[f], 0)
    tell_p.start()
    push_chunk(1)

    def tick(n):
        for age, act in ((4, "step_five"), (3, "step_four"), (2, "step_three"), (1, "step_two"), (0, "step_one")):
            if 0 <= n - age < len(spread):
                getattr(spread[n - age], act)()
        if n + 2 < len(spread):
            push_chunk(n + 2)

    ag_x.step_two()
    tick(0)
    ag_x.step_three()
    tick(1)
    ag_x.step_four()
    tick(2)
    ag_x.step_five()
    tick(3)
    gain_item.wait_recv()

    memp[0:own_rows] = mem_ref[...]
    memp[own_rows:padded] = jnp.zeros((padded - own_rows, D), BF16)

    positions = []
    before_large = jnp.int32(0)
    mine_rank = jnp.int32(0)
    for i in range(ranks):
        group = res_ref[0, i]
        spot = jnp.where(group == 1, lay.half + before_large, i - before_large)
        positions.append(spot)
        mine_rank = jnp.where(me == i, spot, mine_rank)
        before_large = before_large + group

    def example_of(rank):
        found = jnp.int32(0)
        for i in range(ranks):
            found = jnp.where(positions[i] == rank, i, found)
        return found

    gain = [jnp.concatenate([gainb[i, n : n + 1] for i in range(columns)], axis=1) for n in range(3)]

    mine = example_of(me)
    resid = xb[mine]
    hat_one, rs_one = normed(resid)
    n1 = (hat_one * gain[0]).astype(BF16)

    lanes = lax.broadcasted_iota(jnp.int32, (1, 256), 1)
    head_f32 = [(lax.div(lanes, HEAD_DIM) == h).astype(F32) for h in range(4)]
    head_b16 = [m.astype(BF16) for m in head_f32]

    def stack(value):
        return jnp.concatenate([value * m for m in head_b16], axis=0)

    def unstack(value):
        rows = value.shape[0] // 4
        total = value[0:rows] * head_f32[0]
        for h in range(1, 4):
            total = total + value[h * rows : (h + 1) * rows] * head_f32[h]
        return total

    tick(4)
    q = mm(n1, wb[:, 0:D]).astype(BF16)
    k = mm(n1, wb[:, D : 2 * D]).astype(BF16)
    v = mm(n1, wb[:, 2 * D : 3 * D]).astype(BF16)
    scale = HEAD_DIM**-0.5
    qs = (q.astype(F32) * scale).astype(BF16)
    row_at = lax.broadcasted_iota(jnp.int32, (SUFFIX, SUFFIX), 0)
    col_at = lax.broadcasted_iota(jnp.int32, (SUFFIX, SUFFIX), 1)
    causal = jnp.concatenate([(row_at >= col_at).astype(F32)] * 4, axis=0) > 0.0
    self_p = []
    mixed = []
    for g in range(3):
        sl = slice(256 * g, 256 * g + 256)
        s = mm_nt(stack(qs[:, sl]), k[:, sl])
        s = jnp.where(causal, s, NONE)
        e = jnp.exp(s - jnp.max(s, axis=-1, keepdims=True))
        p = e / jnp.sum(e, axis=-1, keepdims=True)
        self_p.append(p)
        mixed.append(unstack(mm(p.astype(BF16), v[:, sl])))
    sm = jnp.concatenate(mixed, axis=1).astype(BF16)

    tick(5)
    after_self = resid + mm(sm, wb[:, LANE_SO : LANE_SO + D])
    hat_two, rs_two = normed(after_self)
    n2 = (hat_two * gain[1]).astype(BF16)
    cq = mm(n2, wb[:, LANE_CQ : LANE_CQ + D]).astype(BF16)
    cqb[...] = cq

    my_first, my_last = lay.first_device(me), lay.last_device(me)
    held_first, held_last = lay.first_rank(me), lay.last_rank(me)

    def piece_copy(src, dst, at, sent, landed, target):
        return pltpu.make_async_remote_copy(
            src_ref=src, dst_ref=dst, send_sem=psend.at[at, sent], recv_sem=precv.at[at, landed],
            device_id=(target, f), device_id_type=MESH,
        )

    def to_holders(pairs):
        for i in range(SLOTS):
            target = my_first + i
            slot = me - lay.first_rank(target)
            there = target <= my_last

            @pl.when(there & (target == me))
            def _():
                for src, dst, at in pairs:
                    dst[slot] = src[...]

            @pl.when(there & (target != me))
            def _():
                for src, dst, at in pairs:
                    piece_copy(src, dst.at[slot], at, i, slot, target).start()

    def to_holders_sent(pairs):
        for i in range(SLOTS):
            target = my_first + i

            @pl.when((target <= my_last) & (target != me))
            def _():
                for src, dst, at in pairs:
                    piece_copy(src, dst.at[0], at, i, 0, target).wait_send()

    def at_holders(pairs):
        for s in range(SLOTS):
            rank = held_first + s

            @pl.when((rank <= held_last) & (rank != me))
            def _():
                for src, dst, at in pairs:
                    piece_copy(src, dst.at[s], at, 0, s, rank).wait_recv()

    def to_owners(pairs):
        for s in range(SLOTS):
            rank = held_first + s
            index = me - lay.first_device(rank)
            there = rank <= held_last

            @pl.when(there & (rank == me))
            def _():
                for src, dst, at in pairs:
                    dst[index] = src[s]

            @pl.when(there & (rank != me))
            def _():
                for src, dst, at in pairs:
                    piece_copy(src.at[s], dst.at[index], at, s, index, rank).start()

    def to_owners_sent(pairs):
        for s in range(SLOTS):
            rank = held_first + s

            @pl.when((rank <= held_last) & (rank != me))
            def _():
                for src, dst, at in pairs:
                    piece_copy(src.at[s], dst.at[0], at, s, 0, rank).wait_send()

    def at_owners(pairs):
        for i in range(SLOTS):
            target = my_first + i

            @pl.when((target <= my_last) & (target != me))
            def _():
                for src, dst, at in pairs:
                    piece_copy(src.at[0], dst.at[i], at, 0, i, target).wait_recv()

    q_pairs = [(cqb, qbuf, 0)]
    o_pairs = [(osend, obuf, 1), (ostat_send, ostat, 2)]
    d_pairs = [(dob, dobuf, 3), (dstat_b, dstat, 4)]
    dq_pairs = [(dqsend, dqbuf, 5)]

    to_holders(q_pairs)

    tick(6)
    ag_c.step_one()

    def kv_step(i, carry):
        lane = pl.multiple_of(i * 256, 256)
        kvb[:, pl.ds(lane, 256)] = mm(memp[...], wb[:, pl.ds(LANE_CKV + lane, 256)]).astype(BF16)
        return carry

    lax.fori_loop(0, 6, kv_step, 0)

    tell_p.wait()
    lane_f = lax.broadcasted_iota(jnp.int32, (SUFFIX, padded), 1).astype(F32)
    allowed = []
    for s in range(SLOTS):
        rank = held_first + s
        ok = rank <= held_last
        example = example_of(jnp.minimum(rank, ranks - 1))
        prefix = pb[example][0:1, 0:1]
        low = (lay.start(rank) - me * own_rows).astype(F32)
        patches = jnp.where(rank < lay.half, PATCH_S, PATCH_L).astype(F32)
        high = jnp.minimum(low + patches + prefix, jnp.float32(own_rows))
        high = jnp.where(ok, high, jnp.float32(-1.0))
        allowed.append(((lane_f >= low) & (lane_f < high)).astype(F32))
    allowed = jnp.concatenate(allowed * 4, axis=0) > 0.0

    at_holders(q_pairs)
    qh = jnp.concatenate([qbuf[s] for s in range(SLOTS)], axis=0)
    qh = (qh.astype(F32) * scale).astype(BF16)
    lane_c = lax.broadcasted_iota(jnp.int32, (SUFFIX, 128), 1)
    top_c = [jnp.zeros((SUFFIX, 128), F32) for _ in range(SLOTS)]
    sum_c = [jnp.zeros((SUFFIX, 128), F32) for _ in range(SLOTS)]
    for g in range(3):
        sl = slice(256 * g, 256 * g + 256)
        s = mm_nt(stack(qh[:, sl]), kvb[:, sl])
        s = jnp.where(allowed, s, NONE)
        top = jnp.max(s, axis=-1, keepdims=True)
        e = jnp.where(allowed, jnp.exp(s - top), 0.0)
        total = jnp.sum(e, axis=-1, keepdims=True)
        o = mm(e.astype(BF16), kvb[:, D + 256 * g : D + 256 * g + 256])
        o = o * jnp.where(total > 0.0, 1.0 / jnp.where(total > 0.0, total, 1.0), 0.0)
        o = unstack(o).astype(BF16)
        for n in range(SLOTS):
            osend[n, :, sl] = o[n * SUFFIX : (n + 1) * SUFFIX]
            for h in range(4):
                at = h * SLOTS * SUFFIX + n * SUFFIX
                hit = lane_c == 4 * g + h
                top_c[n] = jnp.where(hit, top[at : at + SUFFIX], top_c[n])
                sum_c[n] = jnp.where(hit, total[at : at + SUFFIX], sum_c[n])
    for n in range(SLOTS):
        ostat_send[n, 0] = top_c[n]
        ostat_send[n, 1] = sum_c[n]
    to_owners(o_pairs)

    tick(7)
    ag_c.step_two()
    at_owners(o_pairs)

    def expand(compact):
        low = lane_c < HEAD_DIM
        return jnp.concatenate(
            [jnp.where(low, compact[:, 2 * t : 2 * t + 1], compact[:, 2 * t + 1 : 2 * t + 2]) for t in range(6)],
            axis=1,
        )

    tops = [ostat[i, 0] for i in range(SLOTS)]
    top_all = jnp.maximum(jnp.maximum(tops[0], tops[1]), tops[2])
    shares = [ostat[i, 1] * jnp.exp(tops[i] - top_all) for i in range(SLOTS)]
    whole = shares[0] + shares[1] + shares[2]
    whole = jnp.where(whole > 0.0, whole, 1.0)
    lse = top_all + jnp.log(whole)
    cross = jnp.zeros((SUFFIX, D), F32)
    for i in range(SLOTS):
        cross = cross + expand(shares[i] / whole) * obuf[i].astype(F32)
    cm = cross.astype(BF16)

    after_cross = after_self + mm(cm, wb[:, LANE_CO : LANE_CO + D])
    hat_three, rs_three = normed(after_cross)
    n3 = (hat_three * gain[2]).astype(BF16)
    nb[token_rows(f, c, chip)] = n3
    ag_n.step_one()

    tick(8)
    ag_c.step_three()
    ag_n.step_two()
    tick(9)
    ag_c.step_four()
    ag_n.step_three()
    ag_c.step_five()
    out_low = cb[mine]
    cot = out_low.astype(F32)
    acts, up_grads = [], []
    hidden_grad = [mm_nt(out_low, wb[:, LANE_FO + D * j : LANE_FO + D * (j + 1)]) for j in range(4)]

    def by_hidden(j):
        parts = []
        for t in range(D // half_rows):
            at = D * j + t * half_rows
            col, unit = at // (4 * half_rows), (at % (4 * half_rows)) // half_rows
            parts.append(hidden_grad[unit][:, col * half_rows : (col + 1) * half_rows])
        return jnp.concatenate(parts, axis=1)

    n3_grad = jnp.zeros((SUFFIX, D), F32)
    for j in range(4):
        weight = wb[:, LANE_FI + D * j : LANE_FI + D * (j + 1)]
        value, slope = gelu_parts(mm(n3, weight))
        acts.append(value.astype(BF16))
        part = (by_hidden(j) * slope).astype(BF16)
        n3_grad = n3_grad + mm_nt(part, weight)
    act = jnp.concatenate(acts, axis=1)

    part, ffn_gain_grad = norm_back(n3_grad, hat_three, rs_three, gain[2])
    cross_res = cot + part
    cross_low = cross_res.astype(BF16)
    d_mixed = mm_nt(cross_low, wb[:, LANE_CO : LANE_CO + D]).astype(BF16)
    dob[...] = d_mixed
    prod = d_mixed.astype(F32) * cross
    delta = jnp.zeros((SUFFIX, 128), F32)
    for t in range(6):
        tile = prod[:, 128 * t : 128 * (t + 1)]
        left = jnp.sum(jnp.where(lane_c < HEAD_DIM, tile, 0.0), axis=-1, keepdims=True)
        right = jnp.sum(jnp.where(lane_c < HEAD_DIM, 0.0, tile), axis=-1, keepdims=True)
        delta = jnp.where(lane_c == 2 * t, left, delta)
        delta = jnp.where(lane_c == 2 * t + 1, right, delta)
    dstat_b[0] = lse
    dstat_b[1] = delta
    to_holders(d_pairs)
    for r in range(ranks):
        olr[token_rows(f, r % CORES, r // CORES)] = cb[example_of(r)]
    across_o = Across(olr, 0)
    across_n = Across(nb, 1)
    across_o.start()

    down = jnp.zeros((SUFFIX, D), F32)
    for j in range(4):
        lhs = jnp.concatenate(
            [act[:, i * 4 * half_rows + j * half_rows : i * 4 * half_rows + (j + 1) * half_rows] for i in range(columns)],
            axis=1,
        )
        down = down + mm(lhs, wb[:, LANE_FO + D * j : LANE_FO + D * (j + 1)])
    ob[me, 0:SUFFIX] = (after_cross + down).astype(BF16)

    def unit_device(h):
        return CORES * (h + 1) if h < HALF_UNITS else CORES * (h - HALF_UNITS + 1) + 1

    unit_items = []

    def push_unit(h, left, right):
        to = unit_device(h)
        sb[h, :, 0:D] = left
        sb[h, :, D : D + PIECE] = right

        @pl.when(me == to)
        def _():
            rb[rows_of(me)] = sb[h]

        @pl.when(me != to)
        def _():
            pltpu.make_async_remote_copy(
                src_ref=sb.at[h], dst_ref=rb.at[rows_of(me)], send_sem=usend.at[h],
                recv_sem=urecv.at[me], device_id=(to, f), device_id_type=MESH,
            ).start()

        unit_items.append((h, to))

    ag_n.step_four()
    ag_n.step_five()
    across_n.start()
    push_unit(HALF_UNITS + 4, cm, cross_low[:, 0:PIECE])
    push_unit(HALF_UNITS + 5, cm, cross_low[:, PIECE:])

    at_holders(d_pairs)

    doh = jnp.concatenate([dobuf[s] for s in range(SLOTS)], axis=0)
    for g in range(3):
        sl = slice(256 * g, 256 * g + 256)
        kg = kvb[:, sl]
        vg = kvb[:, D + 256 * g : D + 256 * g + 256]
        q4 = stack(qh[:, sl])
        do4 = stack(doh[:, sl])
        lse_col = jnp.concatenate([dstat[n, 0][:, 4 * g + h : 4 * g + h + 1] for h in range(4) for n in range(SLOTS)], axis=0)
        del_col = jnp.concatenate([dstat[n, 1][:, 4 * g + h : 4 * g + h + 1] for h in range(4) for n in range(SLOTS)], axis=0)
        s = mm_nt(q4, kg)
        p = jnp.where(allowed, jnp.exp(jnp.where(allowed, s - lse_col, 0.0)), 0.0)
        dp = mm_nt(do4, vg)
        ds = (p * (dp - del_col)).astype(BF16)
        kvg[:, D + 256 * g : D + 256 * g + 256] = mm_tn(p.astype(BF16), do4).astype(BF16)
        kvg[:, sl] = mm_tn(ds, q4).astype(BF16)
        dq = unstack(mm(ds, kg)) * scale
        for n in range(SLOTS):
            dqsend[n, :, sl] = dq[n * SUFFIX : (n + 1) * SUFFIX]
    to_owners(dq_pairs)

    at_owners(dq_pairs)
    cqg = (dqbuf[0] + dqbuf[1] + dqbuf[2]).astype(BF16)
    n2_grad = mm_nt(cqg, wb[:, LANE_CQ : LANE_CQ + D])
    part, cross_gain_grad = norm_back(n2_grad, hat_two, rs_two, gain[1])
    self_res = cross_res + part
    self_low = self_res.astype(BF16)
    dmix = mm_nt(self_low, wb[:, LANE_SO : LANE_SO + D]).astype(BF16)
    dqs, dks, dvs = [], [], []
    for g in range(3):
        sl = slice(256 * g, 256 * g + 256)
        q4 = stack(qs[:, sl])
        do4 = stack(dmix[:, sl])
        p = self_p[g]
        dp = mm_nt(do4, v[:, sl])
        ds = (p * (dp - jnp.sum(p * dp, axis=-1, keepdims=True))).astype(BF16)
        dvs.append(mm_tn(p.astype(BF16), do4))
        dks.append(mm_tn(ds, q4))
        dqs.append(unstack(mm(ds, k[:, sl])) * scale)
    packed_grad = [jnp.concatenate(parts, axis=1).astype(BF16) for parts in (dqs, dks, dvs)]
    for h in range(HALF_UNITS):
        push_unit(h, n1, packed_grad[h // 2][:, (h % 2) * PIECE : (h % 2 + 1) * PIECE])
    for h in range(2):
        push_unit(HALF_UNITS + 2 + h, n2, cqg[:, h * PIECE : (h + 1) * PIECE])
        push_unit(HALF_UNITS + h, sm, self_low[:, h * PIECE : (h + 1) * PIECE])

    def gb_view(lane_of):
        def view(zz, xx, cc):
            return gb.at[:, pl.ds(pl.multiple_of(lane_of(zz * SIDE + xx, cc), 128), PIECE)]

        return view

    n1_grad = jnp.zeros((SUFFIX, D), F32)
    for j in range(3):
        n1_grad = n1_grad + mm_nt(packed_grad[j], wb[:, D * j : D * (j + 1)])
    part, self_gain_grad = norm_back(n1_grad, hat_one, rs_one, gain[0])
    ob[me, SUFFIX : 2 * SUFFIX] = (self_res + part).astype(BF16)
    gmine[...] = jnp.concatenate(
        [self_gain_grad, cross_gain_grad, ffn_gain_grad, jnp.zeros((5, D), F32)], axis=0
    )
    g_item = push_y(gmine, gpeer, 2)

    def kp_step(i, carry):
        lane = pl.multiple_of(i * 256, 256)
        kp[:, pl.ds(lane, 256)] = mm_tn(memp[...], kvg[:, pl.ds(lane, 256)]).astype(BF16)
        return carry

    lax.fori_loop(0, 6, kp_step, 0)
    kr_item = pltpu.make_async_remote_copy(
        src_ref=kp.at[pl.ds(pl.multiple_of((1 - c) * half_rows, 128), half_rows)], dst_ref=kr,
        send_sem=ksend.at[2 * chips], recv_sem=krecv.at[chips], device_id=mate, device_id_type=MESH,
    )
    kr_item.start()

    across_o.relay()
    across_n.relay()
    across_o.wait()
    across_n.wait()

    rows_step = 128
    hidden = [col * 4 * half_rows + D * c for col in range(columns)]

    def ffn_rows(first, last):
        def one(i, carry):
            at = pl.ds(pl.multiple_of(i * rows_step, rows_step), rows_step)
            for col in range(columns):
                lane = pl.multiple_of(LANE_FI + hidden[col], 128)
                value, slope = gelu_parts(mm(nb[at], wb[:, pl.ds(lane, D)]))

                @pl.when(f == col)
                def _():
                    ab[at] = value.astype(BF16)

                back = []
                for t in range(CORES):
                    lane_o = pl.multiple_of(LANE_FO + D * (2 * c + t), 128)
                    back.append(mm_nt(olr[at], wb[col * half_rows : (col + 1) * half_rows, pl.ds(lane_o, D)]))
                hb[col, at] = (jnp.concatenate(back, axis=1) * slope).astype(BF16)
            return carry

        lax.fori_loop(first, last, one, 0)

    own_lanes = pl.ds(pl.multiple_of(f * half_rows, 128), half_rows)

    def ffn_in_sum(col):
        lane = pl.multiple_of(LANE_FI + hidden[col], 128)
        for part in range(0, D, PIECE):
            total = mm_tn(nb[:, own_lanes], hb[col, :, part : part + PIECE])
            gb[:, pl.ds(lane + part, PIECE)] = total.astype(BF16)

    def ffn_out_sum(t):
        lane = pl.multiple_of(LANE_FO + D * (2 * c + t), 128)
        for part in range(0, D, PIECE):
            total = mm_tn(ab[:, t * half_rows : (t + 1) * half_rows], olr[:, part : part + PIECE])
            gb[:, pl.ds(lane + part, PIECE)] = total.astype(BF16)

    f_items = []

    def to_mate(lane, width):
        ref = gb.at[:, pl.ds(pl.multiple_of(lane, 128), width)]
        item = pltpu.make_async_remote_copy(
            src_ref=ref, dst_ref=ref, send_sem=fsend.at[len(f_items)], recv_sem=frecv.at[len(f_items)],
            device_id=mate, device_id_type=MESH,
        )
        item.start()
        f_items.append(item)

    ffn_rows(0, columns * ranks * SUFFIX // rows_step)
    for col in range(columns):
        ffn_in_sum(col)
        to_mate(LANE_FI + hidden[col], D)
    for t in range(CORES):
        ffn_out_sum(t)
    to_mate(LANE_FO + CORES * D * c, CORES * D)

    has_unit = (chip >= 1) & (chip <= HALF_UNITS)

    def unit_lane(n, cc):
        n = n - 1
        kind = lax.div(n, 2)
        base = jnp.where(kind == 0, LANE_SO, jnp.where(kind == 1, LANE_CQ, LANE_CO))
        return jnp.where(cc == 0, PIECE * n, base + PIECE * lax.rem(n, 2))

    u_items = []

    def unit_sum(pred, at):
        @pl.when(pred)
        def _():
            def take(i, carry):
                @pl.when(i != me)
                def _():
                    pltpu.make_async_remote_copy(
                        src_ref=sb.at[0], dst_ref=rb.at[rows_of(i)], send_sem=usend.at[0],
                        recv_sem=urecv.at[i], device_id=mate, device_id_type=MESH,
                    ).wait_recv()

                return carry

            lax.fori_loop(0, ranks, take, 0)
            for col in range(columns):
                ug[col] = mm_tn(rb[:, col * half_rows : (col + 1) * half_rows], rb[:, D : D + PIECE])
            usend_b[...] = ug[other].astype(BF16)
            pltpu.make_async_remote_copy(
                src_ref=usend_b, dst_ref=urecv_b, send_sem=ysend.at[at], recv_sem=yrecv.at[at],
                device_id=(me, other), device_id_type=MESH,
            ).start()

    def unit_join(pred, at):
        @pl.when(pred)
        def _():
            item = pltpu.make_async_remote_copy(
                src_ref=usend_b, dst_ref=urecv_b, send_sem=ysend.at[at], recv_sem=yrecv.at[at],
                device_id=(me, other), device_id_type=MESH,
            )
            item.wait_recv()
            gb[:, pl.ds(pl.multiple_of(unit_lane(chip, c), 128), PIECE)] = (
                ug[f] + urecv_b[...].astype(F32)
            ).astype(BF16)
            item.wait_send()

    def has_block(zz, xx, cc):
        n = zz * SIDE + xx
        return (n >= 1) & (n <= HALF_UNITS)

    ag_u = Gather(place, gb_view(unit_lane), sems, 3, has_block)
    unit_sum(has_unit, 3)

    kr_item.wait_recv()
    kc[...] = (
        kp[pl.ds(pl.multiple_of(c * half_rows, 128), half_rows)].astype(F32) + kr[...].astype(F32)
    ).astype(BF16)
    ky_item = pltpu.make_async_remote_copy(
        src_ref=kc, dst_ref=ky, send_sem=ksend.at[2 * chips + 1], recv_sem=krecv.at[chips + 1],
        device_id=(me, other), device_id_type=MESH,
    )

    @pl.when(c != f)
    def _():
        ky_item.start()

    unit_join(has_unit, 3)
    ag_u.step_one()
    half_slabs = half_rows // SIDE
    kx_item = pltpu.make_async_remote_copy(
        src_ref=kc.at[pl.ds(pl.multiple_of((1 - x) * half_slabs, 16), half_slabs)], dst_ref=kx,
        send_sem=ksend.at[2 * chips + 2], recv_sem=krecv.at[chips + 2],
        device_id=(z * (SIDE * CORES) + (1 - x) * CORES + c, f), device_id_type=MESH,
    )

    @pl.when(c == f)
    def _():
        ky_item.wait_recv()
        kc[...] = (kc[...].astype(F32) + ky[...].astype(F32)).astype(BF16)
        kx_item.start()

    g_item.wait_recv()
    tb[me] = gmine[...] + gpeer[...]
    tell_g = Tell(tb, 1)
    tell_g.start()
    ag_o = Gather(place, block_view(ob), sems, 4)
    ag_o.step_one()
    ag_u.step_two()
    k_items = []

    def k_copy(t, j):
        return pltpu.make_async_remote_copy(
            src_ref=ks.at[pl.ds(t * slab, slab), pl.ds(j * D, D)], dst_ref=cp.at[z],
            send_sem=ksend.at[t * CORES + j], recv_sem=krecv.at[z],
            device_id=(t * (SIDE * CORES) + x * CORES + j, f), device_id_type=MESH,
        )

    @pl.when(c == f)
    def _():
        kx_item.wait_recv()
        ks[...] = (
            kc[pl.ds(pl.multiple_of(x * half_slabs, 16), half_slabs)].astype(F32) + kx[...].astype(F32)
        ).astype(BF16)

    for t in range(RING):
        for j in range(CORES):
            here = (z == t) & (c == j)

            @pl.when((c == f) & here)
            def _():
                cp[z] = ks[t * slab : (t + 1) * slab, j * D : (j + 1) * D]

            @pl.when((c == f) & jnp.logical_not(here))
            def _():
                k_copy(t, j).start()

            k_items.append((t, j, here))


    def take_k(i, carry):
        @pl.when((i != z) | (c != f))
        def _():
            pltpu.make_async_remote_copy(
                src_ref=ks.at[pl.ds(0, slab), pl.ds(0, D)], dst_ref=cp.at[i], send_sem=ksend.at[0],
                recv_sem=krecv.at[i], device_id=mate, device_id_type=MESH,
            ).wait_recv()

        return carry

    lax.fori_loop(0, RING, take_k, 0)
    total = cp[0].astype(F32)
    for i in range(1, RING):
        total = total + cp[i].astype(F32)
    k_lane = pl.multiple_of(LANE_CKV + c * D, 128)
    gb[pl.ds(pl.multiple_of(x * half_slabs + z * slab, 16), slab), pl.ds(k_lane, D)] = total.astype(BF16)

    def kv_view(zz, xx, cc):
        row = pl.multiple_of(xx * half_slabs + zz * slab, 16)
        return gb.at[pl.ds(row, slab), pl.ds(pl.multiple_of(LANE_CKV + cc * D, 128), D)]

    ag_k = Gather(place, kv_view, sems, 5)
    ag_k.step_one()
    ag_u.step_three()
    ag_o.step_two()
    ag_k.step_two()

    def mg_step(i, carry):
        row = pl.multiple_of(i * 128, 128)
        memgrad_ref[pl.ds(row, 128)] = mm_nt(kvg[pl.ds(row, 128)], wb[:, LANE_CKV : LANE_CKV + 2 * D])
        return carry

    full = own_rows // 128
    lax.fori_loop(0, full, mg_step, 0)
    if own_rows % 128:
        tail = mm_nt(kvg[full * 128 : (full + 1) * 128], wb[:, LANE_CKV : LANE_CKV + 2 * D])
        memgrad_ref[full * 128 : own_rows] = tail[0 : own_rows - full * 128]

    ag_u.step_four()
    ag_o.step_three()
    ag_k.step_three()
    ag_o.step_four()
    ag_k.step_four()
    tell_g.wait()
    gains_all = tb[0]
    for i in range(1, ranks):
        gains_all = gains_all + tb[i]
    own_gain = gains_all[:, 0:half_rows]
    for i in range(1, columns):
        own_gain = jnp.where(f == i, gains_all[:, i * half_rows : (i + 1) * half_rows], own_gain)
    gain_out_ref[...] = own_gain
    ag_o.step_five()
    out_ref[...] = ob[mine_rank, 0:SUFFIX].astype(F32)
    grad_ref[...] = ob[mine_rank, SUFFIX : 2 * SUFFIX].astype(F32)
    ag_k.step_five()
    ag_u.step_five()
    for n, (lane, width) in enumerate(
        [(LANE_FI + col * 4 * half_rows + D * (1 - c), D) for col in range(columns)] + [(LANE_FO + CORES * D * (1 - c), CORES * D)]
    ):
        ref = gb.at[:, pl.ds(pl.multiple_of(lane, 128), width)]
        pltpu.make_async_remote_copy(
            src_ref=ref, dst_ref=ref, send_sem=fsend.at[n], recv_sem=frecv.at[n], device_id=mate, device_id_type=MESH,
        ).wait_recv()
    done = pltpu.make_async_copy(gb, weights_out_ref, load_sem.at[0])
    done.start()

    to_holders_sent(q_pairs)
    to_owners_sent(o_pairs)
    to_holders_sent(d_pairs)
    to_owners_sent(dq_pairs)
    for h, to in unit_items:
        @pl.when(me != to)
        def _():
            pltpu.make_async_remote_copy(
                src_ref=sb.at[h], dst_ref=rb.at[rows_of(me)], send_sem=usend.at[h],
                recv_sem=urecv.at[0], device_id=(to, f), device_id_type=MESH,
            ).wait_send()
    for t, j, here in k_items:
        @pl.when((c == f) & jnp.logical_not(here))
        def _():
            k_copy(t, j).wait_send()

    @pl.when(c == f)
    def _():
        kx_item.wait_send()

    across_o.finish()
    across_n.finish()
    for item in f_items:
        item.wait_send()
    kr_item.wait_send()

    @pl.when(c != f)
    def _():
        ky_item.wait_send()

    for item in y_items:
        item.wait_send()
    tell_p.finish()
    tell_g.finish()
    for item in [ag_x, *spread, ag_c, ag_n, ag_u, ag_o, ag_k]:
        item.finish()
    done.wait()


def fused_body(
    ranks, columns,
    decoder_in, memory, res_group, prefix_len, self_gain, self_qkv, self_out, cross_gain, cross_query,
    cross_kv, cross_out, ffn_gain, ffn_in, ffn_out, cotangent,
):
    half_rows = D // columns
    chips = ranks // CORES
    slab = half_rows // chips
    own_rows = memory.shape[1]
    padded = -(-own_rows // 128) * 128
    tokens = ranks * SUFFIX
    gains = jnp.stack([self_gain, cross_gain, ffn_gain]).astype(F32)
    gains = jnp.pad(gains, ((0, 5), (0, 0)))
    vm = pl.BlockSpec(memory_space=pltpu.VMEM)
    sm = pl.BlockSpec(memory_space=pltpu.SMEM)
    hbm = pl.BlockSpec(memory_space=pl.ANY)
    dma = pltpu.SemaphoreType.DMA
    scratch = [
        pltpu.VMEM((D, UNITS * D), BF16),
        pltpu.VMEM((half_rows, UNITS * D), BF16),
        pltpu.VMEM((tokens, D + PIECE), BF16),
        pltpu.VMEM((2 * HALF_UNITS, SUFFIX, D + PIECE), BF16),
        pltpu.VMEM((ranks, SUFFIX, D), F32),
        pltpu.VMEM((ranks, SUFFIX, D), BF16),
        pltpu.VMEM((columns * tokens, D), BF16),
        pltpu.VMEM((columns * tokens, D), BF16),
        pltpu.VMEM((ranks, 2 * SUFFIX, D), BF16),
        pltpu.VMEM((ranks, 8, D), F32),
        pltpu.VMEM((ranks, 8, 128), F32),
        pltpu.VMEM((columns, 8, half_rows), F32),
        pltpu.VMEM((padded, D), BF16),
        pltpu.VMEM((padded, 2 * D), BF16),
        pltpu.VMEM((padded, 2 * D), BF16),
        pltpu.VMEM((D, 2 * D), BF16),
        pltpu.VMEM((half_rows, 2 * D), BF16),
        pltpu.VMEM((half_rows, 2 * D), BF16),
        pltpu.VMEM((half_rows, 2 * D), BF16),
        pltpu.VMEM((RING, slab, D), BF16),
        pltpu.VMEM((half_rows // SIDE, 2 * D), BF16),
        pltpu.VMEM((half_rows // SIDE, 2 * D), BF16),
        pltpu.VMEM((columns, columns * tokens, D), BF16),
        pltpu.VMEM((columns * tokens, D), BF16),
        pltpu.VMEM((columns, half_rows, PIECE), F32),
        pltpu.VMEM((half_rows, PIECE), BF16),
        pltpu.VMEM((half_rows, PIECE), BF16),
        pltpu.VMEM((SUFFIX, D), BF16),
        pltpu.VMEM((SLOTS, SUFFIX, D), BF16),
        pltpu.VMEM((SLOTS, SUFFIX, D), BF16),
        pltpu.VMEM((SLOTS, 2, SUFFIX, 128), F32),
        pltpu.VMEM((SLOTS, SUFFIX, D), BF16),
        pltpu.VMEM((SLOTS, 2, SUFFIX, 128), F32),
        pltpu.VMEM((SUFFIX, D), BF16),
        pltpu.VMEM((2, SUFFIX, 128), F32),
        pltpu.VMEM((SLOTS, SUFFIX, D), BF16),
        pltpu.VMEM((SLOTS, 2, SUFFIX, 128), F32),
        pltpu.VMEM((SLOTS, SUFFIX, D), F32),
        pltpu.VMEM((SLOTS, SUFFIX, D), F32),
        pltpu.VMEM((8, D), F32),
        pltpu.VMEM((8, D), F32),
        dma((10,)),
        dma((len(CHUNKS), 30)),
        dma((len(CHUNKS), 18)),
        dma((6, 29)),
        dma((6, 16)),
        dma((2, ranks)),
        dma((2, ranks)),
        dma((2, 2)),
        dma((2, 2)),
        dma((3,)),
        dma((3,)),
        dma((4,)),
        dma((4,)),
        dma((6, SLOTS)),
        dma((6, SLOTS)),
        dma((2 * HALF_UNITS,)),
        dma((ranks,)),
        dma((2 * chips + 3,)),
        dma((chips + 3,)),
    ]
    out, grad, memgrad, gain_grads, weight_grads = pl.pallas_call(
        partial(layer_kernel, ranks, columns),
        out_shape=(
            jax.ShapeDtypeStruct((SUFFIX, D), F32),
            jax.ShapeDtypeStruct((SUFFIX, D), F32),
            jax.ShapeDtypeStruct((own_rows, D), F32),
            jax.ShapeDtypeStruct((8, half_rows), F32),
            jax.ShapeDtypeStruct((half_rows, UNITS * D), BF16),
        ),
        in_specs=[vm, vm, vm, sm, sm, vm] + [hbm] * 7,
        out_specs=(vm, vm, vm, vm, hbm),
        scratch_shapes=scratch,
        compiler_params=pltpu.CompilerParams(
            collective_id=0, has_side_effects=True, vmem_limit_bytes=63 * 2**20
        ),
        name="layer",
    )(
        decoder_in[0], cotangent[0], memory[0], res_group, prefix_len, gains,
        self_qkv, self_out, cross_query, cross_kv, cross_out, ffn_in, ffn_out,
    )

    def lanes(low, width):
        return weight_grads[:, low : low + width].astype(F32)

    ffn_out_grad = jnp.concatenate([lanes(LANE_FO + D * j, D) for j in range(4)], axis=0)
    return (
        out[None], grad[None], memgrad[None],
        gain_grads[0], lanes(LANE_QKV, 3 * D), lanes(LANE_SO, D),
        gain_grads[1], lanes(LANE_CQ, D), lanes(LANE_CKV, 2 * D), lanes(LANE_CO, D),
        gain_grads[2], lanes(LANE_FI, 4 * D), ffn_out_grad,
    )


def layer_norm(value, gain):
    mean = jnp.mean(value, axis=-1, keepdims=True)
    centred = value - mean
    variance = jnp.mean(centred * centred, axis=-1, keepdims=True)
    return centred * lax.rsqrt(variance + norm_eps) * gain


def product(left, right):
    return jnp.dot(left, right, preferred_element_type=jnp.float32)


def outer_sum(left, right):
    flat_left = left.reshape(-1, left.shape[-1])
    flat_right = right.reshape(-1, right.shape[-1])
    return lax.dot_general(
        flat_left, flat_right, (((0,), (0,)), ((), ())), preferred_element_type=jnp.float32
    )


def back_product(grad, weight):
    return lax.dot_general(
        grad, weight, (((grad.ndim - 1,), (1,)), ((), ())), preferred_element_type=jnp.float32
    )


def attend(query, keys, values, allowed, scale):
    scores = jnp.einsum("eqhd,ekhd->ehqk", query, keys, preferred_element_type=jnp.float32) * scale
    scores = jnp.where(allowed[:, None], scores, -1e30)
    top = jnp.max(scores, axis=-1, keepdims=True)
    weights = jnp.exp(scores - top)
    probs = weights / jnp.sum(weights, axis=-1, keepdims=True)
    mixed = jnp.einsum(
        "ehqk,ekhd->eqhd", probs.astype(jnp.bfloat16), values, preferred_element_type=jnp.float32
    )
    return (mixed.astype(jnp.bfloat16), probs)


def attend_back(grad_mixed, query, keys, values, probs, scale):
    probs_low = probs.astype(jnp.bfloat16)
    grad_values = jnp.einsum(
        "ehqk,eqhd->ekhd", probs_low, grad_mixed, preferred_element_type=jnp.float32
    )
    grad_probs = jnp.einsum(
        "eqhd,ekhd->ehqk", grad_mixed, values, preferred_element_type=jnp.float32
    )
    grad_scores = probs * (grad_probs - jnp.sum(probs * grad_probs, axis=-1, keepdims=True))
    grad_low = grad_scores.astype(jnp.bfloat16)
    grad_query = (
        jnp.einsum("ehqk,ekhd->eqhd", grad_low, keys, preferred_element_type=jnp.float32) * scale
    )
    grad_keys = (
        jnp.einsum("ehqk,eqhd->ekhd", grad_low, query, preferred_element_type=jnp.float32) * scale
    )
    return (grad_query, grad_keys, grad_values)


def window_layout(res_group, mem_col):
    small = 1 - res_group
    small_count = jnp.sum(small, axis=-1, keepdims=True)
    small_before = jnp.cumsum(small, axis=-1) - small
    large_before = jnp.cumsum(res_group, axis=-1) - res_group
    offset = jnp.where(
        res_group == 1, SLOT_S * small_count + SLOT_L * large_before, SLOT_S * small_before
    )
    start = jnp.minimum(offset, mem_col - SLOT_L)
    return (offset, start)


def take_windows(column, starts):
    return jax.vmap(lambda begin: lax.dynamic_slice_in_dim(column, begin, SLOT_L, 0))(starts)


def forward(decoder_rows, windows, cross_allowed, weights):
    (
        self_gain,
        self_qkv,
        self_out,
        cross_gain,
        cross_query,
        cross_kv,
        cross_out,
        ffn_gain,
        ffn_in,
        ffn_out,
    ) = weights
    count = decoder_rows.shape[0] // SUFFIX
    scale = HEAD_DIM ** (-0.5)
    row_index = lax.broadcasted_iota(jnp.int32, (SUFFIX, SUFFIX), 0)
    col_index = lax.broadcasted_iota(jnp.int32, (SUFFIX, SUFFIX), 1)
    causal = (row_index >= col_index)[None]
    resid = decoder_rows.reshape(count, SUFFIX, D)
    normed_one = layer_norm(resid, self_gain.astype(jnp.float32)).astype(jnp.bfloat16)
    packed = product(normed_one, self_qkv).astype(jnp.bfloat16)
    heads = packed.reshape(count, SUFFIX, 3, HEADS, HEAD_DIM)
    self_mixed, self_probs = attend(heads[:, :, 0], heads[:, :, 1], heads[:, :, 2], causal, scale)
    self_mixed = self_mixed.reshape(count, SUFFIX, D)
    after_self = resid + product(self_mixed, self_out)
    normed_two = layer_norm(after_self, cross_gain.astype(jnp.float32)).astype(jnp.bfloat16)
    cross_q = product(normed_two, cross_query).astype(jnp.bfloat16)
    window_kv = product(windows, cross_kv).astype(jnp.bfloat16)
    query_heads = cross_q.reshape(count, SUFFIX, HEADS, HEAD_DIM)
    kv_heads = window_kv.reshape(count, SLOT_L, 2, HEADS, HEAD_DIM)
    cross_mixed, cross_probs = attend(
        query_heads, kv_heads[:, :, 0], kv_heads[:, :, 1], cross_allowed, scale
    )
    cross_mixed = cross_mixed.reshape(count, SUFFIX, D)
    after_cross = after_self + product(cross_mixed, cross_out)
    normed_three = layer_norm(after_cross, ffn_gain.astype(jnp.float32)).astype(jnp.bfloat16)
    up = product(normed_three, ffn_in)
    act = jax.nn.gelu(up, approximate=True).astype(jnp.bfloat16)
    result = after_cross + product(act, ffn_out)
    return (
        resid,
        normed_one,
        packed,
        self_probs,
        self_mixed,
        after_self,
        normed_two,
        cross_q,
        window_kv,
        cross_probs,
        cross_mixed,
        after_cross,
        normed_three,
        up,
        act,
        result,
    )


def backward(grad_out, saved, weights):
    (
        self_gain,
        self_qkv,
        self_out,
        cross_gain,
        cross_query,
        cross_kv,
        cross_out,
        ffn_gain,
        ffn_in,
        ffn_out,
    ) = weights
    (
        resid,
        normed_one,
        packed,
        self_probs,
        self_mixed,
        after_self,
        normed_two,
        cross_q,
        window_kv,
        cross_probs,
        cross_mixed,
        after_cross,
        normed_three,
        up,
        act,
        result,
    ) = saved
    count = resid.shape[0]
    scale = HEAD_DIM ** (-0.5)
    grad_out = grad_out.reshape(count, SUFFIX, D)
    out_low = grad_out.astype(jnp.bfloat16)
    ffn_out_grad = outer_sum(act, out_low)
    act_grad = back_product(out_low, ffn_out)
    gelu_value, gelu_back = jax.vjp(partial(jax.nn.gelu, approximate=True), up)
    up_grad = gelu_back(act_grad)[0].astype(jnp.bfloat16)
    ffn_in_grad = outer_sum(normed_three, up_grad)
    normed_three_grad = back_product(up_grad, ffn_in)
    norm_value, norm_back = jax.vjp(layer_norm, after_cross, ffn_gain.astype(jnp.float32))
    resid_part, ffn_gain_grad = norm_back(normed_three_grad)
    cross_res_grad = grad_out + resid_part
    cross_low = cross_res_grad.astype(jnp.bfloat16)
    cross_out_grad = outer_sum(cross_mixed, cross_low)
    mixed_grad = (
        back_product(cross_low, cross_out)
        .astype(jnp.bfloat16)
        .reshape(count, SUFFIX, HEADS, HEAD_DIM)
    )
    query_heads = cross_q.reshape(count, SUFFIX, HEADS, HEAD_DIM)
    kv_heads = window_kv.reshape(count, SLOT_L, 2, HEADS, HEAD_DIM)
    query_grad, keys_grad, values_grad = attend_back(
        mixed_grad, query_heads, kv_heads[:, :, 0], kv_heads[:, :, 1], cross_probs, scale
    )
    cross_q_grad = query_grad.reshape(count, SUFFIX, D).astype(jnp.bfloat16)
    window_kv_grad = (
        jnp.stack((keys_grad, values_grad), axis=2)
        .reshape(count, SLOT_L, 2 * D)
        .astype(jnp.bfloat16)
    )
    cross_query_grad = outer_sum(normed_two, cross_q_grad)
    normed_two_grad = back_product(cross_q_grad, cross_query)
    norm_value, norm_back = jax.vjp(layer_norm, after_self, cross_gain.astype(jnp.float32))
    resid_part, cross_gain_grad = norm_back(normed_two_grad)
    self_res_grad = cross_res_grad + resid_part
    self_low = self_res_grad.astype(jnp.bfloat16)
    self_out_grad = outer_sum(self_mixed, self_low)
    mixed_grad = (
        back_product(self_low, self_out)
        .astype(jnp.bfloat16)
        .reshape(count, SUFFIX, HEADS, HEAD_DIM)
    )
    heads = packed.reshape(count, SUFFIX, 3, HEADS, HEAD_DIM)
    query_grad, keys_grad, values_grad = attend_back(
        mixed_grad, heads[:, :, 0], heads[:, :, 1], heads[:, :, 2], self_probs, scale
    )
    packed_grad = (
        jnp.stack((query_grad, keys_grad, values_grad), axis=2)
        .reshape(count, SUFFIX, 3 * D)
        .astype(jnp.bfloat16)
    )
    self_qkv_grad = outer_sum(normed_one, packed_grad)
    normed_one_grad = back_product(packed_grad, self_qkv)
    norm_value, norm_back = jax.vjp(layer_norm, resid, self_gain.astype(jnp.float32))
    resid_part, self_gain_grad = norm_back(normed_one_grad)
    decoder_grad = self_res_grad + resid_part
    weight_grads = (
        self_gain_grad,
        self_qkv_grad,
        self_out_grad,
        cross_gain_grad,
        cross_query_grad,
        cross_out_grad,
        ffn_gain_grad,
        ffn_in_grad,
        ffn_out_grad,
    )
    return (decoder_grad, window_kv_grad, weight_grads)


def make_placer(all_starts, lowest, own_rows):

    def place(total, piece, begin):

        def add_one(item, acc):
            relative = all_starts[item] - lowest
            inside = ((relative > -SLOT_L) & (relative < own_rows)).astype(jnp.float32)
            spot = jnp.clip(relative + SLOT_L, 0, own_rows + SLOT_L)
            current = lax.dynamic_slice_in_dim(acc, spot, SLOT_L, 0)
            added = current + piece[item].astype(jnp.float32) * inside
            return lax.dynamic_update_slice_in_dim(acc, added, spot, 0)

        return lax.fori_loop(0, piece.shape[0], add_one, total)

    return place


def body(
    decoder_in,
    memory,
    res_group,
    prefix_len,
    self_gain,
    self_qkv,
    self_out,
    cross_gain,
    cross_query,
    cross_kv,
    cross_out,
    ffn_gain,
    ffn_in,
    ffn_out,
    cotangent,
):
    count = prefix_len.shape[1]
    own_rows = memory.shape[1]
    mem_col = own_rows * lax.axis_size("dp")
    offset, start = window_layout(res_group, mem_col)
    all_starts = start[0]
    first = lax.axis_index("dp") * count
    own_offset = lax.dynamic_slice_in_dim(offset[0], first, count)
    own_start = lax.dynamic_slice_in_dim(all_starts, first, count)
    own_group = lax.dynamic_slice_in_dim(res_group[0], first, count)
    valid = jnp.where(own_group == 1, PATCH_L, PATCH_S) + prefix_len[0]
    positions = own_start[:, None] + jnp.arange(SLOT_L, dtype=jnp.int32)[None]
    cross_allowed = (
        (positions >= own_offset[:, None]) & (positions < (own_offset + valid)[:, None])
    )[:, None]
    weights = (
        lax.all_gather(self_gain, "fsdp", axis=0, tiled=True),
        lax.all_gather(self_qkv, "fsdp", axis=0, tiled=True),
        lax.all_gather(self_out, "fsdp", axis=0, tiled=True),
        lax.all_gather(cross_gain, "fsdp", axis=0, tiled=True),
        lax.all_gather(cross_query, "fsdp", axis=0, tiled=True),
        lax.all_gather(cross_kv, "fsdp", axis=0, tiled=True),
        lax.all_gather(cross_out, "fsdp", axis=0, tiled=True),
        lax.all_gather(ffn_gain, "fsdp", axis=0, tiled=True),
        lax.all_gather(ffn_in, "fsdp", axis=0, tiled=True),
        lax.all_gather(ffn_out, "fsdp", axis=0, tiled=True),
    )
    column = lax.all_gather(memory[0], "dp", axis=0, tiled=True)
    windows = take_windows(column, own_start)
    saved = forward(decoder_in[0], windows, cross_allowed, weights)
    decoder_out = saved[-1]
    weights = (
        lax.all_gather(self_gain, "fsdp", axis=0, tiled=True),
        lax.all_gather(self_qkv, "fsdp", axis=0, tiled=True),
        lax.all_gather(self_out, "fsdp", axis=0, tiled=True),
        lax.all_gather(cross_gain, "fsdp", axis=0, tiled=True),
        lax.all_gather(cross_query, "fsdp", axis=0, tiled=True),
        lax.all_gather(cross_kv, "fsdp", axis=0, tiled=True),
        lax.all_gather(cross_out, "fsdp", axis=0, tiled=True),
        lax.all_gather(ffn_gain, "fsdp", axis=0, tiled=True),
        lax.all_gather(ffn_in, "fsdp", axis=0, tiled=True),
        lax.all_gather(ffn_out, "fsdp", axis=0, tiled=True),
    )
    column = lax.all_gather(memory[0], "dp", axis=0, tiled=True)
    windows = take_windows(column, own_start)
    saved = forward(decoder_in[0], windows, cross_allowed, weights)
    whole_kv = weights[5]
    decoder_grad, window_kv_grad, local_grads = backward(cotangent[0], saved, weights)
    lowest = lax.axis_index("dp") * own_rows
    place = make_placer(all_starts, lowest, own_rows)
    empty = jnp.zeros((own_rows + 2 * SLOT_L, 2 * D), jnp.float32)
    summed = place(empty, lax.all_gather(window_kv_grad, "dp", axis=0, tiled=True), jnp.int32(0))
    own_kv_grad = summed[SLOT_L : SLOT_L + own_rows].astype(jnp.bfloat16)
    memory_grad = back_product(own_kv_grad, whole_kv)
    cross_kv_part = outer_sum(memory[0], own_kv_grad)
    grads = (
        local_grads[0],
        local_grads[1],
        local_grads[2],
        local_grads[3],
        local_grads[4],
        cross_kv_part,
        local_grads[5],
        local_grads[6],
        local_grads[7],
        local_grads[8],
    )
    shards = (
        lax.psum_scatter(
            grads[0].astype(jnp.bfloat16), "fsdp", scatter_dimension=0, tiled=True
        ).astype(jnp.float32),
        lax.psum_scatter(
            grads[1].astype(jnp.bfloat16), "fsdp", scatter_dimension=0, tiled=True
        ).astype(jnp.float32),
        lax.psum_scatter(
            grads[2].astype(jnp.bfloat16), "fsdp", scatter_dimension=0, tiled=True
        ).astype(jnp.float32),
        lax.psum_scatter(
            grads[3].astype(jnp.bfloat16), "fsdp", scatter_dimension=0, tiled=True
        ).astype(jnp.float32),
        lax.psum_scatter(
            grads[4].astype(jnp.bfloat16), "fsdp", scatter_dimension=0, tiled=True
        ).astype(jnp.float32),
        lax.psum_scatter(
            grads[5].astype(jnp.bfloat16), "fsdp", scatter_dimension=0, tiled=True
        ).astype(jnp.float32),
        lax.psum_scatter(
            grads[6].astype(jnp.bfloat16), "fsdp", scatter_dimension=0, tiled=True
        ).astype(jnp.float32),
        lax.psum_scatter(
            grads[7].astype(jnp.bfloat16), "fsdp", scatter_dimension=0, tiled=True
        ).astype(jnp.float32),
        lax.psum_scatter(
            grads[8].astype(jnp.bfloat16), "fsdp", scatter_dimension=0, tiled=True
        ).astype(jnp.float32),
        lax.psum_scatter(
            grads[9].astype(jnp.bfloat16), "fsdp", scatter_dimension=0, tiled=True
        ).astype(jnp.float32),
    )
    totals = (
        lax.psum(shards[0].astype(jnp.bfloat16), "dp").astype(jnp.float32),
        lax.psum(shards[1].astype(jnp.bfloat16), "dp").astype(jnp.float32),
        lax.psum(shards[2].astype(jnp.bfloat16), "dp").astype(jnp.float32),
        lax.psum(shards[3].astype(jnp.bfloat16), "dp").astype(jnp.float32),
        lax.psum(shards[4].astype(jnp.bfloat16), "dp").astype(jnp.float32),
        lax.psum(shards[5].astype(jnp.bfloat16), "dp").astype(jnp.float32),
        lax.psum(shards[6].astype(jnp.bfloat16), "dp").astype(jnp.float32),
        lax.psum(shards[7].astype(jnp.bfloat16), "dp").astype(jnp.float32),
        lax.psum(shards[8].astype(jnp.bfloat16), "dp").astype(jnp.float32),
        lax.psum(shards[9].astype(jnp.bfloat16), "dp").astype(jnp.float32),
    )
    return (
        decoder_out,
        decoder_grad,
        memory_grad[None],
        totals[0],
        totals[1],
        totals[2],
        totals[3],
        totals[4],
        totals[5],
        totals[6],
        totals[7],
        totals[8],
        totals[9],
    )


def choose(mesh):
    ranks, columns = mesh.shape["dp"], mesh.shape["fsdp"]
    slabs = (D // columns) % (16 * (ranks // CORES)) == 0
    if slabs and columns == 2 and ranks == RING * SIDE * CORES:
        return partial(fused_body, ranks, columns)
    return body


def solution(mesh):
    placed = (
        P("fsdp", "dp", None),
        P("fsdp", "dp", None),
        P("fsdp", None),
        P("fsdp", "dp"),
        P("fsdp"),
        P("fsdp", None),
        P("fsdp", None),
        P("fsdp"),
        P("fsdp", None),
        P("fsdp", None),
        P("fsdp", None),
        P("fsdp"),
        P("fsdp", None),
        P("fsdp", None),
        P("fsdp", "dp", None),
    )
    return jax.shard_map(
        choose(mesh),
        mesh=mesh,
        in_specs=placed,
        out_specs=(
            P("fsdp", "dp", None),
            P("fsdp", "dp", None),
            P("fsdp", "dp", None),
            P("fsdp"),
            P("fsdp", None),
            P("fsdp", None),
            P("fsdp"),
            P("fsdp", None),
            P("fsdp", None),
            P("fsdp", None),
            P("fsdp"),
            P("fsdp", None),
            P("fsdp", None),
        ),
        check_vma=False,
    )
```

```python
from functools import partial

import jax
import jax.numpy as jnp
from jax import lax
from jax.experimental import pallas as pl
from jax.experimental.pallas import tpu as pltpu
from jax.sharding import PartitionSpec as P

D = 768
HEADS = 12
HEAD_DIM = 64
SUFFIX = 32
PATCH_S = 196
PATCH_L = 576
SLOT_S = 228
SLOT_L = 608
RING = 4
SIDE = 2
CORES = 2
norm_eps = 1e-06
MESH = pl.DeviceIdType.MESH
F32 = jnp.float32
BF16 = jnp.bfloat16
NONE = -1e30


def mm(left, right):
    return jnp.dot(left, right, preferred_element_type=F32)


def mm_nt(left, right):
    return lax.dot_general(left, right, (((1,), (1,)), ((), ())), preferred_element_type=F32)


def mm_tn(left, right):
    return lax.dot_general(left, right, (((0,), (0,)), ((), ())), preferred_element_type=F32)


def normed(value):
    mean = jnp.mean(value, axis=-1, keepdims=True)
    centred = value - mean
    variance = jnp.mean(centred * centred, axis=-1, keepdims=True)
    scale = lax.rsqrt(variance + norm_eps)
    return centred * scale, scale


def norm_back(grad, hat, scale, gain):
    inner = grad * gain
    mean_one = jnp.mean(inner, axis=-1, keepdims=True)
    mean_two = jnp.mean(inner * hat, axis=-1, keepdims=True)
    gain_grad = jnp.sum(grad * hat, axis=0, keepdims=True)
    return scale * (inner - mean_one - hat * mean_two), gain_grad


def gelu_parts(up):
    inner = 0.7978845608 * (up + 0.044715 * up * up * up)
    tanh = jnp.tanh(inner)
    slope = 0.7978845608 * (1.0 + 3.0 * 0.044715 * up * up)
    value = 0.5 * up * (1.0 + tanh)
    grad = 0.5 * (1.0 + tanh) + 0.5 * up * (1.0 - tanh * tanh) * slope
    return value, grad


class Gather:
    def __init__(self, place, view, bulk, sems, at, has=None):
        self.z, self.x, self.c, self.f = place
        self.view, self.bulk = view, bulk
        self.send, self.recv = sems
        self.at = at
        self.has = has
        self.sent = []

    def place_at(self, k):
        return lax.rem(self.z + k + RING, RING)

    def copy(self, ref, target, into, index):
        z, x, c = target
        return pltpu.make_async_remote_copy(
            src_ref=ref,
            dst_ref=ref,
            send_sem=self.send.at[self.at, index],
            recv_sem=self.recv.at[self.at, into],
            device_id=(z * (SIDE * CORES) + x * CORES + c, self.f),
            device_id_type=MESH,
        )

    def holds(self, block, cond):
        return cond if self.has is None else cond & self.has(*block)

    def go(self, block, target, into, cond):
        item = self.copy(self.view(*block), target, into, len(self.sent))
        cond = self.holds(block, cond)
        pl.when(cond)(item.start)
        self.sent.append((cond, item))

    def wait(self, block, into, cond):
        item = self.copy(self.view(*block), (self.z, 1 - self.x, self.c), into, 0)
        pl.when(self.holds(block, cond))(item.wait_recv)

    def line(self, block, up, down, cond):
        z, x, c = self.z, self.x, self.c
        if up:
            self.go(block, (self.place_at(1), x, c), block[0], cond & (z < RING - 1))
        if down:
            self.go(block, (self.place_at(-1), x, c), block[0], cond & (z > 0))

    def across(self, block, cond):
        self.go(block, (self.z, 1 - self.x, self.c), RING + block[0], cond)

    def step_one(self):
        own = (self.z, self.x, self.c)
        self.line(own, True, True, self.z >= 0)
        self.across(own, self.z >= 0)

    def arrive(self, k):
        low, high = (self.place_at(-k), self.x, self.c), (self.place_at(k), self.x, self.c)
        self.wait(low, low[0], self.z >= k)
        self.line(low, True, False, self.z >= k)
        self.wait(high, high[0], self.z < RING - k)
        self.line(high, False, True, self.z < RING - k)
        self.across(low, self.z >= k)
        self.across(high, self.z < RING - k)

    def side(self, k):
        for at, cond in ((self.place_at(-k), self.z >= k), (self.place_at(k), self.z < RING - k))[: 1 if k == 0 else 2]:
            self.wait((at, 1 - self.x, self.c), RING + at, cond)

    def step_two(self):
        self.arrive(1)

    def step_three(self):
        self.arrive(2)
        self.side(0)
        self.side(1)

    def step_four(self):
        self.arrive(3)
        self.side(2)

    def step_five(self):
        self.side(3)
        item = self.copy(self.bulk(self.c), (self.z, self.x, 1 - self.c), 2 * RING, len(self.sent))
        item.start()
        self.sent.append((None, item))

    def step_six(self):
        self.copy(self.bulk(1 - self.c), (self.z, self.x, 1 - self.c), 2 * RING, 0).wait_recv()

    def finish(self):
        for cond, item in self.sent:
            if cond is None:
                item.wait_send()
            else:
                pl.when(cond)(item.wait_send)


class Spread(Gather):
    def __init__(self, place, theirs, mine, bulk, sems, at):
        super().__init__(place, theirs, bulk, sems, at)
        self.mine = mine
        self.pushed = []

    def push(self):
        z, x, c = self.z, self.x, self.c
        for n, block in enumerate(((z, x, c), (z, 1 - x, c))):
            ref = self.mine(*block)
            item = pltpu.make_async_remote_copy(
                src_ref=ref, dst_ref=ref, send_sem=self.send.at[self.at, 15 + n], recv_sem=self.recv.at[self.at, 9 + n],
                device_id=(z * (SIDE * CORES) + x * CORES + c, 1 - self.f), device_id_type=MESH,
            )
            item.start()
            self.pushed.append(item)

    def step_one(self):
        always = self.z >= 0
        own = (self.z, self.x, self.c)
        self.wait(own, 9, always)
        self.line(own, True, True, always)

    def step_three(self):
        self.arrive(2)
        self.side(1)

    def step_five(self):
        self.wait((self.z, 1 - self.x, self.c), 10, self.z >= 0)
        super().step_five()

    def finish(self):
        super().finish()
        for item in self.pushed:
            item.wait_send()


class Pieces:
    def __init__(self, count, own_rows):
        self.half = count // 2
        self.edge = self.half * SLOT_S
        self.rows = own_rows
        self.count = count

    def start(self, rank):
        return jnp.where(
            rank < self.half, SLOT_S * rank, self.edge + SLOT_L * (rank - self.half)
        )

    def size(self, rank):
        return jnp.where(rank < self.half, SLOT_S, SLOT_L)

    def rank_of(self, row):
        return jnp.where(
            row < self.edge,
            lax.div(row, SLOT_S),
            self.half + lax.div(jnp.maximum(row - self.edge, 0), SLOT_L),
        )

    def first_rank(self, device):
        return self.rank_of(device * self.rows)

    def last_rank(self, device):
        return self.rank_of(device * self.rows + self.rows - 1)

    def first_device(self, rank):
        return lax.div(self.start(rank), self.rows)

    def last_device(self, rank):
        return lax.div(self.start(rank) + self.size(rank) - 1, self.rows)


SLOTS = 3
UNITS = 16
LANE_QKV, LANE_SO, LANE_CQ, LANE_CO, LANE_CKV, LANE_FI, LANE_FO = 0, 2304, 3072, 3840, 4608, 6144, 9216
CHUNKS = ((0, 2304), (2304, 2304), (4608, 1536), (6144, 2048), (8192, 2048), (10240, 2048))
LOADS_BY_CHUNK = ((0,), (1, 2, 3), (4,), (5,), (6, 7), (8, 9))
PIECE = 384
HALF_UNITS = 6


def layer_kernel(
    ranks,
    columns,
    x_ref, cot_ref, mem_ref, res_ref, pre_ref, gains_ref,
    qkv_ref, so_ref, cq_ref, ckv_ref, co_ref, fi_ref, fo_ref,
    out_ref, grad_ref, memgrad_ref, gain_out_ref, weights_out_ref,
    wb, gb, rb, sb, xb, cb, nb, olr, ob, tb, pb, gainb, memp, kvb, kvg, kp, kr, kc, ky, cp,
    kx, ks, hb, ab, ug, usend_b, urecv_b,
    cqb, qbuf, osend, ostat_send, obuf, ostat, dob, dstat_b, dobuf, dstat, dqsend, dqbuf, gmine, gpeer,
    load_sem, wsend, wrecv, gsend, grecv, bsend, brecv, asend, arecv, fsend, frecv, ysend, yrecv, psend, precv, usend, urecv,
    ksend, krecv,
):
    me = lax.axis_index("dp")
    f = lax.axis_index("fsdp")
    z = lax.div(me, SIDE * CORES)
    x = lax.rem(lax.div(me, CORES), SIDE)
    c = lax.rem(me, CORES)
    chip = lax.div(me, CORES)
    chips = ranks // CORES
    place = (z, x, c, f)
    half_rows = D // columns
    slab = half_rows // chips
    own_rows = mem_ref.shape[0]
    padded = memp.shape[0]
    lay = Pieces(ranks, own_rows)
    other = 1 - f
    mate = (z * (SIDE * CORES) + x * CORES + (1 - c), f)
    everyone = ranks * columns
    lin = f * ranks + me

    loads = []

    def load(src, lane, width):
        item = pltpu.make_async_copy(
            src, wb.at[pl.ds(pl.multiple_of(f * half_rows, 128), half_rows), pl.ds(lane, width)],
            load_sem.at[len(loads)],
        )
        item.start()
        loads.append(item)

    load(qkv_ref, LANE_QKV, 3 * D)
    load(so_ref, LANE_SO, D)
    load(cq_ref, LANE_CQ, D)
    load(co_ref, LANE_CO, D)
    load(ckv_ref, LANE_CKV, 2 * D)
    load(fi_ref, LANE_FI, 4 * D)
    for j in range(4):
        load(fo_ref.at[pl.ds(j * half_rows, half_rows)], LANE_FO + D * j, D)

    for s in range(SLOTS):
        qbuf[s] = jnp.zeros_like(qbuf[s])
        obuf[s] = jnp.zeros_like(obuf[s])
        ostat[s, 0] = jnp.full_like(ostat[s, 0], NONE)
        ostat[s, 1] = jnp.zeros_like(ostat[s, 1])
        dobuf[s] = jnp.zeros_like(dobuf[s])
        dstat[s] = jnp.zeros_like(dstat[s])
        dqbuf[s] = jnp.zeros_like(dqbuf[s])

    def rows_of(device):
        return pl.ds(pl.multiple_of(device * SUFFIX, SUFFIX), SUFFIX)

    def slot_of(device):
        return lax.rem(device, CORES) * chips + lax.div(device, CORES)

    my_slot = slot_of(me)
    xb[my_slot] = x_ref[...]
    cb[my_slot] = cot_ref[...].astype(BF16)
    pb[my_slot] = jnp.full((8, 128), pre_ref[0, 0].astype(F32), F32)
    gainb[f] = gains_ref[...]

    barrier = pltpu.get_barrier_semaphore()

    def greet(i, carry):
        to = lax.rem(me + i, ranks)
        pl.semaphore_signal(barrier, inc=1, device_id=(to, f), device_id_type=MESH)
        return carry

    lax.fori_loop(1, ranks, greet, 0)
    pl.semaphore_signal(barrier, inc=1, device_id=(me, other), device_id_type=MESH)
    pl.semaphore_wait(barrier, ranks)

    y_items = []

    def push_y(src, dst, at):
        item = pltpu.make_async_remote_copy(
            src_ref=src, dst_ref=dst, send_sem=ysend.at[at], recv_sem=yrecv.at[at],
            device_id=(me, other), device_id_type=MESH,
        )
        item.start()
        y_items.append(item)
        return item

    class Tell:
        def __init__(self, ref, at):
            self.ref, self.at = ref, at

        def copy(self, source, index, to):
            return pltpu.make_async_remote_copy(
                src_ref=self.ref.at[slot_of(source)], dst_ref=self.ref.at[slot_of(source)], send_sem=bsend.at[self.at, index],
                recv_sem=brecv.at[self.at, source], device_id=(to, f), device_id_type=MESH,
            )

        def start(self):
            def one(i, carry):
                self.copy(me, i, lax.rem(me + i, ranks)).start()
                return carry

            lax.fori_loop(1, ranks, one, 0)

        def wait(self):
            def one(i, carry):
                source = lax.rem(me + i, ranks)
                self.copy(source, i, source).wait_recv()
                return carry

            lax.fori_loop(1, ranks, one, 0)

        def finish(self):
            def one(i, carry):
                self.copy(me, i, lax.rem(me + i, ranks)).wait_send()
                return carry

            lax.fori_loop(1, ranks, one, 0)

    def slab_view(first, width, rows_from):
        half = width // CORES

        def view(zz, xx, cc):
            row = pl.multiple_of(rows_from * half_rows + (zz * SIDE + xx) * slab, 16)
            lane = pl.multiple_of(first + cc * half, 128)
            return wb.at[pl.ds(row, slab), pl.ds(lane, half)]

        return view

    def block_view(ref):
        def view(zz, xx, cc):
            return ref.at[cc * chips + zz * SIDE + xx]

        return view

    def block_bulk(ref):
        return lambda cc: ref.at[pl.ds(cc * chips, chips)]

    def token_rows(col, cc, at):
        return pl.ds(pl.multiple_of(((col * CORES + cc) * chips + at) * SUFFIX, SUFFIX), SUFFIX)

    def token_view(ref):
        def view(zz, xx, cc):
            return ref.at[token_rows(f, cc, zz * SIDE + xx)]

        return view

    def token_bulk(ref):
        rows = chips * SUFFIX
        return lambda cc: ref.at[pl.ds(pl.multiple_of((f * CORES + cc) * rows, rows), rows)]

    def chunk_bulk(first, width):
        half = width // CORES
        rows = pl.ds(pl.multiple_of(other * half_rows, 128), half_rows)
        return lambda cc: wb.at[rows, pl.ds(pl.multiple_of(first + cc * half, 128), half)]

    plane = pl.ds(pl.multiple_of((f * CORES + c) * chips * SUFFIX, SUFFIX), chips * SUFFIX)
    plane_in = pl.ds(pl.multiple_of((other * CORES + c) * chips * SUFFIX, SUFFIX), chips * SUFFIX)
    plane_mate = pl.ds(pl.multiple_of((other * CORES + 1 - c) * chips * SUFFIX, SUFFIX), chips * SUFFIX)

    class Across:
        def __init__(self, ref, at):
            self.ref, self.at = ref, at

        def copy(self, rows, n, to):
            ref = self.ref.at[rows]
            return pltpu.make_async_remote_copy(
                src_ref=ref, dst_ref=ref, send_sem=asend.at[self.at, n], recv_sem=arecv.at[self.at, n],
                device_id=to, device_id_type=MESH,
            )

        def start(self):
            self.copy(plane, 0, (me, other)).start()

        def relay(self):
            self.copy(plane_in, 0, (me, other)).wait_recv()
            self.copy(plane_in, 1, mate).start()

        def wait(self):
            self.copy(plane_mate, 1, mate).wait_recv()

        def finish(self):
            self.copy(plane, 0, (me, other)).wait_send()
            self.copy(plane_in, 1, mate).wait_send()

    sems = (gsend, grecv)
    ag_x = Gather(place, block_view(xb), block_bulk(xb), sems, 0)
    ag_c = Gather(place, block_view(cb), block_bulk(cb), sems, 1)
    ag_n = Gather(place, token_view(nb), token_bulk(nb), sems, 2)
    tell_p = Tell(pb, 0)
    spread = [
        Spread(place, slab_view(first, width, other), slab_view(first, width, f), chunk_bulk(first, width), (wsend, wrecv), n)
        for n, (first, width) in enumerate(CHUNKS)
    ]

    def push_chunk(n):
        for i in LOADS_BY_CHUNK[n]:
            loads[i].wait()
        spread[n].push()

    ag_x.step_one()
    push_chunk(0)
    gain_item = push_y(gainb.at[f], gainb.at[f], 0)
    tell_p.start()
    push_chunk(1)

    def tick(n):
        for age, act in ((4, "step_five"), (3, "step_four"), (2, "step_three"), (1, "step_two"), (0, "step_one")):
            if 0 <= n - age < len(spread):
                getattr(spread[n - age], act)()
        if n + 2 < len(spread):
            push_chunk(n + 2)

    ag_x.step_two()
    tick(0)
    ag_c.step_one()
    ag_x.step_three()
    tick(1)
    ag_c.step_two()
    ag_x.step_four()
    tick(2)
    ag_c.step_three()
    ag_x.step_five()
    ag_x.step_six()
    tick(3)
    ag_c.step_four()
    gain_item.wait_recv()

    memp[0:own_rows] = mem_ref[...]
    memp[own_rows:padded] = jnp.zeros((padded - own_rows, D), BF16)

    positions = []
    before_large = jnp.int32(0)
    mine_rank = jnp.int32(0)
    for i in range(ranks):
        group = res_ref[0, i]
        spot = jnp.where(group == 1, lay.half + before_large, i - before_large)
        positions.append(spot)
        mine_rank = jnp.where(me == i, spot, mine_rank)
        before_large = before_large + group

    slots = [(i % CORES) * chips + i // CORES for i in range(ranks)]

    def example_of(rank):
        found = jnp.int32(0)
        for i in range(ranks):
            found = jnp.where(positions[i] == rank, slots[i], found)
        return found

    out_slot = jnp.int32(0)
    for i in range(ranks):
        out_slot = jnp.where(mine_rank == i, slots[i], out_slot)

    tiles = half_rows // 128
    gain = [
        jnp.concatenate([gainb[i, tiles * n + j : tiles * n + j + 1] for i in range(columns) for j in range(tiles)], axis=1)
        for n in range(3)
    ]

    mine = example_of(me)
    resid = xb[mine]
    hat_one, rs_one = normed(resid)
    n1 = (hat_one * gain[0]).astype(BF16)

    lanes = lax.broadcasted_iota(jnp.int32, (1, 256), 1)
    head_f32 = [(lax.div(lanes, HEAD_DIM) == h).astype(F32) for h in range(4)]
    head_b16 = [m.astype(BF16) for m in head_f32]

    def stack(value):
        return jnp.concatenate([value * m for m in head_b16], axis=0)

    def unstack(value):
        rows = value.shape[0] // 4
        total = value[0:rows] * head_f32[0]
        for h in range(1, 4):
            total = total + value[h * rows : (h + 1) * rows] * head_f32[h]
        return total

    tick(4)
    ag_c.step_five()
    spread[0].step_six()
    q = mm(n1, wb[:, 0:D]).astype(BF16)
    k = mm(n1, wb[:, D : 2 * D]).astype(BF16)
    v = mm(n1, wb[:, 2 * D : 3 * D]).astype(BF16)
    scale = HEAD_DIM**-0.5
    qs = (q.astype(F32) * scale).astype(BF16)
    row_at = lax.broadcasted_iota(jnp.int32, (SUFFIX, SUFFIX), 0)
    col_at = lax.broadcasted_iota(jnp.int32, (SUFFIX, SUFFIX), 1)
    causal = jnp.concatenate([(row_at >= col_at).astype(F32)] * 4, axis=0) > 0.0
    self_p = []
    mixed = []
    for g in range(3):
        sl = slice(256 * g, 256 * g + 256)
        s = mm_nt(stack(qs[:, sl]), k[:, sl])
        s = jnp.where(causal, s, NONE)
        e = jnp.exp(s - jnp.max(s, axis=-1, keepdims=True))
        p = e / jnp.sum(e, axis=-1, keepdims=True)
        self_p.append(p)
        mixed.append(unstack(mm(p.astype(BF16), v[:, sl])))
    sm = jnp.concatenate(mixed, axis=1).astype(BF16)

    tick(5)
    ag_c.step_six()
    spread[1].step_six()
    after_self = resid + mm(sm, wb[:, LANE_SO : LANE_SO + D])
    hat_two, rs_two = normed(after_self)
    n2 = (hat_two * gain[1]).astype(BF16)
    cq = mm(n2, wb[:, LANE_CQ : LANE_CQ + D]).astype(BF16)
    cqb[...] = cq

    my_first, my_last = lay.first_device(me), lay.last_device(me)
    held_first, held_last = lay.first_rank(me), lay.last_rank(me)

    def piece_copy(src, dst, at, sent, landed, target):
        return pltpu.make_async_remote_copy(
            src_ref=src, dst_ref=dst, send_sem=psend.at[at, sent], recv_sem=precv.at[at, landed],
            device_id=(target, f), device_id_type=MESH,
        )

    def to_holders(pairs):
        for i in range(SLOTS):
            target = my_first + i
            slot = me - lay.first_rank(target)
            there = target <= my_last

            @pl.when(there & (target == me))
            def _():
                for src, dst, at in pairs:
                    dst[slot] = src[...]

            @pl.when(there & (target != me))
            def _():
                for src, dst, at in pairs:
                    piece_copy(src, dst.at[slot], at, i, slot, target).start()

    def to_holders_sent(pairs):
        for i in range(SLOTS):
            target = my_first + i

            @pl.when((target <= my_last) & (target != me))
            def _():
                for src, dst, at in pairs:
                    piece_copy(src, dst.at[0], at, i, 0, target).wait_send()

    def at_holders(pairs):
        for s in range(SLOTS):
            rank = held_first + s

            @pl.when((rank <= held_last) & (rank != me))
            def _():
                for src, dst, at in pairs:
                    piece_copy(src, dst.at[s], at, 0, s, rank).wait_recv()

    def to_owners(pairs):
        for s in range(SLOTS):
            rank = held_first + s
            index = me - lay.first_device(rank)
            there = rank <= held_last

            @pl.when(there & (rank == me))
            def _():
                for src, dst, at in pairs:
                    dst[index] = src[s]

            @pl.when(there & (rank != me))
            def _():
                for src, dst, at in pairs:
                    piece_copy(src.at[s], dst.at[index], at, s, index, rank).start()

    def to_owners_sent(pairs):
        for s in range(SLOTS):
            rank = held_first + s

            @pl.when((rank <= held_last) & (rank != me))
            def _():
                for src, dst, at in pairs:
                    piece_copy(src.at[s], dst.at[0], at, s, 0, rank).wait_send()

    def at_owners(pairs):
        for i in range(SLOTS):
            target = my_first + i

            @pl.when((target <= my_last) & (target != me))
            def _():
                for src, dst, at in pairs:
                    piece_copy(src.at[0], dst.at[i], at, 0, i, target).wait_recv()

    q_pairs = [(cqb, qbuf, 0)]
    o_pairs = [(osend, obuf, 1), (ostat_send, ostat, 2)]
    d_pairs = [(dob, dobuf, 3), (dstat_b, dstat, 4)]
    dq_pairs = [(dqsend, dqbuf, 5)]

    to_holders(q_pairs)

    tick(6)
    spread[2].step_six()

    for r in range(ranks):
        olr[token_rows(f, r % CORES, r // CORES)] = cb[example_of(r)]
    across_o = Across(olr, 0)
    across_n = Across(nb, 1)
    across_o.start()


    def kv_step(i, carry):
        lane = pl.multiple_of(i * 256, 256)
        kvb[:, pl.ds(lane, 256)] = mm(memp[...], wb[:, pl.ds(LANE_CKV + lane, 256)]).astype(BF16)
        return carry

    lax.fori_loop(0, 6, kv_step, 0)

    tell_p.wait()
    lane_f = lax.broadcasted_iota(jnp.int32, (SUFFIX, padded), 1).astype(F32)
    allowed = []
    for s in range(SLOTS):
        rank = held_first + s
        ok = rank <= held_last
        example = example_of(jnp.minimum(rank, ranks - 1))
        prefix = pb[example][0:1, 0:1]
        low = (lay.start(rank) - me * own_rows).astype(F32)
        patches = jnp.where(rank < lay.half, PATCH_S, PATCH_L).astype(F32)
        high = jnp.minimum(low + patches + prefix, jnp.float32(own_rows))
        high = jnp.where(ok, high, jnp.float32(-1.0))
        allowed.append(((lane_f >= low) & (lane_f < high)).astype(F32))
    allowed = jnp.concatenate(allowed * 4, axis=0) > 0.0

    at_holders(q_pairs)
    qh = jnp.concatenate([qbuf[s] for s in range(SLOTS)], axis=0)
    qh = (qh.astype(F32) * scale).astype(BF16)
    lane_c = lax.broadcasted_iota(jnp.int32, (SUFFIX, 128), 1)
    top_c = [jnp.zeros((SUFFIX, 128), F32) for _ in range(SLOTS)]
    sum_c = [jnp.zeros((SUFFIX, 128), F32) for _ in range(SLOTS)]
    for g in range(3):
        sl = slice(256 * g, 256 * g + 256)
        s = mm_nt(stack(qh[:, sl]), kvb[:, sl])
        s = jnp.where(allowed, s, NONE)
        top = jnp.max(s, axis=-1, keepdims=True)
        e = jnp.where(allowed, jnp.exp(s - top), 0.0)
        total = jnp.sum(e, axis=-1, keepdims=True)
        o = mm(e.astype(BF16), kvb[:, D + 256 * g : D + 256 * g + 256])
        o = o * jnp.where(total > 0.0, 1.0 / jnp.where(total > 0.0, total, 1.0), 0.0)
        o = unstack(o).astype(BF16)
        for n in range(SLOTS):
            osend[n, :, sl] = o[n * SUFFIX : (n + 1) * SUFFIX]
            for h in range(4):
                at = h * SLOTS * SUFFIX + n * SUFFIX
                hit = lane_c == 4 * g + h
                top_c[n] = jnp.where(hit, top[at : at + SUFFIX], top_c[n])
                sum_c[n] = jnp.where(hit, total[at : at + SUFFIX], sum_c[n])
    for n in range(SLOTS):
        ostat_send[n, 0] = top_c[n]
        ostat_send[n, 1] = sum_c[n]
    to_owners(o_pairs)

    tick(7)
    at_owners(o_pairs)

    def expand(compact):
        low = lane_c < HEAD_DIM
        return jnp.concatenate(
            [jnp.where(low, compact[:, 2 * t : 2 * t + 1], compact[:, 2 * t + 1 : 2 * t + 2]) for t in range(6)],
            axis=1,
        )

    tops = [ostat[i, 0] for i in range(SLOTS)]
    top_all = jnp.maximum(jnp.maximum(tops[0], tops[1]), tops[2])
    shares = [ostat[i, 1] * jnp.exp(tops[i] - top_all) for i in range(SLOTS)]
    whole = shares[0] + shares[1] + shares[2]
    whole = jnp.where(whole > 0.0, whole, 1.0)
    lse = top_all + jnp.log(whole)
    cross = jnp.zeros((SUFFIX, D), F32)
    for i in range(SLOTS):
        cross = cross + expand(shares[i] / whole) * obuf[i].astype(F32)
    cm = cross.astype(BF16)

    after_cross = after_self + mm(cm, wb[:, LANE_CO : LANE_CO + D])
    hat_three, rs_three = normed(after_cross)
    n3 = (hat_three * gain[2]).astype(BF16)
    nb[token_rows(f, c, chip)] = n3
    ag_n.step_one()

    tick(8)
    tick(9)
    for n in (3, 4, 5):
        spread[n].step_six()
    out_low = cb[mine]
    cot = out_low.astype(F32)
    acts, up_grads = [], []
    hidden_grad = [mm_nt(out_low, wb[:, LANE_FO + D * j : LANE_FO + D * (j + 1)]) for j in range(4)]

    def by_hidden(j):
        parts = []
        for t in range(D // half_rows):
            at = D * j + t * half_rows
            col, unit = at // (4 * half_rows), (at % (4 * half_rows)) // half_rows
            parts.append(hidden_grad[unit][:, col * half_rows : (col + 1) * half_rows])
        return jnp.concatenate(parts, axis=1)

    n3_grad = jnp.zeros((SUFFIX, D), F32)
    for j in range(4):
        weight = wb[:, LANE_FI + D * j : LANE_FI + D * (j + 1)]
        value, slope = gelu_parts(mm(n3, weight))
        acts.append(value.astype(BF16))
        part = (by_hidden(j) * slope).astype(BF16)
        n3_grad = n3_grad + mm_nt(part, weight)
    act = jnp.concatenate(acts, axis=1)

    ag_n.step_two()
    part, ffn_gain_grad = norm_back(n3_grad, hat_three, rs_three, gain[2])
    cross_res = cot + part
    cross_low = cross_res.astype(BF16)
    d_mixed = mm_nt(cross_low, wb[:, LANE_CO : LANE_CO + D]).astype(BF16)
    dob[...] = d_mixed
    prod = d_mixed.astype(F32) * cross
    delta = jnp.zeros((SUFFIX, 128), F32)
    for t in range(6):
        tile = prod[:, 128 * t : 128 * (t + 1)]
        left = jnp.sum(jnp.where(lane_c < HEAD_DIM, tile, 0.0), axis=-1, keepdims=True)
        right = jnp.sum(jnp.where(lane_c < HEAD_DIM, 0.0, tile), axis=-1, keepdims=True)
        delta = jnp.where(lane_c == 2 * t, left, delta)
        delta = jnp.where(lane_c == 2 * t + 1, right, delta)
    dstat_b[0] = lse
    dstat_b[1] = delta
    to_holders(d_pairs)
    down = jnp.zeros((SUFFIX, D), F32)
    for j in range(4):
        lhs = jnp.concatenate(
            [act[:, i * 4 * half_rows + j * half_rows : i * 4 * half_rows + (j + 1) * half_rows] for i in range(columns)],
            axis=1,
        )
        down = down + mm(lhs, wb[:, LANE_FO + D * j : LANE_FO + D * (j + 1)])
    ob[0, my_slot] = (after_cross + down).astype(BF16)
    ag_out = Gather(place, block_view(ob.at[0]), block_bulk(ob.at[0]), sems, 4)
    ag_out.step_one()
    ag_n.step_three()

    def unit_device(h):
        return CORES * (h + 1) if h < HALF_UNITS else CORES * (h - HALF_UNITS + 1) + 1

    unit_items = []

    def push_unit(h, left, right):
        to = unit_device(h)
        sb[h, :, 0:D] = left
        sb[h, :, D : D + PIECE] = right

        @pl.when(me == to)
        def _():
            rb[rows_of(me)] = sb[h]

        @pl.when(me != to)
        def _():
            pltpu.make_async_remote_copy(
                src_ref=sb.at[h], dst_ref=rb.at[rows_of(me)], send_sem=usend.at[h],
                recv_sem=urecv.at[me], device_id=(to, f), device_id_type=MESH,
            ).start()

        unit_items.append((h, to))

    push_unit(HALF_UNITS + 4, cm, cross_low[:, 0:PIECE])
    push_unit(HALF_UNITS + 5, cm, cross_low[:, PIECE:])

    at_holders(d_pairs)

    doh = jnp.concatenate([dobuf[s] for s in range(SLOTS)], axis=0)
    for g in range(3):
        sl = slice(256 * g, 256 * g + 256)
        kg = kvb[:, sl]
        vg = kvb[:, D + 256 * g : D + 256 * g + 256]
        q4 = stack(qh[:, sl])
        do4 = stack(doh[:, sl])
        lse_col = jnp.concatenate([dstat[n, 0][:, 4 * g + h : 4 * g + h + 1] for h in range(4) for n in range(SLOTS)], axis=0)
        del_col = jnp.concatenate([dstat[n, 1][:, 4 * g + h : 4 * g + h + 1] for h in range(4) for n in range(SLOTS)], axis=0)
        s = mm_nt(q4, kg)
        p = jnp.where(allowed, jnp.exp(jnp.where(allowed, s - lse_col, 0.0)), 0.0)
        dp = mm_nt(do4, vg)
        ds = (p * (dp - del_col)).astype(BF16)
        kvg[:, D + 256 * g : D + 256 * g + 256] = mm_tn(p.astype(BF16), do4).astype(BF16)
        kvg[:, sl] = mm_tn(ds, q4).astype(BF16)
        dq = unstack(mm(ds, kg)) * scale
        for n in range(SLOTS):
            dqsend[n, :, sl] = dq[n * SUFFIX : (n + 1) * SUFFIX].astype(BF16)
    to_owners(dq_pairs)
    ag_n.step_four()
    def kp_step(i, carry):
        lane = pl.multiple_of(i * 256, 256)
        kp[:, pl.ds(lane, 256)] = mm_tn(memp[...], kvg[:, pl.ds(lane, 256)]).astype(BF16)
        return carry

    lax.fori_loop(0, 6, kp_step, 0)
    kr_item = pltpu.make_async_remote_copy(
        src_ref=kp.at[pl.ds(pl.multiple_of((1 - c) * half_rows, 128), half_rows)], dst_ref=kr,
        send_sem=ksend.at[2 * chips], recv_sem=krecv.at[chips], device_id=mate, device_id_type=MESH,
    )
    kr_item.start()

    ag_n.step_five()
    across_n.start()
    across_o.relay()
    ag_out.step_two()
    at_owners(dq_pairs)
    cqg = (dqbuf[0].astype(F32) + dqbuf[1].astype(F32) + dqbuf[2].astype(F32)).astype(BF16)
    n2_grad = mm_nt(cqg, wb[:, LANE_CQ : LANE_CQ + D])
    part, cross_gain_grad = norm_back(n2_grad, hat_two, rs_two, gain[1])
    self_res = cross_res + part
    self_low = self_res.astype(BF16)
    dmix = mm_nt(self_low, wb[:, LANE_SO : LANE_SO + D]).astype(BF16)
    dqs, dks, dvs = [], [], []
    for g in range(3):
        sl = slice(256 * g, 256 * g + 256)
        q4 = stack(qs[:, sl])
        do4 = stack(dmix[:, sl])
        p = self_p[g]
        dp = mm_nt(do4, v[:, sl])
        ds = (p * (dp - jnp.sum(p * dp, axis=-1, keepdims=True))).astype(BF16)
        dvs.append(mm_tn(p.astype(BF16), do4))
        dks.append(mm_tn(ds, q4))
        dqs.append(unstack(mm(ds, k[:, sl])) * scale)
    packed_grad = [jnp.concatenate(parts, axis=1).astype(BF16) for parts in (dqs, dks, dvs)]
    for h in range(HALF_UNITS):
        push_unit(h, n1, packed_grad[h // 2][:, (h % 2) * PIECE : (h % 2 + 1) * PIECE])
    for h in range(2):
        push_unit(HALF_UNITS + 2 + h, n2, cqg[:, h * PIECE : (h + 1) * PIECE])
        push_unit(HALF_UNITS + h, sm, self_low[:, h * PIECE : (h + 1) * PIECE])

    def gb_view(lane_of):
        def view(zz, xx, cc):
            return gb.at[:, pl.ds(pl.multiple_of(lane_of(zz * SIDE + xx, cc), 128), PIECE)]

        return view

    n1_grad = jnp.zeros((SUFFIX, D), F32)
    for j in range(3):
        n1_grad = n1_grad + mm_nt(packed_grad[j], wb[:, D * j : D * (j + 1)])
    part, self_gain_grad = norm_back(n1_grad, hat_one, rs_one, gain[0])
    ob[1, my_slot] = (self_res + part).astype(BF16)
    ag_grad = Gather(place, block_view(ob.at[1]), block_bulk(ob.at[1]), sems, 6)
    gmine[...] = jnp.concatenate(
        [self_gain_grad, cross_gain_grad, ffn_gain_grad, jnp.zeros((5, D), F32)], axis=0
    )
    tb[my_slot] = gmine[...]
    tell_g = Tell(tb, 1)
    tell_g.start()
    kr_item.wait_recv()
    kc[...] = (
        kp[pl.ds(pl.multiple_of(c * half_rows, 128), half_rows)].astype(F32) + kr[...].astype(F32)
    ).astype(BF16)
    ky_item = pltpu.make_async_remote_copy(
        src_ref=kc, dst_ref=ky, send_sem=ksend.at[2 * chips + 1], recv_sem=krecv.at[chips + 1],
        device_id=(me, other), device_id_type=MESH,
    )

    @pl.when(c != f)
    def _():
        ky_item.start()

    ag_grad.step_one()
    ag_out.step_three()

    across_n.relay()
    ag_n.step_six()
    across_o.wait()
    across_n.wait()

    rows_step = 128
    hidden = [col * 4 * half_rows + D * c for col in range(columns)]

    def ffn_rows(first, last):
        def one(i, carry):
            at = pl.ds(pl.multiple_of(i * rows_step, rows_step), rows_step)
            for col in range(columns):
                lane = pl.multiple_of(LANE_FI + hidden[col], 128)
                value, slope = gelu_parts(mm(nb[at], wb[:, pl.ds(lane, D)]))

                @pl.when(f == col)
                def _():
                    ab[at] = value.astype(BF16)

                back = []
                for t in range(CORES):
                    lane_o = pl.multiple_of(LANE_FO + D * (2 * c + t), 128)
                    back.append(mm_nt(olr[at], wb[col * half_rows : (col + 1) * half_rows, pl.ds(lane_o, D)]))
                hb[col, at] = (jnp.concatenate(back, axis=1) * slope).astype(BF16)
            return carry

        lax.fori_loop(first, last, one, 0)

    own_lanes = pl.ds(pl.multiple_of(f * half_rows, 128), half_rows)

    def ffn_in_sum(col):
        lane = pl.multiple_of(LANE_FI + hidden[col], 128)
        for part in range(0, D, PIECE):
            total = mm_tn(nb[:, own_lanes], hb[col, :, part : part + PIECE])
            gb[:, pl.ds(lane + part, PIECE)] = total.astype(BF16)

    def ffn_out_sum(t):
        lane = pl.multiple_of(LANE_FO + D * (2 * c + t), 128)
        for part in range(0, D, PIECE):
            total = mm_tn(ab[:, t * half_rows : (t + 1) * half_rows], olr[:, part : part + PIECE])
            gb[:, pl.ds(lane + part, PIECE)] = total.astype(BF16)

    f_items = []

    def to_mate(lane, width):
        ref = gb.at[:, pl.ds(pl.multiple_of(lane, 128), width)]
        item = pltpu.make_async_remote_copy(
            src_ref=ref, dst_ref=ref, send_sem=fsend.at[len(f_items)], recv_sem=frecv.at[len(f_items)],
            device_id=mate, device_id_type=MESH,
        )
        item.start()
        f_items.append(item)

    has_unit = (chip >= 1) & (chip <= HALF_UNITS)

    def unit_lane(n, cc):
        return PIECE * (n - 1) + HALF_UNITS * PIECE * cc

    def unit_sum(pred, at):
        @pl.when(pred)
        def _():
            def take(i, carry):
                @pl.when(i != me)
                def _():
                    pltpu.make_async_remote_copy(
                        src_ref=sb.at[0], dst_ref=rb.at[rows_of(i)], send_sem=usend.at[0],
                        recv_sem=urecv.at[i], device_id=mate, device_id_type=MESH,
                    ).wait_recv()

                return carry

            lax.fori_loop(0, ranks, take, 0)
            for col in range(columns):
                ug[col] = mm_tn(rb[:, col * half_rows : (col + 1) * half_rows], rb[:, D : D + PIECE])
            usend_b[...] = ug[other].astype(BF16)
            pltpu.make_async_remote_copy(
                src_ref=usend_b, dst_ref=urecv_b, send_sem=ysend.at[at], recv_sem=yrecv.at[at],
                device_id=(me, other), device_id_type=MESH,
            ).start()

    def unit_join(pred, at):
        @pl.when(pred)
        def _():
            item = pltpu.make_async_remote_copy(
                src_ref=usend_b, dst_ref=urecv_b, send_sem=ysend.at[at], recv_sem=yrecv.at[at],
                device_id=(me, other), device_id_type=MESH,
            )
            item.wait_recv()
            gb[:, pl.ds(pl.multiple_of(unit_lane(chip, c), 128), PIECE)] = (
                ug[f] + urecv_b[...].astype(F32)
            ).astype(BF16)
            item.wait_send()

    def has_block(zz, xx, cc):
        n = zz * SIDE + xx
        return (n >= 1) & (n <= HALF_UNITS)

    def unit_bulk(cc):
        return gb.at[:, pl.ds(pl.multiple_of(HALF_UNITS * PIECE * cc, 128), HALF_UNITS * PIECE)]

    ag_u = Gather(place, gb_view(unit_lane), unit_bulk, sems, 3, has_block)

    ffn_rows(0, 4)
    half_slabs = half_rows // SIDE
    kx_item = pltpu.make_async_remote_copy(
        src_ref=kc.at[pl.ds(pl.multiple_of((1 - x) * half_slabs, 16), half_slabs)], dst_ref=kx,
        send_sem=ksend.at[2 * chips + 2], recv_sem=krecv.at[chips + 2],
        device_id=(z * (SIDE * CORES) + (1 - x) * CORES + c, f), device_id_type=MESH,
    )

    @pl.when(c == f)
    def _():
        ky_item.wait_recv()
        kc[...] = (kc[...].astype(F32) + ky[...].astype(F32)).astype(BF16)
        kx_item.start()

    ffn_rows(4, 6)
    unit_sum(has_unit, 3)
    ffn_rows(6, 8)
    k_items = []

    def k_copy(t, j):
        return pltpu.make_async_remote_copy(
            src_ref=ks.at[pl.ds(t * slab, slab), pl.ds(j * D, D)], dst_ref=cp.at[z],
            send_sem=ksend.at[t * CORES + j], recv_sem=krecv.at[z],
            device_id=(t * (SIDE * CORES) + x * CORES + j, f), device_id_type=MESH,
        )

    @pl.when(c == f)
    def _():
        kx_item.wait_recv()
        ks[...] = (
            kc[pl.ds(pl.multiple_of(x * half_slabs, 16), half_slabs)].astype(F32) + kx[...].astype(F32)
        ).astype(BF16)

    for t in range(RING):
        for j in range(CORES):
            here = (z == t) & (c == j)

            @pl.when((c == f) & here)
            def _():
                cp[z] = ks[t * slab : (t + 1) * slab, j * D : (j + 1) * D]

            @pl.when((c == f) & jnp.logical_not(here))
            def _():
                k_copy(t, j).start()

            k_items.append((t, j, here))

    unit_join(has_unit, 3)
    ag_u.step_one()
    ag_grad.step_two()
    ag_out.step_four()
    ffn_in_sum(0)
    to_mate(LANE_FI + hidden[0], D)
    ffn_in_sum(1)
    to_mate(LANE_FI + hidden[1], D)
    ag_u.step_two()

    def take_k(i, carry):
        @pl.when((i != z) | (c != f))
        def _():
            pltpu.make_async_remote_copy(
                src_ref=ks.at[pl.ds(0, slab), pl.ds(0, D)], dst_ref=cp.at[i], send_sem=ksend.at[0],
                recv_sem=krecv.at[i], device_id=mate, device_id_type=MESH,
            ).wait_recv()

        return carry

    lax.fori_loop(0, RING, take_k, 0)
    total = cp[0].astype(F32)
    for i in range(1, RING):
        total = total + cp[i].astype(F32)
    k_lane = pl.multiple_of(LANE_CKV + c * D, 128)
    gb[pl.ds(pl.multiple_of(x * half_slabs + z * slab, 16), slab), pl.ds(k_lane, D)] = total.astype(BF16)

    def kv_view(zz, xx, cc):
        row = pl.multiple_of(xx * half_slabs + zz * slab, 16)
        return gb.at[pl.ds(row, slab), pl.ds(pl.multiple_of(LANE_CKV + cc * D, 128), D)]

    ag_k = Gather(place, kv_view, lambda cc: gb.at[:, pl.ds(pl.multiple_of(LANE_CKV + cc * D, 128), D)], sems, 5)
    ag_k.step_one()
    ag_grad.step_three()
    ag_out.step_five()
    ffn_out_sum(0)
    ffn_out_sum(1)
    to_mate(LANE_FO + CORES * D * c, CORES * D)
    ag_u.step_three()
    ag_k.step_two()
    ag_grad.step_four()
    ag_out.step_six()

    def mg_step(i, carry):
        row = pl.multiple_of(i * 128, 128)
        memgrad_ref[pl.ds(row, 128)] = mm_nt(kvg[pl.ds(row, 128)], wb[:, LANE_CKV : LANE_CKV + 2 * D])
        return carry

    full = own_rows // 128
    lax.fori_loop(0, full, mg_step, 0)
    if own_rows % 128:
        tail = mm_nt(kvg[full * 128 : (full + 1) * 128], wb[:, LANE_CKV : LANE_CKV + 2 * D])
        memgrad_ref[full * 128 : own_rows] = tail[0 : own_rows - full * 128]


    ag_u.step_four()
    ag_k.step_three()
    ag_grad.step_five()
    tell_g.wait()
    gmine[...] = tb[0]
    for i in range(1, ranks):
        gmine[...] += tb[i]
    g_item = push_y(gmine, gpeer, 2)
    for n, (lane, width) in enumerate(
        [(LANE_FI + col * 4 * half_rows + D * (1 - c), D) for col in range(columns)] + [(LANE_FO + CORES * D * (1 - c), CORES * D)]
    ):
        ref = gb.at[:, pl.ds(pl.multiple_of(lane, 128), width)]
        pltpu.make_async_remote_copy(
            src_ref=ref, dst_ref=ref, send_sem=fsend.at[n], recv_sem=frecv.at[n], device_id=mate, device_id_type=MESH,
        ).wait_recv()
    outs = []

    def write(lane, width):
        lanes = pl.ds(lane, width)
        item = pltpu.make_async_copy(gb.at[:, lanes], weights_out_ref.at[:, lanes], load_sem.at[len(outs)])
        item.start()
        outs.append(item)

    write(LANE_FI, 8 * D)
    ag_u.step_five()
    ag_k.step_four()
    ag_k.step_five()
    ag_grad.step_six()
    out_ref[...] = ob[0, out_slot].astype(F32)
    grad_ref[...] = ob[1, out_slot].astype(F32)
    g_item.wait_recv()
    gains_all = gmine[...] + gpeer[...]
    own_gain = gains_all[:, 0:half_rows]
    for i in range(1, columns):
        own_gain = jnp.where(f == i, gains_all[:, i * half_rows : (i + 1) * half_rows], own_gain)
    gain_out_ref[...] = own_gain
    ag_u.step_six()
    write(0, LANE_CKV)
    ag_k.step_six()
    write(LANE_CKV, 2 * D)

    to_holders_sent(q_pairs)
    to_owners_sent(o_pairs)
    to_holders_sent(d_pairs)
    to_owners_sent(dq_pairs)
    for h, to in unit_items:
        @pl.when(me != to)
        def _():
            pltpu.make_async_remote_copy(
                src_ref=sb.at[h], dst_ref=rb.at[rows_of(me)], send_sem=usend.at[h],
                recv_sem=urecv.at[0], device_id=(to, f), device_id_type=MESH,
            ).wait_send()
    for t, j, here in k_items:
        @pl.when((c == f) & jnp.logical_not(here))
        def _():
            k_copy(t, j).wait_send()

    @pl.when(c == f)
    def _():
        kx_item.wait_send()

    across_o.finish()
    across_n.finish()
    for item in f_items:
        item.wait_send()
    kr_item.wait_send()

    @pl.when(c != f)
    def _():
        ky_item.wait_send()

    for item in y_items:
        item.wait_send()
    tell_p.finish()
    tell_g.finish()
    for item in [ag_x, *spread, ag_c, ag_n, ag_u, ag_out, ag_grad, ag_k]:
        item.finish()
    for item in outs:
        item.wait()


def fused_body(
    ranks, columns,
    decoder_in, memory, res_group, prefix_len, self_gain, self_qkv, self_out, cross_gain, cross_query,
    cross_kv, cross_out, ffn_gain, ffn_in, ffn_out, cotangent,
):
    half_rows = D // columns
    chips = ranks // CORES
    slab = half_rows // chips
    own_rows = memory.shape[1]
    padded = -(-own_rows // 128) * 128
    tokens = ranks * SUFFIX
    gains = jnp.concatenate([self_gain, cross_gain, ffn_gain]).astype(F32)
    gains = jnp.pad(gains, (0, 16 * 128 - gains.shape[0])).reshape(16, 128)
    vm = pl.BlockSpec(memory_space=pltpu.VMEM)
    sm = pl.BlockSpec(memory_space=pltpu.SMEM)
    hbm = pl.BlockSpec(memory_space=pl.ANY)
    dma = pltpu.SemaphoreType.DMA
    scratch = [
        pltpu.VMEM((D, UNITS * D), BF16),
        pltpu.VMEM((half_rows, UNITS * D), BF16),
        pltpu.VMEM((tokens, D + PIECE), BF16),
        pltpu.VMEM((2 * HALF_UNITS, SUFFIX, D + PIECE), BF16),
        pltpu.VMEM((ranks, SUFFIX, D), F32),
        pltpu.VMEM((ranks, SUFFIX, D), BF16),
        pltpu.VMEM((columns * tokens, D), BF16),
        pltpu.VMEM((columns * tokens, D), BF16),
        pltpu.VMEM((2, ranks, SUFFIX, D), BF16),
        pltpu.VMEM((ranks, 8, D), F32),
        pltpu.VMEM((ranks, 8, 128), F32),
        pltpu.VMEM((columns, 16, 128), F32),
        pltpu.VMEM((padded, D), BF16),
        pltpu.VMEM((padded, 2 * D), BF16),
        pltpu.VMEM((padded, 2 * D), BF16),
        pltpu.VMEM((D, 2 * D), BF16),
        pltpu.VMEM((half_rows, 2 * D), BF16),
        pltpu.VMEM((half_rows, 2 * D), BF16),
        pltpu.VMEM((half_rows, 2 * D), BF16),
        pltpu.VMEM((RING, slab, D), BF16),
        pltpu.VMEM((half_rows // SIDE, 2 * D), BF16),
        pltpu.VMEM((half_rows // SIDE, 2 * D), BF16),
        pltpu.VMEM((columns, columns * tokens, D), BF16),
        pltpu.VMEM((columns * tokens, D), BF16),
        pltpu.VMEM((columns, half_rows, PIECE), F32),
        pltpu.VMEM((half_rows, PIECE), BF16),
        pltpu.VMEM((half_rows, PIECE), BF16),
        pltpu.VMEM((SUFFIX, D), BF16),
        pltpu.VMEM((SLOTS, SUFFIX, D), BF16),
        pltpu.VMEM((SLOTS, SUFFIX, D), BF16),
        pltpu.VMEM((SLOTS, 2, SUFFIX, 128), F32),
        pltpu.VMEM((SLOTS, SUFFIX, D), BF16),
        pltpu.VMEM((SLOTS, 2, SUFFIX, 128), F32),
        pltpu.VMEM((SUFFIX, D), BF16),
        pltpu.VMEM((2, SUFFIX, 128), F32),
        pltpu.VMEM((SLOTS, SUFFIX, D), BF16),
        pltpu.VMEM((SLOTS, 2, SUFFIX, 128), F32),
        pltpu.VMEM((SLOTS, SUFFIX, D), BF16),
        pltpu.VMEM((SLOTS, SUFFIX, D), BF16),
        pltpu.VMEM((8, D), F32),
        pltpu.VMEM((8, D), F32),
        dma((10,)),
        dma((len(CHUNKS), 17)),
        dma((len(CHUNKS), 11)),
        dma((7, 16)),
        dma((7, 9)),
        dma((2, ranks)),
        dma((2, ranks)),
        dma((2, 2)),
        dma((2, 2)),
        dma((3,)),
        dma((3,)),
        dma((4,)),
        dma((4,)),
        dma((6, SLOTS)),
        dma((6, SLOTS)),
        dma((2 * HALF_UNITS,)),
        dma((ranks,)),
        dma((2 * chips + 3,)),
        dma((chips + 3,)),
    ]
    out, grad, memgrad, gain_grads, weight_grads = pl.pallas_call(
        partial(layer_kernel, ranks, columns),
        out_shape=(
            jax.ShapeDtypeStruct((SUFFIX, D), F32),
            jax.ShapeDtypeStruct((SUFFIX, D), F32),
            jax.ShapeDtypeStruct((own_rows, D), F32),
            jax.ShapeDtypeStruct((8, half_rows), F32),
            jax.ShapeDtypeStruct((half_rows, UNITS * D), BF16),
        ),
        in_specs=[vm, vm, vm, sm, sm, vm] + [hbm] * 7,
        out_specs=(vm, vm, vm, vm, hbm),
        scratch_shapes=scratch,
        compiler_params=pltpu.CompilerParams(
            collective_id=0, has_side_effects=True, vmem_limit_bytes=63 * 2**20
        ),
        name="layer",
    )(
        decoder_in[0], cotangent[0], memory[0], res_group, prefix_len, gains,
        self_qkv, self_out, cross_query, cross_kv, cross_out, ffn_in, ffn_out,
    )

    return unpack(half_rows, columns, weight_grads, memgrad, out, grad, gain_grads)


SPLIT = (
    (LANE_QKV, 3 * D), (LANE_SO, D), (LANE_CQ, D), (LANE_CKV, 2 * D), (LANE_CO, D), (LANE_FI, 4 * D)
)


def unpack_kernel(w_ref, m_ref, o_ref, g_ref, *refs):
    *weights, ffn_out_ref, mem_ref, out_ref, grad_ref = refs
    for (low, width), ref in zip(SPLIT, weights):
        ref[...] = w_ref[:, low : low + width].astype(F32)
    for j in range(4):
        ffn_out_ref[j] = w_ref[:, LANE_FO + D * j : LANE_FO + D * (j + 1)].astype(F32)
    mem_ref[:, 0, :] = m_ref[...]
    out_ref[...] = o_ref[...]
    grad_ref[...] = g_ref[...]


def unpack(half_rows, columns, weight_grads, memgrad, out, grad, gain_grads):
    steps = 2
    rows = half_rows // steps
    own_rows = memgrad.shape[0]
    mem_rows = -(-own_rows // (8 * steps)) * 8
    tokens = out.shape[0] // steps
    block = lambda height, width: pl.BlockSpec((height, width), lambda i: (i, 0))
    results = pl.pallas_call(
        unpack_kernel,
        grid=(steps,),
        out_shape=[jax.ShapeDtypeStruct((half_rows, width), F32) for low, width in SPLIT]
        + [
            jax.ShapeDtypeStruct((4, half_rows, D), F32),
            jax.ShapeDtypeStruct((own_rows, 1, D), F32),
            jax.ShapeDtypeStruct(out.shape, F32),
            jax.ShapeDtypeStruct(grad.shape, F32),
        ],
        in_specs=[block(rows, UNITS * D), block(mem_rows, D), block(tokens, D), block(tokens, D)],
        out_specs=[block(rows, width) for low, width in SPLIT]
        + [
            pl.BlockSpec((4, rows, D), lambda i: (0, i, 0)),
            pl.BlockSpec((mem_rows, 1, D), lambda i: (i, 0, 0)),
            block(tokens, D),
            block(tokens, D),
        ],
        compiler_params=pltpu.CompilerParams(vmem_limit_bytes=63 * 2**20),
        name="unpack",
    )(weight_grads, memgrad, out, grad)
    qkv, so, cq, ckv, co, fi, fo, mem, out, grad = results
    return (
        out[None], grad[None], mem.reshape(1, own_rows, D),
        gain_grads[0], qkv, so, gain_grads[1], cq, ckv, co, gain_grads[2], fi, fo.reshape(4 * half_rows, D),
    )


def layer_norm(value, gain):
    mean = jnp.mean(value, axis=-1, keepdims=True)
    centred = value - mean
    variance = jnp.mean(centred * centred, axis=-1, keepdims=True)
    return centred * lax.rsqrt(variance + norm_eps) * gain


def product(left, right):
    return jnp.dot(left, right, preferred_element_type=jnp.float32)


def outer_sum(left, right):
    flat_left = left.reshape(-1, left.shape[-1])
    flat_right = right.reshape(-1, right.shape[-1])
    return lax.dot_general(
        flat_left, flat_right, (((0,), (0,)), ((), ())), preferred_element_type=jnp.float32
    )


def back_product(grad, weight):
    return lax.dot_general(
        grad, weight, (((grad.ndim - 1,), (1,)), ((), ())), preferred_element_type=jnp.float32
    )


def attend(query, keys, values, allowed, scale):
    scores = jnp.einsum("eqhd,ekhd->ehqk", query, keys, preferred_element_type=jnp.float32) * scale
    scores = jnp.where(allowed[:, None], scores, -1e30)
    top = jnp.max(scores, axis=-1, keepdims=True)
    weights = jnp.exp(scores - top)
    probs = weights / jnp.sum(weights, axis=-1, keepdims=True)
    mixed = jnp.einsum(
        "ehqk,ekhd->eqhd", probs.astype(jnp.bfloat16), values, preferred_element_type=jnp.float32
    )
    return (mixed.astype(jnp.bfloat16), probs)


def attend_back(grad_mixed, query, keys, values, probs, scale):
    probs_low = probs.astype(jnp.bfloat16)
    grad_values = jnp.einsum(
        "ehqk,eqhd->ekhd", probs_low, grad_mixed, preferred_element_type=jnp.float32
    )
    grad_probs = jnp.einsum(
        "eqhd,ekhd->ehqk", grad_mixed, values, preferred_element_type=jnp.float32
    )
    grad_scores = probs * (grad_probs - jnp.sum(probs * grad_probs, axis=-1, keepdims=True))
    grad_low = grad_scores.astype(jnp.bfloat16)
    grad_query = (
        jnp.einsum("ehqk,ekhd->eqhd", grad_low, keys, preferred_element_type=jnp.float32) * scale
    )
    grad_keys = (
        jnp.einsum("ehqk,eqhd->ekhd", grad_low, query, preferred_element_type=jnp.float32) * scale
    )
    return (grad_query, grad_keys, grad_values)


def window_layout(res_group, mem_col):
    small = 1 - res_group
    small_count = jnp.sum(small, axis=-1, keepdims=True)
    small_before = jnp.cumsum(small, axis=-1) - small
    large_before = jnp.cumsum(res_group, axis=-1) - res_group
    offset = jnp.where(
        res_group == 1, SLOT_S * small_count + SLOT_L * large_before, SLOT_S * small_before
    )
    start = jnp.minimum(offset, mem_col - SLOT_L)
    return (offset, start)


def take_windows(column, starts):
    return jax.vmap(lambda begin: lax.dynamic_slice_in_dim(column, begin, SLOT_L, 0))(starts)


def forward(decoder_rows, windows, cross_allowed, weights):
    (
        self_gain,
        self_qkv,
        self_out,
        cross_gain,
        cross_query,
        cross_kv,
        cross_out,
        ffn_gain,
        ffn_in,
        ffn_out,
    ) = weights
    count = decoder_rows.shape[0] // SUFFIX
    scale = HEAD_DIM ** (-0.5)
    row_index = lax.broadcasted_iota(jnp.int32, (SUFFIX, SUFFIX), 0)
    col_index = lax.broadcasted_iota(jnp.int32, (SUFFIX, SUFFIX), 1)
    causal = (row_index >= col_index)[None]
    resid = decoder_rows.reshape(count, SUFFIX, D)
    normed_one = layer_norm(resid, self_gain.astype(jnp.float32)).astype(jnp.bfloat16)
    packed = product(normed_one, self_qkv).astype(jnp.bfloat16)
    heads = packed.reshape(count, SUFFIX, 3, HEADS, HEAD_DIM)
    self_mixed, self_probs = attend(heads[:, :, 0], heads[:, :, 1], heads[:, :, 2], causal, scale)
    self_mixed = self_mixed.reshape(count, SUFFIX, D)
    after_self = resid + product(self_mixed, self_out)
    normed_two = layer_norm(after_self, cross_gain.astype(jnp.float32)).astype(jnp.bfloat16)
    cross_q = product(normed_two, cross_query).astype(jnp.bfloat16)
    window_kv = product(windows, cross_kv).astype(jnp.bfloat16)
    query_heads = cross_q.reshape(count, SUFFIX, HEADS, HEAD_DIM)
    kv_heads = window_kv.reshape(count, SLOT_L, 2, HEADS, HEAD_DIM)
    cross_mixed, cross_probs = attend(
        query_heads, kv_heads[:, :, 0], kv_heads[:, :, 1], cross_allowed, scale
    )
    cross_mixed = cross_mixed.reshape(count, SUFFIX, D)
    after_cross = after_self + product(cross_mixed, cross_out)
    normed_three = layer_norm(after_cross, ffn_gain.astype(jnp.float32)).astype(jnp.bfloat16)
    up = product(normed_three, ffn_in)
    act = jax.nn.gelu(up, approximate=True).astype(jnp.bfloat16)
    result = after_cross + product(act, ffn_out)
    return (
        resid,
        normed_one,
        packed,
        self_probs,
        self_mixed,
        after_self,
        normed_two,
        cross_q,
        window_kv,
        cross_probs,
        cross_mixed,
        after_cross,
        normed_three,
        up,
        act,
        result,
    )


def backward(grad_out, saved, weights):
    (
        self_gain,
        self_qkv,
        self_out,
        cross_gain,
        cross_query,
        cross_kv,
        cross_out,
        ffn_gain,
        ffn_in,
        ffn_out,
    ) = weights
    (
        resid,
        normed_one,
        packed,
        self_probs,
        self_mixed,
        after_self,
        normed_two,
        cross_q,
        window_kv,
        cross_probs,
        cross_mixed,
        after_cross,
        normed_three,
        up,
        act,
        result,
    ) = saved
    count = resid.shape[0]
    scale = HEAD_DIM ** (-0.5)
    grad_out = grad_out.reshape(count, SUFFIX, D)
    out_low = grad_out.astype(jnp.bfloat16)
    ffn_out_grad = outer_sum(act, out_low)
    act_grad = back_product(out_low, ffn_out)
    gelu_value, gelu_back = jax.vjp(partial(jax.nn.gelu, approximate=True), up)
    up_grad = gelu_back(act_grad)[0].astype(jnp.bfloat16)
    ffn_in_grad = outer_sum(normed_three, up_grad)
    normed_three_grad = back_product(up_grad, ffn_in)
    norm_value, norm_back = jax.vjp(layer_norm, after_cross, ffn_gain.astype(jnp.float32))
    resid_part, ffn_gain_grad = norm_back(normed_three_grad)
    cross_res_grad = grad_out + resid_part
    cross_low = cross_res_grad.astype(jnp.bfloat16)
    cross_out_grad = outer_sum(cross_mixed, cross_low)
    mixed_grad = (
        back_product(cross_low, cross_out)
        .astype(jnp.bfloat16)
        .reshape(count, SUFFIX, HEADS, HEAD_DIM)
    )
    query_heads = cross_q.reshape(count, SUFFIX, HEADS, HEAD_DIM)
    kv_heads = window_kv.reshape(count, SLOT_L, 2, HEADS, HEAD_DIM)
    query_grad, keys_grad, values_grad = attend_back(
        mixed_grad, query_heads, kv_heads[:, :, 0], kv_heads[:, :, 1], cross_probs, scale
    )
    cross_q_grad = query_grad.reshape(count, SUFFIX, D).astype(jnp.bfloat16)
    window_kv_grad = (
        jnp.stack((keys_grad, values_grad), axis=2)
        .reshape(count, SLOT_L, 2 * D)
        .astype(jnp.bfloat16)
    )
    cross_query_grad = outer_sum(normed_two, cross_q_grad)
    normed_two_grad = back_product(cross_q_grad, cross_query)
    norm_value, norm_back = jax.vjp(layer_norm, after_self, cross_gain.astype(jnp.float32))
    resid_part, cross_gain_grad = norm_back(normed_two_grad)
    self_res_grad = cross_res_grad + resid_part
    self_low = self_res_grad.astype(jnp.bfloat16)
    self_out_grad = outer_sum(self_mixed, self_low)
    mixed_grad = (
        back_product(self_low, self_out)
        .astype(jnp.bfloat16)
        .reshape(count, SUFFIX, HEADS, HEAD_DIM)
    )
    heads = packed.reshape(count, SUFFIX, 3, HEADS, HEAD_DIM)
    query_grad, keys_grad, values_grad = attend_back(
        mixed_grad, heads[:, :, 0], heads[:, :, 1], heads[:, :, 2], self_probs, scale
    )
    packed_grad = (
        jnp.stack((query_grad, keys_grad, values_grad), axis=2)
        .reshape(count, SUFFIX, 3 * D)
        .astype(jnp.bfloat16)
    )
    self_qkv_grad = outer_sum(normed_one, packed_grad)
    normed_one_grad = back_product(packed_grad, self_qkv)
    norm_value, norm_back = jax.vjp(layer_norm, resid, self_gain.astype(jnp.float32))
    resid_part, self_gain_grad = norm_back(normed_one_grad)
    decoder_grad = self_res_grad + resid_part
    weight_grads = (
        self_gain_grad,
        self_qkv_grad,
        self_out_grad,
        cross_gain_grad,
        cross_query_grad,
        cross_out_grad,
        ffn_gain_grad,
        ffn_in_grad,
        ffn_out_grad,
    )
    return (decoder_grad, window_kv_grad, weight_grads)


def make_placer(all_starts, lowest, own_rows):

    def place(total, piece, begin):

        def add_one(item, acc):
            relative = all_starts[item] - lowest
            inside = ((relative > -SLOT_L) & (relative < own_rows)).astype(jnp.float32)
            spot = jnp.clip(relative + SLOT_L, 0, own_rows + SLOT_L)
            current = lax.dynamic_slice_in_dim(acc, spot, SLOT_L, 0)
            added = current + piece[item].astype(jnp.float32) * inside
            return lax.dynamic_update_slice_in_dim(acc, added, spot, 0)

        return lax.fori_loop(0, piece.shape[0], add_one, total)

    return place


def body(
    decoder_in,
    memory,
    res_group,
    prefix_len,
    self_gain,
    self_qkv,
    self_out,
    cross_gain,
    cross_query,
    cross_kv,
    cross_out,
    ffn_gain,
    ffn_in,
    ffn_out,
    cotangent,
):
    count = prefix_len.shape[1]
    own_rows = memory.shape[1]
    mem_col = own_rows * lax.axis_size("dp")
    offset, start = window_layout(res_group, mem_col)
    all_starts = start[0]
    first = lax.axis_index("dp") * count
    own_offset = lax.dynamic_slice_in_dim(offset[0], first, count)
    own_start = lax.dynamic_slice_in_dim(all_starts, first, count)
    own_group = lax.dynamic_slice_in_dim(res_group[0], first, count)
    valid = jnp.where(own_group == 1, PATCH_L, PATCH_S) + prefix_len[0]
    positions = own_start[:, None] + jnp.arange(SLOT_L, dtype=jnp.int32)[None]
    cross_allowed = (
        (positions >= own_offset[:, None]) & (positions < (own_offset + valid)[:, None])
    )[:, None]
    weights = (
        lax.all_gather(self_gain, "fsdp", axis=0, tiled=True),
        lax.all_gather(self_qkv, "fsdp", axis=0, tiled=True),
        lax.all_gather(self_out, "fsdp", axis=0, tiled=True),
        lax.all_gather(cross_gain, "fsdp", axis=0, tiled=True),
        lax.all_gather(cross_query, "fsdp", axis=0, tiled=True),
        lax.all_gather(cross_kv, "fsdp", axis=0, tiled=True),
        lax.all_gather(cross_out, "fsdp", axis=0, tiled=True),
        lax.all_gather(ffn_gain, "fsdp", axis=0, tiled=True),
        lax.all_gather(ffn_in, "fsdp", axis=0, tiled=True),
        lax.all_gather(ffn_out, "fsdp", axis=0, tiled=True),
    )
    column = lax.all_gather(memory[0], "dp", axis=0, tiled=True)
    windows = take_windows(column, own_start)
    saved = forward(decoder_in[0], windows, cross_allowed, weights)
    decoder_out = saved[-1]
    weights = (
        lax.all_gather(self_gain, "fsdp", axis=0, tiled=True),
        lax.all_gather(self_qkv, "fsdp", axis=0, tiled=True),
        lax.all_gather(self_out, "fsdp", axis=0, tiled=True),
        lax.all_gather(cross_gain, "fsdp", axis=0, tiled=True),
        lax.all_gather(cross_query, "fsdp", axis=0, tiled=True),
        lax.all_gather(cross_kv, "fsdp", axis=0, tiled=True),
        lax.all_gather(cross_out, "fsdp", axis=0, tiled=True),
        lax.all_gather(ffn_gain, "fsdp", axis=0, tiled=True),
        lax.all_gather(ffn_in, "fsdp", axis=0, tiled=True),
        lax.all_gather(ffn_out, "fsdp", axis=0, tiled=True),
    )
    column = lax.all_gather(memory[0], "dp", axis=0, tiled=True)
    windows = take_windows(column, own_start)
    saved = forward(decoder_in[0], windows, cross_allowed, weights)
    whole_kv = weights[5]
    decoder_grad, window_kv_grad, local_grads = backward(cotangent[0], saved, weights)
    lowest = lax.axis_index("dp") * own_rows
    place = make_placer(all_starts, lowest, own_rows)
    empty = jnp.zeros((own_rows + 2 * SLOT_L, 2 * D), jnp.float32)
    summed = place(empty, lax.all_gather(window_kv_grad, "dp", axis=0, tiled=True), jnp.int32(0))
    own_kv_grad = summed[SLOT_L : SLOT_L + own_rows].astype(jnp.bfloat16)
    memory_grad = back_product(own_kv_grad, whole_kv)
    cross_kv_part = outer_sum(memory[0], own_kv_grad)
    grads = (
        local_grads[0],
        local_grads[1],
        local_grads[2],
        local_grads[3],
        local_grads[4],
        cross_kv_part,
        local_grads[5],
        local_grads[6],
        local_grads[7],
        local_grads[8],
    )
    shards = (
        lax.psum_scatter(
            grads[0].astype(jnp.bfloat16), "fsdp", scatter_dimension=0, tiled=True
        ).astype(jnp.float32),
        lax.psum_scatter(
            grads[1].astype(jnp.bfloat16), "fsdp", scatter_dimension=0, tiled=True
        ).astype(jnp.float32),
        lax.psum_scatter(
            grads[2].astype(jnp.bfloat16), "fsdp", scatter_dimension=0, tiled=True
        ).astype(jnp.float32),
        lax.psum_scatter(
            grads[3].astype(jnp.bfloat16), "fsdp", scatter_dimension=0, tiled=True
        ).astype(jnp.float32),
        lax.psum_scatter(
            grads[4].astype(jnp.bfloat16), "fsdp", scatter_dimension=0, tiled=True
        ).astype(jnp.float32),
        lax.psum_scatter(
            grads[5].astype(jnp.bfloat16), "fsdp", scatter_dimension=0, tiled=True
        ).astype(jnp.float32),
        lax.psum_scatter(
            grads[6].astype(jnp.bfloat16), "fsdp", scatter_dimension=0, tiled=True
        ).astype(jnp.float32),
        lax.psum_scatter(
            grads[7].astype(jnp.bfloat16), "fsdp", scatter_dimension=0, tiled=True
        ).astype(jnp.float32),
        lax.psum_scatter(
            grads[8].astype(jnp.bfloat16), "fsdp", scatter_dimension=0, tiled=True
        ).astype(jnp.float32),
        lax.psum_scatter(
            grads[9].astype(jnp.bfloat16), "fsdp", scatter_dimension=0, tiled=True
        ).astype(jnp.float32),
    )
    totals = (
        lax.psum(shards[0].astype(jnp.bfloat16), "dp").astype(jnp.float32),
        lax.psum(shards[1].astype(jnp.bfloat16), "dp").astype(jnp.float32),
        lax.psum(shards[2].astype(jnp.bfloat16), "dp").astype(jnp.float32),
        lax.psum(shards[3].astype(jnp.bfloat16), "dp").astype(jnp.float32),
        lax.psum(shards[4].astype(jnp.bfloat16), "dp").astype(jnp.float32),
        lax.psum(shards[5].astype(jnp.bfloat16), "dp").astype(jnp.float32),
        lax.psum(shards[6].astype(jnp.bfloat16), "dp").astype(jnp.float32),
        lax.psum(shards[7].astype(jnp.bfloat16), "dp").astype(jnp.float32),
        lax.psum(shards[8].astype(jnp.bfloat16), "dp").astype(jnp.float32),
        lax.psum(shards[9].astype(jnp.bfloat16), "dp").astype(jnp.float32),
    )
    return (
        decoder_out,
        decoder_grad,
        memory_grad[None],
        totals[0],
        totals[1],
        totals[2],
        totals[3],
        totals[4],
        totals[5],
        totals[6],
        totals[7],
        totals[8],
        totals[9],
    )


def choose(mesh):
    ranks, columns = mesh.shape["dp"], mesh.shape["fsdp"]
    slabs = (D // columns) % (16 * (ranks // CORES)) == 0
    if slabs and columns == 2 and ranks == RING * SIDE * CORES:
        return partial(fused_body, ranks, columns)
    return body


def solution(mesh):
    placed = (
        P("fsdp", "dp", None),
        P("fsdp", "dp", None),
        P("fsdp", None),
        P("fsdp", "dp"),
        P("fsdp"),
        P("fsdp", None),
        P("fsdp", None),
        P("fsdp"),
        P("fsdp", None),
        P("fsdp", None),
        P("fsdp", None),
        P("fsdp"),
        P("fsdp", None),
        P("fsdp", None),
        P("fsdp", "dp", None),
    )
    return jax.shard_map(
        choose(mesh),
        mesh=mesh,
        in_specs=placed,
        out_specs=(
            P("fsdp", "dp", None),
            P("fsdp", "dp", None),
            P("fsdp", "dp", None),
            P("fsdp"),
            P("fsdp", None),
            P("fsdp", None),
            P("fsdp"),
            P("fsdp", None),
            P("fsdp", None),
            P("fsdp", None),
            P("fsdp"),
            P("fsdp", None),
            P("fsdp", None),
        ),
        check_vma=False,
    )
```

```python
from functools import partial

import jax
import jax.numpy as jnp
from jax import lax
from jax.experimental import pallas as pl
from jax.experimental.pallas import tpu as pltpu
from jax.sharding import PartitionSpec as P

D = 768
HEADS = 12
HEAD_DIM = 64
SUFFIX = 32
PATCH_S = 196
PATCH_L = 576
SLOT_S = 228
SLOT_L = 608
RING = 4
SIDE = 2
CORES = 2
norm_eps = 1e-06
MESH = pl.DeviceIdType.MESH
F32 = jnp.float32
BF16 = jnp.bfloat16
NONE = -1e30


def mm(left, right):
    return jnp.dot(left, right, preferred_element_type=F32)


def mm_nt(left, right):
    return lax.dot_general(left, right, (((1,), (1,)), ((), ())), preferred_element_type=F32)


def mm_tn(left, right):
    return lax.dot_general(left, right, (((0,), (0,)), ((), ())), preferred_element_type=F32)


def normed(value):
    mean = jnp.mean(value, axis=-1, keepdims=True)
    centred = value - mean
    variance = jnp.mean(centred * centred, axis=-1, keepdims=True)
    scale = lax.rsqrt(variance + norm_eps)
    return centred * scale, scale


def norm_back(grad, hat, scale, gain):
    inner = grad * gain
    mean_one = jnp.mean(inner, axis=-1, keepdims=True)
    mean_two = jnp.mean(inner * hat, axis=-1, keepdims=True)
    gain_grad = jnp.sum(grad * hat, axis=0, keepdims=True)
    return scale * (inner - mean_one - hat * mean_two), gain_grad


def gelu_parts(up):
    inner = 0.7978845608 * (up + 0.044715 * up * up * up)
    tanh = jnp.tanh(inner)
    slope = 0.7978845608 * (1.0 + 3.0 * 0.044715 * up * up)
    value = 0.5 * up * (1.0 + tanh)
    grad = 0.5 * (1.0 + tanh) + 0.5 * up * (1.0 - tanh * tanh) * slope
    return value, grad


class Gather:
    def __init__(self, place, view, bulk, sems, at, has=None, plane=None):
        self.z, self.x, self.c, self.f = place
        self.plane = plane
        self.view, self.bulk = view, bulk
        self.send, self.recv = sems
        self.at = at
        self.has = has
        self.sent = []

    def place_at(self, k):
        return lax.rem(self.z + k + RING, RING)

    def copy(self, ref, target, into, index):
        z, x, c = target
        return pltpu.make_async_remote_copy(
            src_ref=ref,
            dst_ref=ref,
            send_sem=self.send.at[self.at, index],
            recv_sem=self.recv.at[self.at, into],
            device_id=(z * (SIDE * CORES) + x * CORES + c, self.f),
            device_id_type=MESH,
        )

    def holds(self, block, cond):
        return cond if self.has is None else cond & self.has(*block)

    def go(self, block, target, into, cond):
        item = self.copy(self.view(*block), target, into, len(self.sent))
        cond = self.holds(block, cond)
        pl.when(cond)(item.start)
        self.sent.append((cond, item))

    def wait(self, block, into, cond):
        item = self.copy(self.view(*block), (self.z, 1 - self.x, self.c), into, 0)
        pl.when(self.holds(block, cond))(item.wait_recv)

    def line(self, block, up, down, cond):
        z, x, c = self.z, self.x, self.c
        if up:
            self.go(block, (self.place_at(1), x, c), block[0], cond & (z < RING - 1))
        if down:
            self.go(block, (self.place_at(-1), x, c), block[0], cond & (z > 0))

    def across(self, block, cond):
        self.go(block, (self.z, 1 - self.x, self.c), RING + block[0], cond)

    def step_one(self):
        own = (self.z, self.x, self.c)
        self.line(own, True, True, self.z >= 0)
        self.across(own, self.z >= 0)

    def arrive(self, k):
        low, high = (self.place_at(-k), self.x, self.c), (self.place_at(k), self.x, self.c)
        self.wait(low, low[0], self.z >= k)
        self.line(low, True, False, self.z >= k)
        self.wait(high, high[0], self.z < RING - k)
        self.line(high, False, True, self.z < RING - k)
        self.across(low, self.z >= k)
        self.across(high, self.z < RING - k)

    def side(self, k):
        for at, cond in ((self.place_at(-k), self.z >= k), (self.place_at(k), self.z < RING - k))[: 1 if k == 0 else 2]:
            self.wait((at, 1 - self.x, self.c), RING + at, cond)

    def step_two(self):
        self.arrive(1)

    def step_three(self):
        self.arrive(2)
        self.side(0)
        self.side(1)

    def step_four(self):
        self.arrive(3)
        self.side(2)

    def step_five(self):
        self.side(3)
        self.hand_over()

    def hand_over(self):
        item = self.copy(self.bulk(self.c), (self.z, self.x, 1 - self.c), 2 * RING, len(self.sent))
        mine = self.c >= 0 if self.plane is None else self.c == self.plane
        pl.when(mine)(item.start)
        self.sent.append((mine, item))

    def step_six(self):
        theirs = self.c >= 0 if self.plane is None else self.c != self.plane
        item = self.copy(self.bulk(1 - self.c), (self.z, self.x, 1 - self.c), 2 * RING, 0)
        pl.when(theirs)(item.wait_recv)

    def finish(self):
        for cond, item in self.sent:
            pl.when(cond)(item.wait_send)


class ShortGather(Gather):
    def step_one(self):
        own = (self.z, self.x, self.c)
        for k in range(1, RING):
            self.go(own, (self.place_at(k), self.x, self.c), self.z, self.z >= 0)
        self.across(own, self.z >= 0)

    def step_two(self):
        for k in range(1, RING):
            block = (self.place_at(k), self.x, self.c)
            self.wait(block, block[0], self.z >= 0)
            self.across(block, self.z >= 0)

    def step_three(self):
        for k in range(RING):
            at = self.place_at(k)
            self.wait((at, 1 - self.x, self.c), RING + at, self.z >= 0)
        self.hand_over()


class Spread(Gather):
    def __init__(self, place, theirs, mine, bulk, sems, at):
        super().__init__(place, theirs, bulk, sems, at)
        self.mine = mine
        z, x, c = self.z, self.x, self.c
        always, end = z >= 0, (z == 0) | (z == RING - 1)
        self.opposite = RING - 1 - z
        self.over = (
            ((z, x, c), None, always),
            ((z, 1 - x, c), None, always),
            ((self.opposite, x, c), 1, end),
            ((self.opposite, 1 - x, c), 1, end),
        )
        self.pushed = []

    def over_copy(self, n, view):
        block, part, cond = self.over[n]
        ref = view(*block, part)
        return pltpu.make_async_remote_copy(
            src_ref=ref, dst_ref=ref, send_sem=self.send.at[self.at, 15 + n], recv_sem=self.recv.at[self.at, 9 + n],
            device_id=(self.z * (SIDE * CORES) + self.x * CORES + self.c, 1 - self.f), device_id_type=MESH,
        )

    def push(self):
        for n in range(4):
            item, cond = self.over_copy(n, self.mine), self.over[n][2]
            pl.when(cond)(item.start)
            self.pushed.append((cond, item))

    def landed(self, n):
        pl.when(self.over[n][2])(self.over_copy(n, self.view).wait_recv)

    def step_one(self):
        always = self.z >= 0
        own = (self.z, self.x, self.c)
        self.landed(0)
        self.line(own, True, True, always)

    def step_three(self):
        z, x, c = self.z, self.x, self.c
        low, high = (self.place_at(-2), x, c), (self.place_at(2), x, c)
        self.wait(low, low[0], z >= 2)
        self.go((*low, 0), (self.place_at(1), x, c), low[0], z == RING - 2)
        self.wait(high, high[0], z < RING - 2)
        self.go((*high, 0), (self.place_at(-1), x, c), high[0], z == 1)
        self.across(low, z >= 2)
        self.across(high, z < RING - 2)
        self.side(1)

    def step_four(self):
        z, x, c = self.z, self.x, self.c
        end = (z == 0) | (z == RING - 1)
        block = (self.opposite, x, c, 0)
        self.wait(block, self.opposite, end)
        self.across(block, end)
        self.side(2)

    def step_five(self):
        z, x, c = self.z, self.x, self.c
        self.landed(1)
        self.landed(2)
        self.landed(3)
        self.wait((self.opposite, 1 - x, c, 0), RING + self.opposite, (z == 0) | (z == RING - 1))
        self.hand_over()

    def finish(self):
        super().finish()
        for cond, item in self.pushed:
            pl.when(cond)(item.wait_send)


class Pieces:
    def __init__(self, count, own_rows):
        self.half = count // 2
        self.edge = self.half * SLOT_S
        self.rows = own_rows
        self.count = count

    def start(self, rank):
        return jnp.where(
            rank < self.half, SLOT_S * rank, self.edge + SLOT_L * (rank - self.half)
        )

    def size(self, rank):
        return jnp.where(rank < self.half, SLOT_S, SLOT_L)

    def rank_of(self, row):
        return jnp.where(
            row < self.edge,
            lax.div(row, SLOT_S),
            self.half + lax.div(jnp.maximum(row - self.edge, 0), SLOT_L),
        )

    def first_rank(self, device):
        return self.rank_of(device * self.rows)

    def last_rank(self, device):
        return self.rank_of(device * self.rows + self.rows - 1)

    def first_device(self, rank):
        return lax.div(self.start(rank), self.rows)

    def last_device(self, rank):
        return lax.div(self.start(rank) + self.size(rank) - 1, self.rows)


SLOTS = 3
UNITS = 16
LANE_QKV, LANE_SO, LANE_CQ, LANE_CKV, LANE_CO, LANE_FI, LANE_FO = 0, 2304, 3072, 3840, 5376, 6144, 9216
OUT_CO, OUT_CKV = 3840, 4608
CHUNKS = ((0, 2304), (2304, 1536), (3840, 1536), (5376, 3072), (8448, 2304), (10752, 1536))
LOADS_BY_CHUNK = ((0,), (1, 2), (3,), (4, 5), (6, 7), (8, 9))
PIECE = 384
UNIT_CHIPS = 6


def layer_kernel(
    ranks,
    columns,
    x_ref, cot_ref, mem_ref, res_ref, pre_ref, gains_ref,
    qkv_ref, so_ref, cq_ref, ckv_ref, co_ref, fi_ref, fo_ref,
    out_ref, grad_ref, memgrad_ref, gain_out_ref, weights_out_ref,
    wb, gb, rl, rr, lb, sb, xb, cb, nb, olr, ob, tb, pb, gainb, memp, kvb, kvg, kp, kr, kc, ky, cp,
    kx, ks, hb, ab, ug, usend_b, urecv_b,
    cqb, qbuf, osend, ostat_send, obuf, ostat, dob, dstat_b, dobuf, dstat, dqsend, dqbuf, gmine, gpeer,
    load_sem, wsend, wrecv, gsend, grecv, bsend, brecv, asend, arecv, fsend, frecv, ysend, yrecv, psend, precv, usend, urecv,
    ksend, krecv,
):
    me = lax.axis_index("dp")
    f = lax.axis_index("fsdp")
    z = lax.div(me, SIDE * CORES)
    x = lax.rem(lax.div(me, CORES), SIDE)
    c = lax.rem(me, CORES)
    chip = lax.div(me, CORES)
    chips = ranks // CORES
    place = (z, x, c, f)
    half_rows = D // columns
    slab = half_rows // chips
    own_rows = mem_ref.shape[0]
    padded = memp.shape[0]
    lay = Pieces(ranks, own_rows)
    other = 1 - f
    mate = (z * (SIDE * CORES) + x * CORES + (1 - c), f)
    everyone = ranks * columns
    lin = f * ranks + me

    loads = []

    def load(src, lane, width):
        item = pltpu.make_async_copy(
            src, wb.at[pl.ds(pl.multiple_of(f * half_rows, 128), half_rows), pl.ds(lane, width)],
            load_sem.at[len(loads)],
        )
        item.start()
        loads.append(item)

    load(qkv_ref, LANE_QKV, 3 * D)
    load(so_ref, LANE_SO, D)
    load(cq_ref, LANE_CQ, D)
    load(ckv_ref, LANE_CKV, 2 * D)
    load(co_ref, LANE_CO, D)
    load(fi_ref, LANE_FI, 4 * D)
    for j in range(4):
        load(fo_ref.at[pl.ds(j * half_rows, half_rows)], LANE_FO + D * j, D)

    for s in range(SLOTS):
        qbuf[s] = jnp.zeros_like(qbuf[s])
        obuf[s] = jnp.zeros_like(obuf[s])
        ostat[s, 0] = jnp.full_like(ostat[s, 0], NONE)
        ostat[s, 1] = jnp.zeros_like(ostat[s, 1])
        dobuf[s] = jnp.zeros_like(dobuf[s])
        dstat[s] = jnp.zeros_like(dstat[s])
        dqbuf[s] = jnp.zeros_like(dqbuf[s])

    def rows_of(device):
        return pl.ds(pl.multiple_of(device * SUFFIX, SUFFIX), SUFFIX)

    def slot_of(device):
        return lax.rem(device, CORES) * chips + lax.div(device, CORES)

    my_slot = slot_of(me)
    xb[my_slot] = x_ref[...]
    cb[my_slot] = cot_ref[...].astype(BF16)
    pb[my_slot] = jnp.full((8, 128), pre_ref[0, 0].astype(F32), F32)
    gainb[f] = gains_ref[...]

    barrier = pltpu.get_barrier_semaphore()

    def greet(i, carry):
        to = lax.rem(me + i, ranks)
        pl.semaphore_signal(barrier, inc=1, device_id=(to, f), device_id_type=MESH)
        return carry

    lax.fori_loop(1, ranks, greet, 0)
    pl.semaphore_signal(barrier, inc=1, device_id=(me, other), device_id_type=MESH)
    pl.semaphore_wait(barrier, ranks)

    y_items = []

    def push_y(src, dst, at):
        item = pltpu.make_async_remote_copy(
            src_ref=src, dst_ref=dst, send_sem=ysend.at[at], recv_sem=yrecv.at[at],
            device_id=(me, other), device_id_type=MESH,
        )
        item.start()
        y_items.append(item)
        return item

    class Tell:
        def __init__(self, ref, at):
            self.ref, self.at = ref, at

        def copy(self, source, index, to):
            return pltpu.make_async_remote_copy(
                src_ref=self.ref.at[slot_of(source)], dst_ref=self.ref.at[slot_of(source)], send_sem=bsend.at[self.at, index],
                recv_sem=brecv.at[self.at, source], device_id=(to, f), device_id_type=MESH,
            )

        def start(self):
            def one(i, carry):
                self.copy(me, i, lax.rem(me + i, ranks)).start()
                return carry

            lax.fori_loop(1, ranks, one, 0)

        def wait(self):
            def one(i, carry):
                source = lax.rem(me + i, ranks)
                self.copy(source, i, source).wait_recv()
                return carry

            lax.fori_loop(1, ranks, one, 0)

        def finish(self):
            def one(i, carry):
                self.copy(me, i, lax.rem(me + i, ranks)).wait_send()
                return carry

            lax.fori_loop(1, ranks, one, 0)

    def slab_view(first, width, rows_from):
        half = width // CORES

        cut = (half // 256) * 128

        def view(zz, xx, cc, part=None):
            low, size = {None: (0, half), 0: (0, half - cut), 1: (half - cut, cut)}[part]
            row = pl.multiple_of(rows_from * half_rows + (zz * SIDE + xx) * slab, 16)
            lane = pl.multiple_of(first + cc * half + low, 128)
            return wb.at[pl.ds(row, slab), pl.ds(lane, size)]

        return view

    def block_view(ref):
        def view(zz, xx, cc):
            return ref.at[cc * chips + zz * SIDE + xx]

        return view

    def block_bulk(ref):
        return lambda cc: ref.at[pl.ds(cc * chips, chips)]

    def token_rows(col, cc, at):
        return pl.ds(pl.multiple_of(((col * CORES + cc) * chips + at) * SUFFIX, SUFFIX), SUFFIX)

    def token_view(ref):
        def view(zz, xx, cc):
            return ref.at[token_rows(f, cc, zz * SIDE + xx)]

        return view

    def token_bulk(ref):
        rows = chips * SUFFIX
        return lambda cc: ref.at[pl.ds(pl.multiple_of((f * CORES + cc) * rows, rows), rows)]

    def chunk_bulk(first, width):
        half = width // CORES
        rows = pl.ds(pl.multiple_of(other * half_rows, 128), half_rows)
        return lambda cc: wb.at[rows, pl.ds(pl.multiple_of(first + cc * half, 128), half)]

    plane = pl.ds(pl.multiple_of((f * CORES + c) * chips * SUFFIX, SUFFIX), chips * SUFFIX)
    plane_in = pl.ds(pl.multiple_of((other * CORES + c) * chips * SUFFIX, SUFFIX), chips * SUFFIX)
    plane_mate = pl.ds(pl.multiple_of((other * CORES + 1 - c) * chips * SUFFIX, SUFFIX), chips * SUFFIX)

    class Across:
        def __init__(self, ref, at):
            self.ref, self.at = ref, at

        def copy(self, rows, n, to):
            ref = self.ref.at[rows]
            return pltpu.make_async_remote_copy(
                src_ref=ref, dst_ref=ref, send_sem=asend.at[self.at, n], recv_sem=arecv.at[self.at, n],
                device_id=to, device_id_type=MESH,
            )

        def start(self):
            self.copy(plane, 0, (me, other)).start()

        def relay(self):
            self.copy(plane_in, 0, (me, other)).wait_recv()
            self.copy(plane_in, 1, mate).start()

        def wait(self):
            self.copy(plane_mate, 1, mate).wait_recv()

        def finish(self):
            self.copy(plane, 0, (me, other)).wait_send()
            self.copy(plane_in, 1, mate).wait_send()

    sems = (gsend, grecv)
    ag_x = Gather(place, block_view(xb), block_bulk(xb), sems, 0)
    ag_c = Gather(place, block_view(cb), block_bulk(cb), sems, 1)
    ag_n = ShortGather(place, token_view(nb), token_bulk(nb), sems, 2)
    tell_p = Tell(pb, 0)
    spread = [
        Spread(place, slab_view(first, width, other), slab_view(first, width, f), chunk_bulk(first, width), (wsend, wrecv), n)
        for n, (first, width) in enumerate(CHUNKS)
    ]

    def push_chunk(n):
        for i in LOADS_BY_CHUNK[n]:
            loads[i].wait()
        spread[n].push()

    ag_x.step_one()
    push_chunk(0)
    gain_item = push_y(gainb.at[f], gainb.at[f], 0)
    tell_p.start()
    push_chunk(1)

    def tick(n):
        for age, act in ((4, "step_five"), (3, "step_four"), (2, "step_three"), (1, "step_two"), (0, "step_one")):
            if 0 <= n - age < len(spread):
                getattr(spread[n - age], act)()
        if n + 2 < len(spread):
            push_chunk(n + 2)

    ag_x.step_two()
    tick(0)
    ag_x.step_three()
    tick(1)
    ag_x.step_four()
    tick(2)
    ag_x.step_five()
    ag_x.step_six()
    tick(3)
    gain_item.wait_recv()

    memp[0:own_rows] = mem_ref[...]
    memp[own_rows:padded] = jnp.zeros((padded - own_rows, D), BF16)

    positions = []
    before_large = jnp.int32(0)
    mine_rank = jnp.int32(0)
    for i in range(ranks):
        group = res_ref[0, i]
        spot = jnp.where(group == 1, lay.half + before_large, i - before_large)
        positions.append(spot)
        mine_rank = jnp.where(me == i, spot, mine_rank)
        before_large = before_large + group

    slots = [(i % CORES) * chips + i // CORES for i in range(ranks)]

    def example_of(rank):
        found = jnp.int32(0)
        for i in range(ranks):
            found = jnp.where(positions[i] == rank, slots[i], found)
        return found

    by_rank = [example_of(r) for r in range(ranks)]
    out_slot = jnp.int32(0)
    for i in range(ranks):
        out_slot = jnp.where(mine_rank == i, slots[i], out_slot)

    tiles = half_rows // 128
    gain = [
        jnp.concatenate([gainb[i, tiles * n + j : tiles * n + j + 1] for i in range(columns) for j in range(tiles)], axis=1)
        for n in range(3)
    ]

    mine = example_of(me)
    resid = xb[mine]
    hat_one, rs_one = normed(resid)
    n1 = (hat_one * gain[0]).astype(BF16)

    lanes = lax.broadcasted_iota(jnp.int32, (1, 256), 1)
    head_f32 = [(lax.div(lanes, HEAD_DIM) == h).astype(F32) for h in range(4)]
    head_b16 = [m.astype(BF16) for m in head_f32]

    def stack(value):
        return jnp.concatenate([value * m for m in head_b16], axis=0)

    def unstack(value):
        rows = value.shape[0] // 4
        total = value[0:rows] * head_f32[0]
        for h in range(1, 4):
            total = total + value[h * rows : (h + 1) * rows] * head_f32[h]
        return total

    tick(4)
    ag_c.step_one()
    spread[0].step_six()
    q = mm(n1, wb[:, 0:D]).astype(BF16)
    k = mm(n1, wb[:, D : 2 * D]).astype(BF16)
    v = mm(n1, wb[:, 2 * D : 3 * D]).astype(BF16)
    scale = HEAD_DIM**-0.5
    qs = (q.astype(F32) * scale).astype(BF16)
    row_at = lax.broadcasted_iota(jnp.int32, (SUFFIX, SUFFIX), 0)
    col_at = lax.broadcasted_iota(jnp.int32, (SUFFIX, SUFFIX), 1)
    causal = jnp.concatenate([(row_at >= col_at).astype(F32)] * 4, axis=0) > 0.0
    self_p = []
    mixed = []
    for g in range(3):
        sl = slice(256 * g, 256 * g + 256)
        s = mm_nt(stack(qs[:, sl]), k[:, sl])
        s = jnp.where(causal, s, NONE)
        e = jnp.exp(s - jnp.max(s, axis=-1, keepdims=True))
        p = e / jnp.sum(e, axis=-1, keepdims=True)
        self_p.append(p)
        mixed.append(unstack(mm(p.astype(BF16), v[:, sl])))
    sm = jnp.concatenate(mixed, axis=1).astype(BF16)

    tick(5)
    ag_c.step_two()
    spread[1].step_six()
    after_self = resid + mm(sm, wb[:, LANE_SO : LANE_SO + D])
    hat_two, rs_two = normed(after_self)
    n2 = (hat_two * gain[1]).astype(BF16)
    cq = mm(n2, wb[:, LANE_CQ : LANE_CQ + D]).astype(BF16)
    cqb[...] = cq

    my_first, my_last = lay.first_device(me), lay.last_device(me)
    held_first, held_last = lay.first_rank(me), lay.last_rank(me)

    def piece_copy(src, dst, at, sent, landed, target):
        return pltpu.make_async_remote_copy(
            src_ref=src, dst_ref=dst, send_sem=psend.at[at, sent], recv_sem=precv.at[at, landed],
            device_id=(target, f), device_id_type=MESH,
        )

    def to_holders(pairs):
        for i in range(SLOTS):
            target = my_first + i
            slot = me - lay.first_rank(target)
            there = target <= my_last

            @pl.when(there & (target == me))
            def _():
                for src, dst, at in pairs:
                    dst[slot] = src[...]

            @pl.when(there & (target != me))
            def _():
                for src, dst, at in pairs:
                    piece_copy(src, dst.at[slot], at, i, slot, target).start()

    def to_holders_sent(pairs):
        for i in range(SLOTS):
            target = my_first + i

            @pl.when((target <= my_last) & (target != me))
            def _():
                for src, dst, at in pairs:
                    piece_copy(src, dst.at[0], at, i, 0, target).wait_send()

    def at_holders(pairs):
        for s in range(SLOTS):
            rank = held_first + s

            @pl.when((rank <= held_last) & (rank != me))
            def _():
                for src, dst, at in pairs:
                    piece_copy(src, dst.at[s], at, 0, s, rank).wait_recv()

    def to_owners(pairs):
        for s in range(SLOTS):
            rank = held_first + s
            index = me - lay.first_device(rank)
            there = rank <= held_last

            @pl.when(there & (rank == me))
            def _():
                for src, dst, at in pairs:
                    dst[index] = src[s]

            @pl.when(there & (rank != me))
            def _():
                for src, dst, at in pairs:
                    piece_copy(src.at[s], dst.at[index], at, s, index, rank).start()

    def to_owners_sent(pairs):
        for s in range(SLOTS):
            rank = held_first + s

            @pl.when((rank <= held_last) & (rank != me))
            def _():
                for src, dst, at in pairs:
                    piece_copy(src.at[s], dst.at[0], at, s, 0, rank).wait_send()

    def at_owners(pairs):
        for i in range(SLOTS):
            target = my_first + i

            @pl.when((target <= my_last) & (target != me))
            def _():
                for src, dst, at in pairs:
                    piece_copy(src.at[0], dst.at[i], at, 0, i, target).wait_recv()

    q_pairs = [(cqb, qbuf, 0)]
    o_pairs = [(osend, obuf, 1), (ostat_send, ostat, 2)]
    d_pairs = [(dob, dobuf, 3), (dstat_b, dstat, 4)]
    dq_pairs = [(dqsend, dqbuf, 5)]

    to_holders(q_pairs)

    tick(6)
    ag_c.step_three()
    spread[2].step_six()


    def kv_step(i, carry):
        lane = pl.multiple_of(i * 256, 256)
        kvb[:, pl.ds(lane, 256)] = mm(memp[...], wb[:, pl.ds(LANE_CKV + lane, 256)]).astype(BF16)
        return carry

    lax.fori_loop(0, 6, kv_step, 0)

    tell_p.wait()
    lane_f = lax.broadcasted_iota(jnp.int32, (SUFFIX, padded), 1).astype(F32)
    allowed = []
    for s in range(SLOTS):
        rank = held_first + s
        ok = rank <= held_last
        example = example_of(jnp.minimum(rank, ranks - 1))
        prefix = pb[example][0:1, 0:1]
        low = (lay.start(rank) - me * own_rows).astype(F32)
        patches = jnp.where(rank < lay.half, PATCH_S, PATCH_L).astype(F32)
        high = jnp.minimum(low + patches + prefix, jnp.float32(own_rows))
        high = jnp.where(ok, high, jnp.float32(-1.0))
        allowed.append(((lane_f >= low) & (lane_f < high)).astype(F32))
    allowed = jnp.concatenate(allowed * 4, axis=0) > 0.0

    at_holders(q_pairs)
    qh = jnp.concatenate([qbuf[s] for s in range(SLOTS)], axis=0)
    qh = (qh.astype(F32) * scale).astype(BF16)
    lane_c = lax.broadcasted_iota(jnp.int32, (SUFFIX, 128), 1)
    top_c = [jnp.zeros((SUFFIX, 128), F32) for _ in range(SLOTS)]
    sum_c = [jnp.zeros((SUFFIX, 128), F32) for _ in range(SLOTS)]
    for g in range(3):
        sl = slice(256 * g, 256 * g + 256)
        s = mm_nt(stack(qh[:, sl]), kvb[:, sl])
        s = jnp.where(allowed, s, NONE)
        top = jnp.max(s, axis=-1, keepdims=True)
        e = jnp.where(allowed, jnp.exp(s - top), 0.0)
        total = jnp.sum(e, axis=-1, keepdims=True)
        o = mm(e.astype(BF16), kvb[:, D + 256 * g : D + 256 * g + 256])
        o = o * jnp.where(total > 0.0, 1.0 / jnp.where(total > 0.0, total, 1.0), 0.0)
        o = unstack(o).astype(BF16)
        for n in range(SLOTS):
            osend[n, :, sl] = o[n * SUFFIX : (n + 1) * SUFFIX]
            for h in range(4):
                at = h * SLOTS * SUFFIX + n * SUFFIX
                hit = lane_c == 4 * g + h
                top_c[n] = jnp.where(hit, top[at : at + SUFFIX], top_c[n])
                sum_c[n] = jnp.where(hit, total[at : at + SUFFIX], sum_c[n])
    for n in range(SLOTS):
        ostat_send[n, 0] = top_c[n]
        ostat_send[n, 1] = sum_c[n]
    to_owners(o_pairs)

    tick(7)
    ag_c.step_four()
    at_owners(o_pairs)
    spread[3].step_six()

    def expand(compact):
        low = lane_c < HEAD_DIM
        return jnp.concatenate(
            [jnp.where(low, compact[:, 2 * t : 2 * t + 1], compact[:, 2 * t + 1 : 2 * t + 2]) for t in range(6)],
            axis=1,
        )

    tops = [ostat[i, 0] for i in range(SLOTS)]
    top_all = jnp.maximum(jnp.maximum(tops[0], tops[1]), tops[2])
    shares = [ostat[i, 1] * jnp.exp(tops[i] - top_all) for i in range(SLOTS)]
    whole = shares[0] + shares[1] + shares[2]
    whole = jnp.where(whole > 0.0, whole, 1.0)
    lse = top_all + jnp.log(whole)
    cross = jnp.zeros((SUFFIX, D), F32)
    for i in range(SLOTS):
        cross = cross + expand(shares[i] / whole) * obuf[i].astype(F32)
    cm = cross.astype(BF16)

    after_cross = after_self + mm(cm, wb[:, LANE_CO : LANE_CO + D])
    hat_three, rs_three = normed(after_cross)
    n3 = (hat_three * gain[2]).astype(BF16)
    nb[token_rows(f, c, chip)] = n3
    ag_n.step_one()

    tick(8)
    ag_c.step_five()
    tick(9)
    for n in (4, 5):
        spread[n].step_six()
    ag_c.step_six()
    for r in range(ranks):
        olr[token_rows(f, r % CORES, r // CORES)] = cb[by_rank[r]]
    across_o = Across(olr, 0)
    across_n = Across(nb, 1)
    across_o.start()

    unit_items = []

    def push_part(which, at, to, src, dst):
        @pl.when(me == to)
        def _():
            dst[...] = src[...]

        @pl.when(me != to)
        def _():
            pltpu.make_async_remote_copy(
                src_ref=src, dst_ref=dst, send_sem=usend.at[which, at],
                recv_sem=urecv.at[which, me], device_id=(to, f), device_id_type=MESH,
            ).start()

        unit_items.append((which, at, to, src, dst))

    def push_left(units, at, left):
        lb[at] = left
        for unit in units:
            for j in range(CORES):
                lanes = pl.ds(j * PIECE, PIECE)
                push_part(0, CORES * unit + j, CORES * (unit + 1) + j, lb.at[at, :, lanes], rl.at[rows_of(me), lanes])

    def push_right(unit, right):
        for j in range(CORES):
            sb[unit, j] = right[:, j * PIECE : (j + 1) * PIECE]
            push_part(1, CORES * unit + j, CORES * (unit + 1) + j, sb.at[unit, j], rr.at[rows_of(me)])

    out_low = cb[mine]
    cot = out_low.astype(F32)
    acts, up_grads = [], []
    hidden_grad = [mm_nt(out_low, wb[:, LANE_FO + D * j : LANE_FO + D * (j + 1)]) for j in range(4)]

    def by_hidden(j):
        parts = []
        for t in range(D // half_rows):
            at = D * j + t * half_rows
            col, unit = at // (4 * half_rows), (at % (4 * half_rows)) // half_rows
            parts.append(hidden_grad[unit][:, col * half_rows : (col + 1) * half_rows])
        return jnp.concatenate(parts, axis=1)

    n3_grad = jnp.zeros((SUFFIX, D), F32)
    for j in range(4):
        weight = wb[:, LANE_FI + D * j : LANE_FI + D * (j + 1)]
        value, slope = gelu_parts(mm(n3, weight))
        acts.append(value.astype(BF16))
        part = (by_hidden(j) * slope).astype(BF16)
        n3_grad = n3_grad + mm_nt(part, weight)
    act = jnp.concatenate(acts, axis=1)

    ag_n.step_two()
    part, ffn_gain_grad = norm_back(n3_grad, hat_three, rs_three, gain[2])
    cross_res = cot + part
    cross_low = cross_res.astype(BF16)
    d_mixed = mm_nt(cross_low, wb[:, LANE_CO : LANE_CO + D]).astype(BF16)
    dob[...] = d_mixed
    prod = d_mixed.astype(F32) * cross
    delta = jnp.zeros((SUFFIX, 128), F32)
    for t in range(6):
        tile = prod[:, 128 * t : 128 * (t + 1)]
        left = jnp.sum(jnp.where(lane_c < HEAD_DIM, tile, 0.0), axis=-1, keepdims=True)
        right = jnp.sum(jnp.where(lane_c < HEAD_DIM, 0.0, tile), axis=-1, keepdims=True)
        delta = jnp.where(lane_c == 2 * t, left, delta)
        delta = jnp.where(lane_c == 2 * t + 1, right, delta)
    dstat_b[0] = lse
    dstat_b[1] = delta
    to_holders(d_pairs)
    push_left((0, 1, 2), 0, n1)
    down = jnp.zeros((SUFFIX, D), F32)
    for j in range(4):
        lhs = jnp.concatenate(
            [act[:, i * 4 * half_rows + j * half_rows : i * 4 * half_rows + (j + 1) * half_rows] for i in range(columns)],
            axis=1,
        )
        down = down + mm(lhs, wb[:, LANE_FO + D * j : LANE_FO + D * (j + 1)])
    ob[0, my_slot] = (after_cross + down).astype(BF16)
    ag_out = ShortGather(place, block_view(ob.at[0]), block_bulk(ob.at[0]), sems, 4)
    ag_out.step_one()

    at_holders(d_pairs)

    push_left((4,), 2, n2)
    push_left((3,), 1, sm)
    doh = jnp.concatenate([dobuf[s] for s in range(SLOTS)], axis=0)
    for g in range(3):
        sl = slice(256 * g, 256 * g + 256)
        kg = kvb[:, sl]
        vg = kvb[:, D + 256 * g : D + 256 * g + 256]
        q4 = stack(qh[:, sl])
        do4 = stack(doh[:, sl])
        lse_col = jnp.concatenate([dstat[n, 0][:, 4 * g + h : 4 * g + h + 1] for h in range(4) for n in range(SLOTS)], axis=0)
        del_col = jnp.concatenate([dstat[n, 1][:, 4 * g + h : 4 * g + h + 1] for h in range(4) for n in range(SLOTS)], axis=0)
        s = mm_nt(q4, kg)
        p = jnp.where(allowed, jnp.exp(jnp.where(allowed, s - lse_col, 0.0)), 0.0)
        dp = mm_nt(do4, vg)
        ds = (p * (dp - del_col)).astype(BF16)
        kvg[:, D + 256 * g : D + 256 * g + 256] = mm_tn(p.astype(BF16), do4).astype(BF16)
        kvg[:, sl] = mm_tn(ds, q4).astype(BF16)
        dq = unstack(mm(ds, kg)) * scale
        for n in range(SLOTS):
            dqsend[n, :, sl] = dq[n * SUFFIX : (n + 1) * SUFFIX].astype(BF16)
    to_owners(dq_pairs)
    ag_n.step_three()
    across_n.start()
    def kp_step(i, carry):
        lane = pl.multiple_of(i * 256, 256)
        kp[:, pl.ds(lane, 256)] = mm_tn(memp[...], kvg[:, pl.ds(lane, 256)]).astype(BF16)
        return carry

    lax.fori_loop(0, 6, kp_step, 0)
    kr_item = pltpu.make_async_remote_copy(
        src_ref=kp.at[pl.ds(pl.multiple_of((1 - c) * half_rows, 128), half_rows)], dst_ref=kr,
        send_sem=ksend.at[2 * chips], recv_sem=krecv.at[chips], device_id=mate, device_id_type=MESH,
    )
    kr_item.start()

    across_o.relay()
    ag_out.step_two()
    at_owners(dq_pairs)
    push_left((5,), 3, cm)
    push_right(5, cross_low)
    kr_item.wait_recv()
    kc[...] = (
        kp[pl.ds(pl.multiple_of(c * half_rows, 128), half_rows)].astype(F32) + kr[...].astype(F32)
    ).astype(BF16)
    half_slabs = half_rows // SIDE

    def ky_copy(j):
        lanes = pl.ds(j * D, D)
        return pltpu.make_async_remote_copy(
            src_ref=kc.at[:, lanes], dst_ref=ky.at[:, lanes], send_sem=ksend.at[2 * chips + 1 + j],
            recv_sem=krecv.at[chips + 1 + j], device_id=(me, other), device_id_type=MESH,
        )

    def kx_copy(j):
        lanes = pl.ds(j * D, D)
        return pltpu.make_async_remote_copy(
            src_ref=kc.at[pl.ds(pl.multiple_of((1 - x) * half_slabs, 16), half_slabs), lanes], dst_ref=kx.at[:, lanes],
            send_sem=ksend.at[2 * chips + 3 + j], recv_sem=krecv.at[chips + 3 + j],
            device_id=(z * (SIDE * CORES) + (1 - x) * CORES + c, f), device_id_type=MESH,
        )

    @pl.when(c != f)
    def _():
        ky_copy(0).start()
        ky_copy(1).start()

    cqg = (dqbuf[0].astype(F32) + dqbuf[1].astype(F32) + dqbuf[2].astype(F32)).astype(BF16)
    n2_grad = mm_nt(cqg, wb[:, LANE_CQ : LANE_CQ + D])
    part, cross_gain_grad = norm_back(n2_grad, hat_two, rs_two, gain[1])
    self_res = cross_res + part
    self_low = self_res.astype(BF16)
    dmix = mm_nt(self_low, wb[:, LANE_SO : LANE_SO + D]).astype(BF16)
    dqs, dks, dvs = [], [], []
    for g in range(3):
        sl = slice(256 * g, 256 * g + 256)
        q4 = stack(qs[:, sl])
        do4 = stack(dmix[:, sl])
        p = self_p[g]
        dp = mm_nt(do4, v[:, sl])
        ds = (p * (dp - jnp.sum(p * dp, axis=-1, keepdims=True))).astype(BF16)
        dvs.append(mm_tn(p.astype(BF16), do4))
        dks.append(mm_tn(ds, q4))
        dqs.append(unstack(mm(ds, k[:, sl])) * scale)
    packed_grad = [jnp.concatenate(parts, axis=1).astype(BF16) for parts in (dqs, dks, dvs)]
    for j in range(3):
        push_right(j, packed_grad[j])
    push_right(4, cqg)
    push_right(3, self_low)

    n1_grad = jnp.zeros((SUFFIX, D), F32)
    for j in range(3):
        n1_grad = n1_grad + mm_nt(packed_grad[j], wb[:, D * j : D * (j + 1)])
    part, self_gain_grad = norm_back(n1_grad, hat_one, rs_one, gain[0])
    ob[1, my_slot] = (self_res + part).astype(BF16)
    ag_grad = ShortGather(place, block_view(ob.at[1]), block_bulk(ob.at[1]), sems, 6)
    gmine[...] = jnp.concatenate(
        [self_gain_grad, cross_gain_grad, ffn_gain_grad, jnp.zeros((5, D), F32)], axis=0
    )
    tb[my_slot] = gmine[...]
    tell_g = Tell(tb, 1)
    tell_g.start()
    ag_grad.step_one()
    ag_out.step_three()

    ag_n.step_six()
    across_n.relay()
    across_o.wait()
    across_n.wait()

    rows_step = 128
    hidden = [col * 4 * half_rows + D * c for col in range(columns)]

    def ffn_rows(first, last):
        def one(i, carry):
            at = pl.ds(pl.multiple_of(i * rows_step, rows_step), rows_step)
            for col in range(columns):
                lane = pl.multiple_of(LANE_FI + hidden[col], 128)
                value, slope = gelu_parts(mm(nb[at], wb[:, pl.ds(lane, D)]))

                @pl.when(f == col)
                def _():
                    ab[at] = value.astype(BF16)

                back = []
                for t in range(CORES):
                    lane_o = pl.multiple_of(LANE_FO + D * (2 * c + t), 128)
                    back.append(mm_nt(olr[at], wb[col * half_rows : (col + 1) * half_rows, pl.ds(lane_o, D)]))
                hb[col, at] = (jnp.concatenate(back, axis=1) * slope).astype(BF16)
            return carry

        lax.fori_loop(first, last, one, 0)

    own_lanes = pl.ds(pl.multiple_of(f * half_rows, 128), half_rows)

    def ffn_in_sum(col):
        lane = pl.multiple_of(LANE_FI + hidden[col], 128)
        for part in range(0, D, PIECE):
            total = mm_tn(nb[:, own_lanes], hb[col, :, part : part + PIECE])
            gb[:, pl.ds(lane + part, PIECE)] = total.astype(BF16)

    def ffn_out_sum(t):
        lane = pl.multiple_of(LANE_FO + D * (2 * c + t), 128)
        for part in range(0, D, PIECE):
            total = mm_tn(ab[:, t * half_rows : (t + 1) * half_rows], olr[:, part : part + PIECE])
            gb[:, pl.ds(lane + part, PIECE)] = total.astype(BF16)

    f_items = []

    def to_mate(lane, width):
        ref = gb.at[:, pl.ds(pl.multiple_of(lane, 128), width)]
        item = pltpu.make_async_remote_copy(
            src_ref=ref, dst_ref=ref, send_sem=fsend.at[len(f_items)], recv_sem=frecv.at[len(f_items)],
            device_id=mate, device_id_type=MESH,
        )
        item.start()
        f_items.append(item)

    has_unit = (chip >= 1) & (chip <= UNIT_CHIPS)

    def unit_lane(n, cc):
        return PIECE * (n - 1) + UNIT_CHIPS * PIECE * cc

    def unit_take(which, src, dst):
        def take(i, carry):
            @pl.when(i != me)
            def _():
                pltpu.make_async_remote_copy(
                    src_ref=src, dst_ref=dst(i), send_sem=usend.at[which, 0],
                    recv_sem=urecv.at[which, i], device_id=mate, device_id_type=MESH,
                ).wait_recv()

            return carry

        lax.fori_loop(0, ranks, take, 0)

    def left_lanes(core):
        return pl.ds(pl.multiple_of(core * PIECE, 128), PIECE)

    def left_copy(core):
        ref = rl.at[:, left_lanes(core)]
        return pltpu.make_async_remote_copy(
            src_ref=ref, dst_ref=ref, send_sem=ysend.at[1], recv_sem=yrecv.at[1], device_id=mate, device_id_type=MESH,
        )

    def unit_left(pred):
        @pl.when(pred)
        def _():
            unit_take(0, lb.at[0, :, pl.ds(0, PIECE)], lambda i: rl.at[rows_of(i), left_lanes(c)])
            left_copy(c).start()

    def unit_rows(n):
        return pl.ds(n * (half_rows // 2), half_rows // 2)

    def unit_copy(n):
        rows = unit_rows(n)
        return pltpu.make_async_remote_copy(
            src_ref=usend_b.at[rows], dst_ref=urecv_b.at[rows], send_sem=ysend.at[3 + n], recv_sem=yrecv.at[3 + n],
            device_id=(me, other), device_id_type=MESH,
        )

    def unit_sum(pred):
        @pl.when(pred)
        def _():
            unit_take(1, sb.at[0, 0], lambda i: rr.at[rows_of(i)])
            left_copy(1 - c).wait_recv()
            for col in range(columns):
                ug[col] = mm_tn(rl[:, col * half_rows : (col + 1) * half_rows], rr[...])
            usend_b[...] = ug[other].astype(BF16)
            for n in range(2):
                unit_copy(n).start()

    def unit_join(pred, n):
        @pl.when(pred)
        def _():
            unit_copy(n).wait_recv()
            rows = unit_rows(n)
            gb[rows, pl.ds(pl.multiple_of(unit_lane(chip, c), 128), PIECE)] = (
                ug[f, rows] + urecv_b[rows].astype(F32)
            ).astype(BF16)

    def has_block(zz, xx, cc):
        n = zz * SIDE + xx
        return (n >= 1) & (n <= UNIT_CHIPS)

    def unit_bulk(rows):
        width = UNIT_CHIPS * PIECE
        return lambda cc: gb.at[rows, pl.ds(pl.multiple_of(width * cc, 128), width)]

    def gb_view(lane_of, rows):
        def view(zz, xx, cc):
            return gb.at[rows, pl.ds(pl.multiple_of(lane_of(zz * SIDE + xx, cc), 128), PIECE)]

        return view

    class UnitGather:
        def __init__(self):
            parts = [unit_rows(n) for n in range(2)]
            self.gathers = [
                Gather(place, gb_view(unit_lane, rows), unit_bulk(rows), sems, at, has_block)
                for at, rows in zip((3, 7), parts)
            ]

        def step(self, name):
            for gather in self.gathers:
                getattr(gather, name)()

    ag_u = UnitGather()

    k_items = []

    def k_copy(t, j):
        return pltpu.make_async_remote_copy(
            src_ref=ks.at[pl.ds(t * slab, slab), pl.ds(j * D, D)], dst_ref=cp.at[z],
            send_sem=ksend.at[t * CORES + j], recv_sem=krecv.at[z],
            device_id=(t * (SIDE * CORES) + x * CORES + j, f), device_id_type=MESH,
        )

    def k_over_x(j):
        lanes = pl.ds(j * D, D)

        @pl.when(c == f)
        def _():
            ky_copy(j).wait_recv()
            kc[:, lanes] = (kc[:, lanes].astype(F32) + ky[:, lanes].astype(F32)).astype(BF16)
            kx_copy(j).start()

    def k_on_line(j):
        lanes = pl.ds(j * D, D)

        @pl.when(c == f)
        def _():
            kx_copy(j).wait_recv()
            ks[:, lanes] = (
                kc[pl.ds(pl.multiple_of(x * half_slabs, 16), half_slabs), lanes].astype(F32) + kx[:, lanes].astype(F32)
            ).astype(BF16)

        for t in range(RING):
            here = (z == t) & (c == j)

            @pl.when((c == f) & here)
            def _():
                cp[z] = ks[t * slab : (t + 1) * slab, j * D : (j + 1) * D]

            @pl.when((c == f) & jnp.logical_not(here))
            def _():
                k_copy(t, j).start()

            k_items.append((t, j, here))

    k_over_x(0)
    ffn_rows(0, 2)
    unit_left(has_unit)
    k_on_line(0)
    k_over_x(1)
    unit_sum(has_unit)
    ffn_rows(2, 4)
    k_on_line(1)
    unit_join(has_unit, 0)
    ag_u.gathers[0].step_one()
    ffn_rows(4, 5)
    unit_join(has_unit, 1)
    ag_u.gathers[1].step_one()
    ffn_rows(5, 6)

    def take_k(i, carry):
        @pl.when((i != z) | (c != f))
        def _():
            pltpu.make_async_remote_copy(
                src_ref=ks.at[pl.ds(0, slab), pl.ds(0, D)], dst_ref=cp.at[i], send_sem=ksend.at[0],
                recv_sem=krecv.at[i], device_id=mate, device_id_type=MESH,
            ).wait_recv()

        return carry

    lax.fori_loop(0, RING, take_k, 0)
    total = cp[0].astype(F32)
    for i in range(1, RING):
        total = total + cp[i].astype(F32)
    k_lane = pl.multiple_of(OUT_CKV + c * D, 128)
    gb[pl.ds(pl.multiple_of(x * half_slabs + z * slab, 16), slab), pl.ds(k_lane, D)] = total.astype(BF16)

    def kv_view(zz, xx, cc):
        row = pl.multiple_of(xx * half_slabs + zz * slab, 16)
        return gb.at[pl.ds(row, slab), pl.ds(pl.multiple_of(OUT_CKV + cc * D, 128), D)]

    ag_k = Gather(place, kv_view, lambda cc: gb.at[:, pl.ds(pl.multiple_of(OUT_CKV + cc * D, 128), D)], sems, 5)
    ag_k.step_one()

    def mg_step(i, carry):
        row = pl.multiple_of(i * 128, 128)
        memgrad_ref[pl.ds(row, 128)] = mm_nt(kvg[pl.ds(row, 128)], wb[:, LANE_CKV : LANE_CKV + 2 * D])
        return carry

    full = own_rows // 128
    lax.fori_loop(0, full, mg_step, 0)
    if own_rows % 128:
        tail = mm_nt(kvg[full * 128 : (full + 1) * 128], wb[:, LANE_CKV : LANE_CKV + 2 * D])
        memgrad_ref[full * 128 : own_rows] = tail[0 : own_rows - full * 128]


    ag_u.step("step_two")
    ffn_rows(6, 8)
    ag_u.step("step_three")
    ag_k.step_two()
    ffn_in_sum(0)
    to_mate(LANE_FI + hidden[0], D)
    ag_grad.step_two()
    ag_k.step_three()
    ag_u.step("step_four")
    ffn_in_sum(1)
    to_mate(LANE_FI + hidden[1], D)
    ag_k.step_four()
    ag_grad.step_three()
    ag_out.step_six()
    ffn_out_sum(0)
    ffn_out_sum(1)
    to_mate(LANE_FO + CORES * D * c, CORES * D)
    ag_u.step("step_five")
    tell_g.wait()
    gmine[...] = tb[0]
    for i in range(1, ranks):
        gmine[...] += tb[i]
    g_item = push_y(gmine, gpeer, 2)
    for n, (lane, width) in enumerate(
        [(LANE_FI + col * 4 * half_rows + D * (1 - c), D) for col in range(columns)] + [(LANE_FO + CORES * D * (1 - c), CORES * D)]
    ):
        ref = gb.at[:, pl.ds(pl.multiple_of(lane, 128), width)]
        pltpu.make_async_remote_copy(
            src_ref=ref, dst_ref=ref, send_sem=fsend.at[n], recv_sem=frecv.at[n], device_id=mate, device_id_type=MESH,
        ).wait_recv()
    outs = []

    def write(lane, width):
        lanes = pl.ds(lane, width)
        item = pltpu.make_async_copy(gb.at[:, lanes], weights_out_ref.at[:, lanes], load_sem.at[len(outs)])
        item.start()
        outs.append(item)

    write(LANE_FI, 8 * D)
    ag_k.step_five()
    ag_grad.step_six()
    out_ref[...] = ob[0, out_slot].astype(F32)
    grad_ref[...] = ob[1, out_slot].astype(F32)
    g_item.wait_recv()
    gains_all = gmine[...] + gpeer[...]
    own_gain = gains_all[:, 0:half_rows]
    for i in range(1, columns):
        own_gain = jnp.where(f == i, gains_all[:, i * half_rows : (i + 1) * half_rows], own_gain)
    gain_out_ref[...] = own_gain
    ag_u.step("step_six")
    write(0, OUT_CKV)
    ag_k.step_six()
    write(OUT_CKV, 2 * D)

    to_holders_sent(q_pairs)
    to_owners_sent(o_pairs)
    to_holders_sent(d_pairs)
    to_owners_sent(dq_pairs)
    for which, at, to, src, dst in unit_items:
        @pl.when(me != to)
        def _():
            pltpu.make_async_remote_copy(
                src_ref=src, dst_ref=dst, send_sem=usend.at[which, at],
                recv_sem=urecv.at[which, 0], device_id=(to, f), device_id_type=MESH,
            ).wait_send()
    @pl.when(has_unit)
    def _():
        for n in range(2):
            unit_copy(n).wait_send()
        left_copy(c).wait_send()

    for t, j, here in k_items:
        @pl.when((c == f) & jnp.logical_not(here))
        def _():
            k_copy(t, j).wait_send()

    @pl.when(c == f)
    def _():
        kx_copy(0).wait_send()
        kx_copy(1).wait_send()

    across_o.finish()
    across_n.finish()
    for item in f_items:
        item.wait_send()
    kr_item.wait_send()

    @pl.when(c != f)
    def _():
        ky_copy(0).wait_send()
        ky_copy(1).wait_send()

    for item in y_items:
        item.wait_send()
    tell_p.finish()
    tell_g.finish()
    for item in [ag_x, *spread, ag_c, ag_n, *ag_u.gathers, ag_out, ag_grad, ag_k]:
        item.finish()
    for item in outs:
        item.wait()


def fused_body(
    ranks, columns,
    decoder_in, memory, res_group, prefix_len, self_gain, self_qkv, self_out, cross_gain, cross_query,
    cross_kv, cross_out, ffn_gain, ffn_in, ffn_out, cotangent,
):
    half_rows = D // columns
    chips = ranks // CORES
    slab = half_rows // chips
    own_rows = memory.shape[1]
    padded = -(-own_rows // 128) * 128
    tokens = ranks * SUFFIX
    gains = jnp.concatenate([self_gain, cross_gain, ffn_gain]).astype(F32)
    gains = jnp.pad(gains, (0, 16 * 128 - gains.shape[0])).reshape(16, 128)
    vm = pl.BlockSpec(memory_space=pltpu.VMEM)
    sm = pl.BlockSpec(memory_space=pltpu.SMEM)
    hbm = pl.BlockSpec(memory_space=pl.ANY)
    dma = pltpu.SemaphoreType.DMA
    scratch = [
        pltpu.VMEM((D, UNITS * D), BF16),
        pltpu.VMEM((half_rows, UNITS * D), BF16),
        pltpu.VMEM((tokens, D), BF16),
        pltpu.VMEM((tokens, PIECE), BF16),
        pltpu.VMEM((4, SUFFIX, D), BF16),
        pltpu.VMEM((UNIT_CHIPS, CORES, SUFFIX, PIECE), BF16),
        pltpu.VMEM((ranks, SUFFIX, D), F32),
        pltpu.VMEM((ranks, SUFFIX, D), BF16),
        pltpu.VMEM((columns * tokens, D), BF16),
        pltpu.VMEM((columns * tokens, D), BF16),
        pltpu.VMEM((2, ranks, SUFFIX, D), BF16),
        pltpu.VMEM((ranks, 8, D), F32),
        pltpu.VMEM((ranks, 8, 128), F32),
        pltpu.VMEM((columns, 16, 128), F32),
        pltpu.VMEM((padded, D), BF16),
        pltpu.VMEM((padded, 2 * D), BF16),
        pltpu.VMEM((padded, 2 * D), BF16),
        pltpu.VMEM((D, 2 * D), BF16),
        pltpu.VMEM((half_rows, 2 * D), BF16),
        pltpu.VMEM((half_rows, 2 * D), BF16),
        pltpu.VMEM((half_rows, 2 * D), BF16),
        pltpu.VMEM((RING, slab, D), BF16),
        pltpu.VMEM((half_rows // SIDE, 2 * D), BF16),
        pltpu.VMEM((half_rows // SIDE, 2 * D), BF16),
        pltpu.VMEM((columns, columns * tokens, D), BF16),
        pltpu.VMEM((columns * tokens, D), BF16),
        pltpu.VMEM((columns, half_rows, PIECE), F32),
        pltpu.VMEM((half_rows, PIECE), BF16),
        pltpu.VMEM((half_rows, PIECE), BF16),
        pltpu.VMEM((SUFFIX, D), BF16),
        pltpu.VMEM((SLOTS, SUFFIX, D), BF16),
        pltpu.VMEM((SLOTS, SUFFIX, D), BF16),
        pltpu.VMEM((SLOTS, 2, SUFFIX, 128), F32),
        pltpu.VMEM((SLOTS, SUFFIX, D), BF16),
        pltpu.VMEM((SLOTS, 2, SUFFIX, 128), F32),
        pltpu.VMEM((SUFFIX, D), BF16),
        pltpu.VMEM((2, SUFFIX, 128), F32),
        pltpu.VMEM((SLOTS, SUFFIX, D), BF16),
        pltpu.VMEM((SLOTS, 2, SUFFIX, 128), F32),
        pltpu.VMEM((SLOTS, SUFFIX, D), BF16),
        pltpu.VMEM((SLOTS, SUFFIX, D), BF16),
        pltpu.VMEM((8, D), F32),
        pltpu.VMEM((8, D), F32),
        dma((10,)),
        dma((len(CHUNKS), 19)),
        dma((len(CHUNKS), 13)),
        dma((8, 16)),
        dma((8, 9)),
        dma((2, ranks)),
        dma((2, ranks)),
        dma((2, 2)),
        dma((2, 2)),
        dma((3,)),
        dma((3,)),
        dma((5,)),
        dma((5,)),
        dma((6, SLOTS)),
        dma((6, SLOTS)),
        dma((2, CORES * UNIT_CHIPS)),
        dma((2, ranks)),
        dma((2 * chips + 5,)),
        dma((chips + 5,)),
    ]
    out, grad, memgrad, gain_grads, weight_grads = pl.pallas_call(
        partial(layer_kernel, ranks, columns),
        out_shape=(
            jax.ShapeDtypeStruct((SUFFIX, D), F32),
            jax.ShapeDtypeStruct((SUFFIX, D), F32),
            jax.ShapeDtypeStruct((own_rows, D), F32),
            jax.ShapeDtypeStruct((8, half_rows), F32),
            jax.ShapeDtypeStruct((half_rows, UNITS * D), BF16),
        ),
        in_specs=[vm, vm, vm, sm, sm, vm] + [hbm] * 7,
        out_specs=(vm, vm, vm, vm, hbm),
        scratch_shapes=scratch,
        compiler_params=pltpu.CompilerParams(
            collective_id=0, has_side_effects=True, vmem_limit_bytes=63 * 2**20
        ),
        name="layer",
    )(
        decoder_in[0], cotangent[0], memory[0], res_group, prefix_len, gains,
        self_qkv, self_out, cross_query, cross_kv, cross_out, ffn_in, ffn_out,
    )

    return unpack(half_rows, columns, weight_grads, memgrad, out, grad, gain_grads)


SPLIT = ((0, 3), (3, 1), (4, 1), (OUT_CKV, 2 * D), (5, 1), (LANE_FI, 4 * D))
WHOLE = (OUT_CKV, LANE_FI)


def unpack_kernel(w_ref, m_ref, o_ref, g_ref, *refs):
    *weights, ffn_out_ref, mem_ref, out_ref, grad_ref = refs
    for (low, width), ref in zip(SPLIT, weights):
        if low in WHOLE:
            ref[...] = w_ref[:, low : low + width].astype(F32)
            continue
        for n in range(width):
            for j in range(CORES):
                at = (UNIT_CHIPS * j + low + n) * PIECE
                to = (CORES * n + j) * PIECE
                ref[:, to : to + PIECE] = w_ref[:, at : at + PIECE].astype(F32)
    for j in range(4):
        ffn_out_ref[j] = w_ref[:, LANE_FO + D * j : LANE_FO + D * (j + 1)].astype(F32)
    mem_ref[:, 0, :] = m_ref[...]
    out_ref[...] = o_ref[...]
    grad_ref[...] = g_ref[...]


def unpack(half_rows, columns, weight_grads, memgrad, out, grad, gain_grads):
    steps = 2
    rows = half_rows // steps
    own_rows = memgrad.shape[0]
    mem_rows = -(-own_rows // (8 * steps)) * 8
    tokens = out.shape[0] // steps
    block = lambda height, width: pl.BlockSpec((height, width), lambda i: (i, 0))
    results = pl.pallas_call(
        unpack_kernel,
        grid=(steps,),
        out_shape=[jax.ShapeDtypeStruct((half_rows, width if low in WHOLE else width * D), F32) for low, width in SPLIT]
        + [
            jax.ShapeDtypeStruct((4, half_rows, D), F32),
            jax.ShapeDtypeStruct((own_rows, 1, D), F32),
            jax.ShapeDtypeStruct(out.shape, F32),
            jax.ShapeDtypeStruct(grad.shape, F32),
        ],
        in_specs=[block(rows, UNITS * D), block(mem_rows, D), block(tokens, D), block(tokens, D)],
        out_specs=[block(rows, width if low in WHOLE else width * D) for low, width in SPLIT]
        + [
            pl.BlockSpec((4, rows, D), lambda i: (0, i, 0)),
            pl.BlockSpec((mem_rows, 1, D), lambda i: (i, 0, 0)),
            block(tokens, D),
            block(tokens, D),
        ],
        compiler_params=pltpu.CompilerParams(vmem_limit_bytes=63 * 2**20),
        name="unpack",
    )(weight_grads, memgrad, out, grad)
    qkv, so, cq, ckv, co, fi, fo, mem, out, grad = results
    return (
        out[None], grad[None], mem.reshape(1, own_rows, D),
        gain_grads[0], qkv, so, gain_grads[1], cq, ckv, co, gain_grads[2], fi, fo.reshape(4 * half_rows, D),
    )


def layer_norm(value, gain):
    mean = jnp.mean(value, axis=-1, keepdims=True)
    centred = value - mean
    variance = jnp.mean(centred * centred, axis=-1, keepdims=True)
    return centred * lax.rsqrt(variance + norm_eps) * gain


def product(left, right):
    return jnp.dot(left, right, preferred_element_type=jnp.float32)


def outer_sum(left, right):
    flat_left = left.reshape(-1, left.shape[-1])
    flat_right = right.reshape(-1, right.shape[-1])
    return lax.dot_general(
        flat_left, flat_right, (((0,), (0,)), ((), ())), preferred_element_type=jnp.float32
    )


def back_product(grad, weight):
    return lax.dot_general(
        grad, weight, (((grad.ndim - 1,), (1,)), ((), ())), preferred_element_type=jnp.float32
    )


def attend(query, keys, values, allowed, scale):
    scores = jnp.einsum("eqhd,ekhd->ehqk", query, keys, preferred_element_type=jnp.float32) * scale
    scores = jnp.where(allowed[:, None], scores, -1e30)
    top = jnp.max(scores, axis=-1, keepdims=True)
    weights = jnp.exp(scores - top)
    probs = weights / jnp.sum(weights, axis=-1, keepdims=True)
    mixed = jnp.einsum(
        "ehqk,ekhd->eqhd", probs.astype(jnp.bfloat16), values, preferred_element_type=jnp.float32
    )
    return (mixed.astype(jnp.bfloat16), probs)


def attend_back(grad_mixed, query, keys, values, probs, scale):
    probs_low = probs.astype(jnp.bfloat16)
    grad_values = jnp.einsum(
        "ehqk,eqhd->ekhd", probs_low, grad_mixed, preferred_element_type=jnp.float32
    )
    grad_probs = jnp.einsum(
        "eqhd,ekhd->ehqk", grad_mixed, values, preferred_element_type=jnp.float32
    )
    grad_scores = probs * (grad_probs - jnp.sum(probs * grad_probs, axis=-1, keepdims=True))
    grad_low = grad_scores.astype(jnp.bfloat16)
    grad_query = (
        jnp.einsum("ehqk,ekhd->eqhd", grad_low, keys, preferred_element_type=jnp.float32) * scale
    )
    grad_keys = (
        jnp.einsum("ehqk,eqhd->ekhd", grad_low, query, preferred_element_type=jnp.float32) * scale
    )
    return (grad_query, grad_keys, grad_values)


def window_layout(res_group, mem_col):
    small = 1 - res_group
    small_count = jnp.sum(small, axis=-1, keepdims=True)
    small_before = jnp.cumsum(small, axis=-1) - small
    large_before = jnp.cumsum(res_group, axis=-1) - res_group
    offset = jnp.where(
        res_group == 1, SLOT_S * small_count + SLOT_L * large_before, SLOT_S * small_before
    )
    start = jnp.minimum(offset, mem_col - SLOT_L)
    return (offset, start)


def take_windows(column, starts):
    return jax.vmap(lambda begin: lax.dynamic_slice_in_dim(column, begin, SLOT_L, 0))(starts)


def forward(decoder_rows, windows, cross_allowed, weights):
    (
        self_gain,
        self_qkv,
        self_out,
        cross_gain,
        cross_query,
        cross_kv,
        cross_out,
        ffn_gain,
        ffn_in,
        ffn_out,
    ) = weights
    count = decoder_rows.shape[0] // SUFFIX
    scale = HEAD_DIM ** (-0.5)
    row_index = lax.broadcasted_iota(jnp.int32, (SUFFIX, SUFFIX), 0)
    col_index = lax.broadcasted_iota(jnp.int32, (SUFFIX, SUFFIX), 1)
    causal = (row_index >= col_index)[None]
    resid = decoder_rows.reshape(count, SUFFIX, D)
    normed_one = layer_norm(resid, self_gain.astype(jnp.float32)).astype(jnp.bfloat16)
    packed = product(normed_one, self_qkv).astype(jnp.bfloat16)
    heads = packed.reshape(count, SUFFIX, 3, HEADS, HEAD_DIM)
    self_mixed, self_probs = attend(heads[:, :, 0], heads[:, :, 1], heads[:, :, 2], causal, scale)
    self_mixed = self_mixed.reshape(count, SUFFIX, D)
    after_self = resid + product(self_mixed, self_out)
    normed_two = layer_norm(after_self, cross_gain.astype(jnp.float32)).astype(jnp.bfloat16)
    cross_q = product(normed_two, cross_query).astype(jnp.bfloat16)
    window_kv = product(windows, cross_kv).astype(jnp.bfloat16)
    query_heads = cross_q.reshape(count, SUFFIX, HEADS, HEAD_DIM)
    kv_heads = window_kv.reshape(count, SLOT_L, 2, HEADS, HEAD_DIM)
    cross_mixed, cross_probs = attend(
        query_heads, kv_heads[:, :, 0], kv_heads[:, :, 1], cross_allowed, scale
    )
    cross_mixed = cross_mixed.reshape(count, SUFFIX, D)
    after_cross = after_self + product(cross_mixed, cross_out)
    normed_three = layer_norm(after_cross, ffn_gain.astype(jnp.float32)).astype(jnp.bfloat16)
    up = product(normed_three, ffn_in)
    act = jax.nn.gelu(up, approximate=True).astype(jnp.bfloat16)
    result = after_cross + product(act, ffn_out)
    return (
        resid,
        normed_one,
        packed,
        self_probs,
        self_mixed,
        after_self,
        normed_two,
        cross_q,
        window_kv,
        cross_probs,
        cross_mixed,
        after_cross,
        normed_three,
        up,
        act,
        result,
    )


def backward(grad_out, saved, weights):
    (
        self_gain,
        self_qkv,
        self_out,
        cross_gain,
        cross_query,
        cross_kv,
        cross_out,
        ffn_gain,
        ffn_in,
        ffn_out,
    ) = weights
    (
        resid,
        normed_one,
        packed,
        self_probs,
        self_mixed,
        after_self,
        normed_two,
        cross_q,
        window_kv,
        cross_probs,
        cross_mixed,
        after_cross,
        normed_three,
        up,
        act,
        result,
    ) = saved
    count = resid.shape[0]
    scale = HEAD_DIM ** (-0.5)
    grad_out = grad_out.reshape(count, SUFFIX, D)
    out_low = grad_out.astype(jnp.bfloat16)
    ffn_out_grad = outer_sum(act, out_low)
    act_grad = back_product(out_low, ffn_out)
    gelu_value, gelu_back = jax.vjp(partial(jax.nn.gelu, approximate=True), up)
    up_grad = gelu_back(act_grad)[0].astype(jnp.bfloat16)
    ffn_in_grad = outer_sum(normed_three, up_grad)
    normed_three_grad = back_product(up_grad, ffn_in)
    norm_value, norm_back = jax.vjp(layer_norm, after_cross, ffn_gain.astype(jnp.float32))
    resid_part, ffn_gain_grad = norm_back(normed_three_grad)
    cross_res_grad = grad_out + resid_part
    cross_low = cross_res_grad.astype(jnp.bfloat16)
    cross_out_grad = outer_sum(cross_mixed, cross_low)
    mixed_grad = (
        back_product(cross_low, cross_out)
        .astype(jnp.bfloat16)
        .reshape(count, SUFFIX, HEADS, HEAD_DIM)
    )
    query_heads = cross_q.reshape(count, SUFFIX, HEADS, HEAD_DIM)
    kv_heads = window_kv.reshape(count, SLOT_L, 2, HEADS, HEAD_DIM)
    query_grad, keys_grad, values_grad = attend_back(
        mixed_grad, query_heads, kv_heads[:, :, 0], kv_heads[:, :, 1], cross_probs, scale
    )
    cross_q_grad = query_grad.reshape(count, SUFFIX, D).astype(jnp.bfloat16)
    window_kv_grad = (
        jnp.stack((keys_grad, values_grad), axis=2)
        .reshape(count, SLOT_L, 2 * D)
        .astype(jnp.bfloat16)
    )
    cross_query_grad = outer_sum(normed_two, cross_q_grad)
    normed_two_grad = back_product(cross_q_grad, cross_query)
    norm_value, norm_back = jax.vjp(layer_norm, after_self, cross_gain.astype(jnp.float32))
    resid_part, cross_gain_grad = norm_back(normed_two_grad)
    self_res_grad = cross_res_grad + resid_part
    self_low = self_res_grad.astype(jnp.bfloat16)
    self_out_grad = outer_sum(self_mixed, self_low)
    mixed_grad = (
        back_product(self_low, self_out)
        .astype(jnp.bfloat16)
        .reshape(count, SUFFIX, HEADS, HEAD_DIM)
    )
    heads = packed.reshape(count, SUFFIX, 3, HEADS, HEAD_DIM)
    query_grad, keys_grad, values_grad = attend_back(
        mixed_grad, heads[:, :, 0], heads[:, :, 1], heads[:, :, 2], self_probs, scale
    )
    packed_grad = (
        jnp.stack((query_grad, keys_grad, values_grad), axis=2)
        .reshape(count, SUFFIX, 3 * D)
        .astype(jnp.bfloat16)
    )
    self_qkv_grad = outer_sum(normed_one, packed_grad)
    normed_one_grad = back_product(packed_grad, self_qkv)
    norm_value, norm_back = jax.vjp(layer_norm, resid, self_gain.astype(jnp.float32))
    resid_part, self_gain_grad = norm_back(normed_one_grad)
    decoder_grad = self_res_grad + resid_part
    weight_grads = (
        self_gain_grad,
        self_qkv_grad,
        self_out_grad,
        cross_gain_grad,
        cross_query_grad,
        cross_out_grad,
        ffn_gain_grad,
        ffn_in_grad,
        ffn_out_grad,
    )
    return (decoder_grad, window_kv_grad, weight_grads)


def make_placer(all_starts, lowest, own_rows):

    def place(total, piece, begin):

        def add_one(item, acc):
            relative = all_starts[item] - lowest
            inside = ((relative > -SLOT_L) & (relative < own_rows)).astype(jnp.float32)
            spot = jnp.clip(relative + SLOT_L, 0, own_rows + SLOT_L)
            current = lax.dynamic_slice_in_dim(acc, spot, SLOT_L, 0)
            added = current + piece[item].astype(jnp.float32) * inside
            return lax.dynamic_update_slice_in_dim(acc, added, spot, 0)

        return lax.fori_loop(0, piece.shape[0], add_one, total)

    return place


def body(
    decoder_in,
    memory,
    res_group,
    prefix_len,
    self_gain,
    self_qkv,
    self_out,
    cross_gain,
    cross_query,
    cross_kv,
    cross_out,
    ffn_gain,
    ffn_in,
    ffn_out,
    cotangent,
):
    count = prefix_len.shape[1]
    own_rows = memory.shape[1]
    mem_col = own_rows * lax.axis_size("dp")
    offset, start = window_layout(res_group, mem_col)
    all_starts = start[0]
    first = lax.axis_index("dp") * count
    own_offset = lax.dynamic_slice_in_dim(offset[0], first, count)
    own_start = lax.dynamic_slice_in_dim(all_starts, first, count)
    own_group = lax.dynamic_slice_in_dim(res_group[0], first, count)
    valid = jnp.where(own_group == 1, PATCH_L, PATCH_S) + prefix_len[0]
    positions = own_start[:, None] + jnp.arange(SLOT_L, dtype=jnp.int32)[None]
    cross_allowed = (
        (positions >= own_offset[:, None]) & (positions < (own_offset + valid)[:, None])
    )[:, None]
    weights = (
        lax.all_gather(self_gain, "fsdp", axis=0, tiled=True),
        lax.all_gather(self_qkv, "fsdp", axis=0, tiled=True),
        lax.all_gather(self_out, "fsdp", axis=0, tiled=True),
        lax.all_gather(cross_gain, "fsdp", axis=0, tiled=True),
        lax.all_gather(cross_query, "fsdp", axis=0, tiled=True),
        lax.all_gather(cross_kv, "fsdp", axis=0, tiled=True),
        lax.all_gather(cross_out, "fsdp", axis=0, tiled=True),
        lax.all_gather(ffn_gain, "fsdp", axis=0, tiled=True),
        lax.all_gather(ffn_in, "fsdp", axis=0, tiled=True),
        lax.all_gather(ffn_out, "fsdp", axis=0, tiled=True),
    )
    column = lax.all_gather(memory[0], "dp", axis=0, tiled=True)
    windows = take_windows(column, own_start)
    saved = forward(decoder_in[0], windows, cross_allowed, weights)
    decoder_out = saved[-1]
    weights = (
        lax.all_gather(self_gain, "fsdp", axis=0, tiled=True),
        lax.all_gather(self_qkv, "fsdp", axis=0, tiled=True),
        lax.all_gather(self_out, "fsdp", axis=0, tiled=True),
        lax.all_gather(cross_gain, "fsdp", axis=0, tiled=True),
        lax.all_gather(cross_query, "fsdp", axis=0, tiled=True),
        lax.all_gather(cross_kv, "fsdp", axis=0, tiled=True),
        lax.all_gather(cross_out, "fsdp", axis=0, tiled=True),
        lax.all_gather(ffn_gain, "fsdp", axis=0, tiled=True),
        lax.all_gather(ffn_in, "fsdp", axis=0, tiled=True),
        lax.all_gather(ffn_out, "fsdp", axis=0, tiled=True),
    )
    column = lax.all_gather(memory[0], "dp", axis=0, tiled=True)
    windows = take_windows(column, own_start)
    saved = forward(decoder_in[0], windows, cross_allowed, weights)
    whole_kv = weights[5]
    decoder_grad, window_kv_grad, local_grads = backward(cotangent[0], saved, weights)
    lowest = lax.axis_index("dp") * own_rows
    place = make_placer(all_starts, lowest, own_rows)
    empty = jnp.zeros((own_rows + 2 * SLOT_L, 2 * D), jnp.float32)
    summed = place(empty, lax.all_gather(window_kv_grad, "dp", axis=0, tiled=True), jnp.int32(0))
    own_kv_grad = summed[SLOT_L : SLOT_L + own_rows].astype(jnp.bfloat16)
    memory_grad = back_product(own_kv_grad, whole_kv)
    cross_kv_part = outer_sum(memory[0], own_kv_grad)
    grads = (
        local_grads[0],
        local_grads[1],
        local_grads[2],
        local_grads[3],
        local_grads[4],
        cross_kv_part,
        local_grads[5],
        local_grads[6],
        local_grads[7],
        local_grads[8],
    )
    shards = (
        lax.psum_scatter(
            grads[0].astype(jnp.bfloat16), "fsdp", scatter_dimension=0, tiled=True
        ).astype(jnp.float32),
        lax.psum_scatter(
            grads[1].astype(jnp.bfloat16), "fsdp", scatter_dimension=0, tiled=True
        ).astype(jnp.float32),
        lax.psum_scatter(
            grads[2].astype(jnp.bfloat16), "fsdp", scatter_dimension=0, tiled=True
        ).astype(jnp.float32),
        lax.psum_scatter(
            grads[3].astype(jnp.bfloat16), "fsdp", scatter_dimension=0, tiled=True
        ).astype(jnp.float32),
        lax.psum_scatter(
            grads[4].astype(jnp.bfloat16), "fsdp", scatter_dimension=0, tiled=True
        ).astype(jnp.float32),
        lax.psum_scatter(
            grads[5].astype(jnp.bfloat16), "fsdp", scatter_dimension=0, tiled=True
        ).astype(jnp.float32),
        lax.psum_scatter(
            grads[6].astype(jnp.bfloat16), "fsdp", scatter_dimension=0, tiled=True
        ).astype(jnp.float32),
        lax.psum_scatter(
            grads[7].astype(jnp.bfloat16), "fsdp", scatter_dimension=0, tiled=True
        ).astype(jnp.float32),
        lax.psum_scatter(
            grads[8].astype(jnp.bfloat16), "fsdp", scatter_dimension=0, tiled=True
        ).astype(jnp.float32),
        lax.psum_scatter(
            grads[9].astype(jnp.bfloat16), "fsdp", scatter_dimension=0, tiled=True
        ).astype(jnp.float32),
    )
    totals = (
        lax.psum(shards[0].astype(jnp.bfloat16), "dp").astype(jnp.float32),
        lax.psum(shards[1].astype(jnp.bfloat16), "dp").astype(jnp.float32),
        lax.psum(shards[2].astype(jnp.bfloat16), "dp").astype(jnp.float32),
        lax.psum(shards[3].astype(jnp.bfloat16), "dp").astype(jnp.float32),
        lax.psum(shards[4].astype(jnp.bfloat16), "dp").astype(jnp.float32),
        lax.psum(shards[5].astype(jnp.bfloat16), "dp").astype(jnp.float32),
        lax.psum(shards[6].astype(jnp.bfloat16), "dp").astype(jnp.float32),
        lax.psum(shards[7].astype(jnp.bfloat16), "dp").astype(jnp.float32),
        lax.psum(shards[8].astype(jnp.bfloat16), "dp").astype(jnp.float32),
        lax.psum(shards[9].astype(jnp.bfloat16), "dp").astype(jnp.float32),
    )
    return (
        decoder_out,
        decoder_grad,
        memory_grad[None],
        totals[0],
        totals[1],
        totals[2],
        totals[3],
        totals[4],
        totals[5],
        totals[6],
        totals[7],
        totals[8],
        totals[9],
    )


def choose(mesh):
    ranks, columns = mesh.shape["dp"], mesh.shape["fsdp"]
    slabs = (D // columns) % (16 * (ranks // CORES)) == 0
    if slabs and columns == 2 and ranks == RING * SIDE * CORES:
        return partial(fused_body, ranks, columns)
    return body


def solution(mesh):
    placed = (
        P("fsdp", "dp", None),
        P("fsdp", "dp", None),
        P("fsdp", None),
        P("fsdp", "dp"),
        P("fsdp"),
        P("fsdp", None),
        P("fsdp", None),
        P("fsdp"),
        P("fsdp", None),
        P("fsdp", None),
        P("fsdp", None),
        P("fsdp"),
        P("fsdp", None),
        P("fsdp", None),
        P("fsdp", "dp", None),
    )
    return jax.shard_map(
        choose(mesh),
        mesh=mesh,
        in_specs=placed,
        out_specs=(
            P("fsdp", "dp", None),
            P("fsdp", "dp", None),
            P("fsdp", "dp", None),
            P("fsdp"),
            P("fsdp", None),
            P("fsdp", None),
            P("fsdp"),
            P("fsdp", None),
            P("fsdp", None),
            P("fsdp", None),
            P("fsdp"),
            P("fsdp", None),
            P("fsdp", None),
        ),
        check_vma=False,
    )
```

```python
from functools import partial

import jax
import jax.numpy as jnp
from jax import lax
from jax.experimental import pallas as pl
from jax.experimental.pallas import tpu as pltpu
from jax.sharding import PartitionSpec as P

D = 768
HEADS = 12
HEAD_DIM = 64
SUFFIX = 32
PATCH_S = 196
PATCH_L = 576
SLOT_S = 228
SLOT_L = 608
RING = 4
SIDE = 2
CORES = 2
norm_eps = 1e-06
MESH = pl.DeviceIdType.MESH
F32 = jnp.float32
BF16 = jnp.bfloat16
NONE = -1e30


def mm(left, right):
    return jnp.dot(left, right, preferred_element_type=F32)


def mm_nt(left, right):
    return lax.dot_general(left, right, (((1,), (1,)), ((), ())), preferred_element_type=F32)


def mm_tn(left, right):
    return lax.dot_general(left, right, (((0,), (0,)), ((), ())), preferred_element_type=F32)


def normed(value):
    mean = jnp.mean(value, axis=-1, keepdims=True)
    centred = value - mean
    variance = jnp.mean(centred * centred, axis=-1, keepdims=True)
    scale = lax.rsqrt(variance + norm_eps)
    return centred * scale, scale


def norm_back(grad, hat, scale, gain):
    inner = grad * gain
    mean_one = jnp.mean(inner, axis=-1, keepdims=True)
    mean_two = jnp.mean(inner * hat, axis=-1, keepdims=True)
    gain_grad = jnp.sum(grad * hat, axis=0, keepdims=True)
    return scale * (inner - mean_one - hat * mean_two), gain_grad


def gelu_parts(up):
    inner = 0.7978845608 * (up + 0.044715 * up * up * up)
    tanh = jnp.tanh(inner)
    slope = 0.7978845608 * (1.0 + 3.0 * 0.044715 * up * up)
    value = 0.5 * up * (1.0 + tanh)
    grad = 0.5 * (1.0 + tanh) + 0.5 * up * (1.0 - tanh * tanh) * slope
    return value, grad


class Gather:
    def __init__(self, place, view, bulk, sems, at, has=None):
        self.z, self.x, self.c, self.f = place
        self.view, self.bulk = view, bulk
        self.send, self.recv = sems
        self.at = at
        self.has = has
        self.sent = []

    def place_at(self, k):
        return lax.rem(self.z + k + RING, RING)

    def copy(self, ref, target, into, index):
        z, x, c = target
        return pltpu.make_async_remote_copy(
            src_ref=ref,
            dst_ref=ref,
            send_sem=self.send.at[self.at, index],
            recv_sem=self.recv.at[self.at, into],
            device_id=(z * (SIDE * CORES) + x * CORES + c, self.f),
            device_id_type=MESH,
        )

    def holds(self, block, cond):
        return cond if self.has is None else cond & self.has(*block)

    def go(self, block, target, into, cond):
        item = self.copy(self.view(*block), target, into, len(self.sent))
        cond = self.holds(block, cond)
        pl.when(cond)(item.start)
        self.sent.append((cond, item))

    def wait(self, block, into, cond):
        item = self.copy(self.view(*block), (self.z, 1 - self.x, self.c), into, 0)
        pl.when(self.holds(block, cond))(item.wait_recv)

    def line(self, block, up, down, cond):
        z, x, c = self.z, self.x, self.c
        if up:
            self.go(block, (self.place_at(1), x, c), block[0], cond & (z < RING - 1))
        if down:
            self.go(block, (self.place_at(-1), x, c), block[0], cond & (z > 0))

    def across(self, block, cond):
        self.go(block, (self.z, 1 - self.x, self.c), RING + block[0], cond)

    def step_one(self):
        own = (self.z, self.x, self.c)
        self.line(own, True, True, self.z >= 0)
        self.across(own, self.z >= 0)

    def arrive(self, k):
        low, high = (self.place_at(-k), self.x, self.c), (self.place_at(k), self.x, self.c)
        self.wait(low, low[0], self.z >= k)
        self.line(low, True, False, self.z >= k)
        self.wait(high, high[0], self.z < RING - k)
        self.line(high, False, True, self.z < RING - k)
        self.across(low, self.z >= k)
        self.across(high, self.z < RING - k)

    def side(self, k):
        for at, cond in ((self.place_at(-k), self.z >= k), (self.place_at(k), self.z < RING - k))[: 1 if k == 0 else 2]:
            self.wait((at, 1 - self.x, self.c), RING + at, cond)

    def step_two(self):
        self.arrive(1)

    def step_three(self):
        self.arrive(2)
        self.side(0)
        self.side(1)

    def step_four(self):
        self.arrive(3)
        self.hand_over(0)
        self.side(2)

    def step_five(self):
        self.side(3)
        self.hand_over(1)

    def hand_over(self, n):
        item = self.copy(self.bulk(self.c, self.x + n * (1 - 2 * self.x)), (self.z, self.x, 1 - self.c), 2 * RING + n, len(self.sent))
        item.start()
        self.sent.append((self.z >= 0, item))

    def step_six(self):
        for n in range(2):
            ref = self.bulk(1 - self.c, self.x + n * (1 - 2 * self.x))
            self.copy(ref, (self.z, self.x, 1 - self.c), 2 * RING + n, 0).wait_recv()

    def finish(self):
        for cond, item in self.sent:
            pl.when(cond)(item.wait_send)


class ShortGather(Gather):
    def step_one(self):
        own = (self.z, self.x, self.c)
        for k in range(1, RING):
            self.go(own, (self.place_at(k), self.x, self.c), self.z, self.z >= 0)
        self.across(own, self.z >= 0)

    def step_two(self):
        for k in range(1, RING):
            block = (self.place_at(k), self.x, self.c)
            self.wait(block, block[0], self.z >= 0)
            self.across(block, self.z >= 0)
        self.hand_over(0)

    def step_three(self):
        for k in range(RING):
            at = self.place_at(k)
            self.wait((at, 1 - self.x, self.c), RING + at, self.z >= 0)
        self.hand_over(1)


class Spread(Gather):
    def __init__(self, place, theirs, mine, bulk, sems, at):
        super().__init__(place, theirs, bulk, sems, at)
        self.mine = mine
        z, x, c = self.z, self.x, self.c
        always, end = z >= 0, (z == 0) | (z == RING - 1)
        self.opposite = RING - 1 - z
        self.over = (
            ((z, x, c), None, always),
            ((z, 1 - x, c), None, always),
            ((self.opposite, x, c), 1, end),
            ((self.opposite, 1 - x, c), 1, end),
        )
        self.pushed = []

    def over_copy(self, n, view):
        block, part, cond = self.over[n]
        ref = view(*block, part)
        return pltpu.make_async_remote_copy(
            src_ref=ref, dst_ref=ref, send_sem=self.send.at[self.at, 15 + n], recv_sem=self.recv.at[self.at, 10 + n],
            device_id=(self.z * (SIDE * CORES) + self.x * CORES + self.c, 1 - self.f), device_id_type=MESH,
        )

    def push(self):
        for n in range(4):
            item, cond = self.over_copy(n, self.mine), self.over[n][2]
            pl.when(cond)(item.start)
            self.pushed.append((cond, item))

    def landed(self, n):
        pl.when(self.over[n][2])(self.over_copy(n, self.view).wait_recv)

    def step_one(self):
        always = self.z >= 0
        own = (self.z, self.x, self.c)
        self.landed(0)
        self.line(own, True, True, always)

    def step_three(self):
        z, x, c = self.z, self.x, self.c
        low, high = (self.place_at(-2), x, c), (self.place_at(2), x, c)
        self.wait(low, low[0], z >= 2)
        self.go((*low, 0), (self.place_at(1), x, c), low[0], z == RING - 2)
        self.wait(high, high[0], z < RING - 2)
        self.go((*high, 0), (self.place_at(-1), x, c), high[0], z == 1)
        self.across(low, z >= 2)
        self.across(high, z < RING - 2)
        self.side(1)

    def step_four(self):
        z, x, c = self.z, self.x, self.c
        end = (z == 0) | (z == RING - 1)
        block = (self.opposite, x, c, 0)
        self.wait(block, self.opposite, end)
        self.across(block, end)
        self.landed(2)
        self.hand_over(0)
        self.side(2)

    def step_five(self):
        z, x, c = self.z, self.x, self.c
        self.landed(1)
        self.landed(3)
        self.wait((self.opposite, 1 - x, c, 0), RING + self.opposite, (z == 0) | (z == RING - 1))
        self.hand_over(1)

    def finish(self):
        super().finish()
        for cond, item in self.pushed:
            pl.when(cond)(item.wait_send)


class Pieces:
    def __init__(self, count, own_rows):
        self.half = count // 2
        self.edge = self.half * SLOT_S
        self.rows = own_rows
        self.count = count

    def start(self, rank):
        return jnp.where(
            rank < self.half, SLOT_S * rank, self.edge + SLOT_L * (rank - self.half)
        )

    def size(self, rank):
        return jnp.where(rank < self.half, SLOT_S, SLOT_L)

    def rank_of(self, row):
        return jnp.where(
            row < self.edge,
            lax.div(row, SLOT_S),
            self.half + lax.div(jnp.maximum(row - self.edge, 0), SLOT_L),
        )

    def first_rank(self, device):
        return self.rank_of(device * self.rows)

    def last_rank(self, device):
        return self.rank_of(device * self.rows + self.rows - 1)

    def first_device(self, rank):
        return lax.div(self.start(rank), self.rows)

    def last_device(self, rank):
        return lax.div(self.start(rank) + self.size(rank) - 1, self.rows)


SLOTS = 3
UNITS = 16
LANE_QKV, LANE_SO, LANE_CQ, LANE_CKV, LANE_CO, LANE_FI, LANE_FO = 0, 2304, 3072, 3840, 5376, 6144, 9216
OUT_CO, OUT_CKV = 3840, 4608
CHUNKS = ((0, 2304), (2304, 1536), (3840, 1536), (5376, 3072), (8448, 2304), (10752, 1536))
LOADS_BY_CHUNK = ((0,), (1, 2), (3,), (4, 5), (6, 7), (8, 9))
PIECE = 384
UNIT_CHIPS = 6


def layer_kernel(
    ranks,
    columns,
    x_ref, cot_ref, mem_ref, res_ref, pre_ref, gain_one_ref, gain_two_ref, gain_three_ref,
    qkv_ref, so_ref, cq_ref, ckv_ref, co_ref, fi_ref, fo_ref,
    out_ref, grad_ref, memgrad_ref, gain_out_ref, weights_out_ref,
    wb, gb, rl, rr, lb, sb, xb, cb, nb, olr, ob, pb, gainb, memp, kvb, kvg, kp, kr, kc, ky, cp,
    kx, ks, hb, ab, ug, usend_b, urecv_b,
    cqb, qbuf, osend, ostat_send, obuf, ostat, dob, dstat_b, dobuf, dstat, dqsend, dqbuf, gmine, gpeer,
    load_sem, wsend, wrecv, gsend, grecv, bsend, brecv, gain_sem, asend, arecv, fsend, frecv, ysend, yrecv, psend, precv, usend, urecv,
    ksend, krecv,
):
    me = lax.axis_index("dp")
    f = lax.axis_index("fsdp")
    z = lax.div(me, SIDE * CORES)
    x = lax.rem(lax.div(me, CORES), SIDE)
    c = lax.rem(me, CORES)
    seat = x * RING + z
    chips = ranks // CORES
    place = (z, x, c, f)
    half_rows = D // columns
    slab = half_rows // chips
    own_rows = mem_ref.shape[0]
    padded = memp.shape[0]
    lay = Pieces(ranks, own_rows)
    other = 1 - f
    mate = (z * (SIDE * CORES) + x * CORES + (1 - c), f)
    everyone = ranks * columns
    lin = f * ranks + me

    loads = []

    def load(src, lane, width):
        item = pltpu.make_async_copy(
            src, wb.at[pl.ds(pl.multiple_of(f * half_rows, 128), half_rows), pl.ds(lane, width)],
            load_sem.at[len(loads)],
        )
        item.start()
        loads.append(item)

    load(qkv_ref, LANE_QKV, 3 * D)
    load(so_ref, LANE_SO, D)
    load(cq_ref, LANE_CQ, D)
    load(ckv_ref, LANE_CKV, 2 * D)
    load(co_ref, LANE_CO, D)
    load(fi_ref, LANE_FI, 4 * D)
    for j in range(4):
        load(fo_ref.at[pl.ds(j * half_rows, half_rows)], LANE_FO + D * j, D)

    for s in range(SLOTS):
        qbuf[s] = jnp.zeros_like(qbuf[s])
        obuf[s] = jnp.zeros_like(obuf[s])
        ostat[s] = jnp.where(lax.broadcasted_iota(jnp.int32, ostat.shape[1:], 1) < 64, NONE, 0.0)
        dobuf[s] = jnp.zeros_like(dobuf[s])
        dstat[s] = jnp.zeros_like(dstat[s])
        dqbuf[s] = jnp.zeros_like(dqbuf[s])

    def rows_of(device):
        return pl.ds(pl.multiple_of(device * SUFFIX, SUFFIX), SUFFIX)

    def slot_of(device):
        side = lax.rem(lax.div(device, CORES), SIDE)
        return lax.rem(device, CORES) * chips + side * RING + lax.div(device, SIDE * CORES)

    my_slot = slot_of(me)
    xb[my_slot] = x_ref[...]
    cb[my_slot] = cot_ref[...].astype(BF16)
    pb[my_slot] = jnp.full((8, 128), pre_ref[0, 0].astype(F32), F32)
    for n, ref in enumerate((gain_one_ref, gain_two_ref, gain_three_ref)):
        values = ref[...].astype(F32).reshape(1, half_rows)
        for j in range(half_rows // 128):
            at = n * (half_rows // 128) + j
            gainb[f, at : at + 1] = values[:, 128 * j : 128 * (j + 1)]

    barrier = pltpu.get_barrier_semaphore()

    def greet(i, carry):
        to = lax.rem(me + i, ranks)
        pl.semaphore_signal(barrier, inc=1, device_id=(to, f), device_id_type=MESH)
        return carry

    lax.fori_loop(1, ranks, greet, 0)
    pl.semaphore_signal(barrier, inc=1, device_id=(me, other), device_id_type=MESH)
    pl.semaphore_wait(barrier, ranks)

    y_items = []

    def push_y(src, dst, at):
        item = pltpu.make_async_remote_copy(
            src_ref=src, dst_ref=dst, send_sem=ysend.at[at], recv_sem=yrecv.at[at],
            device_id=(me, other), device_id_type=MESH,
        )
        item.start()
        y_items.append(item)
        return item

    class Tell:
        def __init__(self, ref, at):
            self.ref, self.at = ref, at

        def copy(self, source, index, to):
            return pltpu.make_async_remote_copy(
                src_ref=self.ref.at[slot_of(source)], dst_ref=self.ref.at[slot_of(source)], send_sem=bsend.at[self.at, index],
                recv_sem=brecv.at[self.at, source], device_id=(to, f), device_id_type=MESH,
            )

        def start(self):
            def one(i, carry):
                self.copy(me, i, lax.rem(me + i, ranks)).start()
                return carry

            lax.fori_loop(1, ranks, one, 0)

        def wait(self):
            def one(i, carry):
                source = lax.rem(me + i, ranks)
                self.copy(source, i, source).wait_recv()
                return carry

            lax.fori_loop(1, ranks, one, 0)

        def finish(self):
            def one(i, carry):
                self.copy(me, i, lax.rem(me + i, ranks)).wait_send()
                return carry

            lax.fori_loop(1, ranks, one, 0)

    def slab_view(first, width, rows_from):
        half = width // CORES

        cut = (half // 256) * 128

        def view(zz, xx, cc, part=None):
            low, size = {None: (0, half), 0: (0, half - cut), 1: (half - cut, cut)}[part]
            row = pl.multiple_of(rows_from * half_rows + (xx * RING + zz) * slab, 16)
            lane = pl.multiple_of(first + cc * half + low, 128)
            return wb.at[pl.ds(row, slab), pl.ds(lane, size)]

        return view

    def block_view(ref):
        def view(zz, xx, cc):
            return ref.at[cc * chips + xx * RING + zz]

        return view

    def block_bulk(ref):
        return lambda cc, xx: ref.at[pl.ds(cc * chips + xx * RING, RING)]

    def token_rows(col, cc, at):
        return pl.ds(pl.multiple_of(((col * CORES + cc) * chips + at) * SUFFIX, SUFFIX), SUFFIX)

    def token_view(ref):
        def view(zz, xx, cc):
            return ref.at[token_rows(f, cc, xx * RING + zz)]

        return view

    def token_bulk(ref):
        rows = RING * SUFFIX
        return lambda cc, xx: ref.at[pl.ds(pl.multiple_of(((f * CORES + cc) * SIDE + xx) * rows, rows), rows)]

    def chunk_bulk(first, width):
        half = width // CORES
        rows = RING * slab

        def bulk(cc, xx):
            row = pl.multiple_of(other * half_rows + xx * rows, 16)
            return wb.at[pl.ds(row, rows), pl.ds(pl.multiple_of(first + cc * half, 128), half)]

        return bulk

    plane = pl.ds(pl.multiple_of((f * CORES + c) * chips * SUFFIX, SUFFIX), chips * SUFFIX)
    plane_in = pl.ds(pl.multiple_of((other * CORES + c) * chips * SUFFIX, SUFFIX), chips * SUFFIX)
    plane_mate = pl.ds(pl.multiple_of((other * CORES + 1 - c) * chips * SUFFIX, SUFFIX), chips * SUFFIX)

    class Across:
        def __init__(self, ref, at):
            self.ref, self.at = ref, at

        def copy(self, rows, n, to):
            ref = self.ref.at[rows]
            return pltpu.make_async_remote_copy(
                src_ref=ref, dst_ref=ref, send_sem=asend.at[self.at, n], recv_sem=arecv.at[self.at, n],
                device_id=to, device_id_type=MESH,
            )

        def start(self):
            self.copy(plane, 0, (me, other)).start()

        def relay(self):
            self.copy(plane_in, 0, (me, other)).wait_recv()
            self.copy(plane_in, 1, mate).start()

        def wait(self):
            self.copy(plane_mate, 1, mate).wait_recv()

        def finish(self):
            self.copy(plane, 0, (me, other)).wait_send()
            self.copy(plane_in, 1, mate).wait_send()

    sems = (gsend, grecv)
    ag_x = Gather(place, block_view(xb), block_bulk(xb), sems, 0)
    ag_c = Gather(place, block_view(cb), block_bulk(cb), sems, 1)
    ag_n = ShortGather(place, token_view(nb), token_bulk(nb), sems, 2)
    tell_p = Tell(pb, 0)
    spread = [
        Spread(place, slab_view(first, width, other), slab_view(first, width, f), chunk_bulk(first, width), (wsend, wrecv), n)
        for n, (first, width) in enumerate(CHUNKS)
    ]

    def push_chunk(n):
        for i in LOADS_BY_CHUNK[n]:
            loads[i].wait()
        spread[n].push()

    ag_x.step_one()
    push_chunk(0)
    gain_item = push_y(gainb.at[f], gainb.at[f], 0)
    tell_p.start()
    push_chunk(1)

    def tick(n):
        for age, act in ((4, "step_five"), (3, "step_four"), (2, "step_three"), (1, "step_two"), (0, "step_one")):
            if 0 <= n - age < len(spread):
                getattr(spread[n - age], act)()
        if n + 2 < len(spread):
            push_chunk(n + 2)

    ag_x.step_two()
    tick(0)
    ag_x.step_three()
    tick(1)
    ag_x.step_four()
    tick(2)
    ag_x.step_five()
    ag_x.step_six()
    tick(3)
    gain_item.wait_recv()

    memp[0:own_rows] = mem_ref[...]
    memp[own_rows:padded] = jnp.zeros((padded - own_rows, D), BF16)

    positions = []
    before_large = jnp.int32(0)
    mine_rank = jnp.int32(0)
    for i in range(ranks):
        group = res_ref[0, i]
        spot = jnp.where(group == 1, lay.half + before_large, i - before_large)
        positions.append(spot)
        mine_rank = jnp.where(me == i, spot, mine_rank)
        before_large = before_large + group

    spots = [i // CORES % SIDE * RING + i // (SIDE * CORES) for i in range(ranks)]
    slots = [(i % CORES) * chips + spots[i] for i in range(ranks)]

    def example_of(rank):
        found = jnp.int32(0)
        for i in range(ranks):
            found = jnp.where(positions[i] == rank, slots[i], found)
        return found

    by_rank = [example_of(r) for r in range(ranks)]
    out_slot = jnp.int32(0)
    for i in range(ranks):
        out_slot = jnp.where(mine_rank == i, slots[i], out_slot)

    tiles = half_rows // 128
    gain = [
        jnp.concatenate([gainb[i, tiles * n + j : tiles * n + j + 1] for i in range(columns) for j in range(tiles)], axis=1)
        for n in range(3)
    ]

    mine = example_of(me)
    resid = xb[mine]
    hat_one, rs_one = normed(resid)
    n1 = (hat_one * gain[0]).astype(BF16)

    lanes = lax.broadcasted_iota(jnp.int32, (1, 256), 1)
    head_f32 = [(lax.div(lanes, HEAD_DIM) == h).astype(F32) for h in range(4)]
    head_b16 = [m.astype(BF16) for m in head_f32]

    def stack(value):
        return jnp.concatenate([value * m for m in head_b16], axis=0)

    def unstack(value):
        rows = value.shape[0] // 4
        total = value[0:rows] * head_f32[0]
        for h in range(1, 4):
            total = total + value[h * rows : (h + 1) * rows] * head_f32[h]
        return total

    tick(4)
    ag_c.step_one()
    spread[0].step_six()
    q = mm(n1, wb[:, 0:D]).astype(BF16)
    k = mm(n1, wb[:, D : 2 * D]).astype(BF16)
    v = mm(n1, wb[:, 2 * D : 3 * D]).astype(BF16)
    scale = HEAD_DIM**-0.5
    qs = (q.astype(F32) * scale).astype(BF16)
    row_at = lax.broadcasted_iota(jnp.int32, (SUFFIX, SUFFIX), 0)
    col_at = lax.broadcasted_iota(jnp.int32, (SUFFIX, SUFFIX), 1)
    causal = jnp.concatenate([(row_at >= col_at).astype(F32)] * 4, axis=0) > 0.0
    self_p = []
    mixed = []
    for g in range(3):
        sl = slice(256 * g, 256 * g + 256)
        s = mm_nt(stack(qs[:, sl]), k[:, sl])
        s = jnp.where(causal, s, NONE)
        e = jnp.exp(s - jnp.max(s, axis=-1, keepdims=True))
        p = e / jnp.sum(e, axis=-1, keepdims=True)
        self_p.append(p)
        mixed.append(unstack(mm(p.astype(BF16), v[:, sl])))
    sm = jnp.concatenate(mixed, axis=1).astype(BF16)

    tick(5)
    ag_c.step_two()
    spread[1].step_six()
    after_self = resid + mm(sm, wb[:, LANE_SO : LANE_SO + D])
    hat_two, rs_two = normed(after_self)
    n2 = (hat_two * gain[1]).astype(BF16)
    cq = mm(n2, wb[:, LANE_CQ : LANE_CQ + D]).astype(BF16)
    cqb[...] = cq

    my_first, my_last = lay.first_device(me), lay.last_device(me)
    held_first, held_last = lay.first_rank(me), lay.last_rank(me)

    def piece_copy(src, dst, at, sent, landed, target):
        return pltpu.make_async_remote_copy(
            src_ref=src, dst_ref=dst, send_sem=psend.at[at, sent], recv_sem=precv.at[at, landed],
            device_id=(target, f), device_id_type=MESH,
        )

    def to_holders(pairs):
        for i in range(SLOTS):
            target = my_first + i
            slot = me - lay.first_rank(target)
            there = target <= my_last

            @pl.when(there & (target == me))
            def _():
                for src, dst, at in pairs:
                    dst[slot] = src[...]

            @pl.when(there & (target != me))
            def _():
                for src, dst, at in pairs:
                    piece_copy(src, dst.at[slot], at, i, slot, target).start()

    def to_holders_sent(pairs):
        for i in range(SLOTS):
            target = my_first + i

            @pl.when((target <= my_last) & (target != me))
            def _():
                for src, dst, at in pairs:
                    piece_copy(src, dst.at[0], at, i, 0, target).wait_send()

    def at_holders(pairs):
        for s in range(SLOTS):
            rank = held_first + s

            @pl.when((rank <= held_last) & (rank != me))
            def _():
                for src, dst, at in pairs:
                    piece_copy(src, dst.at[s], at, 0, s, rank).wait_recv()

    def to_owners(pairs):
        for s in range(SLOTS):
            rank = held_first + s
            index = me - lay.first_device(rank)
            there = rank <= held_last

            @pl.when(there & (rank == me))
            def _():
                for src, dst, at in pairs:
                    dst[index] = src[s]

            @pl.when(there & (rank != me))
            def _():
                for src, dst, at in pairs:
                    piece_copy(src.at[s], dst.at[index], at, s, index, rank).start()

    def to_owners_sent(pairs):
        for s in range(SLOTS):
            rank = held_first + s

            @pl.when((rank <= held_last) & (rank != me))
            def _():
                for src, dst, at in pairs:
                    piece_copy(src.at[s], dst.at[0], at, s, 0, rank).wait_send()

    def at_owners(pairs):
        for i in range(SLOTS):
            target = my_first + i

            @pl.when((target <= my_last) & (target != me))
            def _():
                for src, dst, at in pairs:
                    piece_copy(src.at[0], dst.at[i], at, 0, i, target).wait_recv()

    q_pairs = [(cqb, qbuf, 0)]
    o_pairs = [(osend, obuf, 1), (ostat_send, ostat, 2)]
    d_pairs = [(dob, dobuf, 3), (dstat_b, dstat, 4)]
    dq_pairs = [(dqsend, dqbuf, 5)]

    to_holders(q_pairs)

    tick(6)
    ag_c.step_three()
    spread[2].step_six()


    def kv_step(i, carry):
        lane = pl.multiple_of(i * 256, 256)
        kvb[:, pl.ds(lane, 256)] = mm(memp[...], wb[:, pl.ds(LANE_CKV + lane, 256)]).astype(BF16)
        return carry

    lax.fori_loop(0, 6, kv_step, 0)

    tell_p.wait()
    lane_f = lax.broadcasted_iota(jnp.int32, (SUFFIX, padded), 1).astype(F32)
    allowed = []
    for s in range(SLOTS):
        rank = held_first + s
        ok = rank <= held_last
        example = example_of(jnp.minimum(rank, ranks - 1))
        prefix = pb[example][0:1, 0:1]
        low = (lay.start(rank) - me * own_rows).astype(F32)
        patches = jnp.where(rank < lay.half, PATCH_S, PATCH_L).astype(F32)
        high = jnp.minimum(low + patches + prefix, jnp.float32(own_rows))
        high = jnp.where(ok, high, jnp.float32(-1.0))
        allowed.append(((lane_f >= low) & (lane_f < high)).astype(F32))
    allowed = jnp.concatenate(allowed * 4, axis=0) > 0.0

    at_holders(q_pairs)
    qh = jnp.concatenate([qbuf[s] for s in range(SLOTS)], axis=0)
    qh = (qh.astype(F32) * scale).astype(BF16)
    lane_c = lax.broadcasted_iota(jnp.int32, (SUFFIX, 128), 1)
    def swap(tile):
        return jnp.concatenate([tile[:, 64:], tile[:, :64]], axis=1)

    top_c = [jnp.zeros((SUFFIX, 128), F32) for _ in range(SLOTS)]
    sum_c = [jnp.zeros((SUFFIX, 128), F32) for _ in range(SLOTS)]
    for g in range(3):
        sl = slice(256 * g, 256 * g + 256)
        s = mm_nt(stack(qh[:, sl]), kvb[:, sl])
        s = jnp.where(allowed, s, NONE)
        top = jnp.max(s, axis=-1, keepdims=True)
        e = jnp.where(allowed, jnp.exp(s - top), 0.0)
        total = jnp.sum(e, axis=-1, keepdims=True)
        o = mm(e.astype(BF16), kvb[:, D + 256 * g : D + 256 * g + 256])
        o = o * jnp.where(total > 0.0, 1.0 / jnp.where(total > 0.0, total, 1.0), 0.0)
        o = unstack(o).astype(BF16)
        for n in range(SLOTS):
            osend[n, :, sl] = o[n * SUFFIX : (n + 1) * SUFFIX]
            for h in range(4):
                at = h * SLOTS * SUFFIX + n * SUFFIX
                hit = lane_c == 4 * g + h
                top_c[n] = jnp.where(hit, top[at : at + SUFFIX], top_c[n])
                sum_c[n] = jnp.where(hit, total[at : at + SUFFIX], sum_c[n])
    for n in range(SLOTS):
        ostat_send[n] = jnp.where(lane_c < 64, top_c[n], swap(sum_c[n]))
    to_owners(o_pairs)

    tick(7)
    ag_c.step_four()
    at_owners(o_pairs)
    spread[3].step_six()

    def expand(compact):
        low = lane_c < HEAD_DIM
        return jnp.concatenate(
            [jnp.where(low, compact[:, 2 * t : 2 * t + 1], compact[:, 2 * t + 1 : 2 * t + 2]) for t in range(6)],
            axis=1,
        )

    tops = [ostat[i] for i in range(SLOTS)]
    top_all = jnp.maximum(jnp.maximum(tops[0], tops[1]), tops[2])
    shares = [jnp.where(lane_c < 64, swap(tops[i]) * jnp.exp(tops[i] - top_all), 0.0) for i in range(SLOTS)]
    whole = shares[0] + shares[1] + shares[2]
    whole = jnp.where(whole > 0.0, whole, 1.0)
    lse = top_all + jnp.log(whole)
    cross = jnp.zeros((SUFFIX, D), F32)
    for i in range(SLOTS):
        cross = cross + expand(shares[i] / whole) * obuf[i].astype(F32)
    cm = cross.astype(BF16)

    after_cross = after_self + mm(cm, wb[:, LANE_CO : LANE_CO + D])
    hat_three, rs_three = normed(after_cross)
    n3 = (hat_three * gain[2]).astype(BF16)
    nb[token_rows(f, c, seat)] = n3
    ag_n.step_one()

    tick(8)
    ag_c.step_five()
    tick(9)
    spread[4].step_six()
    acts, slopes = [], []
    for j in range(4):
        value, slope = gelu_parts(mm(n3, wb[:, LANE_FI + D * j : LANE_FI + D * (j + 1)]))
        acts.append(value.astype(BF16))
        slopes.append(slope)
    act = jnp.concatenate(acts, axis=1)
    ag_c.step_six()
    for r in range(ranks):
        olr[token_rows(f, r % CORES, spots[r])] = cb[by_rank[r]]
    across_o = Across(olr, 0)
    across_n = Across(nb, 1)
    across_o.start()
    spread[5].step_six()
    unit_items = []

    def unit_device(unit, j):
        at = unit + 1
        return at % RING * (SIDE * CORES) + at // RING * CORES + j

    def push_part(which, at, to, src, dst):
        @pl.when(me == to)
        def _():
            dst[...] = src[...]

        @pl.when(me != to)
        def _():
            pltpu.make_async_remote_copy(
                src_ref=src, dst_ref=dst, send_sem=usend.at[which, at],
                recv_sem=urecv.at[which, me], device_id=(to, f), device_id_type=MESH,
            ).start()

        unit_items.append((which, at, to, src, dst))

    def push_left(units, at, left):
        lb[at] = left
        for unit in units:
            for j in range(CORES):
                lanes = pl.ds(j * PIECE, PIECE)
                push_part(0, CORES * unit + j, unit_device(unit, j), lb.at[at, :, lanes], rl.at[rows_of(me), lanes])

    def push_right(unit, right):
        for j in range(CORES):
            sb[unit, j] = right[:, j * PIECE : (j + 1) * PIECE]
            push_part(1, CORES * unit + j, unit_device(unit, j), sb.at[unit, j], rr.at[rows_of(me)])

    out_low = cb[mine]
    cot = out_low.astype(F32)
    hidden_grad = [mm_nt(out_low, wb[:, LANE_FO + D * j : LANE_FO + D * (j + 1)]) for j in range(4)]

    def by_hidden(j):
        parts = []
        for t in range(D // half_rows):
            at = D * j + t * half_rows
            col, unit = at // (4 * half_rows), (at % (4 * half_rows)) // half_rows
            parts.append(hidden_grad[unit][:, col * half_rows : (col + 1) * half_rows])
        return jnp.concatenate(parts, axis=1)

    n3_grad = jnp.zeros((SUFFIX, D), F32)
    for j in range(4):
        part = (by_hidden(j) * slopes[j]).astype(BF16)
        n3_grad = n3_grad + mm_nt(part, wb[:, LANE_FI + D * j : LANE_FI + D * (j + 1)])

    ag_n.step_two()
    part, ffn_gain_grad = norm_back(n3_grad, hat_three, rs_three, gain[2])
    cross_res = cot + part
    cross_low = cross_res.astype(BF16)
    d_mixed = mm_nt(cross_low, wb[:, LANE_CO : LANE_CO + D]).astype(BF16)
    dob[...] = d_mixed
    prod = d_mixed.astype(F32) * cross
    delta = jnp.zeros((SUFFIX, 128), F32)
    for t in range(6):
        tile = prod[:, 128 * t : 128 * (t + 1)]
        left = jnp.sum(jnp.where(lane_c < HEAD_DIM, tile, 0.0), axis=-1, keepdims=True)
        right = jnp.sum(jnp.where(lane_c < HEAD_DIM, 0.0, tile), axis=-1, keepdims=True)
        delta = jnp.where(lane_c == 2 * t, left, delta)
        delta = jnp.where(lane_c == 2 * t + 1, right, delta)
    dstat_b[...] = jnp.where(lane_c < 64, lse, swap(delta))
    to_holders(d_pairs)
    push_left((0, 1, 2), 0, n1)
    down = jnp.zeros((SUFFIX, D), F32)
    for j in range(4):
        lhs = jnp.concatenate(
            [act[:, i * 4 * half_rows + j * half_rows : i * 4 * half_rows + (j + 1) * half_rows] for i in range(columns)],
            axis=1,
        )
        down = down + mm(lhs, wb[:, LANE_FO + D * j : LANE_FO + D * (j + 1)])
    ob[0, my_slot] = (after_cross + down).astype(BF16)
    ag_out = ShortGather(place, block_view(ob.at[0]), block_bulk(ob.at[0]), sems, 4)
    ag_out.step_one()

    at_holders(d_pairs)

    push_left((4,), 2, n2)
    push_left((3,), 1, sm)
    doh = jnp.concatenate([dobuf[s] for s in range(SLOTS)], axis=0)
    for g in range(3):
        sl = slice(256 * g, 256 * g + 256)
        kg = kvb[:, sl]
        vg = kvb[:, D + 256 * g : D + 256 * g + 256]
        q4 = stack(qh[:, sl])
        do4 = stack(doh[:, sl])
        lse_col = jnp.concatenate([dstat[n][:, 4 * g + h : 4 * g + h + 1] for h in range(4) for n in range(SLOTS)], axis=0)
        del_col = jnp.concatenate([dstat[n][:, 64 + 4 * g + h : 65 + 4 * g + h] for h in range(4) for n in range(SLOTS)], axis=0)
        s = mm_nt(q4, kg)
        p = jnp.where(allowed, jnp.exp(jnp.where(allowed, s - lse_col, 0.0)), 0.0)
        dp = mm_nt(do4, vg)
        ds = (p * (dp - del_col)).astype(BF16)
        kvg[:, D + 256 * g : D + 256 * g + 256] = mm_tn(p.astype(BF16), do4).astype(BF16)
        kvg[:, sl] = mm_tn(ds, q4).astype(BF16)
        dq = unstack(mm(ds, kg)) * scale
        for n in range(SLOTS):
            dqsend[n, :, sl] = dq[n * SUFFIX : (n + 1) * SUFFIX].astype(BF16)
    to_owners(dq_pairs)
    ag_n.step_three()
    across_n.start()
    def kp_step(i, carry):
        lane = pl.multiple_of(i * 256, 256)
        kp[:, pl.ds(lane, 256)] = mm_tn(memp[...], kvg[:, pl.ds(lane, 256)]).astype(BF16)
        return carry

    lax.fori_loop(0, 6, kp_step, 0)
    kr_item = pltpu.make_async_remote_copy(
        src_ref=kp.at[pl.ds(pl.multiple_of((1 - c) * half_rows, 128), half_rows)], dst_ref=kr,
        send_sem=ksend.at[2 * chips], recv_sem=krecv.at[chips], device_id=mate, device_id_type=MESH,
    )
    kr_item.start()

    across_o.relay()
    ag_out.step_two()
    at_owners(dq_pairs)
    push_left((5,), 3, cm)
    push_right(5, cross_low)
    kr_item.wait_recv()
    kc[...] = (
        kp[pl.ds(pl.multiple_of(c * half_rows, 128), half_rows)].astype(F32) + kr[...].astype(F32)
    ).astype(BF16)
    half_slabs = half_rows // SIDE

    def ky_copy(j):
        lanes = pl.ds(j * D, D)
        return pltpu.make_async_remote_copy(
            src_ref=kc.at[:, lanes], dst_ref=ky.at[:, lanes], send_sem=ksend.at[2 * chips + 1 + j],
            recv_sem=krecv.at[chips + 1 + j], device_id=(me, other), device_id_type=MESH,
        )

    def kx_copy(j):
        lanes = pl.ds(j * D, D)
        return pltpu.make_async_remote_copy(
            src_ref=kc.at[pl.ds(pl.multiple_of((1 - x) * half_slabs, 16), half_slabs), lanes], dst_ref=kx.at[:, lanes],
            send_sem=ksend.at[2 * chips + 3 + j], recv_sem=krecv.at[chips + 3 + j],
            device_id=(z * (SIDE * CORES) + (1 - x) * CORES + c, f), device_id_type=MESH,
        )

    @pl.when(c != f)
    def _():
        ky_copy(0).start()
        ky_copy(1).start()

    cqg = (dqbuf[0].astype(F32) + dqbuf[1].astype(F32) + dqbuf[2].astype(F32)).astype(BF16)
    n2_grad = mm_nt(cqg, wb[:, LANE_CQ : LANE_CQ + D])
    part, cross_gain_grad = norm_back(n2_grad, hat_two, rs_two, gain[1])
    self_res = cross_res + part
    self_low = self_res.astype(BF16)
    dmix = mm_nt(self_low, wb[:, LANE_SO : LANE_SO + D]).astype(BF16)
    dqs, dks, dvs = [], [], []
    for g in range(3):
        sl = slice(256 * g, 256 * g + 256)
        q4 = stack(qs[:, sl])
        do4 = stack(dmix[:, sl])
        p = self_p[g]
        dp = mm_nt(do4, v[:, sl])
        ds = (p * (dp - jnp.sum(p * dp, axis=-1, keepdims=True))).astype(BF16)
        dvs.append(mm_tn(p.astype(BF16), do4))
        dks.append(mm_tn(ds, q4))
        dqs.append(unstack(mm(ds, k[:, sl])) * scale)
    packed_grad = [jnp.concatenate(parts, axis=1).astype(BF16) for parts in (dqs, dks, dvs)]
    for j in range(3):
        push_right(j, packed_grad[j])
    push_right(4, cqg)
    push_right(3, self_low)

    n1_grad = jnp.zeros((SUFFIX, D), F32)
    for j in range(3):
        n1_grad = n1_grad + mm_nt(packed_grad[j], wb[:, D * j : D * (j + 1)])
    part, self_gain_grad = norm_back(n1_grad, hat_one, rs_one, gain[0])
    ob[1, my_slot] = (self_res + part).astype(BF16)
    ag_grad = ShortGather(place, block_view(ob.at[1]), block_bulk(ob.at[1]), sems, 6)
    gmine[0] = jnp.concatenate(
        [self_gain_grad, cross_gain_grad, ffn_gain_grad, jnp.zeros((5, D), F32)], axis=0
    )
    partners = (
        mate,
        (me, other),
        (z * (SIDE * CORES) + (1 - x) * CORES + c, f),
        ((z + 1 - 2 * lax.rem(z, 2)) * (SIDE * CORES) + x * CORES + c, f),
        (lax.rem(z + 2, RING) * (SIDE * CORES) + x * CORES + c, f),
    )

    def gain_copy(k):
        return pltpu.make_async_remote_copy(
            src_ref=gmine.at[k], dst_ref=gpeer.at[k], send_sem=gain_sem.at[0, k], recv_sem=gain_sem.at[1, k],
            device_id=partners[k], device_id_type=MESH,
        )

    def gain_step(k):
        gain_copy(k - 1).wait_recv()
        total = gmine[k - 1] + gpeer[k - 1]
        if k == len(partners):
            return total
        gmine[k] = total
        gain_copy(k).start()

    gain_copy(0).start()
    ag_grad.step_one()
    ag_out.step_three()

    ag_n.step_six()
    across_n.relay()
    across_o.wait()
    across_n.wait()

    rows_step = 128
    hidden = [col * 4 * half_rows + D * c for col in range(columns)]

    def ffn_rows(first, last):
        def one(i, carry):
            at = pl.ds(pl.multiple_of(i * rows_step, rows_step), rows_step)
            for col in range(columns):
                lane = pl.multiple_of(LANE_FI + hidden[col], 128)
                value, slope = gelu_parts(mm(nb[at], wb[:, pl.ds(lane, D)]))

                @pl.when(f == col)
                def _():
                    ab[at] = value.astype(BF16)

                back = []
                for t in range(CORES):
                    lane_o = pl.multiple_of(LANE_FO + D * (2 * c + t), 128)
                    back.append(mm_nt(olr[at], wb[col * half_rows : (col + 1) * half_rows, pl.ds(lane_o, D)]))
                hb[col, at] = (jnp.concatenate(back, axis=1) * slope).astype(BF16)
            return carry

        lax.fori_loop(first, last, one, 0)

    own_lanes = pl.ds(pl.multiple_of(f * half_rows, 128), half_rows)

    def ffn_in_sum(col):
        lane = pl.multiple_of(LANE_FI + hidden[col], 128)
        for part in range(0, D, PIECE):
            total = mm_tn(nb[:, own_lanes], hb[col, :, part : part + PIECE])
            gb[:, pl.ds(lane + part, PIECE)] = total.astype(BF16)

    def ffn_out_sum(t):
        lane = pl.multiple_of(LANE_FO + D * (2 * c + t), 128)
        for part in range(0, D, PIECE):
            total = mm_tn(ab[:, t * half_rows : (t + 1) * half_rows], olr[:, part : part + PIECE])
            gb[:, pl.ds(lane + part, PIECE)] = total.astype(BF16)

    f_items = []

    def to_mate(lane, width):
        ref = gb.at[:, pl.ds(pl.multiple_of(lane, 128), width)]
        item = pltpu.make_async_remote_copy(
            src_ref=ref, dst_ref=ref, send_sem=fsend.at[len(f_items)], recv_sem=frecv.at[len(f_items)],
            device_id=mate, device_id_type=MESH,
        )
        item.start()
        f_items.append(item)

    has_unit = (seat >= 1) & (seat <= UNIT_CHIPS)

    def unit_lane(n, cc):
        return PIECE * (n - 1) + UNIT_CHIPS * PIECE * cc

    def unit_take(which, src, dst):
        def take(i, carry):
            @pl.when(i != me)
            def _():
                pltpu.make_async_remote_copy(
                    src_ref=src, dst_ref=dst(i), send_sem=usend.at[which, 0],
                    recv_sem=urecv.at[which, i], device_id=mate, device_id_type=MESH,
                ).wait_recv()

            return carry

        lax.fori_loop(0, ranks, take, 0)

    def left_lanes(core):
        return pl.ds(pl.multiple_of(core * PIECE, 128), PIECE)

    def left_copy(core):
        ref = rl.at[:, left_lanes(core)]
        return pltpu.make_async_remote_copy(
            src_ref=ref, dst_ref=ref, send_sem=ysend.at[1], recv_sem=yrecv.at[1], device_id=mate, device_id_type=MESH,
        )

    def unit_left(pred):
        @pl.when(pred)
        def _():
            unit_take(0, lb.at[0, :, pl.ds(0, PIECE)], lambda i: rl.at[rows_of(i), left_lanes(c)])
            left_copy(c).start()

    def unit_rows(n):
        return pl.ds(n * (half_rows // 2), half_rows // 2)

    def unit_copy(n):
        rows = unit_rows(n)
        return pltpu.make_async_remote_copy(
            src_ref=usend_b.at[rows], dst_ref=urecv_b.at[rows], send_sem=ysend.at[3 + n], recv_sem=yrecv.at[3 + n],
            device_id=(me, other), device_id_type=MESH,
        )

    def unit_sum(pred):
        @pl.when(pred)
        def _():
            unit_take(1, sb.at[0, 0], lambda i: rr.at[rows_of(i)])
            left_copy(1 - c).wait_recv()
            for col in range(columns):
                ug[col] = mm_tn(rl[:, col * half_rows : (col + 1) * half_rows], rr[...])
            usend_b[...] = ug[other].astype(BF16)
            for n in range(2):
                unit_copy(n).start()

    def unit_join(pred, n):
        @pl.when(pred)
        def _():
            unit_copy(n).wait_recv()
            rows = unit_rows(n)
            gb[rows, pl.ds(pl.multiple_of(unit_lane(seat, c), 128), PIECE)] = (
                ug[f, rows] + urecv_b[rows].astype(F32)
            ).astype(BF16)

    def has_block(zz, xx, cc):
        n = xx * RING + zz
        return (n >= 1) & (n <= UNIT_CHIPS)

    def unit_bulk(rows):
        width = UNIT_CHIPS * PIECE // SIDE
        return lambda cc, xx: gb.at[rows, pl.ds(pl.multiple_of(width * (SIDE * cc + xx), 128), width)]

    def gb_view(lane_of, rows):
        def view(zz, xx, cc):
            return gb.at[rows, pl.ds(pl.multiple_of(lane_of(xx * RING + zz, cc), 128), PIECE)]

        return view

    class UnitGather:
        def __init__(self):
            parts = [unit_rows(n) for n in range(2)]
            self.gathers = [
                Gather(place, gb_view(unit_lane, rows), unit_bulk(rows), sems, at, has_block)
                for at, rows in zip((3, 7), parts)
            ]

        def step(self, name):
            for gather in self.gathers:
                getattr(gather, name)()

    ag_u = UnitGather()

    k_items = []

    def k_copy(t, j):
        return pltpu.make_async_remote_copy(
            src_ref=ks.at[pl.ds(t * slab, slab), pl.ds(j * D, D)], dst_ref=cp.at[z],
            send_sem=ksend.at[t * CORES + j], recv_sem=krecv.at[z],
            device_id=(t * (SIDE * CORES) + x * CORES + j, f), device_id_type=MESH,
        )

    def k_over_x(j):
        lanes = pl.ds(j * D, D)

        @pl.when(c == f)
        def _():
            ky_copy(j).wait_recv()
            kc[:, lanes] = (kc[:, lanes].astype(F32) + ky[:, lanes].astype(F32)).astype(BF16)
            kx_copy(j).start()

    def k_on_line(j):
        lanes = pl.ds(j * D, D)

        @pl.when(c == f)
        def _():
            kx_copy(j).wait_recv()
            ks[:, lanes] = (
                kc[pl.ds(pl.multiple_of(x * half_slabs, 16), half_slabs), lanes].astype(F32) + kx[:, lanes].astype(F32)
            ).astype(BF16)

        for t in range(RING):
            here = (z == t) & (c == j)

            @pl.when((c == f) & here)
            def _():
                cp[z] = ks[t * slab : (t + 1) * slab, j * D : (j + 1) * D]

            @pl.when((c == f) & jnp.logical_not(here))
            def _():
                k_copy(t, j).start()

            k_items.append((t, j, here))

    k_over_x(0)
    ffn_rows(0, 2)
    gain_step(1)
    unit_left(has_unit)
    k_on_line(0)
    k_over_x(1)
    unit_sum(has_unit)
    ffn_rows(2, 4)
    gain_step(2)
    k_on_line(1)
    unit_join(has_unit, 0)
    ag_u.gathers[0].step_one()
    ffn_rows(4, 5)
    unit_join(has_unit, 1)
    ag_u.gathers[1].step_one()
    ffn_rows(5, 6)
    gain_step(3)

    def take_k(i, carry):
        @pl.when((i != z) | (c != f))
        def _():
            pltpu.make_async_remote_copy(
                src_ref=ks.at[pl.ds(0, slab), pl.ds(0, D)], dst_ref=cp.at[i], send_sem=ksend.at[0],
                recv_sem=krecv.at[i], device_id=mate, device_id_type=MESH,
            ).wait_recv()

        return carry

    lax.fori_loop(0, RING, take_k, 0)
    total = cp[0].astype(F32)
    for i in range(1, RING):
        total = total + cp[i].astype(F32)
    k_lane = pl.multiple_of(OUT_CKV + c * D, 128)
    gb[pl.ds(pl.multiple_of(x * half_slabs + z * slab, 16), slab), pl.ds(k_lane, D)] = total.astype(BF16)

    def kv_view(zz, xx, cc):
        row = pl.multiple_of(xx * half_slabs + zz * slab, 16)
        return gb.at[pl.ds(row, slab), pl.ds(pl.multiple_of(OUT_CKV + cc * D, 128), D)]

    ag_k = Gather(place, kv_view, lambda cc, xx: gb.at[pl.ds(pl.multiple_of(xx * half_slabs, 16), half_slabs), pl.ds(pl.multiple_of(OUT_CKV + cc * D, 128), D)], sems, 5)
    ag_k.step_one()

    def mg_step(i, carry):
        row = pl.multiple_of(i * 128, 128)
        memgrad_ref[pl.ds(row, 128)] = mm_nt(kvg[pl.ds(row, 128)], wb[:, LANE_CKV : LANE_CKV + 2 * D])
        return carry

    full = own_rows // 128
    lax.fori_loop(0, full, mg_step, 0)
    if own_rows % 128:
        tail = mm_nt(kvg[full * 128 : (full + 1) * 128], wb[:, LANE_CKV : LANE_CKV + 2 * D])
        memgrad_ref[full * 128 : own_rows] = tail[0 : own_rows - full * 128]


    ag_u.step("step_two")
    ffn_rows(6, 8)
    gain_step(4)
    ag_u.step("step_three")
    ag_k.step_two()
    ffn_in_sum(0)
    to_mate(LANE_FI + hidden[0], D)
    ag_grad.step_two()
    ag_k.step_three()
    ag_u.step("step_four")
    ffn_in_sum(1)
    to_mate(LANE_FI + hidden[1], D)
    ag_k.step_four()
    ag_grad.step_three()
    ag_out.step_six()
    ffn_out_sum(0)
    ffn_out_sum(1)
    to_mate(LANE_FO + CORES * D * c, CORES * D)
    ag_u.step("step_five")
    for n, (lane, width) in enumerate(
        [(LANE_FI + col * 4 * half_rows + D * (1 - c), D) for col in range(columns)] + [(LANE_FO + CORES * D * (1 - c), CORES * D)]
    ):
        ref = gb.at[:, pl.ds(pl.multiple_of(lane, 128), width)]
        pltpu.make_async_remote_copy(
            src_ref=ref, dst_ref=ref, send_sem=fsend.at[n], recv_sem=frecv.at[n], device_id=mate, device_id_type=MESH,
        ).wait_recv()
    outs = []

    def write(lane, width):
        lanes = pl.ds(lane, width)
        item = pltpu.make_async_copy(gb.at[:, lanes], weights_out_ref.at[:, lanes], load_sem.at[len(outs)])
        item.start()
        outs.append(item)

    write(LANE_FI, 8 * D)
    ag_k.step_five()
    ag_grad.step_six()
    out_ref[...] = ob[0, out_slot].astype(F32)
    grad_ref[...] = ob[1, out_slot].astype(F32)
    gains_all = gain_step(5)
    own_gain = gains_all[:, 0:half_rows]
    for i in range(1, columns):
        own_gain = jnp.where(f == i, gains_all[:, i * half_rows : (i + 1) * half_rows], own_gain)
    gain_out_ref[...] = own_gain
    ag_u.step("step_six")
    write(0, OUT_CKV)
    ag_k.step_six()
    write(OUT_CKV, 2 * D)

    to_holders_sent(q_pairs)
    to_owners_sent(o_pairs)
    to_holders_sent(d_pairs)
    to_owners_sent(dq_pairs)
    for which, at, to, src, dst in unit_items:
        @pl.when(me != to)
        def _():
            pltpu.make_async_remote_copy(
                src_ref=src, dst_ref=dst, send_sem=usend.at[which, at],
                recv_sem=urecv.at[which, 0], device_id=(to, f), device_id_type=MESH,
            ).wait_send()
    @pl.when(has_unit)
    def _():
        for n in range(2):
            unit_copy(n).wait_send()
        left_copy(c).wait_send()

    for t, j, here in k_items:
        @pl.when((c == f) & jnp.logical_not(here))
        def _():
            k_copy(t, j).wait_send()

    @pl.when(c == f)
    def _():
        kx_copy(0).wait_send()
        kx_copy(1).wait_send()

    across_o.finish()
    across_n.finish()
    for item in f_items:
        item.wait_send()
    kr_item.wait_send()

    @pl.when(c != f)
    def _():
        ky_copy(0).wait_send()
        ky_copy(1).wait_send()

    for item in y_items:
        item.wait_send()
    tell_p.finish()
    for k in range(len(partners)):
        gain_copy(k).wait_send()
    for item in [ag_x, *spread, ag_c, ag_n, *ag_u.gathers, ag_out, ag_grad, ag_k]:
        item.finish()
    for item in outs:
        item.wait()


def fused_body(
    ranks, columns,
    decoder_in, memory, res_group, prefix_len, self_gain, self_qkv, self_out, cross_gain, cross_query,
    cross_kv, cross_out, ffn_gain, ffn_in, ffn_out, cotangent,
):
    half_rows = D // columns
    chips = ranks // CORES
    slab = half_rows // chips
    own_rows = memory.shape[1]
    padded = -(-own_rows // 128) * 128
    tokens = ranks * SUFFIX
    vm = pl.BlockSpec(memory_space=pltpu.VMEM)
    sm = pl.BlockSpec(memory_space=pltpu.SMEM)
    hbm = pl.BlockSpec(memory_space=pl.ANY)
    dma = pltpu.SemaphoreType.DMA
    scratch = [
        pltpu.VMEM((D, UNITS * D), BF16),
        pltpu.VMEM((half_rows, UNITS * D), BF16),
        pltpu.VMEM((tokens, D), BF16),
        pltpu.VMEM((tokens, PIECE), BF16),
        pltpu.VMEM((4, SUFFIX, D), BF16),
        pltpu.VMEM((UNIT_CHIPS, CORES, SUFFIX, PIECE), BF16),
        pltpu.VMEM((ranks, SUFFIX, D), F32),
        pltpu.VMEM((ranks, SUFFIX, D), BF16),
        pltpu.VMEM((columns * tokens, D), BF16),
        pltpu.VMEM((columns * tokens, D), BF16),
        pltpu.VMEM((2, ranks, SUFFIX, D), BF16),
        pltpu.VMEM((ranks, 8, 128), F32),
        pltpu.VMEM((columns, 16, 128), F32),
        pltpu.VMEM((padded, D), BF16),
        pltpu.VMEM((padded, 2 * D), BF16),
        pltpu.VMEM((padded, 2 * D), BF16),
        pltpu.VMEM((D, 2 * D), BF16),
        pltpu.VMEM((half_rows, 2 * D), BF16),
        pltpu.VMEM((half_rows, 2 * D), BF16),
        pltpu.VMEM((half_rows, 2 * D), BF16),
        pltpu.VMEM((RING, slab, D), BF16),
        pltpu.VMEM((half_rows // SIDE, 2 * D), BF16),
        pltpu.VMEM((half_rows // SIDE, 2 * D), BF16),
        pltpu.VMEM((columns, columns * tokens, D), BF16),
        pltpu.VMEM((columns * tokens, D), BF16),
        pltpu.VMEM((columns, half_rows, PIECE), F32),
        pltpu.VMEM((half_rows, PIECE), BF16),
        pltpu.VMEM((half_rows, PIECE), BF16),
        pltpu.VMEM((SUFFIX, D), BF16),
        pltpu.VMEM((SLOTS, SUFFIX, D), BF16),
        pltpu.VMEM((SLOTS, SUFFIX, D), BF16),
        pltpu.VMEM((SLOTS, SUFFIX, 128), F32),
        pltpu.VMEM((SLOTS, SUFFIX, D), BF16),
        pltpu.VMEM((SLOTS, SUFFIX, 128), F32),
        pltpu.VMEM((SUFFIX, D), BF16),
        pltpu.VMEM((SUFFIX, 128), F32),
        pltpu.VMEM((SLOTS, SUFFIX, D), BF16),
        pltpu.VMEM((SLOTS, SUFFIX, 128), F32),
        pltpu.VMEM((SLOTS, SUFFIX, D), BF16),
        pltpu.VMEM((SLOTS, SUFFIX, D), BF16),
        pltpu.VMEM((5, 8, D), F32),
        pltpu.VMEM((5, 8, D), F32),
        dma((10,)),
        dma((len(CHUNKS), 19)),
        dma((len(CHUNKS), 14)),
        dma((8, 17)),
        dma((8, 10)),
        dma((1, ranks)),
        dma((1, ranks)),
        dma((2, 5)),
        dma((2, 2)),
        dma((2, 2)),
        dma((3,)),
        dma((3,)),
        dma((5,)),
        dma((5,)),
        dma((6, SLOTS)),
        dma((6, SLOTS)),
        dma((2, CORES * UNIT_CHIPS)),
        dma((2, ranks)),
        dma((2 * chips + 5,)),
        dma((chips + 5,)),
    ]
    out, grad, memgrad, gain_grads, weight_grads = pl.pallas_call(
        partial(layer_kernel, ranks, columns),
        out_shape=(
            jax.ShapeDtypeStruct((SUFFIX, D), F32),
            jax.ShapeDtypeStruct((SUFFIX, D), F32),
            jax.ShapeDtypeStruct((own_rows, D), F32),
            jax.ShapeDtypeStruct((8, half_rows), F32),
            jax.ShapeDtypeStruct((half_rows, UNITS * D), BF16),
        ),
        in_specs=[vm, vm, vm, sm, sm, vm, vm, vm] + [hbm] * 7,
        out_specs=(vm, vm, vm, vm, hbm),
        scratch_shapes=scratch,
        compiler_params=pltpu.CompilerParams(
            collective_id=0, has_side_effects=True, vmem_limit_bytes=63 * 2**20
        ),
        name="layer",
    )(
        decoder_in[0], cotangent[0], memory[0], res_group, prefix_len, self_gain, cross_gain, ffn_gain,
        self_qkv, self_out, cross_query, cross_kv, cross_out, ffn_in, ffn_out,
    )

    return unpack(half_rows, columns, weight_grads, memgrad, out, grad, gain_grads)


SPLIT = ((0, 3), (3, 1), (4, 1), (OUT_CKV, 2 * D), (5, 1), (LANE_FI, 4 * D))
WHOLE = (OUT_CKV, LANE_FI)


def unpack_kernel(w_ref, m_ref, o_ref, g_ref, gains_ref, *refs):
    *weights, ffn_out_ref, mem_ref, out_ref, grad_ref, one_ref, two_ref, three_ref = refs
    for n, ref in enumerate((one_ref, two_ref, three_ref)):
        ref[...] = gains_ref[n : n + 1].reshape(ref.shape)
    for (low, width), ref in zip(SPLIT, weights):
        if low in WHOLE:
            ref[...] = w_ref[:, low : low + width].astype(F32)
            continue
        for n in range(width):
            for j in range(CORES):
                at = (UNIT_CHIPS * j + low + n) * PIECE
                to = (CORES * n + j) * PIECE
                ref[:, to : to + PIECE] = w_ref[:, at : at + PIECE].astype(F32)
    for j in range(4):
        ffn_out_ref[j] = w_ref[:, LANE_FO + D * j : LANE_FO + D * (j + 1)].astype(F32)
    mem_ref[:, 0, :] = m_ref[...]
    out_ref[...] = o_ref[...]
    grad_ref[...] = g_ref[...]


def unpack(half_rows, columns, weight_grads, memgrad, out, grad, gain_grads):
    steps = 2
    rows = half_rows // steps
    own_rows = memgrad.shape[0]
    mem_rows = -(-own_rows // (8 * steps)) * 8
    tokens = out.shape[0] // steps
    block = lambda height, width: pl.BlockSpec((height, width), lambda i: (i, 0))
    results = pl.pallas_call(
        unpack_kernel,
        grid=(steps,),
        out_shape=[jax.ShapeDtypeStruct((half_rows, width if low in WHOLE else width * D), F32) for low, width in SPLIT]
        + [
            jax.ShapeDtypeStruct((4, half_rows, D), F32),
            jax.ShapeDtypeStruct((own_rows, 1, D), F32),
            jax.ShapeDtypeStruct(out.shape, F32),
            jax.ShapeDtypeStruct(grad.shape, F32),
        ]
        + [jax.ShapeDtypeStruct((half_rows,), F32)] * 3,
        in_specs=[block(rows, UNITS * D), block(mem_rows, D), block(tokens, D), block(tokens, D), pl.BlockSpec(gain_grads.shape, lambda i: (0, 0))],
        out_specs=[block(rows, width if low in WHOLE else width * D) for low, width in SPLIT]
        + [
            pl.BlockSpec((4, rows, D), lambda i: (0, i, 0)),
            pl.BlockSpec((mem_rows, 1, D), lambda i: (i, 0, 0)),
            block(tokens, D),
            block(tokens, D),
        ]
        + [pl.BlockSpec((half_rows,), lambda i: (0,))] * 3,
        compiler_params=pltpu.CompilerParams(vmem_limit_bytes=63 * 2**20),
        name="unpack",
    )(weight_grads, memgrad, out, grad, gain_grads)
    qkv, so, cq, ckv, co, fi, fo, mem, out, grad, gain_one, gain_two, gain_three = results
    return (
        out[None], grad[None], mem.reshape(1, own_rows, D),
        gain_one, qkv, so, gain_two, cq, ckv, co, gain_three, fi, fo.reshape(4 * half_rows, D),
    )


def layer_norm(value, gain):
    mean = jnp.mean(value, axis=-1, keepdims=True)
    centred = value - mean
    variance = jnp.mean(centred * centred, axis=-1, keepdims=True)
    return centred * lax.rsqrt(variance + norm_eps) * gain


def product(left, right):
    return jnp.dot(left, right, preferred_element_type=jnp.float32)


def outer_sum(left, right):
    flat_left = left.reshape(-1, left.shape[-1])
    flat_right = right.reshape(-1, right.shape[-1])
    return lax.dot_general(
        flat_left, flat_right, (((0,), (0,)), ((), ())), preferred_element_type=jnp.float32
    )


def back_product(grad, weight):
    return lax.dot_general(
        grad, weight, (((grad.ndim - 1,), (1,)), ((), ())), preferred_element_type=jnp.float32
    )


def attend(query, keys, values, allowed, scale):
    scores = jnp.einsum("eqhd,ekhd->ehqk", query, keys, preferred_element_type=jnp.float32) * scale
    scores = jnp.where(allowed[:, None], scores, -1e30)
    top = jnp.max(scores, axis=-1, keepdims=True)
    weights = jnp.exp(scores - top)
    probs = weights / jnp.sum(weights, axis=-1, keepdims=True)
    mixed = jnp.einsum(
        "ehqk,ekhd->eqhd", probs.astype(jnp.bfloat16), values, preferred_element_type=jnp.float32
    )
    return (mixed.astype(jnp.bfloat16), probs)


def attend_back(grad_mixed, query, keys, values, probs, scale):
    probs_low = probs.astype(jnp.bfloat16)
    grad_values = jnp.einsum(
        "ehqk,eqhd->ekhd", probs_low, grad_mixed, preferred_element_type=jnp.float32
    )
    grad_probs = jnp.einsum(
        "eqhd,ekhd->ehqk", grad_mixed, values, preferred_element_type=jnp.float32
    )
    grad_scores = probs * (grad_probs - jnp.sum(probs * grad_probs, axis=-1, keepdims=True))
    grad_low = grad_scores.astype(jnp.bfloat16)
    grad_query = (
        jnp.einsum("ehqk,ekhd->eqhd", grad_low, keys, preferred_element_type=jnp.float32) * scale
    )
    grad_keys = (
        jnp.einsum("ehqk,eqhd->ekhd", grad_low, query, preferred_element_type=jnp.float32) * scale
    )
    return (grad_query, grad_keys, grad_values)


def window_layout(res_group, mem_col):
    small = 1 - res_group
    small_count = jnp.sum(small, axis=-1, keepdims=True)
    small_before = jnp.cumsum(small, axis=-1) - small
    large_before = jnp.cumsum(res_group, axis=-1) - res_group
    offset = jnp.where(
        res_group == 1, SLOT_S * small_count + SLOT_L * large_before, SLOT_S * small_before
    )
    start = jnp.minimum(offset, mem_col - SLOT_L)
    return (offset, start)


def take_windows(column, starts):
    return jax.vmap(lambda begin: lax.dynamic_slice_in_dim(column, begin, SLOT_L, 0))(starts)


def forward(decoder_rows, windows, cross_allowed, weights):
    (
        self_gain,
        self_qkv,
        self_out,
        cross_gain,
        cross_query,
        cross_kv,
        cross_out,
        ffn_gain,
        ffn_in,
        ffn_out,
    ) = weights
    count = decoder_rows.shape[0] // SUFFIX
    scale = HEAD_DIM ** (-0.5)
    row_index = lax.broadcasted_iota(jnp.int32, (SUFFIX, SUFFIX), 0)
    col_index = lax.broadcasted_iota(jnp.int32, (SUFFIX, SUFFIX), 1)
    causal = (row_index >= col_index)[None]
    resid = decoder_rows.reshape(count, SUFFIX, D)
    normed_one = layer_norm(resid, self_gain.astype(jnp.float32)).astype(jnp.bfloat16)
    packed = product(normed_one, self_qkv).astype(jnp.bfloat16)
    heads = packed.reshape(count, SUFFIX, 3, HEADS, HEAD_DIM)
    self_mixed, self_probs = attend(heads[:, :, 0], heads[:, :, 1], heads[:, :, 2], causal, scale)
    self_mixed = self_mixed.reshape(count, SUFFIX, D)
    after_self = resid + product(self_mixed, self_out)
    normed_two = layer_norm(after_self, cross_gain.astype(jnp.float32)).astype(jnp.bfloat16)
    cross_q = product(normed_two, cross_query).astype(jnp.bfloat16)
    window_kv = product(windows, cross_kv).astype(jnp.bfloat16)
    query_heads = cross_q.reshape(count, SUFFIX, HEADS, HEAD_DIM)
    kv_heads = window_kv.reshape(count, SLOT_L, 2, HEADS, HEAD_DIM)
    cross_mixed, cross_probs = attend(
        query_heads, kv_heads[:, :, 0], kv_heads[:, :, 1], cross_allowed, scale
    )
    cross_mixed = cross_mixed.reshape(count, SUFFIX, D)
    after_cross = after_self + product(cross_mixed, cross_out)
    normed_three = layer_norm(after_cross, ffn_gain.astype(jnp.float32)).astype(jnp.bfloat16)
    up = product(normed_three, ffn_in)
    act = jax.nn.gelu(up, approximate=True).astype(jnp.bfloat16)
    result = after_cross + product(act, ffn_out)
    return (
        resid,
        normed_one,
        packed,
        self_probs,
        self_mixed,
        after_self,
        normed_two,
        cross_q,
        window_kv,
        cross_probs,
        cross_mixed,
        after_cross,
        normed_three,
        up,
        act,
        result,
    )


def backward(grad_out, saved, weights):
    (
        self_gain,
        self_qkv,
        self_out,
        cross_gain,
        cross_query,
        cross_kv,
        cross_out,
        ffn_gain,
        ffn_in,
        ffn_out,
    ) = weights
    (
        resid,
        normed_one,
        packed,
        self_probs,
        self_mixed,
        after_self,
        normed_two,
        cross_q,
        window_kv,
        cross_probs,
        cross_mixed,
        after_cross,
        normed_three,
        up,
        act,
        result,
    ) = saved
    count = resid.shape[0]
    scale = HEAD_DIM ** (-0.5)
    grad_out = grad_out.reshape(count, SUFFIX, D)
    out_low = grad_out.astype(jnp.bfloat16)
    ffn_out_grad = outer_sum(act, out_low)
    act_grad = back_product(out_low, ffn_out)
    gelu_value, gelu_back = jax.vjp(partial(jax.nn.gelu, approximate=True), up)
    up_grad = gelu_back(act_grad)[0].astype(jnp.bfloat16)
    ffn_in_grad = outer_sum(normed_three, up_grad)
    normed_three_grad = back_product(up_grad, ffn_in)
    norm_value, norm_back = jax.vjp(layer_norm, after_cross, ffn_gain.astype(jnp.float32))
    resid_part, ffn_gain_grad = norm_back(normed_three_grad)
    cross_res_grad = grad_out + resid_part
    cross_low = cross_res_grad.astype(jnp.bfloat16)
    cross_out_grad = outer_sum(cross_mixed, cross_low)
    mixed_grad = (
        back_product(cross_low, cross_out)
        .astype(jnp.bfloat16)
        .reshape(count, SUFFIX, HEADS, HEAD_DIM)
    )
    query_heads = cross_q.reshape(count, SUFFIX, HEADS, HEAD_DIM)
    kv_heads = window_kv.reshape(count, SLOT_L, 2, HEADS, HEAD_DIM)
    query_grad, keys_grad, values_grad = attend_back(
        mixed_grad, query_heads, kv_heads[:, :, 0], kv_heads[:, :, 1], cross_probs, scale
    )
    cross_q_grad = query_grad.reshape(count, SUFFIX, D).astype(jnp.bfloat16)
    window_kv_grad = (
        jnp.stack((keys_grad, values_grad), axis=2)
        .reshape(count, SLOT_L, 2 * D)
        .astype(jnp.bfloat16)
    )
    cross_query_grad = outer_sum(normed_two, cross_q_grad)
    normed_two_grad = back_product(cross_q_grad, cross_query)
    norm_value, norm_back = jax.vjp(layer_norm, after_self, cross_gain.astype(jnp.float32))
    resid_part, cross_gain_grad = norm_back(normed_two_grad)
    self_res_grad = cross_res_grad + resid_part
    self_low = self_res_grad.astype(jnp.bfloat16)
    self_out_grad = outer_sum(self_mixed, self_low)
    mixed_grad = (
        back_product(self_low, self_out)
        .astype(jnp.bfloat16)
        .reshape(count, SUFFIX, HEADS, HEAD_DIM)
    )
    heads = packed.reshape(count, SUFFIX, 3, HEADS, HEAD_DIM)
    query_grad, keys_grad, values_grad = attend_back(
        mixed_grad, heads[:, :, 0], heads[:, :, 1], heads[:, :, 2], self_probs, scale
    )
    packed_grad = (
        jnp.stack((query_grad, keys_grad, values_grad), axis=2)
        .reshape(count, SUFFIX, 3 * D)
        .astype(jnp.bfloat16)
    )
    self_qkv_grad = outer_sum(normed_one, packed_grad)
    normed_one_grad = back_product(packed_grad, self_qkv)
    norm_value, norm_back = jax.vjp(layer_norm, resid, self_gain.astype(jnp.float32))
    resid_part, self_gain_grad = norm_back(normed_one_grad)
    decoder_grad = self_res_grad + resid_part
    weight_grads = (
        self_gain_grad,
        self_qkv_grad,
        self_out_grad,
        cross_gain_grad,
        cross_query_grad,
        cross_out_grad,
        ffn_gain_grad,
        ffn_in_grad,
        ffn_out_grad,
    )
    return (decoder_grad, window_kv_grad, weight_grads)


def make_placer(all_starts, lowest, own_rows):

    def place(total, piece, begin):

        def add_one(item, acc):
            relative = all_starts[item] - lowest
            inside = ((relative > -SLOT_L) & (relative < own_rows)).astype(jnp.float32)
            spot = jnp.clip(relative + SLOT_L, 0, own_rows + SLOT_L)
            current = lax.dynamic_slice_in_dim(acc, spot, SLOT_L, 0)
            added = current + piece[item].astype(jnp.float32) * inside
            return lax.dynamic_update_slice_in_dim(acc, added, spot, 0)

        return lax.fori_loop(0, piece.shape[0], add_one, total)

    return place


def body(
    decoder_in,
    memory,
    res_group,
    prefix_len,
    self_gain,
    self_qkv,
    self_out,
    cross_gain,
    cross_query,
    cross_kv,
    cross_out,
    ffn_gain,
    ffn_in,
    ffn_out,
    cotangent,
):
    count = prefix_len.shape[1]
    own_rows = memory.shape[1]
    mem_col = own_rows * lax.axis_size("dp")
    offset, start = window_layout(res_group, mem_col)
    all_starts = start[0]
    first = lax.axis_index("dp") * count
    own_offset = lax.dynamic_slice_in_dim(offset[0], first, count)
    own_start = lax.dynamic_slice_in_dim(all_starts, first, count)
    own_group = lax.dynamic_slice_in_dim(res_group[0], first, count)
    valid = jnp.where(own_group == 1, PATCH_L, PATCH_S) + prefix_len[0]
    positions = own_start[:, None] + jnp.arange(SLOT_L, dtype=jnp.int32)[None]
    cross_allowed = (
        (positions >= own_offset[:, None]) & (positions < (own_offset + valid)[:, None])
    )[:, None]
    weights = (
        lax.all_gather(self_gain, "fsdp", axis=0, tiled=True),
        lax.all_gather(self_qkv, "fsdp", axis=0, tiled=True),
        lax.all_gather(self_out, "fsdp", axis=0, tiled=True),
        lax.all_gather(cross_gain, "fsdp", axis=0, tiled=True),
        lax.all_gather(cross_query, "fsdp", axis=0, tiled=True),
        lax.all_gather(cross_kv, "fsdp", axis=0, tiled=True),
        lax.all_gather(cross_out, "fsdp", axis=0, tiled=True),
        lax.all_gather(ffn_gain, "fsdp", axis=0, tiled=True),
        lax.all_gather(ffn_in, "fsdp", axis=0, tiled=True),
        lax.all_gather(ffn_out, "fsdp", axis=0, tiled=True),
    )
    column = lax.all_gather(memory[0], "dp", axis=0, tiled=True)
    windows = take_windows(column, own_start)
    saved = forward(decoder_in[0], windows, cross_allowed, weights)
    decoder_out = saved[-1]
    weights = (
        lax.all_gather(self_gain, "fsdp", axis=0, tiled=True),
        lax.all_gather(self_qkv, "fsdp", axis=0, tiled=True),
        lax.all_gather(self_out, "fsdp", axis=0, tiled=True),
        lax.all_gather(cross_gain, "fsdp", axis=0, tiled=True),
        lax.all_gather(cross_query, "fsdp", axis=0, tiled=True),
        lax.all_gather(cross_kv, "fsdp", axis=0, tiled=True),
        lax.all_gather(cross_out, "fsdp", axis=0, tiled=True),
        lax.all_gather(ffn_gain, "fsdp", axis=0, tiled=True),
        lax.all_gather(ffn_in, "fsdp", axis=0, tiled=True),
        lax.all_gather(ffn_out, "fsdp", axis=0, tiled=True),
    )
    column = lax.all_gather(memory[0], "dp", axis=0, tiled=True)
    windows = take_windows(column, own_start)
    saved = forward(decoder_in[0], windows, cross_allowed, weights)
    whole_kv = weights[5]
    decoder_grad, window_kv_grad, local_grads = backward(cotangent[0], saved, weights)
    lowest = lax.axis_index("dp") * own_rows
    place = make_placer(all_starts, lowest, own_rows)
    empty = jnp.zeros((own_rows + 2 * SLOT_L, 2 * D), jnp.float32)
    summed = place(empty, lax.all_gather(window_kv_grad, "dp", axis=0, tiled=True), jnp.int32(0))
    own_kv_grad = summed[SLOT_L : SLOT_L + own_rows].astype(jnp.bfloat16)
    memory_grad = back_product(own_kv_grad, whole_kv)
    cross_kv_part = outer_sum(memory[0], own_kv_grad)
    grads = (
        local_grads[0],
        local_grads[1],
        local_grads[2],
        local_grads[3],
        local_grads[4],
        cross_kv_part,
        local_grads[5],
        local_grads[6],
        local_grads[7],
        local_grads[8],
    )
    shards = (
        lax.psum_scatter(
            grads[0].astype(jnp.bfloat16), "fsdp", scatter_dimension=0, tiled=True
        ).astype(jnp.float32),
        lax.psum_scatter(
            grads[1].astype(jnp.bfloat16), "fsdp", scatter_dimension=0, tiled=True
        ).astype(jnp.float32),
        lax.psum_scatter(
            grads[2].astype(jnp.bfloat16), "fsdp", scatter_dimension=0, tiled=True
        ).astype(jnp.float32),
        lax.psum_scatter(
            grads[3].astype(jnp.bfloat16), "fsdp", scatter_dimension=0, tiled=True
        ).astype(jnp.float32),
        lax.psum_scatter(
            grads[4].astype(jnp.bfloat16), "fsdp", scatter_dimension=0, tiled=True
        ).astype(jnp.float32),
        lax.psum_scatter(
            grads[5].astype(jnp.bfloat16), "fsdp", scatter_dimension=0, tiled=True
        ).astype(jnp.float32),
        lax.psum_scatter(
            grads[6].astype(jnp.bfloat16), "fsdp", scatter_dimension=0, tiled=True
        ).astype(jnp.float32),
        lax.psum_scatter(
            grads[7].astype(jnp.bfloat16), "fsdp", scatter_dimension=0, tiled=True
        ).astype(jnp.float32),
        lax.psum_scatter(
            grads[8].astype(jnp.bfloat16), "fsdp", scatter_dimension=0, tiled=True
        ).astype(jnp.float32),
        lax.psum_scatter(
            grads[9].astype(jnp.bfloat16), "fsdp", scatter_dimension=0, tiled=True
        ).astype(jnp.float32),
    )
    totals = (
        lax.psum(shards[0].astype(jnp.bfloat16), "dp").astype(jnp.float32),
        lax.psum(shards[1].astype(jnp.bfloat16), "dp").astype(jnp.float32),
        lax.psum(shards[2].astype(jnp.bfloat16), "dp").astype(jnp.float32),
        lax.psum(shards[3].astype(jnp.bfloat16), "dp").astype(jnp.float32),
        lax.psum(shards[4].astype(jnp.bfloat16), "dp").astype(jnp.float32),
        lax.psum(shards[5].astype(jnp.bfloat16), "dp").astype(jnp.float32),
        lax.psum(shards[6].astype(jnp.bfloat16), "dp").astype(jnp.float32),
        lax.psum(shards[7].astype(jnp.bfloat16), "dp").astype(jnp.float32),
        lax.psum(shards[8].astype(jnp.bfloat16), "dp").astype(jnp.float32),
        lax.psum(shards[9].astype(jnp.bfloat16), "dp").astype(jnp.float32),
    )
    return (
        decoder_out,
        decoder_grad,
        memory_grad[None],
        totals[0],
        totals[1],
        totals[2],
        totals[3],
        totals[4],
        totals[5],
        totals[6],
        totals[7],
        totals[8],
        totals[9],
    )


def choose(mesh):
    ranks, columns = mesh.shape["dp"], mesh.shape["fsdp"]
    slabs = (D // columns) % (16 * (ranks // CORES)) == 0
    if slabs and columns == 2 and ranks == RING * SIDE * CORES:
        return partial(fused_body, ranks, columns)
    return body


def solution(mesh):
    placed = (
        P("fsdp", "dp", None),
        P("fsdp", "dp", None),
        P("fsdp", None),
        P("fsdp", "dp"),
        P("fsdp"),
        P("fsdp", None),
        P("fsdp", None),
        P("fsdp"),
        P("fsdp", None),
        P("fsdp", None),
        P("fsdp", None),
        P("fsdp"),
        P("fsdp", None),
        P("fsdp", None),
        P("fsdp", "dp", None),
    )
    return jax.shard_map(
        choose(mesh),
        mesh=mesh,
        in_specs=placed,
        out_specs=(
            P("fsdp", "dp", None),
            P("fsdp", "dp", None),
            P("fsdp", "dp", None),
            P("fsdp"),
            P("fsdp", None),
            P("fsdp", None),
            P("fsdp"),
            P("fsdp", None),
            P("fsdp", None),
            P("fsdp", None),
            P("fsdp"),
            P("fsdp", None),
            P("fsdp", None),
        ),
        check_vma=False,
    )
```

```python
from functools import partial

import jax
import jax.numpy as jnp
from jax import lax
from jax.experimental import pallas as pl
from jax.experimental.pallas import tpu as pltpu
from jax.sharding import PartitionSpec as P

D = 768
HEADS = 12
HEAD_DIM = 64
SUFFIX = 32
PATCH_S = 196
PATCH_L = 576
SLOT_S = 228
SLOT_L = 608
RING = 4
SIDE = 2
CORES = 2
norm_eps = 1e-06
MESH = pl.DeviceIdType.MESH
F32 = jnp.float32
BF16 = jnp.bfloat16
NONE = -1e30


def mm(left, right):
    return jnp.dot(left, right, preferred_element_type=F32)


def mm_nt(left, right):
    return lax.dot_general(left, right, (((1,), (1,)), ((), ())), preferred_element_type=F32)


def mm_tn(left, right):
    return lax.dot_general(left, right, (((0,), (0,)), ((), ())), preferred_element_type=F32)


def normed(value):
    mean = jnp.mean(value, axis=-1, keepdims=True)
    centred = value - mean
    variance = jnp.mean(centred * centred, axis=-1, keepdims=True)
    scale = lax.rsqrt(variance + norm_eps)
    return centred * scale, scale


def norm_back(grad, hat, scale, gain):
    inner = grad * gain
    mean_one = jnp.mean(inner, axis=-1, keepdims=True)
    mean_two = jnp.mean(inner * hat, axis=-1, keepdims=True)
    gain_grad = jnp.sum(grad * hat, axis=0, keepdims=True)
    return scale * (inner - mean_one - hat * mean_two), gain_grad


def gelu_parts(up):
    inner = 0.7978845608 * (up + 0.044715 * up * up * up)
    tanh = jnp.tanh(inner)
    slope = 0.7978845608 * (1.0 + 3.0 * 0.044715 * up * up)
    value = 0.5 * up * (1.0 + tanh)
    grad = 0.5 * (1.0 + tanh) + 0.5 * up * (1.0 - tanh * tanh) * slope
    return value, grad


class Gather:
    def __init__(self, place, view, bulk, sems, at, has=None):
        self.z, self.x, self.c, self.f = place
        self.view, self.bulk = view, bulk
        self.send, self.recv = sems
        self.at = at
        self.has = has
        self.sent = []

    def place_at(self, k):
        return lax.rem(self.z + k + RING, RING)

    def copy(self, ref, target, into, index):
        z, x, c = target
        return pltpu.make_async_remote_copy(
            src_ref=ref,
            dst_ref=ref,
            send_sem=self.send.at[self.at, index],
            recv_sem=self.recv.at[self.at, into],
            device_id=(z * (SIDE * CORES) + x * CORES + c, self.f),
            device_id_type=MESH,
        )

    def holds(self, block, cond):
        return cond if self.has is None else cond & self.has(*block)

    def go(self, block, target, into, cond):
        item = self.copy(self.view(*block), target, into, len(self.sent))
        cond = self.holds(block, cond)
        pl.when(cond)(item.start)
        self.sent.append((cond, item))

    def wait(self, block, into, cond):
        item = self.copy(self.view(*block), (self.z, 1 - self.x, self.c), into, 0)
        pl.when(self.holds(block, cond))(item.wait_recv)

    def line(self, block, up, down, cond):
        z, x, c = self.z, self.x, self.c
        if up:
            self.go(block, (self.place_at(1), x, c), block[0], cond & (z < RING - 1))
        if down:
            self.go(block, (self.place_at(-1), x, c), block[0], cond & (z > 0))

    def across(self, block, cond):
        self.go(block, (self.z, 1 - self.x, self.c), RING + block[0], cond)

    def step_one(self):
        own = (self.z, self.x, self.c)
        self.line(own, True, True, self.z >= 0)
        self.across(own, self.z >= 0)

    def arrive(self, k):
        low, high = (self.place_at(-k), self.x, self.c), (self.place_at(k), self.x, self.c)
        self.wait(low, low[0], self.z >= k)
        self.line(low, True, False, self.z >= k)
        self.wait(high, high[0], self.z < RING - k)
        self.line(high, False, True, self.z < RING - k)
        self.across(low, self.z >= k)
        self.across(high, self.z < RING - k)

    def side(self, k):
        for at, cond in ((self.place_at(-k), self.z >= k), (self.place_at(k), self.z < RING - k))[: 1 if k == 0 else 2]:
            self.wait((at, 1 - self.x, self.c), RING + at, cond)

    def step_two(self):
        self.arrive(1)

    def step_three(self):
        self.arrive(2)
        self.side(0)
        self.side(1)

    def step_four(self):
        self.arrive(3)
        self.hand_over(0)
        self.side(2)

    def step_five(self):
        self.side(3)
        self.hand_over(1)

    def hand_over(self, n):
        item = self.copy(self.bulk(self.c, self.x + n * (1 - 2 * self.x)), (self.z, self.x, 1 - self.c), 2 * RING + n, len(self.sent))
        item.start()
        self.sent.append((self.z >= 0, item))

    def step_six(self):
        for n in range(2):
            ref = self.bulk(1 - self.c, self.x + n * (1 - 2 * self.x))
            self.copy(ref, (self.z, self.x, 1 - self.c), 2 * RING + n, 0).wait_recv()

    def finish(self):
        for cond, item in self.sent:
            pl.when(cond)(item.wait_send)


class ShortGather(Gather):
    def step_one(self):
        own = (self.z, self.x, self.c)
        for k in range(1, RING):
            self.go(own, (self.place_at(k), self.x, self.c), self.z, self.z >= 0)
        self.across(own, self.z >= 0)

    def step_two(self):
        for k in range(1, RING):
            block = (self.place_at(k), self.x, self.c)
            self.wait(block, block[0], self.z >= 0)
            self.across(block, self.z >= 0)
        self.hand_over(0)

    def step_three(self):
        for k in range(RING):
            at = self.place_at(k)
            self.wait((at, 1 - self.x, self.c), RING + at, self.z >= 0)
        self.hand_over(1)


class Spread(Gather):
    def __init__(self, place, theirs, mine, bulk, sems, at):
        super().__init__(place, theirs, bulk, sems, at)
        self.mine = mine
        z, x, c = self.z, self.x, self.c
        always, end = z >= 0, (z == 0) | (z == RING - 1)
        self.opposite = RING - 1 - z
        self.over = (
            ((z, x, c), None, always),
            ((z, 1 - x, c), None, always),
            ((self.opposite, x, c), 1, end),
            ((self.opposite, 1 - x, c), 1, end),
        )
        self.pushed = []

    def over_copy(self, n, view):
        block, part, cond = self.over[n]
        ref = view(*block, part)
        return pltpu.make_async_remote_copy(
            src_ref=ref, dst_ref=ref, send_sem=self.send.at[self.at, 13 + n], recv_sem=self.recv.at[self.at, 10 + n],
            device_id=(self.z * (SIDE * CORES) + self.x * CORES + self.c, 1 - self.f), device_id_type=MESH,
        )

    def push(self):
        for n in range(4):
            item, cond = self.over_copy(n, self.mine), self.over[n][2]
            pl.when(cond)(item.start)
            self.pushed.append((cond, item))

    def landed(self, n):
        pl.when(self.over[n][2])(self.over_copy(n, self.view).wait_recv)

    def step_one(self):
        always = self.z >= 0
        own = (self.z, self.x, self.c)
        self.landed(0)
        self.line(own, True, True, always)

    def step_three(self):
        z, x, c = self.z, self.x, self.c
        low, high = (self.place_at(-2), x, c), (self.place_at(2), x, c)
        self.wait(low, low[0], z >= 2)
        self.go((*low, 0), (self.place_at(1), x, c), low[0], z == RING - 2)
        self.wait(high, high[0], z < RING - 2)
        self.go((*high, 0), (self.place_at(-1), x, c), high[0], z == 1)
        self.across(low, z >= 2)
        self.across(high, z < RING - 2)
        self.side(1)

    def step_four(self):
        z, x, c = self.z, self.x, self.c
        end = (z == 0) | (z == RING - 1)
        block = (self.opposite, x, c, 0)
        self.wait(block, self.opposite, end)
        self.across(block, end)
        self.landed(2)
        self.hand_over(0)
        self.side(2)

    def step_five(self):
        z, x, c = self.z, self.x, self.c
        self.landed(1)
        self.landed(3)
        self.wait((self.opposite, 1 - x, c, 0), RING + self.opposite, (z == 0) | (z == RING - 1))
        self.hand_over(1)

    def finish(self):
        super().finish()
        for cond, item in self.pushed:
            pl.when(cond)(item.wait_send)


class Pieces:
    def __init__(self, count, own_rows):
        self.half = count // 2
        self.edge = self.half * SLOT_S
        self.rows = own_rows
        self.count = count

    def start(self, rank):
        return jnp.where(
            rank < self.half, SLOT_S * rank, self.edge + SLOT_L * (rank - self.half)
        )

    def size(self, rank):
        return jnp.where(rank < self.half, SLOT_S, SLOT_L)

    def rank_of(self, row):
        return jnp.where(
            row < self.edge,
            lax.div(row, SLOT_S),
            self.half + lax.div(jnp.maximum(row - self.edge, 0), SLOT_L),
        )

    def first_rank(self, device):
        return self.rank_of(device * self.rows)

    def last_rank(self, device):
        return self.rank_of(device * self.rows + self.rows - 1)

    def first_device(self, rank):
        return lax.div(self.start(rank), self.rows)

    def last_device(self, rank):
        return lax.div(self.start(rank) + self.size(rank) - 1, self.rows)


SLOTS = 3
UNITS = 16
LANE_QKV, LANE_SO, LANE_CQ, LANE_CKV, LANE_CO, LANE_FI, LANE_FO = 0, 2304, 3072, 3840, 5376, 6144, 9216
OUT_CO, OUT_CKV = 3840, 4608
CHUNKS = ((0, 2304), (2304, 1536), (3840, 1536), (5376, 3072), (8448, 2304), (10752, 1536))
LOADS_BY_CHUNK = ((0,), (1, 2), (3,), (4, 5), (6, 7), (8, 9))
PIECE = 384
UNIT_CHIPS = 6


def layer_kernel(
    ranks,
    columns,
    x_ref, cot_ref, mem_ref, res_ref, pre_ref, gain_one_ref, gain_two_ref, gain_three_ref,
    qkv_ref, so_ref, cq_ref, ckv_ref, co_ref, fi_ref, fo_ref,
    out_ref, grad_ref, memgrad_ref, gain_out_ref, weights_out_ref,
    wb, gb, rl, rr, lb, sb, xb, cb, nb, olr, ob, pb, gainb, memp, kvb, kvg, kp, kr, kc, ky, cp,
    kx, ks, hb, ab, ug, usend_b, urecv_b,
    cqb, qbuf, osend, ostat_send, obuf, ostat, dob, dstat_b, dobuf, dstat, dqsend, dqbuf, gmine, gpeer,
    load_sem, wsend, wrecv, gsend, grecv, ssend, srecv, bsend, brecv, gain_sem, asend, arecv, fsend, frecv, ysend, yrecv, psend, precv, usend, urecv,
    ksend, krecv,
):
    me = lax.axis_index("dp")
    f = lax.axis_index("fsdp")
    z = lax.div(me, SIDE * CORES)
    x = lax.rem(lax.div(me, CORES), SIDE)
    c = lax.rem(me, CORES)
    seat = x * RING + z
    chips = ranks // CORES
    place = (z, x, c, f)
    half_rows = D // columns
    slab = half_rows // chips
    own_rows = mem_ref.shape[0]
    padded = memp.shape[0]
    lay = Pieces(ranks, own_rows)
    other = 1 - f
    mate = (z * (SIDE * CORES) + x * CORES + (1 - c), f)
    everyone = ranks * columns
    lin = f * ranks + me

    loads = []

    def load(src, lane, width):
        item = pltpu.make_async_copy(
            src, wb.at[pl.ds(pl.multiple_of(f * half_rows, 128), half_rows), pl.ds(lane, width)],
            load_sem.at[len(loads)],
        )
        item.start()
        loads.append(item)

    load(qkv_ref, LANE_QKV, 3 * D)
    load(so_ref, LANE_SO, D)
    load(cq_ref, LANE_CQ, D)
    load(ckv_ref, LANE_CKV, 2 * D)
    load(co_ref, LANE_CO, D)
    load(fi_ref, LANE_FI, 4 * D)
    for j in range(4):
        load(fo_ref.at[pl.ds(j * half_rows, half_rows)], LANE_FO + D * j, D)

    for s in range(SLOTS):
        qbuf[s] = jnp.zeros_like(qbuf[s])
        obuf[s] = jnp.zeros_like(obuf[s])
        ostat[s] = jnp.where(lax.broadcasted_iota(jnp.int32, ostat.shape[1:], 1) < 64, NONE, 0.0)
        dobuf[s] = jnp.zeros_like(dobuf[s])
        dstat[s] = jnp.zeros_like(dstat[s])
        dqbuf[s] = jnp.zeros_like(dqbuf[s])

    def rows_of(device):
        return pl.ds(pl.multiple_of(device * SUFFIX, SUFFIX), SUFFIX)

    def slot_of(device):
        side = lax.rem(lax.div(device, CORES), SIDE)
        return lax.rem(device, CORES) * chips + side * RING + lax.div(device, SIDE * CORES)

    my_slot = slot_of(me)
    xb[my_slot] = x_ref[...]
    cb[my_slot] = cot_ref[...].astype(BF16)
    pb[my_slot] = jnp.full((8, 128), pre_ref[0, 0].astype(F32), F32)
    for n, ref in enumerate((gain_one_ref, gain_two_ref, gain_three_ref)):
        values = ref[...].astype(F32).reshape(1, half_rows)
        for j in range(half_rows // 128):
            at = n * (half_rows // 128) + j
            gainb[f, at : at + 1] = values[:, 128 * j : 128 * (j + 1)]

    barrier = pltpu.get_barrier_semaphore()

    def greet(i, carry):
        to = lax.rem(me + i, ranks)
        pl.semaphore_signal(barrier, inc=1, device_id=(to, f), device_id_type=MESH)
        return carry

    lax.fori_loop(1, ranks, greet, 0)
    pl.semaphore_signal(barrier, inc=1, device_id=(me, other), device_id_type=MESH)
    pl.semaphore_wait(barrier, ranks)

    y_items = []

    def push_y(src, dst, at):
        item = pltpu.make_async_remote_copy(
            src_ref=src, dst_ref=dst, send_sem=ysend.at[at], recv_sem=yrecv.at[at],
            device_id=(me, other), device_id_type=MESH,
        )
        item.start()
        y_items.append(item)
        return item

    class Tell:
        def __init__(self, ref, at):
            self.ref, self.at = ref, at

        def copy(self, source, index, to):
            return pltpu.make_async_remote_copy(
                src_ref=self.ref.at[slot_of(source)], dst_ref=self.ref.at[slot_of(source)], send_sem=bsend.at[self.at, index],
                recv_sem=brecv.at[self.at, source], device_id=(to, f), device_id_type=MESH,
            )

        def start(self):
            def one(i, carry):
                self.copy(me, i, lax.rem(me + i, ranks)).start()
                return carry

            lax.fori_loop(1, ranks, one, 0)

        def wait(self):
            def one(i, carry):
                source = lax.rem(me + i, ranks)
                self.copy(source, i, source).wait_recv()
                return carry

            lax.fori_loop(1, ranks, one, 0)

        def finish(self):
            def one(i, carry):
                self.copy(me, i, lax.rem(me + i, ranks)).wait_send()
                return carry

            lax.fori_loop(1, ranks, one, 0)

    def slab_view(first, width, rows_from):
        half = width // CORES

        cut = (half // 256) * 128

        def view(zz, xx, cc, part=None):
            low, size = {None: (0, half), 0: (0, half - cut), 1: (half - cut, cut)}[part]
            row = pl.multiple_of(rows_from * half_rows + (xx * RING + zz) * slab, 16)
            lane = pl.multiple_of(first + cc * half + low, 128)
            return wb.at[pl.ds(row, slab), pl.ds(lane, size)]

        return view

    def block_view(ref):
        def view(zz, xx, cc):
            return ref.at[cc * chips + xx * RING + zz]

        return view

    def block_bulk(ref):
        return lambda cc, xx: ref.at[pl.ds(cc * chips + xx * RING, RING)]

    def token_rows(col, cc, at):
        return pl.ds(pl.multiple_of(((col * CORES + cc) * chips + at) * SUFFIX, SUFFIX), SUFFIX)

    def token_view(ref):
        def view(zz, xx, cc):
            return ref.at[token_rows(f, cc, xx * RING + zz)]

        return view

    def token_bulk(ref):
        rows = RING * SUFFIX
        return lambda cc, xx: ref.at[pl.ds(pl.multiple_of(((f * CORES + cc) * SIDE + xx) * rows, rows), rows)]

    def chunk_bulk(first, width):
        half = width // CORES
        rows = RING * slab

        def bulk(cc, xx):
            row = pl.multiple_of(other * half_rows + xx * rows, 16)
            return wb.at[pl.ds(row, rows), pl.ds(pl.multiple_of(first + cc * half, 128), half)]

        return bulk

    plane = pl.ds(pl.multiple_of((f * CORES + c) * chips * SUFFIX, SUFFIX), chips * SUFFIX)
    plane_in = pl.ds(pl.multiple_of((other * CORES + c) * chips * SUFFIX, SUFFIX), chips * SUFFIX)
    plane_mate = pl.ds(pl.multiple_of((other * CORES + 1 - c) * chips * SUFFIX, SUFFIX), chips * SUFFIX)

    class Across:
        def __init__(self, ref, at):
            self.ref, self.at = ref, at

        def copy(self, rows, n, to):
            ref = self.ref.at[rows]
            return pltpu.make_async_remote_copy(
                src_ref=ref, dst_ref=ref, send_sem=asend.at[self.at, n], recv_sem=arecv.at[self.at, n],
                device_id=to, device_id_type=MESH,
            )

        def start(self):
            self.copy(plane, 0, (me, other)).start()

        def relay(self):
            self.copy(plane_in, 0, (me, other)).wait_recv()
            self.copy(plane_in, 1, mate).start()

        def wait(self):
            self.copy(plane_mate, 1, mate).wait_recv()

        def finish(self):
            self.copy(plane, 0, (me, other)).wait_send()
            self.copy(plane_in, 1, mate).wait_send()

    sems, short_sems = (gsend, grecv), (ssend, srecv)
    ag_x = Gather(place, block_view(xb), block_bulk(xb), sems, 0)
    ag_c = Gather(place, block_view(cb), block_bulk(cb), sems, 1)
    ag_n = ShortGather(place, token_view(nb), token_bulk(nb), short_sems, 0)
    tell_p = Tell(pb, 0)
    spread = [
        Spread(place, slab_view(first, width, other), slab_view(first, width, f), chunk_bulk(first, width), (wsend, wrecv), n)
        for n, (first, width) in enumerate(CHUNKS)
    ]

    def push_chunk(n):
        for i in LOADS_BY_CHUNK[n]:
            loads[i].wait()
        spread[n].push()

    ag_x.step_one()
    push_chunk(0)
    gain_item = push_y(gainb.at[f], gainb.at[f], 0)
    tell_p.start()
    push_chunk(1)

    def tick(n):
        for age, act in ((4, "step_five"), (3, "step_four"), (2, "step_three"), (1, "step_two"), (0, "step_one")):
            if 0 <= n - age < len(spread):
                getattr(spread[n - age], act)()
        if n + 2 < len(spread):
            push_chunk(n + 2)

    ag_x.step_two()
    tick(0)
    ag_x.step_three()
    tick(1)
    ag_x.step_four()
    tick(2)
    ag_x.step_five()
    ag_x.step_six()
    tick(3)
    gain_item.wait_recv()

    memp[0:own_rows] = mem_ref[...]
    memp[own_rows:padded] = jnp.zeros((padded - own_rows, D), BF16)

    positions = []
    before_large = jnp.int32(0)
    mine_rank = jnp.int32(0)
    for i in range(ranks):
        group = res_ref[0, i]
        spot = jnp.where(group == 1, lay.half + before_large, i - before_large)
        positions.append(spot)
        mine_rank = jnp.where(me == i, spot, mine_rank)
        before_large = before_large + group

    spots = [i // CORES % SIDE * RING + i // (SIDE * CORES) for i in range(ranks)]
    slots = [(i % CORES) * chips + spots[i] for i in range(ranks)]

    def example_of(rank):
        found = jnp.int32(0)
        for i in range(ranks):
            found = jnp.where(positions[i] == rank, slots[i], found)
        return found

    by_rank = [example_of(r) for r in range(ranks)]
    out_slot = jnp.int32(0)
    for i in range(ranks):
        out_slot = jnp.where(mine_rank == i, slots[i], out_slot)

    tiles = half_rows // 128
    gain = [
        jnp.concatenate([gainb[i, tiles * n + j : tiles * n + j + 1] for i in range(columns) for j in range(tiles)], axis=1)
        for n in range(3)
    ]

    mine = example_of(me)
    resid = xb[mine]
    hat_one, rs_one = normed(resid)
    n1 = (hat_one * gain[0]).astype(BF16)

    lanes = lax.broadcasted_iota(jnp.int32, (1, 256), 1)
    head_f32 = [(lax.div(lanes, HEAD_DIM) == h).astype(F32) for h in range(4)]
    head_b16 = [m.astype(BF16) for m in head_f32]

    def stack(value):
        return jnp.concatenate([value * m for m in head_b16], axis=0)

    def unstack(value):
        rows = value.shape[0] // 4
        total = value[0:rows] * head_f32[0]
        for h in range(1, 4):
            total = total + value[h * rows : (h + 1) * rows] * head_f32[h]
        return total

    tick(4)
    ag_c.step_one()
    spread[0].step_six()
    q = mm(n1, wb[:, 0:D]).astype(BF16)
    k = mm(n1, wb[:, D : 2 * D]).astype(BF16)
    v = mm(n1, wb[:, 2 * D : 3 * D]).astype(BF16)
    scale = HEAD_DIM**-0.5
    qs = (q.astype(F32) * scale).astype(BF16)
    row_at = lax.broadcasted_iota(jnp.int32, (SUFFIX, SUFFIX), 0)
    col_at = lax.broadcasted_iota(jnp.int32, (SUFFIX, SUFFIX), 1)
    causal = jnp.concatenate([(row_at >= col_at).astype(F32)] * 4, axis=0) > 0.0
    self_p = []
    mixed = []
    for g in range(3):
        sl = slice(256 * g, 256 * g + 256)
        s = mm_nt(stack(qs[:, sl]), k[:, sl])
        s = jnp.where(causal, s, NONE)
        e = jnp.exp(s - jnp.max(s, axis=-1, keepdims=True))
        p = e / jnp.sum(e, axis=-1, keepdims=True)
        self_p.append(p)
        mixed.append(unstack(mm(p.astype(BF16), v[:, sl])))
    sm = jnp.concatenate(mixed, axis=1).astype(BF16)

    tick(5)
    ag_c.step_two()
    spread[1].step_six()
    after_self = resid + mm(sm, wb[:, LANE_SO : LANE_SO + D])
    hat_two, rs_two = normed(after_self)
    n2 = (hat_two * gain[1]).astype(BF16)
    cq = mm(n2, wb[:, LANE_CQ : LANE_CQ + D]).astype(BF16)
    cqb[...] = cq

    my_first, my_last = lay.first_device(me), lay.last_device(me)
    held_first, held_last = lay.first_rank(me), lay.last_rank(me)

    def piece_copy(src, dst, at, sent, landed, target):
        return pltpu.make_async_remote_copy(
            src_ref=src, dst_ref=dst, send_sem=psend.at[at, sent], recv_sem=precv.at[at, landed],
            device_id=(target, f), device_id_type=MESH,
        )

    def to_holders(pairs):
        for i in range(SLOTS):
            target = my_first + i
            slot = me - lay.first_rank(target)
            there = target <= my_last

            @pl.when(there & (target == me))
            def _():
                for src, dst, at in pairs:
                    dst[slot] = src[...]

            @pl.when(there & (target != me))
            def _():
                for src, dst, at in pairs:
                    piece_copy(src, dst.at[slot], at, i, slot, target).start()

    def to_holders_sent(pairs):
        for i in range(SLOTS):
            target = my_first + i

            @pl.when((target <= my_last) & (target != me))
            def _():
                for src, dst, at in pairs:
                    piece_copy(src, dst.at[0], at, i, 0, target).wait_send()

    def at_holders(pairs):
        for s in range(SLOTS):
            rank = held_first + s

            @pl.when((rank <= held_last) & (rank != me))
            def _():
                for src, dst, at in pairs:
                    piece_copy(src, dst.at[s], at, 0, s, rank).wait_recv()

    def to_owners(pairs):
        for s in range(SLOTS):
            rank = held_first + s
            index = me - lay.first_device(rank)
            there = rank <= held_last

            @pl.when(there & (rank == me))
            def _():
                for src, dst, at in pairs:
                    dst[index] = src[s]

            @pl.when(there & (rank != me))
            def _():
                for src, dst, at in pairs:
                    piece_copy(src.at[s], dst.at[index], at, s, index, rank).start()

    def to_owners_sent(pairs):
        for s in range(SLOTS):
            rank = held_first + s

            @pl.when((rank <= held_last) & (rank != me))
            def _():
                for src, dst, at in pairs:
                    piece_copy(src.at[s], dst.at[0], at, s, 0, rank).wait_send()

    def at_owners(pairs):
        for i in range(SLOTS):
            target = my_first + i

            @pl.when((target <= my_last) & (target != me))
            def _():
                for src, dst, at in pairs:
                    piece_copy(src.at[0], dst.at[i], at, 0, i, target).wait_recv()

    q_pairs = [(cqb, qbuf, 0)]
    o_pairs = [(osend, obuf, 1), (ostat_send, ostat, 2)]
    d_pairs = [(dob, dobuf, 3), (dstat_b, dstat, 4)]
    dq_pairs = [(dqsend, dqbuf, 5)]

    to_holders(q_pairs)

    tick(6)
    ag_c.step_three()
    spread[2].step_six()


    def kv_step(i, carry):
        lane = pl.multiple_of(i * 256, 256)
        kvb[:, pl.ds(lane, 256)] = mm(memp[...], wb[:, pl.ds(LANE_CKV + lane, 256)]).astype(BF16)
        return carry

    lax.fori_loop(0, 6, kv_step, 0)

    tell_p.wait()
    lane_f = lax.broadcasted_iota(jnp.int32, (SUFFIX, padded), 1).astype(F32)
    allowed = []
    for s in range(SLOTS):
        rank = held_first + s
        ok = rank <= held_last
        example = example_of(jnp.minimum(rank, ranks - 1))
        prefix = pb[example][0:1, 0:1]
        low = (lay.start(rank) - me * own_rows).astype(F32)
        patches = jnp.where(rank < lay.half, PATCH_S, PATCH_L).astype(F32)
        high = jnp.minimum(low + patches + prefix, jnp.float32(own_rows))
        high = jnp.where(ok, high, jnp.float32(-1.0))
        allowed.append(((lane_f >= low) & (lane_f < high)).astype(F32))
    allowed = jnp.concatenate(allowed * 4, axis=0) > 0.0

    at_holders(q_pairs)
    qh = jnp.concatenate([qbuf[s] for s in range(SLOTS)], axis=0)
    qh = (qh.astype(F32) * scale).astype(BF16)
    lane_c = lax.broadcasted_iota(jnp.int32, (SUFFIX, 128), 1)
    def swap(tile):
        return jnp.concatenate([tile[:, 64:], tile[:, :64]], axis=1)

    top_c = [jnp.zeros((SUFFIX, 128), F32) for _ in range(SLOTS)]
    sum_c = [jnp.zeros((SUFFIX, 128), F32) for _ in range(SLOTS)]
    for g in range(3):
        sl = slice(256 * g, 256 * g + 256)
        s = mm_nt(stack(qh[:, sl]), kvb[:, sl])
        s = jnp.where(allowed, s, NONE)
        top = jnp.max(s, axis=-1, keepdims=True)
        e = jnp.where(allowed, jnp.exp(s - top), 0.0)
        total = jnp.sum(e, axis=-1, keepdims=True)
        o = mm(e.astype(BF16), kvb[:, D + 256 * g : D + 256 * g + 256])
        o = o * jnp.where(total > 0.0, 1.0 / jnp.where(total > 0.0, total, 1.0), 0.0)
        o = unstack(o).astype(BF16)
        for n in range(SLOTS):
            osend[n, :, sl] = o[n * SUFFIX : (n + 1) * SUFFIX]
            for h in range(4):
                at = h * SLOTS * SUFFIX + n * SUFFIX
                hit = lane_c == 4 * g + h
                top_c[n] = jnp.where(hit, top[at : at + SUFFIX], top_c[n])
                sum_c[n] = jnp.where(hit, total[at : at + SUFFIX], sum_c[n])
    for n in range(SLOTS):
        ostat_send[n] = jnp.where(lane_c < 64, top_c[n], swap(sum_c[n]))
    to_owners(o_pairs)

    tick(7)
    ag_c.step_four()
    at_owners(o_pairs)
    spread[3].step_six()

    def expand(compact):
        low = lane_c < HEAD_DIM
        return jnp.concatenate(
            [jnp.where(low, compact[:, 2 * t : 2 * t + 1], compact[:, 2 * t + 1 : 2 * t + 2]) for t in range(6)],
            axis=1,
        )

    tops = [ostat[i] for i in range(SLOTS)]
    top_all = jnp.maximum(jnp.maximum(tops[0], tops[1]), tops[2])
    shares = [jnp.where(lane_c < 64, swap(tops[i]) * jnp.exp(tops[i] - top_all), 0.0) for i in range(SLOTS)]
    whole = shares[0] + shares[1] + shares[2]
    whole = jnp.where(whole > 0.0, whole, 1.0)
    lse = top_all + jnp.log(whole)
    cross = jnp.zeros((SUFFIX, D), F32)
    for i in range(SLOTS):
        cross = cross + expand(shares[i] / whole) * obuf[i].astype(F32)
    cm = cross.astype(BF16)

    after_cross = after_self + mm(cm, wb[:, LANE_CO : LANE_CO + D])
    hat_three, rs_three = normed(after_cross)
    n3 = (hat_three * gain[2]).astype(BF16)
    nb[token_rows(f, c, seat)] = n3
    ag_n.step_one()

    tick(8)
    ag_c.step_five()
    tick(9)
    spread[4].step_six()
    acts, slopes = [], []
    for j in range(4):
        value, slope = gelu_parts(mm(n3, wb[:, LANE_FI + D * j : LANE_FI + D * (j + 1)]))
        acts.append(value.astype(BF16))
        slopes.append(slope)
    act = jnp.concatenate(acts, axis=1)
    ag_c.step_six()
    for r in range(ranks):
        olr[token_rows(f, r % CORES, spots[r])] = cb[by_rank[r]]
    across_o = Across(olr, 0)
    across_n = Across(nb, 1)
    across_o.start()
    spread[5].step_six()
    unit_items = []

    def unit_device(unit, j):
        at = unit + 1
        return at % RING * (SIDE * CORES) + at // RING * CORES + j

    def push_part(which, at, to, src, dst):
        @pl.when(me == to)
        def _():
            dst[...] = src[...]

        @pl.when(me != to)
        def _():
            pltpu.make_async_remote_copy(
                src_ref=src, dst_ref=dst, send_sem=usend.at[which, at],
                recv_sem=urecv.at[which, me], device_id=(to, f), device_id_type=MESH,
            ).start()

        unit_items.append((which, at, to, src, dst))

    def push_left(units, at, left):
        lb[at] = left
        for unit in units:
            for j in range(CORES):
                lanes = pl.ds(j * PIECE, PIECE)
                push_part(0, CORES * unit + j, unit_device(unit, j), lb.at[at, :, lanes], rl.at[rows_of(me), lanes])

    def push_right(unit, right):
        for j in range(CORES):
            sb[unit, j] = right[:, j * PIECE : (j + 1) * PIECE]
            push_part(1, CORES * unit + j, unit_device(unit, j), sb.at[unit, j], rr.at[rows_of(me)])

    out_low = cb[mine]
    cot = out_low.astype(F32)
    hidden_grad = [mm_nt(out_low, wb[:, LANE_FO + D * j : LANE_FO + D * (j + 1)]) for j in range(4)]

    def by_hidden(j):
        parts = []
        for t in range(D // half_rows):
            at = D * j + t * half_rows
            col, unit = at // (4 * half_rows), (at % (4 * half_rows)) // half_rows
            parts.append(hidden_grad[unit][:, col * half_rows : (col + 1) * half_rows])
        return jnp.concatenate(parts, axis=1)

    n3_grad = jnp.zeros((SUFFIX, D), F32)
    for j in range(4):
        part = (by_hidden(j) * slopes[j]).astype(BF16)
        n3_grad = n3_grad + mm_nt(part, wb[:, LANE_FI + D * j : LANE_FI + D * (j + 1)])

    ag_n.step_two()
    part, ffn_gain_grad = norm_back(n3_grad, hat_three, rs_three, gain[2])
    cross_res = cot + part
    cross_low = cross_res.astype(BF16)
    d_mixed = mm_nt(cross_low, wb[:, LANE_CO : LANE_CO + D]).astype(BF16)
    dob[...] = d_mixed
    prod = d_mixed.astype(F32) * cross
    delta = jnp.zeros((SUFFIX, 128), F32)
    for t in range(6):
        tile = prod[:, 128 * t : 128 * (t + 1)]
        left = jnp.sum(jnp.where(lane_c < HEAD_DIM, tile, 0.0), axis=-1, keepdims=True)
        right = jnp.sum(jnp.where(lane_c < HEAD_DIM, 0.0, tile), axis=-1, keepdims=True)
        delta = jnp.where(lane_c == 2 * t, left, delta)
        delta = jnp.where(lane_c == 2 * t + 1, right, delta)
    dstat_b[...] = jnp.where(lane_c < 64, lse, swap(delta))
    to_holders(d_pairs)
    push_left((0, 1, 2), 0, n1)
    down = jnp.zeros((SUFFIX, D), F32)
    for j in range(4):
        lhs = jnp.concatenate(
            [act[:, i * 4 * half_rows + j * half_rows : i * 4 * half_rows + (j + 1) * half_rows] for i in range(columns)],
            axis=1,
        )
        down = down + mm(lhs, wb[:, LANE_FO + D * j : LANE_FO + D * (j + 1)])
    ob[0, my_slot] = (after_cross + down).astype(BF16)
    ag_out = ShortGather(place, block_view(ob.at[0]), block_bulk(ob.at[0]), short_sems, 1)
    ag_out.step_one()

    at_holders(d_pairs)

    push_left((4,), 2, n2)
    push_left((3,), 1, sm)
    doh = jnp.concatenate([dobuf[s] for s in range(SLOTS)], axis=0)
    for g in range(3):
        sl = slice(256 * g, 256 * g + 256)
        kg = kvb[:, sl]
        vg = kvb[:, D + 256 * g : D + 256 * g + 256]
        q4 = stack(qh[:, sl])
        do4 = stack(doh[:, sl])
        lse_col = jnp.concatenate([dstat[n][:, 4 * g + h : 4 * g + h + 1] for h in range(4) for n in range(SLOTS)], axis=0)
        del_col = jnp.concatenate([dstat[n][:, 64 + 4 * g + h : 65 + 4 * g + h] for h in range(4) for n in range(SLOTS)], axis=0)
        s = mm_nt(q4, kg)
        p = jnp.where(allowed, jnp.exp(jnp.where(allowed, s - lse_col, 0.0)), 0.0)
        dp = mm_nt(do4, vg)
        ds = (p * (dp - del_col)).astype(BF16)
        kvg[:, D + 256 * g : D + 256 * g + 256] = mm_tn(p.astype(BF16), do4).astype(BF16)
        kvg[:, sl] = mm_tn(ds, q4).astype(BF16)
        dq = unstack(mm(ds, kg)) * scale
        for n in range(SLOTS):
            dqsend[n, :, sl] = dq[n * SUFFIX : (n + 1) * SUFFIX].astype(BF16)
    to_owners(dq_pairs)
    ag_n.step_three()
    across_n.start()
    def kp_step(i, carry):
        lane = pl.multiple_of(i * 256, 256)
        kp[:, pl.ds(lane, 256)] = mm_tn(memp[...], kvg[:, pl.ds(lane, 256)]).astype(BF16)
        return carry

    lax.fori_loop(0, 6, kp_step, 0)
    kr_item = pltpu.make_async_remote_copy(
        src_ref=kp.at[pl.ds(pl.multiple_of((1 - c) * half_rows, 128), half_rows)], dst_ref=kr,
        send_sem=ksend.at[2 * chips], recv_sem=krecv.at[chips], device_id=mate, device_id_type=MESH,
    )
    kr_item.start()

    across_o.relay()
    ag_out.step_two()
    at_owners(dq_pairs)
    push_left((5,), 3, cm)
    push_right(5, cross_low)
    kr_item.wait_recv()
    kc[...] = (
        kp[pl.ds(pl.multiple_of(c * half_rows, 128), half_rows)].astype(F32) + kr[...].astype(F32)
    ).astype(BF16)
    half_slabs = half_rows // SIDE

    def ky_copy(j):
        lanes = pl.ds(j * D, D)
        return pltpu.make_async_remote_copy(
            src_ref=kc.at[:, lanes], dst_ref=ky.at[:, lanes], send_sem=ksend.at[2 * chips + 1 + j],
            recv_sem=krecv.at[chips + 1 + j], device_id=(me, other), device_id_type=MESH,
        )

    def kx_copy(j):
        lanes = pl.ds(j * D, D)
        return pltpu.make_async_remote_copy(
            src_ref=kc.at[pl.ds(pl.multiple_of((1 - x) * half_slabs, 16), half_slabs), lanes], dst_ref=kx.at[:, lanes],
            send_sem=ksend.at[2 * chips + 3 + j], recv_sem=krecv.at[chips + 3 + j],
            device_id=(z * (SIDE * CORES) + (1 - x) * CORES + c, f), device_id_type=MESH,
        )

    @pl.when(c != f)
    def _():
        ky_copy(0).start()
        ky_copy(1).start()

    cqg = (dqbuf[0].astype(F32) + dqbuf[1].astype(F32) + dqbuf[2].astype(F32)).astype(BF16)
    n2_grad = mm_nt(cqg, wb[:, LANE_CQ : LANE_CQ + D])
    part, cross_gain_grad = norm_back(n2_grad, hat_two, rs_two, gain[1])
    self_res = cross_res + part
    self_low = self_res.astype(BF16)
    dmix = mm_nt(self_low, wb[:, LANE_SO : LANE_SO + D]).astype(BF16)
    dqs, dks, dvs = [], [], []
    for g in range(3):
        sl = slice(256 * g, 256 * g + 256)
        q4 = stack(qs[:, sl])
        do4 = stack(dmix[:, sl])
        p = self_p[g]
        dp = mm_nt(do4, v[:, sl])
        ds = (p * (dp - jnp.sum(p * dp, axis=-1, keepdims=True))).astype(BF16)
        dvs.append(mm_tn(p.astype(BF16), do4))
        dks.append(mm_tn(ds, q4))
        dqs.append(unstack(mm(ds, k[:, sl])) * scale)
    packed_grad = [jnp.concatenate(parts, axis=1).astype(BF16) for parts in (dqs, dks, dvs)]
    for j in range(3):
        push_right(j, packed_grad[j])
    push_right(4, cqg)
    push_right(3, self_low)

    n1_grad = jnp.zeros((SUFFIX, D), F32)
    for j in range(3):
        n1_grad = n1_grad + mm_nt(packed_grad[j], wb[:, D * j : D * (j + 1)])
    part, self_gain_grad = norm_back(n1_grad, hat_one, rs_one, gain[0])
    ob[1, my_slot] = (self_res + part).astype(BF16)
    ag_grad = ShortGather(place, block_view(ob.at[1]), block_bulk(ob.at[1]), short_sems, 2)
    gmine[0] = jnp.concatenate(
        [self_gain_grad, cross_gain_grad, ffn_gain_grad, jnp.zeros((5, D), F32)], axis=0
    )
    partners = (
        mate,
        (me, other),
        (z * (SIDE * CORES) + (1 - x) * CORES + c, f),
        ((z + 1 - 2 * lax.rem(z, 2)) * (SIDE * CORES) + x * CORES + c, f),
        (lax.rem(z + 2, RING) * (SIDE * CORES) + x * CORES + c, f),
    )

    def gain_copy(k):
        return pltpu.make_async_remote_copy(
            src_ref=gmine.at[k], dst_ref=gpeer.at[k], send_sem=gain_sem.at[0, k], recv_sem=gain_sem.at[1, k],
            device_id=partners[k], device_id_type=MESH,
        )

    def gain_step(k):
        gain_copy(k - 1).wait_recv()
        total = gmine[k - 1] + gpeer[k - 1]
        if k == len(partners):
            return total
        gmine[k] = total
        gain_copy(k).start()

    gain_copy(0).start()
    ag_grad.step_one()
    ag_out.step_three()

    ag_n.step_six()
    across_n.relay()
    across_o.wait()
    across_n.wait()

    rows_step = 128
    hidden = [col * 4 * half_rows + D * c for col in range(columns)]

    def ffn_rows(first, last):
        def one(i, carry):
            at = pl.ds(pl.multiple_of(i * rows_step, rows_step), rows_step)
            for col in range(columns):
                lane = pl.multiple_of(LANE_FI + hidden[col], 128)
                value, slope = gelu_parts(mm(nb[at], wb[:, pl.ds(lane, D)]))

                @pl.when(f == col)
                def _():
                    ab[at] = value.astype(BF16)

                back = []
                for t in range(CORES):
                    lane_o = pl.multiple_of(LANE_FO + D * (2 * c + t), 128)
                    back.append(mm_nt(olr[at], wb[col * half_rows : (col + 1) * half_rows, pl.ds(lane_o, D)]))
                hb[col, at] = (jnp.concatenate(back, axis=1) * slope).astype(BF16)
            return carry

        lax.fori_loop(first, last, one, 0)

    own_lanes = pl.ds(pl.multiple_of(f * half_rows, 128), half_rows)

    def ffn_in_sum(col):
        lane = pl.multiple_of(LANE_FI + hidden[col], 128)
        for part in range(0, D, PIECE):
            total = mm_tn(nb[:, own_lanes], hb[col, :, part : part + PIECE])
            gb[:, pl.ds(lane + part, PIECE)] = total.astype(BF16)

    def ffn_out_sum(t):
        lane = pl.multiple_of(LANE_FO + D * (2 * c + t), 128)
        for part in range(0, D, PIECE):
            total = mm_tn(ab[:, t * half_rows : (t + 1) * half_rows], olr[:, part : part + PIECE])
            gb[:, pl.ds(lane + part, PIECE)] = total.astype(BF16)

    f_items = []

    def to_mate(lane, width):
        ref = gb.at[:, pl.ds(pl.multiple_of(lane, 128), width)]
        item = pltpu.make_async_remote_copy(
            src_ref=ref, dst_ref=ref, send_sem=fsend.at[len(f_items)], recv_sem=frecv.at[len(f_items)],
            device_id=mate, device_id_type=MESH,
        )
        item.start()
        f_items.append(item)

    has_unit = (seat >= 1) & (seat <= UNIT_CHIPS)

    def unit_lane(n, cc):
        return PIECE * (n - 1) + UNIT_CHIPS * PIECE * cc

    def unit_take(which, src, dst):
        def take(i, carry):
            @pl.when(i != me)
            def _():
                pltpu.make_async_remote_copy(
                    src_ref=src, dst_ref=dst(i), send_sem=usend.at[which, 0],
                    recv_sem=urecv.at[which, i], device_id=mate, device_id_type=MESH,
                ).wait_recv()

            return carry

        lax.fori_loop(0, ranks, take, 0)

    def left_lanes(core):
        return pl.ds(pl.multiple_of(core * PIECE, 128), PIECE)

    def left_copy(core):
        ref = rl.at[:, left_lanes(core)]
        return pltpu.make_async_remote_copy(
            src_ref=ref, dst_ref=ref, send_sem=ysend.at[1], recv_sem=yrecv.at[1], device_id=mate, device_id_type=MESH,
        )

    def unit_left(pred):
        @pl.when(pred)
        def _():
            unit_take(0, lb.at[0, :, pl.ds(0, PIECE)], lambda i: rl.at[rows_of(i), left_lanes(c)])
            left_copy(c).start()

    def unit_rows(n):
        return pl.ds(n * (half_rows // 2), half_rows // 2)

    def unit_copy(n):
        rows = unit_rows(n)
        return pltpu.make_async_remote_copy(
            src_ref=usend_b.at[rows], dst_ref=urecv_b.at[rows], send_sem=ysend.at[3 + n], recv_sem=yrecv.at[3 + n],
            device_id=(me, other), device_id_type=MESH,
        )

    def unit_sum(pred):
        @pl.when(pred)
        def _():
            unit_take(1, sb.at[0, 0], lambda i: rr.at[rows_of(i)])
            left_copy(1 - c).wait_recv()
            for col in range(columns):
                ug[col] = mm_tn(rl[:, col * half_rows : (col + 1) * half_rows], rr[...])
            usend_b[...] = ug[other].astype(BF16)
            for n in range(2):
                unit_copy(n).start()

    def unit_join(pred, n):
        @pl.when(pred)
        def _():
            unit_copy(n).wait_recv()
            rows = unit_rows(n)
            gb[rows, pl.ds(pl.multiple_of(unit_lane(seat, c), 128), PIECE)] = (
                ug[f, rows] + urecv_b[rows].astype(F32)
            ).astype(BF16)

    def has_block(zz, xx, cc):
        n = xx * RING + zz
        return (n >= 1) & (n <= UNIT_CHIPS)

    def unit_bulk(rows):
        width = UNIT_CHIPS * PIECE // SIDE
        return lambda cc, xx: gb.at[rows, pl.ds(pl.multiple_of(width * (SIDE * cc + xx), 128), width)]

    def gb_view(lane_of, rows):
        def view(zz, xx, cc):
            return gb.at[rows, pl.ds(pl.multiple_of(lane_of(xx * RING + zz, cc), 128), PIECE)]

        return view

    class UnitGather:
        def __init__(self):
            parts = [unit_rows(n) for n in range(2)]
            self.gathers = [
                Gather(place, gb_view(unit_lane, rows), unit_bulk(rows), sems, at, has_block)
                for at, rows in zip((2, 3), parts)
            ]

        def step(self, name):
            for gather in self.gathers:
                getattr(gather, name)()

    ag_u = UnitGather()

    k_items = []

    def k_copy(t, j):
        return pltpu.make_async_remote_copy(
            src_ref=ks.at[pl.ds(t * slab, slab), pl.ds(j * D, D)], dst_ref=cp.at[z],
            send_sem=ksend.at[t * CORES + j], recv_sem=krecv.at[z],
            device_id=(t * (SIDE * CORES) + x * CORES + j, f), device_id_type=MESH,
        )

    def k_over_x(j):
        lanes = pl.ds(j * D, D)

        @pl.when(c == f)
        def _():
            ky_copy(j).wait_recv()
            kc[:, lanes] = (kc[:, lanes].astype(F32) + ky[:, lanes].astype(F32)).astype(BF16)
            kx_copy(j).start()

    def k_on_line(j):
        lanes = pl.ds(j * D, D)

        @pl.when(c == f)
        def _():
            kx_copy(j).wait_recv()
            ks[:, lanes] = (
                kc[pl.ds(pl.multiple_of(x * half_slabs, 16), half_slabs), lanes].astype(F32) + kx[:, lanes].astype(F32)
            ).astype(BF16)

        for t in range(RING):
            here = (z == t) & (c == j)

            @pl.when((c == f) & here)
            def _():
                cp[z] = ks[t * slab : (t + 1) * slab, j * D : (j + 1) * D]

            @pl.when((c == f) & jnp.logical_not(here))
            def _():
                k_copy(t, j).start()

            k_items.append((t, j, here))

    k_over_x(0)
    ffn_rows(0, 2)
    gain_step(1)
    unit_left(has_unit)
    k_on_line(0)
    k_over_x(1)
    unit_sum(has_unit)
    ffn_rows(2, 4)
    gain_step(2)
    k_on_line(1)
    unit_join(has_unit, 0)
    ag_u.gathers[0].step_one()
    ffn_rows(4, 5)
    unit_join(has_unit, 1)
    ag_u.gathers[1].step_one()
    ffn_rows(5, 6)
    gain_step(3)

    def take_k(i, carry):
        @pl.when((i != z) | (c != f))
        def _():
            pltpu.make_async_remote_copy(
                src_ref=ks.at[pl.ds(0, slab), pl.ds(0, D)], dst_ref=cp.at[i], send_sem=ksend.at[0],
                recv_sem=krecv.at[i], device_id=mate, device_id_type=MESH,
            ).wait_recv()

        return carry

    lax.fori_loop(0, RING, take_k, 0)
    total = cp[0].astype(F32)
    for i in range(1, RING):
        total = total + cp[i].astype(F32)
    k_lane = pl.multiple_of(OUT_CKV + c * D, 128)
    gb[pl.ds(pl.multiple_of(x * half_slabs + z * slab, 16), slab), pl.ds(k_lane, D)] = total.astype(BF16)

    def kv_view(zz, xx, cc):
        row = pl.multiple_of(xx * half_slabs + zz * slab, 16)
        return gb.at[pl.ds(row, slab), pl.ds(pl.multiple_of(OUT_CKV + cc * D, 128), D)]

    ag_k = Gather(place, kv_view, lambda cc, xx: gb.at[pl.ds(pl.multiple_of(xx * half_slabs, 16), half_slabs), pl.ds(pl.multiple_of(OUT_CKV + cc * D, 128), D)], sems, 4)
    ag_k.step_one()

    def mg_step(i, carry):
        row = pl.multiple_of(i * 128, 128)
        memgrad_ref[pl.ds(row, 128)] = mm_nt(kvg[pl.ds(row, 128)], wb[:, LANE_CKV : LANE_CKV + 2 * D])
        return carry

    full = own_rows // 128
    lax.fori_loop(0, full, mg_step, 0)
    if own_rows % 128:
        tail = mm_nt(kvg[full * 128 : (full + 1) * 128], wb[:, LANE_CKV : LANE_CKV + 2 * D])
        memgrad_ref[full * 128 : own_rows] = tail[0 : own_rows - full * 128]


    ag_u.gathers[0].step_two()
    ffn_rows(6, 7)
    ag_u.gathers[1].step_two()
    ffn_rows(7, 8)
    ag_u.gathers[0].step_three()
    gain_step(4)
    ag_k.step_two()
    ffn_in_sum(0)
    to_mate(LANE_FI + hidden[0], D)
    ag_u.gathers[1].step_three()
    ag_grad.step_two()
    ffn_in_sum(1)
    to_mate(LANE_FI + hidden[1], D)
    ag_u.gathers[0].step_four()
    ag_k.step_three()
    ffn_out_sum(0)
    ag_u.gathers[1].step_four()
    ffn_out_sum(1)
    to_mate(LANE_FO + CORES * D * c, CORES * D)
    ag_grad.step_three()
    ag_out.step_six()
    ag_u.gathers[0].step_five()
    ag_k.step_four()
    ag_u.gathers[1].step_five()
    for n, (lane, width) in enumerate(
        [(LANE_FI + col * 4 * half_rows + D * (1 - c), D) for col in range(columns)] + [(LANE_FO + CORES * D * (1 - c), CORES * D)]
    ):
        ref = gb.at[:, pl.ds(pl.multiple_of(lane, 128), width)]
        pltpu.make_async_remote_copy(
            src_ref=ref, dst_ref=ref, send_sem=fsend.at[n], recv_sem=frecv.at[n], device_id=mate, device_id_type=MESH,
        ).wait_recv()
    outs = []

    def write(lane, width):
        lanes = pl.ds(lane, width)
        item = pltpu.make_async_copy(gb.at[:, lanes], weights_out_ref.at[:, lanes], load_sem.at[len(outs)])
        item.start()
        outs.append(item)

    write(LANE_FI, 8 * D)
    ag_k.step_five()
    ag_grad.step_six()
    out_ref[...] = ob[0, out_slot].astype(F32)
    grad_ref[...] = ob[1, out_slot].astype(F32)
    gains_all = gain_step(5)
    own_gain = gains_all[:, 0:half_rows]
    for i in range(1, columns):
        own_gain = jnp.where(f == i, gains_all[:, i * half_rows : (i + 1) * half_rows], own_gain)
    gain_out_ref[...] = own_gain
    ag_u.step("step_six")
    write(0, OUT_CKV)
    ag_k.step_six()
    write(OUT_CKV, 2 * D)

    to_holders_sent(q_pairs)
    to_owners_sent(o_pairs)
    to_holders_sent(d_pairs)
    to_owners_sent(dq_pairs)
    for which, at, to, src, dst in unit_items:
        @pl.when(me != to)
        def _():
            pltpu.make_async_remote_copy(
                src_ref=src, dst_ref=dst, send_sem=usend.at[which, at],
                recv_sem=urecv.at[which, 0], device_id=(to, f), device_id_type=MESH,
            ).wait_send()
    @pl.when(has_unit)
    def _():
        for n in range(2):
            unit_copy(n).wait_send()
        left_copy(c).wait_send()

    for t, j, here in k_items:
        @pl.when((c == f) & jnp.logical_not(here))
        def _():
            k_copy(t, j).wait_send()

    @pl.when(c == f)
    def _():
        kx_copy(0).wait_send()
        kx_copy(1).wait_send()

    across_o.finish()
    across_n.finish()
    for item in f_items:
        item.wait_send()
    kr_item.wait_send()

    @pl.when(c != f)
    def _():
        ky_copy(0).wait_send()
        ky_copy(1).wait_send()

    for item in y_items:
        item.wait_send()
    tell_p.finish()
    for k in range(len(partners)):
        gain_copy(k).wait_send()
    for item in [ag_x, *spread, ag_c, ag_n, *ag_u.gathers, ag_out, ag_grad, ag_k]:
        item.finish()
    for item in outs:
        item.wait()


def fused_body(
    ranks, columns,
    decoder_in, memory, res_group, prefix_len, self_gain, self_qkv, self_out, cross_gain, cross_query,
    cross_kv, cross_out, ffn_gain, ffn_in, ffn_out, cotangent,
):
    half_rows = D // columns
    chips = ranks // CORES
    slab = half_rows // chips
    own_rows = memory.shape[1]
    padded = -(-own_rows // 128) * 128
    tokens = ranks * SUFFIX
    vm = pl.BlockSpec(memory_space=pltpu.VMEM)
    sm = pl.BlockSpec(memory_space=pltpu.SMEM)
    hbm = pl.BlockSpec(memory_space=pl.ANY)
    dma = pltpu.SemaphoreType.DMA
    scratch = [
        pltpu.VMEM((D, UNITS * D), BF16),
        pltpu.VMEM((half_rows, UNITS * D), BF16),
        pltpu.VMEM((tokens, D), BF16),
        pltpu.VMEM((tokens, PIECE), BF16),
        pltpu.VMEM((4, SUFFIX, D), BF16),
        pltpu.VMEM((UNIT_CHIPS, CORES, SUFFIX, PIECE), BF16),
        pltpu.VMEM((ranks, SUFFIX, D), F32),
        pltpu.VMEM((ranks, SUFFIX, D), BF16),
        pltpu.VMEM((columns * tokens, D), BF16),
        pltpu.VMEM((columns * tokens, D), BF16),
        pltpu.VMEM((2, ranks, SUFFIX, D), BF16),
        pltpu.VMEM((ranks, 8, 128), F32),
        pltpu.VMEM((columns, 16, 128), F32),
        pltpu.VMEM((padded, D), BF16),
        pltpu.VMEM((padded, 2 * D), BF16),
        pltpu.VMEM((padded, 2 * D), BF16),
        pltpu.VMEM((D, 2 * D), BF16),
        pltpu.VMEM((half_rows, 2 * D), BF16),
        pltpu.VMEM((half_rows, 2 * D), BF16),
        pltpu.VMEM((half_rows, 2 * D), BF16),
        pltpu.VMEM((RING, slab, D), BF16),
        pltpu.VMEM((half_rows // SIDE, 2 * D), BF16),
        pltpu.VMEM((half_rows // SIDE, 2 * D), BF16),
        pltpu.VMEM((columns, columns * tokens, D), BF16),
        pltpu.VMEM((columns * tokens, D), BF16),
        pltpu.VMEM((columns, half_rows, PIECE), F32),
        pltpu.VMEM((half_rows, PIECE), BF16),
        pltpu.VMEM((half_rows, PIECE), BF16),
        pltpu.VMEM((SUFFIX, D), BF16),
        pltpu.VMEM((SLOTS, SUFFIX, D), BF16),
        pltpu.VMEM((SLOTS, SUFFIX, D), BF16),
        pltpu.VMEM((SLOTS, SUFFIX, 128), F32),
        pltpu.VMEM((SLOTS, SUFFIX, D), BF16),
        pltpu.VMEM((SLOTS, SUFFIX, 128), F32),
        pltpu.VMEM((SUFFIX, D), BF16),
        pltpu.VMEM((SUFFIX, 128), F32),
        pltpu.VMEM((SLOTS, SUFFIX, D), BF16),
        pltpu.VMEM((SLOTS, SUFFIX, 128), F32),
        pltpu.VMEM((SLOTS, SUFFIX, D), BF16),
        pltpu.VMEM((SLOTS, SUFFIX, D), BF16),
        pltpu.VMEM((5, 8, D), F32),
        pltpu.VMEM((5, 8, D), F32),
        dma((10,)),
        dma((len(CHUNKS), 17)),
        dma((len(CHUNKS), 14)),
        dma((5, 17)),
        dma((5, 10)),
        dma((3, 9)),
        dma((3, 10)),
        dma((1, ranks)),
        dma((1, ranks)),
        dma((2, 5)),
        dma((2, 2)),
        dma((2, 2)),
        dma((3,)),
        dma((3,)),
        dma((5,)),
        dma((5,)),
        dma((6, SLOTS)),
        dma((6, SLOTS)),
        dma((2, CORES * UNIT_CHIPS)),
        dma((2, ranks)),
        dma((2 * chips + 5,)),
        dma((chips + 5,)),
    ]
    out, grad, memgrad, gain_grads, weight_grads = pl.pallas_call(
        partial(layer_kernel, ranks, columns),
        out_shape=(
            jax.ShapeDtypeStruct((SUFFIX, D), F32),
            jax.ShapeDtypeStruct((SUFFIX, D), F32),
            jax.ShapeDtypeStruct((own_rows, D), F32),
            jax.ShapeDtypeStruct((8, half_rows), F32),
            jax.ShapeDtypeStruct((half_rows, UNITS * D), BF16),
        ),
        in_specs=[vm, vm, vm, sm, sm, vm, vm, vm] + [hbm] * 7,
        out_specs=(vm, vm, vm, vm, hbm),
        scratch_shapes=scratch,
        compiler_params=pltpu.CompilerParams(
            collective_id=0, has_side_effects=True, vmem_limit_bytes=63 * 2**20
        ),
        name="layer",
    )(
        decoder_in[0], cotangent[0], memory[0], res_group, prefix_len, self_gain, cross_gain, ffn_gain,
        self_qkv, self_out, cross_query, cross_kv, cross_out, ffn_in, ffn_out,
    )

    return unpack(half_rows, columns, weight_grads, memgrad, out, grad, gain_grads)


SPLIT = ((0, 3), (3, 1), (4, 1), (OUT_CKV, 2 * D), (5, 1), (LANE_FI, 4 * D))
WHOLE = (OUT_CKV, LANE_FI)


def unpack_kernel(w_ref, m_ref, o_ref, g_ref, gains_ref, *refs):
    *weights, ffn_out_ref, mem_ref, out_ref, grad_ref, one_ref, two_ref, three_ref = refs
    for n, ref in enumerate((one_ref, two_ref, three_ref)):
        ref[...] = gains_ref[n : n + 1].reshape(ref.shape)
    for (low, width), ref in zip(SPLIT, weights):
        if low in WHOLE:
            ref[...] = w_ref[:, low : low + width].astype(F32)
            continue
        for n in range(width):
            for j in range(CORES):
                at = (UNIT_CHIPS * j + low + n) * PIECE
                to = (CORES * n + j) * PIECE
                ref[:, to : to + PIECE] = w_ref[:, at : at + PIECE].astype(F32)
    for j in range(4):
        ffn_out_ref[j] = w_ref[:, LANE_FO + D * j : LANE_FO + D * (j + 1)].astype(F32)
    mem_ref[:, 0, :] = m_ref[...]
    out_ref[...] = o_ref[...]
    grad_ref[...] = g_ref[...]


def unpack(half_rows, columns, weight_grads, memgrad, out, grad, gain_grads):
    steps = 2
    rows = half_rows // steps
    own_rows = memgrad.shape[0]
    mem_rows = -(-own_rows // (8 * steps)) * 8
    tokens = out.shape[0] // steps
    block = lambda height, width: pl.BlockSpec((height, width), lambda i: (i, 0))
    results = pl.pallas_call(
        unpack_kernel,
        grid=(steps,),
        out_shape=[jax.ShapeDtypeStruct((half_rows, width if low in WHOLE else width * D), F32) for low, width in SPLIT]
        + [
            jax.ShapeDtypeStruct((4, half_rows, D), F32),
            jax.ShapeDtypeStruct((own_rows, 1, D), F32),
            jax.ShapeDtypeStruct(out.shape, F32),
            jax.ShapeDtypeStruct(grad.shape, F32),
        ]
        + [jax.ShapeDtypeStruct((half_rows,), F32)] * 3,
        in_specs=[block(rows, UNITS * D), block(mem_rows, D), block(tokens, D), block(tokens, D), pl.BlockSpec(gain_grads.shape, lambda i: (0, 0))],
        out_specs=[block(rows, width if low in WHOLE else width * D) for low, width in SPLIT]
        + [
            pl.BlockSpec((4, rows, D), lambda i: (0, i, 0)),
            pl.BlockSpec((mem_rows, 1, D), lambda i: (i, 0, 0)),
            block(tokens, D),
            block(tokens, D),
        ]
        + [pl.BlockSpec((half_rows,), lambda i: (0,))] * 3,
        compiler_params=pltpu.CompilerParams(vmem_limit_bytes=63 * 2**20),
        name="unpack",
    )(weight_grads, memgrad, out, grad, gain_grads)
    qkv, so, cq, ckv, co, fi, fo, mem, out, grad, gain_one, gain_two, gain_three = results
    return (
        out[None], grad[None], mem.reshape(1, own_rows, D),
        gain_one, qkv, so, gain_two, cq, ckv, co, gain_three, fi, fo.reshape(4 * half_rows, D),
    )


def layer_norm(value, gain):
    mean = jnp.mean(value, axis=-1, keepdims=True)
    centred = value - mean
    variance = jnp.mean(centred * centred, axis=-1, keepdims=True)
    return centred * lax.rsqrt(variance + norm_eps) * gain


def product(left, right):
    return jnp.dot(left, right, preferred_element_type=jnp.float32)


def outer_sum(left, right):
    flat_left = left.reshape(-1, left.shape[-1])
    flat_right = right.reshape(-1, right.shape[-1])
    return lax.dot_general(
        flat_left, flat_right, (((0,), (0,)), ((), ())), preferred_element_type=jnp.float32
    )


def back_product(grad, weight):
    return lax.dot_general(
        grad, weight, (((grad.ndim - 1,), (1,)), ((), ())), preferred_element_type=jnp.float32
    )


def attend(query, keys, values, allowed, scale):
    scores = jnp.einsum("eqhd,ekhd->ehqk", query, keys, preferred_element_type=jnp.float32) * scale
    scores = jnp.where(allowed[:, None], scores, -1e30)
    top = jnp.max(scores, axis=-1, keepdims=True)
    weights = jnp.exp(scores - top)
    probs = weights / jnp.sum(weights, axis=-1, keepdims=True)
    mixed = jnp.einsum(
        "ehqk,ekhd->eqhd", probs.astype(jnp.bfloat16), values, preferred_element_type=jnp.float32
    )
    return (mixed.astype(jnp.bfloat16), probs)


def attend_back(grad_mixed, query, keys, values, probs, scale):
    probs_low = probs.astype(jnp.bfloat16)
    grad_values = jnp.einsum(
        "ehqk,eqhd->ekhd", probs_low, grad_mixed, preferred_element_type=jnp.float32
    )
    grad_probs = jnp.einsum(
        "eqhd,ekhd->ehqk", grad_mixed, values, preferred_element_type=jnp.float32
    )
    grad_scores = probs * (grad_probs - jnp.sum(probs * grad_probs, axis=-1, keepdims=True))
    grad_low = grad_scores.astype(jnp.bfloat16)
    grad_query = (
        jnp.einsum("ehqk,ekhd->eqhd", grad_low, keys, preferred_element_type=jnp.float32) * scale
    )
    grad_keys = (
        jnp.einsum("ehqk,eqhd->ekhd", grad_low, query, preferred_element_type=jnp.float32) * scale
    )
    return (grad_query, grad_keys, grad_values)


def window_layout(res_group, mem_col):
    small = 1 - res_group
    small_count = jnp.sum(small, axis=-1, keepdims=True)
    small_before = jnp.cumsum(small, axis=-1) - small
    large_before = jnp.cumsum(res_group, axis=-1) - res_group
    offset = jnp.where(
        res_group == 1, SLOT_S * small_count + SLOT_L * large_before, SLOT_S * small_before
    )
    start = jnp.minimum(offset, mem_col - SLOT_L)
    return (offset, start)


def take_windows(column, starts):
    return jax.vmap(lambda begin: lax.dynamic_slice_in_dim(column, begin, SLOT_L, 0))(starts)


def forward(decoder_rows, windows, cross_allowed, weights):
    (
        self_gain,
        self_qkv,
        self_out,
        cross_gain,
        cross_query,
        cross_kv,
        cross_out,
        ffn_gain,
        ffn_in,
        ffn_out,
    ) = weights
    count = decoder_rows.shape[0] // SUFFIX
    scale = HEAD_DIM ** (-0.5)
    row_index = lax.broadcasted_iota(jnp.int32, (SUFFIX, SUFFIX), 0)
    col_index = lax.broadcasted_iota(jnp.int32, (SUFFIX, SUFFIX), 1)
    causal = (row_index >= col_index)[None]
    resid = decoder_rows.reshape(count, SUFFIX, D)
    normed_one = layer_norm(resid, self_gain.astype(jnp.float32)).astype(jnp.bfloat16)
    packed = product(normed_one, self_qkv).astype(jnp.bfloat16)
    heads = packed.reshape(count, SUFFIX, 3, HEADS, HEAD_DIM)
    self_mixed, self_probs = attend(heads[:, :, 0], heads[:, :, 1], heads[:, :, 2], causal, scale)
    self_mixed = self_mixed.reshape(count, SUFFIX, D)
    after_self = resid + product(self_mixed, self_out)
    normed_two = layer_norm(after_self, cross_gain.astype(jnp.float32)).astype(jnp.bfloat16)
    cross_q = product(normed_two, cross_query).astype(jnp.bfloat16)
    window_kv = product(windows, cross_kv).astype(jnp.bfloat16)
    query_heads = cross_q.reshape(count, SUFFIX, HEADS, HEAD_DIM)
    kv_heads = window_kv.reshape(count, SLOT_L, 2, HEADS, HEAD_DIM)
    cross_mixed, cross_probs = attend(
        query_heads, kv_heads[:, :, 0], kv_heads[:, :, 1], cross_allowed, scale
    )
    cross_mixed = cross_mixed.reshape(count, SUFFIX, D)
    after_cross = after_self + product(cross_mixed, cross_out)
    normed_three = layer_norm(after_cross, ffn_gain.astype(jnp.float32)).astype(jnp.bfloat16)
    up = product(normed_three, ffn_in)
    act = jax.nn.gelu(up, approximate=True).astype(jnp.bfloat16)
    result = after_cross + product(act, ffn_out)
    return (
        resid,
        normed_one,
        packed,
        self_probs,
        self_mixed,
        after_self,
        normed_two,
        cross_q,
        window_kv,
        cross_probs,
        cross_mixed,
        after_cross,
        normed_three,
        up,
        act,
        result,
    )


def backward(grad_out, saved, weights):
    (
        self_gain,
        self_qkv,
        self_out,
        cross_gain,
        cross_query,
        cross_kv,
        cross_out,
        ffn_gain,
        ffn_in,
        ffn_out,
    ) = weights
    (
        resid,
        normed_one,
        packed,
        self_probs,
        self_mixed,
        after_self,
        normed_two,
        cross_q,
        window_kv,
        cross_probs,
        cross_mixed,
        after_cross,
        normed_three,
        up,
        act,
        result,
    ) = saved
    count = resid.shape[0]
    scale = HEAD_DIM ** (-0.5)
    grad_out = grad_out.reshape(count, SUFFIX, D)
    out_low = grad_out.astype(jnp.bfloat16)
    ffn_out_grad = outer_sum(act, out_low)
    act_grad = back_product(out_low, ffn_out)
    gelu_value, gelu_back = jax.vjp(partial(jax.nn.gelu, approximate=True), up)
    up_grad = gelu_back(act_grad)[0].astype(jnp.bfloat16)
    ffn_in_grad = outer_sum(normed_three, up_grad)
    normed_three_grad = back_product(up_grad, ffn_in)
    norm_value, norm_back = jax.vjp(layer_norm, after_cross, ffn_gain.astype(jnp.float32))
    resid_part, ffn_gain_grad = norm_back(normed_three_grad)
    cross_res_grad = grad_out + resid_part
    cross_low = cross_res_grad.astype(jnp.bfloat16)
    cross_out_grad = outer_sum(cross_mixed, cross_low)
    mixed_grad = (
        back_product(cross_low, cross_out)
        .astype(jnp.bfloat16)
        .reshape(count, SUFFIX, HEADS, HEAD_DIM)
    )
    query_heads = cross_q.reshape(count, SUFFIX, HEADS, HEAD_DIM)
    kv_heads = window_kv.reshape(count, SLOT_L, 2, HEADS, HEAD_DIM)
    query_grad, keys_grad, values_grad = attend_back(
        mixed_grad, query_heads, kv_heads[:, :, 0], kv_heads[:, :, 1], cross_probs, scale
    )
    cross_q_grad = query_grad.reshape(count, SUFFIX, D).astype(jnp.bfloat16)
    window_kv_grad = (
        jnp.stack((keys_grad, values_grad), axis=2)
        .reshape(count, SLOT_L, 2 * D)
        .astype(jnp.bfloat16)
    )
    cross_query_grad = outer_sum(normed_two, cross_q_grad)
    normed_two_grad = back_product(cross_q_grad, cross_query)
    norm_value, norm_back = jax.vjp(layer_norm, after_self, cross_gain.astype(jnp.float32))
    resid_part, cross_gain_grad = norm_back(normed_two_grad)
    self_res_grad = cross_res_grad + resid_part
    self_low = self_res_grad.astype(jnp.bfloat16)
    self_out_grad = outer_sum(self_mixed, self_low)
    mixed_grad = (
        back_product(self_low, self_out)
        .astype(jnp.bfloat16)
        .reshape(count, SUFFIX, HEADS, HEAD_DIM)
    )
    heads = packed.reshape(count, SUFFIX, 3, HEADS, HEAD_DIM)
    query_grad, keys_grad, values_grad = attend_back(
        mixed_grad, heads[:, :, 0], heads[:, :, 1], heads[:, :, 2], self_probs, scale
    )
    packed_grad = (
        jnp.stack((query_grad, keys_grad, values_grad), axis=2)
        .reshape(count, SUFFIX, 3 * D)
        .astype(jnp.bfloat16)
    )
    self_qkv_grad = outer_sum(normed_one, packed_grad)
    normed_one_grad = back_product(packed_grad, self_qkv)
    norm_value, norm_back = jax.vjp(layer_norm, resid, self_gain.astype(jnp.float32))
    resid_part, self_gain_grad = norm_back(normed_one_grad)
    decoder_grad = self_res_grad + resid_part
    weight_grads = (
        self_gain_grad,
        self_qkv_grad,
        self_out_grad,
        cross_gain_grad,
        cross_query_grad,
        cross_out_grad,
        ffn_gain_grad,
        ffn_in_grad,
        ffn_out_grad,
    )
    return (decoder_grad, window_kv_grad, weight_grads)


def make_placer(all_starts, lowest, own_rows):

    def place(total, piece, begin):

        def add_one(item, acc):
            relative = all_starts[item] - lowest
            inside = ((relative > -SLOT_L) & (relative < own_rows)).astype(jnp.float32)
            spot = jnp.clip(relative + SLOT_L, 0, own_rows + SLOT_L)
            current = lax.dynamic_slice_in_dim(acc, spot, SLOT_L, 0)
            added = current + piece[item].astype(jnp.float32) * inside
            return lax.dynamic_update_slice_in_dim(acc, added, spot, 0)

        return lax.fori_loop(0, piece.shape[0], add_one, total)

    return place


def body(
    decoder_in,
    memory,
    res_group,
    prefix_len,
    self_gain,
    self_qkv,
    self_out,
    cross_gain,
    cross_query,
    cross_kv,
    cross_out,
    ffn_gain,
    ffn_in,
    ffn_out,
    cotangent,
):
    count = prefix_len.shape[1]
    own_rows = memory.shape[1]
    mem_col = own_rows * lax.axis_size("dp")
    offset, start = window_layout(res_group, mem_col)
    all_starts = start[0]
    first = lax.axis_index("dp") * count
    own_offset = lax.dynamic_slice_in_dim(offset[0], first, count)
    own_start = lax.dynamic_slice_in_dim(all_starts, first, count)
    own_group = lax.dynamic_slice_in_dim(res_group[0], first, count)
    valid = jnp.where(own_group == 1, PATCH_L, PATCH_S) + prefix_len[0]
    positions = own_start[:, None] + jnp.arange(SLOT_L, dtype=jnp.int32)[None]
    cross_allowed = (
        (positions >= own_offset[:, None]) & (positions < (own_offset + valid)[:, None])
    )[:, None]
    weights = (
        lax.all_gather(self_gain, "fsdp", axis=0, tiled=True),
        lax.all_gather(self_qkv, "fsdp", axis=0, tiled=True),
        lax.all_gather(self_out, "fsdp", axis=0, tiled=True),
        lax.all_gather(cross_gain, "fsdp", axis=0, tiled=True),
        lax.all_gather(cross_query, "fsdp", axis=0, tiled=True),
        lax.all_gather(cross_kv, "fsdp", axis=0, tiled=True),
        lax.all_gather(cross_out, "fsdp", axis=0, tiled=True),
        lax.all_gather(ffn_gain, "fsdp", axis=0, tiled=True),
        lax.all_gather(ffn_in, "fsdp", axis=0, tiled=True),
        lax.all_gather(ffn_out, "fsdp", axis=0, tiled=True),
    )
    column = lax.all_gather(memory[0], "dp", axis=0, tiled=True)
    windows = take_windows(column, own_start)
    saved = forward(decoder_in[0], windows, cross_allowed, weights)
    decoder_out = saved[-1]
    weights = (
        lax.all_gather(self_gain, "fsdp", axis=0, tiled=True),
        lax.all_gather(self_qkv, "fsdp", axis=0, tiled=True),
        lax.all_gather(self_out, "fsdp", axis=0, tiled=True),
        lax.all_gather(cross_gain, "fsdp", axis=0, tiled=True),
        lax.all_gather(cross_query, "fsdp", axis=0, tiled=True),
        lax.all_gather(cross_kv, "fsdp", axis=0, tiled=True),
        lax.all_gather(cross_out, "fsdp", axis=0, tiled=True),
        lax.all_gather(ffn_gain, "fsdp", axis=0, tiled=True),
        lax.all_gather(ffn_in, "fsdp", axis=0, tiled=True),
        lax.all_gather(ffn_out, "fsdp", axis=0, tiled=True),
    )
    column = lax.all_gather(memory[0], "dp", axis=0, tiled=True)
    windows = take_windows(column, own_start)
    saved = forward(decoder_in[0], windows, cross_allowed, weights)
    whole_kv = weights[5]
    decoder_grad, window_kv_grad, local_grads = backward(cotangent[0], saved, weights)
    lowest = lax.axis_index("dp") * own_rows
    place = make_placer(all_starts, lowest, own_rows)
    empty = jnp.zeros((own_rows + 2 * SLOT_L, 2 * D), jnp.float32)
    summed = place(empty, lax.all_gather(window_kv_grad, "dp", axis=0, tiled=True), jnp.int32(0))
    own_kv_grad = summed[SLOT_L : SLOT_L + own_rows].astype(jnp.bfloat16)
    memory_grad = back_product(own_kv_grad, whole_kv)
    cross_kv_part = outer_sum(memory[0], own_kv_grad)
    grads = (
        local_grads[0],
        local_grads[1],
        local_grads[2],
        local_grads[3],
        local_grads[4],
        cross_kv_part,
        local_grads[5],
        local_grads[6],
        local_grads[7],
        local_grads[8],
    )
    shards = (
        lax.psum_scatter(
            grads[0].astype(jnp.bfloat16), "fsdp", scatter_dimension=0, tiled=True
        ).astype(jnp.float32),
        lax.psum_scatter(
            grads[1].astype(jnp.bfloat16), "fsdp", scatter_dimension=0, tiled=True
        ).astype(jnp.float32),
        lax.psum_scatter(
            grads[2].astype(jnp.bfloat16), "fsdp", scatter_dimension=0, tiled=True
        ).astype(jnp.float32),
        lax.psum_scatter(
            grads[3].astype(jnp.bfloat16), "fsdp", scatter_dimension=0, tiled=True
        ).astype(jnp.float32),
        lax.psum_scatter(
            grads[4].astype(jnp.bfloat16), "fsdp", scatter_dimension=0, tiled=True
        ).astype(jnp.float32),
        lax.psum_scatter(
            grads[5].astype(jnp.bfloat16), "fsdp", scatter_dimension=0, tiled=True
        ).astype(jnp.float32),
        lax.psum_scatter(
            grads[6].astype(jnp.bfloat16), "fsdp", scatter_dimension=0, tiled=True
        ).astype(jnp.float32),
        lax.psum_scatter(
            grads[7].astype(jnp.bfloat16), "fsdp", scatter_dimension=0, tiled=True
        ).astype(jnp.float32),
        lax.psum_scatter(
            grads[8].astype(jnp.bfloat16), "fsdp", scatter_dimension=0, tiled=True
        ).astype(jnp.float32),
        lax.psum_scatter(
            grads[9].astype(jnp.bfloat16), "fsdp", scatter_dimension=0, tiled=True
        ).astype(jnp.float32),
    )
    totals = (
        lax.psum(shards[0].astype(jnp.bfloat16), "dp").astype(jnp.float32),
        lax.psum(shards[1].astype(jnp.bfloat16), "dp").astype(jnp.float32),
        lax.psum(shards[2].astype(jnp.bfloat16), "dp").astype(jnp.float32),
        lax.psum(shards[3].astype(jnp.bfloat16), "dp").astype(jnp.float32),
        lax.psum(shards[4].astype(jnp.bfloat16), "dp").astype(jnp.float32),
        lax.psum(shards[5].astype(jnp.bfloat16), "dp").astype(jnp.float32),
        lax.psum(shards[6].astype(jnp.bfloat16), "dp").astype(jnp.float32),
        lax.psum(shards[7].astype(jnp.bfloat16), "dp").astype(jnp.float32),
        lax.psum(shards[8].astype(jnp.bfloat16), "dp").astype(jnp.float32),
        lax.psum(shards[9].astype(jnp.bfloat16), "dp").astype(jnp.float32),
    )
    return (
        decoder_out,
        decoder_grad,
        memory_grad[None],
        totals[0],
        totals[1],
        totals[2],
        totals[3],
        totals[4],
        totals[5],
        totals[6],
        totals[7],
        totals[8],
        totals[9],
    )


def choose(mesh):
    ranks, columns = mesh.shape["dp"], mesh.shape["fsdp"]
    slabs = (D // columns) % (16 * (ranks // CORES)) == 0
    if slabs and columns == 2 and ranks == RING * SIDE * CORES:
        return partial(fused_body, ranks, columns)
    return body


def solution(mesh):
    placed = (
        P("fsdp", "dp", None),
        P("fsdp", "dp", None),
        P("fsdp", None),
        P("fsdp", "dp"),
        P("fsdp"),
        P("fsdp", None),
        P("fsdp", None),
        P("fsdp"),
        P("fsdp", None),
        P("fsdp", None),
        P("fsdp", None),
        P("fsdp"),
        P("fsdp", None),
        P("fsdp", None),
        P("fsdp", "dp", None),
    )
    return jax.shard_map(
        choose(mesh),
        mesh=mesh,
        in_specs=placed,
        out_specs=(
            P("fsdp", "dp", None),
            P("fsdp", "dp", None),
            P("fsdp", "dp", None),
            P("fsdp"),
            P("fsdp", None),
            P("fsdp", None),
            P("fsdp"),
            P("fsdp", None),
            P("fsdp", None),
            P("fsdp", None),
            P("fsdp"),
            P("fsdp", None),
            P("fsdp", None),
        ),
        check_vma=False,
    )
```

```python
from functools import partial

import jax
import jax.numpy as jnp
from jax import lax
from jax.experimental import pallas as pl
from jax.experimental.pallas import tpu as pltpu
from jax.sharding import PartitionSpec as P

D = 768
HEADS = 12
HEAD_DIM = 64
SUFFIX = 32
PATCH_S = 196
PATCH_L = 576
SLOT_S = 228
SLOT_L = 608
RING = 4
SIDE = 2
CORES = 2
norm_eps = 1e-06
MESH = pl.DeviceIdType.MESH
F32 = jnp.float32
BF16 = jnp.bfloat16
NONE = -1e30


def mm(left, right):
    return jnp.dot(left, right, preferred_element_type=F32)


def mm_nt(left, right):
    return lax.dot_general(left, right, (((1,), (1,)), ((), ())), preferred_element_type=F32)


def mm_tn(left, right):
    return lax.dot_general(left, right, (((0,), (0,)), ((), ())), preferred_element_type=F32)


def normed(value):
    mean = jnp.mean(value, axis=-1, keepdims=True)
    centred = value - mean
    variance = jnp.mean(centred * centred, axis=-1, keepdims=True)
    scale = lax.rsqrt(variance + norm_eps)
    return centred * scale, scale


def norm_back(grad, hat, scale, gain):
    inner = grad * gain
    mean_one = jnp.mean(inner, axis=-1, keepdims=True)
    mean_two = jnp.mean(inner * hat, axis=-1, keepdims=True)
    gain_grad = jnp.sum(grad * hat, axis=0, keepdims=True)
    return scale * (inner - mean_one - hat * mean_two), gain_grad


def gelu_parts(up):
    inner = 0.7978845608 * (up + 0.044715 * up * up * up)
    tanh = jnp.tanh(inner)
    slope = 0.7978845608 * (1.0 + 3.0 * 0.044715 * up * up)
    value = 0.5 * up * (1.0 + tanh)
    grad = 0.5 * (1.0 + tanh) + 0.5 * up * (1.0 - tanh * tanh) * slope
    return value, grad


class Gather:
    def __init__(self, place, view, bulk, sems, at, has=None):
        self.z, self.x, self.c, self.f = place
        self.view, self.bulk = view, bulk
        self.send, self.recv = sems
        self.at = at
        self.has = has
        self.sent = []

    def place_at(self, k):
        return lax.rem(self.z + k + RING, RING)

    def copy(self, ref, target, into, index):
        z, x, c = target
        return pltpu.make_async_remote_copy(
            src_ref=ref,
            dst_ref=ref,
            send_sem=self.send.at[self.at, index],
            recv_sem=self.recv.at[self.at, into],
            device_id=(z * (SIDE * CORES) + x * CORES + c, self.f),
            device_id_type=MESH,
        )

    def holds(self, block, cond):
        return cond if self.has is None else cond & self.has(*block)

    def go(self, block, target, into, cond):
        item = self.copy(self.view(*block), target, into, len(self.sent))
        cond = self.holds(block, cond)
        pl.when(cond)(item.start)
        self.sent.append((cond, item))

    def wait(self, block, into, cond):
        item = self.copy(self.view(*block), (self.z, 1 - self.x, self.c), into, 0)
        pl.when(self.holds(block, cond))(item.wait_recv)

    def line(self, block, up, down, cond):
        z, x, c = self.z, self.x, self.c
        if up:
            self.go(block, (self.place_at(1), x, c), block[0], cond & (z < RING - 1))
        if down:
            self.go(block, (self.place_at(-1), x, c), block[0], cond & (z > 0))

    def across(self, block, cond):
        self.go(block, (self.z, 1 - self.x, self.c), RING + block[0], cond)

    def step_one(self):
        own = (self.z, self.x, self.c)
        self.line(own, True, True, self.z >= 0)
        self.across(own, self.z >= 0)

    def arrive(self, k):
        low, high = (self.place_at(-k), self.x, self.c), (self.place_at(k), self.x, self.c)
        self.wait(low, low[0], self.z >= k)
        self.line(low, True, False, self.z >= k)
        self.wait(high, high[0], self.z < RING - k)
        self.line(high, False, True, self.z < RING - k)
        self.across(low, self.z >= k)
        self.across(high, self.z < RING - k)

    def side(self, k):
        for at, cond in ((self.place_at(-k), self.z >= k), (self.place_at(k), self.z < RING - k))[: 1 if k == 0 else 2]:
            self.wait((at, 1 - self.x, self.c), RING + at, cond)

    def step_two(self):
        self.arrive(1)

    def step_three(self):
        self.arrive(2)
        self.side(0)
        self.side(1)

    def step_four(self):
        self.arrive(3)
        self.hand_over(0)
        self.side(2)

    def step_five(self):
        self.side(3)
        self.hand_over(1)

    def hand_over(self, n):
        item = self.copy(self.bulk(self.c, self.x + n * (1 - 2 * self.x)), (self.z, self.x, 1 - self.c), 2 * RING + n, len(self.sent))
        item.start()
        self.sent.append((self.z >= 0, item))

    def step_six(self):
        for n in range(2):
            ref = self.bulk(1 - self.c, self.x + n * (1 - 2 * self.x))
            self.copy(ref, (self.z, self.x, 1 - self.c), 2 * RING + n, 0).wait_recv()

    def finish(self):
        for cond, item in self.sent:
            pl.when(cond)(item.wait_send)


class ShortGather(Gather):
    def step_one(self):
        own = (self.z, self.x, self.c)
        for k in range(1, RING):
            self.go(own, (self.place_at(k), self.x, self.c), self.z, self.z >= 0)
        self.across(own, self.z >= 0)

    def step_two(self):
        for k in range(1, RING):
            block = (self.place_at(k), self.x, self.c)
            self.wait(block, block[0], self.z >= 0)
            self.across(block, self.z >= 0)
        self.hand_over(0)

    def step_three(self):
        for k in range(RING):
            at = self.place_at(k)
            self.wait((at, 1 - self.x, self.c), RING + at, self.z >= 0)
        self.hand_over(1)


class Spread(Gather):
    def __init__(self, place, theirs, mine, bulk, sems, at):
        super().__init__(place, theirs, bulk, sems, at)
        self.mine = mine
        z, x, c = self.z, self.x, self.c
        always, end = z >= 0, (z == 0) | (z == RING - 1)
        self.opposite = RING - 1 - z
        self.over = (
            ((z, x, c), None, always),
            ((z, 1 - x, c), None, always),
            ((self.opposite, x, c), 1, end),
            ((self.opposite, 1 - x, c), 1, end),
        )
        self.pushed = []

    def over_copy(self, n, view):
        block, part, cond = self.over[n]
        ref = view(*block, part)
        return pltpu.make_async_remote_copy(
            src_ref=ref, dst_ref=ref, send_sem=self.send.at[self.at, 13 + n], recv_sem=self.recv.at[self.at, 10 + n],
            device_id=(self.z * (SIDE * CORES) + self.x * CORES + self.c, 1 - self.f), device_id_type=MESH,
        )

    def push(self):
        for n in range(4):
            item, cond = self.over_copy(n, self.mine), self.over[n][2]
            pl.when(cond)(item.start)
            self.pushed.append((cond, item))

    def landed(self, n):
        pl.when(self.over[n][2])(self.over_copy(n, self.view).wait_recv)

    def step_one(self):
        always = self.z >= 0
        own = (self.z, self.x, self.c)
        self.landed(0)
        self.line(own, True, True, always)

    def step_three(self):
        z, x, c = self.z, self.x, self.c
        low, high = (self.place_at(-2), x, c), (self.place_at(2), x, c)
        self.wait(low, low[0], z >= 2)
        self.go((*low, 0), (self.place_at(1), x, c), low[0], z == RING - 2)
        self.wait(high, high[0], z < RING - 2)
        self.go((*high, 0), (self.place_at(-1), x, c), high[0], z == 1)
        self.across(low, z >= 2)
        self.across(high, z < RING - 2)
        self.side(1)

    def step_four(self):
        z, x, c = self.z, self.x, self.c
        end = (z == 0) | (z == RING - 1)
        block = (self.opposite, x, c, 0)
        self.wait(block, self.opposite, end)
        self.across(block, end)
        self.landed(2)
        self.hand_over(0)
        self.side(2)

    def step_five(self):
        z, x, c = self.z, self.x, self.c
        self.landed(1)
        self.landed(3)
        self.wait((self.opposite, 1 - x, c, 0), RING + self.opposite, (z == 0) | (z == RING - 1))
        self.hand_over(1)

    def finish(self):
        super().finish()
        for cond, item in self.pushed:
            pl.when(cond)(item.wait_send)


class Pieces:
    def __init__(self, count, own_rows):
        self.half = count // 2
        self.edge = self.half * SLOT_S
        self.rows = own_rows
        self.count = count

    def start(self, rank):
        return jnp.where(
            rank < self.half, SLOT_S * rank, self.edge + SLOT_L * (rank - self.half)
        )

    def size(self, rank):
        return jnp.where(rank < self.half, SLOT_S, SLOT_L)

    def rank_of(self, row):
        return jnp.where(
            row < self.edge,
            lax.div(row, SLOT_S),
            self.half + lax.div(jnp.maximum(row - self.edge, 0), SLOT_L),
        )

    def first_rank(self, device):
        return self.rank_of(device * self.rows)

    def last_rank(self, device):
        return self.rank_of(device * self.rows + self.rows - 1)

    def first_device(self, rank):
        return lax.div(self.start(rank), self.rows)

    def last_device(self, rank):
        return lax.div(self.start(rank) + self.size(rank) - 1, self.rows)


SLOTS = 3
UNITS = 16
LANE_QKV, LANE_SO, LANE_CQ, LANE_CKV, LANE_CO, LANE_FI, LANE_FO = 0, 2304, 3072, 3840, 5376, 6144, 9216
OUT_CO, OUT_CKV = 3840, 4608
CHUNKS = ((0, 2304), (2304, 1536), (3840, 1536), (5376, 3072), (8448, 2304), (10752, 1536))
LOADS_BY_CHUNK = ((0,), (1, 2), (3,), (4, 5), (6, 7), (8, 9))
PIECE = 384
UNIT_CHIPS = 6


def layer_kernel(
    ranks,
    columns,
    x_ref, cot_ref, mem_ref, res_ref, pre_ref, gain_one_ref, gain_two_ref, gain_three_ref,
    qkv_ref, so_ref, cq_ref, ckv_ref, co_ref, fi_ref, fo_ref,
    out_ref, grad_ref, memgrad_ref, gain_out_ref, weights_out_ref,
    wb, gb, rl, rr, lb, sb, xb, cb, nb, olr, ob, pb, gainb, memp, kvb, kvg, kp, kr, kc, ky, cp,
    kx, ks, hb, ab, ug, usend_b, urecv_b,
    cqb, qbuf, osend, ostat_send, obuf, ostat, dob, dstat_b, dobuf, dstat, dqsend, dqbuf, gmine, gpeer,
    load_sem, wsend, wrecv, gsend, grecv, ssend, srecv, bsend, brecv, gain_sem, asend, arecv, fsend, frecv, ysend, yrecv, psend, precv, usend, urecv,
    ksend, krecv,
):
    me = lax.axis_index("dp")
    f = lax.axis_index("fsdp")
    z = lax.div(me, SIDE * CORES)
    x = lax.rem(lax.div(me, CORES), SIDE)
    c = lax.rem(me, CORES)
    seat = x * RING + z
    chips = ranks // CORES
    place = (z, x, c, f)
    half_rows = D // columns
    slab = half_rows // chips
    own_rows = mem_ref.shape[0]
    padded = memp.shape[0]
    lay = Pieces(ranks, own_rows)
    other = 1 - f
    mate = (z * (SIDE * CORES) + x * CORES + (1 - c), f)
    everyone = ranks * columns
    lin = f * ranks + me

    loads = []

    def load(src, lane, width):
        item = pltpu.make_async_copy(
            src, wb.at[pl.ds(pl.multiple_of(f * half_rows, 128), half_rows), pl.ds(lane, width)],
            load_sem.at[len(loads)],
        )
        item.start()
        loads.append(item)

    load(qkv_ref, LANE_QKV, 3 * D)
    load(so_ref, LANE_SO, D)
    load(cq_ref, LANE_CQ, D)
    load(ckv_ref, LANE_CKV, 2 * D)
    load(co_ref, LANE_CO, D)
    load(fi_ref, LANE_FI, 4 * D)
    for j in range(4):
        load(fo_ref.at[pl.ds(j * half_rows, half_rows)], LANE_FO + D * j, D)

    for s in range(SLOTS):
        qbuf[s] = jnp.zeros_like(qbuf[s])
        obuf[s] = jnp.zeros_like(obuf[s])
        ostat[s] = jnp.where(lax.broadcasted_iota(jnp.int32, ostat.shape[1:], 1) < 64, NONE, 0.0)
        dobuf[s] = jnp.zeros_like(dobuf[s])
        dstat[s] = jnp.zeros_like(dstat[s])
        dqbuf[s] = jnp.zeros_like(dqbuf[s])

    def rows_of(device):
        return pl.ds(pl.multiple_of(device * SUFFIX, SUFFIX), SUFFIX)

    def slot_of(device):
        side = lax.rem(lax.div(device, CORES), SIDE)
        return lax.rem(device, CORES) * chips + side * RING + lax.div(device, SIDE * CORES)

    my_slot = slot_of(me)
    xb[my_slot] = x_ref[...]
    cb[my_slot] = cot_ref[...].astype(BF16)
    pb[my_slot] = jnp.full((8, 128), pre_ref[0, 0].astype(F32), F32)
    for n, ref in enumerate((gain_one_ref, gain_two_ref, gain_three_ref)):
        values = ref[...].astype(F32).reshape(1, half_rows)
        for j in range(half_rows // 128):
            at = n * (half_rows // 128) + j
            gainb[f, at : at + 1] = values[:, 128 * j : 128 * (j + 1)]

    barrier = pltpu.get_barrier_semaphore()

    def greet(i, carry):
        to = lax.rem(me + i, ranks)
        pl.semaphore_signal(barrier, inc=1, device_id=(to, f), device_id_type=MESH)
        return carry

    lax.fori_loop(1, ranks, greet, 0)
    pl.semaphore_signal(barrier, inc=1, device_id=(me, other), device_id_type=MESH)
    pl.semaphore_wait(barrier, ranks)

    y_items = []

    def push_y(src, dst, at):
        item = pltpu.make_async_remote_copy(
            src_ref=src, dst_ref=dst, send_sem=ysend.at[at], recv_sem=yrecv.at[at],
            device_id=(me, other), device_id_type=MESH,
        )
        item.start()
        y_items.append(item)
        return item

    class Tell:
        def __init__(self, ref, at):
            self.ref, self.at = ref, at

        def copy(self, source, index, to):
            return pltpu.make_async_remote_copy(
                src_ref=self.ref.at[slot_of(source)], dst_ref=self.ref.at[slot_of(source)], send_sem=bsend.at[self.at, index],
                recv_sem=brecv.at[self.at, source], device_id=(to, f), device_id_type=MESH,
            )

        def start(self):
            def one(i, carry):
                self.copy(me, i, lax.rem(me + i, ranks)).start()
                return carry

            lax.fori_loop(1, ranks, one, 0)

        def wait(self):
            def one(i, carry):
                source = lax.rem(me + i, ranks)
                self.copy(source, i, source).wait_recv()
                return carry

            lax.fori_loop(1, ranks, one, 0)

        def finish(self):
            def one(i, carry):
                self.copy(me, i, lax.rem(me + i, ranks)).wait_send()
                return carry

            lax.fori_loop(1, ranks, one, 0)

    def slab_view(first, width, rows_from):
        half = width // CORES

        cut = (half // 256) * 128

        def view(zz, xx, cc, part=None):
            low, size = {None: (0, half), 0: (0, half - cut), 1: (half - cut, cut)}[part]
            row = pl.multiple_of(rows_from * half_rows + (xx * RING + zz) * slab, 16)
            lane = pl.multiple_of(first + cc * half + low, 128)
            return wb.at[pl.ds(row, slab), pl.ds(lane, size)]

        return view

    def block_view(ref):
        def view(zz, xx, cc):
            return ref.at[cc * chips + xx * RING + zz]

        return view

    def block_bulk(ref):
        return lambda cc, xx: ref.at[pl.ds(cc * chips + xx * RING, RING)]

    def token_rows(col, cc, at):
        return pl.ds(pl.multiple_of(((col * CORES + cc) * chips + at) * SUFFIX, SUFFIX), SUFFIX)

    def token_view(ref):
        def view(zz, xx, cc):
            return ref.at[token_rows(f, cc, xx * RING + zz)]

        return view

    def token_bulk(ref):
        rows = RING * SUFFIX
        return lambda cc, xx: ref.at[pl.ds(pl.multiple_of(((f * CORES + cc) * SIDE + xx) * rows, rows), rows)]

    def chunk_bulk(first, width):
        half = width // CORES
        rows = RING * slab

        def bulk(cc, xx):
            row = pl.multiple_of(other * half_rows + xx * rows, 16)
            return wb.at[pl.ds(row, rows), pl.ds(pl.multiple_of(first + cc * half, 128), half)]

        return bulk

    plane = pl.ds(pl.multiple_of((f * CORES + c) * chips * SUFFIX, SUFFIX), chips * SUFFIX)
    plane_in = pl.ds(pl.multiple_of((other * CORES + c) * chips * SUFFIX, SUFFIX), chips * SUFFIX)
    plane_mate = pl.ds(pl.multiple_of((other * CORES + 1 - c) * chips * SUFFIX, SUFFIX), chips * SUFFIX)

    class Across:
        def __init__(self, ref, at):
            self.ref, self.at = ref, at

        def copy(self, rows, n, to):
            ref = self.ref.at[rows]
            return pltpu.make_async_remote_copy(
                src_ref=ref, dst_ref=ref, send_sem=asend.at[self.at, n], recv_sem=arecv.at[self.at, n],
                device_id=to, device_id_type=MESH,
            )

        def start(self):
            self.copy(plane, 0, (me, other)).start()

        def relay(self):
            self.copy(plane_in, 0, (me, other)).wait_recv()
            self.copy(plane_in, 1, mate).start()

        def wait(self):
            self.copy(plane_mate, 1, mate).wait_recv()

        def finish(self):
            self.copy(plane, 0, (me, other)).wait_send()
            self.copy(plane_in, 1, mate).wait_send()

    sems, short_sems = (gsend, grecv), (ssend, srecv)
    ag_x = Gather(place, block_view(xb), block_bulk(xb), sems, 0)
    ag_c = Gather(place, block_view(cb), block_bulk(cb), sems, 1)
    ag_n = ShortGather(place, token_view(nb), token_bulk(nb), short_sems, 0)
    tell_p = Tell(pb, 0)
    spread = [
        Spread(place, slab_view(first, width, other), slab_view(first, width, f), chunk_bulk(first, width), (wsend, wrecv), n)
        for n, (first, width) in enumerate(CHUNKS)
    ]

    def push_chunk(n):
        for i in LOADS_BY_CHUNK[n]:
            loads[i].wait()
        spread[n].push()

    ag_x.step_one()
    push_chunk(0)
    gain_item = push_y(gainb.at[f], gainb.at[f], 0)
    tell_p.start()
    push_chunk(1)

    def tick(n):
        for age, act in ((4, "step_five"), (3, "step_four"), (2, "step_three"), (1, "step_two"), (0, "step_one")):
            if 0 <= n - age < len(spread):
                getattr(spread[n - age], act)()
        if n + 2 < len(spread):
            push_chunk(n + 2)

    ag_x.step_two()
    tick(0)
    ag_x.step_three()
    tick(1)
    ag_x.step_four()
    tick(2)
    ag_x.step_five()
    ag_x.step_six()
    tick(3)
    gain_item.wait_recv()

    memp[0:own_rows] = mem_ref[...]
    memp[own_rows:padded] = jnp.zeros((padded - own_rows, D), BF16)

    positions = []
    before_large = jnp.int32(0)
    mine_rank = jnp.int32(0)
    for i in range(ranks):
        group = res_ref[0, i]
        spot = jnp.where(group == 1, lay.half + before_large, i - before_large)
        positions.append(spot)
        mine_rank = jnp.where(me == i, spot, mine_rank)
        before_large = before_large + group

    spots = [i // CORES % SIDE * RING + i // (SIDE * CORES) for i in range(ranks)]
    slots = [(i % CORES) * chips + spots[i] for i in range(ranks)]

    def example_of(rank):
        found = jnp.int32(0)
        for i in range(ranks):
            found = jnp.where(positions[i] == rank, slots[i], found)
        return found

    by_rank = [example_of(r) for r in range(ranks)]
    out_slot = jnp.int32(0)
    for i in range(ranks):
        out_slot = jnp.where(mine_rank == i, slots[i], out_slot)

    tiles = half_rows // 128
    gain = [
        jnp.concatenate([gainb[i, tiles * n + j : tiles * n + j + 1] for i in range(columns) for j in range(tiles)], axis=1)
        for n in range(3)
    ]

    mine = example_of(me)
    resid = xb[mine]
    hat_one, rs_one = normed(resid)
    n1 = (hat_one * gain[0]).astype(BF16)

    lanes = lax.broadcasted_iota(jnp.int32, (1, 256), 1)
    head_f32 = [(lax.div(lanes, HEAD_DIM) == h).astype(F32) for h in range(4)]
    head_b16 = [m.astype(BF16) for m in head_f32]

    def stack(value):
        return jnp.concatenate([value * m for m in head_b16], axis=0)

    def unstack(value):
        rows = value.shape[0] // 4
        total = value[0:rows] * head_f32[0]
        for h in range(1, 4):
            total = total + value[h * rows : (h + 1) * rows] * head_f32[h]
        return total

    tick(4)
    ag_c.step_one()
    spread[0].step_six()
    q = mm(n1, wb[:, 0:D]).astype(BF16)
    k = mm(n1, wb[:, D : 2 * D]).astype(BF16)
    v = mm(n1, wb[:, 2 * D : 3 * D]).astype(BF16)
    scale = HEAD_DIM**-0.5
    qs = (q.astype(F32) * scale).astype(BF16)
    row_at = lax.broadcasted_iota(jnp.int32, (SUFFIX, SUFFIX), 0)
    col_at = lax.broadcasted_iota(jnp.int32, (SUFFIX, SUFFIX), 1)
    causal = jnp.concatenate([(row_at >= col_at).astype(F32)] * 4, axis=0) > 0.0
    self_p = []
    mixed = []
    for g in range(3):
        sl = slice(256 * g, 256 * g + 256)
        s = mm_nt(stack(qs[:, sl]), k[:, sl])
        s = jnp.where(causal, s, NONE)
        e = jnp.exp(s - jnp.max(s, axis=-1, keepdims=True))
        p = e / jnp.sum(e, axis=-1, keepdims=True)
        self_p.append(p)
        mixed.append(unstack(mm(p.astype(BF16), v[:, sl])))
    sm = jnp.concatenate(mixed, axis=1).astype(BF16)

    tick(5)
    ag_c.step_two()
    spread[1].step_six()
    after_self = resid + mm(sm, wb[:, LANE_SO : LANE_SO + D])
    hat_two, rs_two = normed(after_self)
    n2 = (hat_two * gain[1]).astype(BF16)
    cq = mm(n2, wb[:, LANE_CQ : LANE_CQ + D]).astype(BF16)
    cqb[...] = cq

    my_first, my_last = lay.first_device(me), lay.last_device(me)
    held_first, held_last = lay.first_rank(me), lay.last_rank(me)

    def piece_copy(src, dst, at, sent, landed, target):
        return pltpu.make_async_remote_copy(
            src_ref=src, dst_ref=dst, send_sem=psend.at[at, sent], recv_sem=precv.at[at, landed],
            device_id=(target, f), device_id_type=MESH,
        )

    def to_holders(pairs):
        for i in range(SLOTS):
            target = my_first + i
            slot = me - lay.first_rank(target)
            there = target <= my_last

            @pl.when(there & (target == me))
            def _():
                for src, dst, at in pairs:
                    dst[slot] = src[...]

            @pl.when(there & (target != me))
            def _():
                for src, dst, at in pairs:
                    piece_copy(src, dst.at[slot], at, i, slot, target).start()

    def to_holders_sent(pairs):
        for i in range(SLOTS):
            target = my_first + i

            @pl.when((target <= my_last) & (target != me))
            def _():
                for src, dst, at in pairs:
                    piece_copy(src, dst.at[0], at, i, 0, target).wait_send()

    def at_holders(pairs):
        for s in range(SLOTS):
            rank = held_first + s

            @pl.when((rank <= held_last) & (rank != me))
            def _():
                for src, dst, at in pairs:
                    piece_copy(src, dst.at[s], at, 0, s, rank).wait_recv()

    def to_owners(pairs):
        for s in range(SLOTS):
            rank = held_first + s
            index = me - lay.first_device(rank)
            there = rank <= held_last

            @pl.when(there & (rank == me))
            def _():
                for src, dst, at in pairs:
                    dst[index] = src[s]

            @pl.when(there & (rank != me))
            def _():
                for src, dst, at in pairs:
                    piece_copy(src.at[s], dst.at[index], at, s, index, rank).start()

    def to_owners_sent(pairs):
        for s in range(SLOTS):
            rank = held_first + s

            @pl.when((rank <= held_last) & (rank != me))
            def _():
                for src, dst, at in pairs:
                    piece_copy(src.at[s], dst.at[0], at, s, 0, rank).wait_send()

    def at_owners(pairs):
        for i in range(SLOTS):
            target = my_first + i

            @pl.when((target <= my_last) & (target != me))
            def _():
                for src, dst, at in pairs:
                    piece_copy(src.at[0], dst.at[i], at, 0, i, target).wait_recv()

    q_pairs = [(cqb, qbuf, 0)]
    o_pairs = [(osend, obuf, 1), (ostat_send, ostat, 2)]
    d_pairs = [(dob, dobuf, 3), (dstat_b, dstat, 4)]
    dq_pairs = [(dqsend, dqbuf, 5)]

    to_holders(q_pairs)

    tick(6)
    ag_c.step_three()
    spread[2].step_six()


    def kv_step(i, carry):
        lane = pl.multiple_of(i * 256, 256)
        kvb[:, pl.ds(lane, 256)] = mm(memp[...], wb[:, pl.ds(LANE_CKV + lane, 256)]).astype(BF16)
        return carry

    lax.fori_loop(0, 6, kv_step, 0)

    tell_p.wait()
    lane_f = lax.broadcasted_iota(jnp.int32, (SUFFIX, padded), 1).astype(F32)
    allowed = []
    for s in range(SLOTS):
        rank = held_first + s
        ok = rank <= held_last
        example = example_of(jnp.minimum(rank, ranks - 1))
        prefix = pb[example][0:1, 0:1]
        low = (lay.start(rank) - me * own_rows).astype(F32)
        patches = jnp.where(rank < lay.half, PATCH_S, PATCH_L).astype(F32)
        high = jnp.minimum(low + patches + prefix, jnp.float32(own_rows))
        high = jnp.where(ok, high, jnp.float32(-1.0))
        allowed.append(((lane_f >= low) & (lane_f < high)).astype(F32))
    allowed = jnp.concatenate(allowed * 4, axis=0) > 0.0

    at_holders(q_pairs)
    qh = jnp.concatenate([qbuf[s] for s in range(SLOTS)], axis=0)
    qh = (qh.astype(F32) * scale).astype(BF16)
    lane_c = lax.broadcasted_iota(jnp.int32, (SUFFIX, 128), 1)
    def swap(tile):
        return jnp.concatenate([tile[:, 64:], tile[:, :64]], axis=1)

    top_c = [jnp.zeros((SUFFIX, 128), F32) for _ in range(SLOTS)]
    sum_c = [jnp.zeros((SUFFIX, 128), F32) for _ in range(SLOTS)]
    for g in range(3):
        sl = slice(256 * g, 256 * g + 256)
        s = mm_nt(stack(qh[:, sl]), kvb[:, sl])
        s = jnp.where(allowed, s, NONE)
        top = jnp.max(s, axis=-1, keepdims=True)
        e = jnp.where(allowed, jnp.exp(s - top), 0.0)
        total = jnp.sum(e, axis=-1, keepdims=True)
        o = mm(e.astype(BF16), kvb[:, D + 256 * g : D + 256 * g + 256])
        o = o * jnp.where(total > 0.0, 1.0 / jnp.where(total > 0.0, total, 1.0), 0.0)
        o = unstack(o).astype(BF16)
        for n in range(SLOTS):
            osend[n, :, sl] = o[n * SUFFIX : (n + 1) * SUFFIX]
            for h in range(4):
                at = h * SLOTS * SUFFIX + n * SUFFIX
                hit = lane_c == 4 * g + h
                top_c[n] = jnp.where(hit, top[at : at + SUFFIX], top_c[n])
                sum_c[n] = jnp.where(hit, total[at : at + SUFFIX], sum_c[n])
    for n in range(SLOTS):
        ostat_send[n] = jnp.where(lane_c < 64, top_c[n], swap(sum_c[n]))
    to_owners(o_pairs)

    tick(7)
    ag_c.step_four()
    at_owners(o_pairs)
    spread[3].step_six()

    def expand(compact):
        low = lane_c < HEAD_DIM
        return jnp.concatenate(
            [jnp.where(low, compact[:, 2 * t : 2 * t + 1], compact[:, 2 * t + 1 : 2 * t + 2]) for t in range(6)],
            axis=1,
        )

    tops = [ostat[i] for i in range(SLOTS)]
    top_all = jnp.maximum(jnp.maximum(tops[0], tops[1]), tops[2])
    shares = [jnp.where(lane_c < 64, swap(tops[i]) * jnp.exp(tops[i] - top_all), 0.0) for i in range(SLOTS)]
    whole = shares[0] + shares[1] + shares[2]
    whole = jnp.where(whole > 0.0, whole, 1.0)
    lse = top_all + jnp.log(whole)
    cross = jnp.zeros((SUFFIX, D), F32)
    for i in range(SLOTS):
        cross = cross + expand(shares[i] / whole) * obuf[i].astype(F32)
    cm = cross.astype(BF16)

    after_cross = after_self + mm(cm, wb[:, LANE_CO : LANE_CO + D])
    hat_three, rs_three = normed(after_cross)
    n3 = (hat_three * gain[2]).astype(BF16)
    nb[token_rows(f, c, seat)] = n3
    ag_n.step_one()

    tick(8)
    ag_c.step_five()
    tick(9)
    spread[4].step_six()
    acts, slopes = [], []
    for j in range(4):
        value, slope = gelu_parts(mm(n3, wb[:, LANE_FI + D * j : LANE_FI + D * (j + 1)]))
        acts.append(value.astype(BF16))
        slopes.append(slope)
    act = jnp.concatenate(acts, axis=1)
    ag_c.step_six()
    for r in range(ranks):
        olr[token_rows(f, r % CORES, spots[r])] = cb[by_rank[r]]
    across_o = Across(olr, 0)
    across_n = Across(nb, 1)
    across_o.start()
    spread[5].step_six()
    unit_items = []

    def unit_device(unit, j):
        at = unit + 1
        return at % RING * (SIDE * CORES) + at // RING * CORES + j

    def push_part(which, at, to, src, dst):
        @pl.when(me == to)
        def _():
            dst[...] = src[...]

        @pl.when(me != to)
        def _():
            pltpu.make_async_remote_copy(
                src_ref=src, dst_ref=dst, send_sem=usend.at[which, at],
                recv_sem=urecv.at[which, me], device_id=(to, f), device_id_type=MESH,
            ).start()

        unit_items.append((which, at, to, src, dst))

    def push_left(units, at, left):
        lb[at] = left
        for unit in units:
            for j in range(CORES):
                lanes = pl.ds(j * PIECE, PIECE)
                push_part(0, CORES * unit + j, unit_device(unit, j), lb.at[at, :, lanes], rl.at[rows_of(me), lanes])

    def push_right(unit, right):
        for j in range(CORES):
            sb[unit, j] = right[:, j * PIECE : (j + 1) * PIECE]
            push_part(1, CORES * unit + j, unit_device(unit, j), sb.at[unit, j], rr.at[rows_of(me)])

    out_low = cb[mine]
    cot = out_low.astype(F32)
    hidden_grad = [mm_nt(out_low, wb[:, LANE_FO + D * j : LANE_FO + D * (j + 1)]) for j in range(4)]

    def by_hidden(j):
        parts = []
        for t in range(D // half_rows):
            at = D * j + t * half_rows
            col, unit = at // (4 * half_rows), (at % (4 * half_rows)) // half_rows
            parts.append(hidden_grad[unit][:, col * half_rows : (col + 1) * half_rows])
        return jnp.concatenate(parts, axis=1)

    n3_grad = jnp.zeros((SUFFIX, D), F32)
    for j in range(4):
        part = (by_hidden(j) * slopes[j]).astype(BF16)
        n3_grad = n3_grad + mm_nt(part, wb[:, LANE_FI + D * j : LANE_FI + D * (j + 1)])

    ag_n.step_two()
    part, ffn_gain_grad = norm_back(n3_grad, hat_three, rs_three, gain[2])
    cross_res = cot + part
    cross_low = cross_res.astype(BF16)
    d_mixed = mm_nt(cross_low, wb[:, LANE_CO : LANE_CO + D]).astype(BF16)
    dob[...] = d_mixed
    prod = d_mixed.astype(F32) * cross
    delta = jnp.zeros((SUFFIX, 128), F32)
    for t in range(6):
        tile = prod[:, 128 * t : 128 * (t + 1)]
        left = jnp.sum(jnp.where(lane_c < HEAD_DIM, tile, 0.0), axis=-1, keepdims=True)
        right = jnp.sum(jnp.where(lane_c < HEAD_DIM, 0.0, tile), axis=-1, keepdims=True)
        delta = jnp.where(lane_c == 2 * t, left, delta)
        delta = jnp.where(lane_c == 2 * t + 1, right, delta)
    dstat_b[...] = jnp.where(lane_c < 64, lse, swap(delta))
    to_holders(d_pairs)
    push_left((0, 1, 2), 0, n1)
    down = jnp.zeros((SUFFIX, D), F32)
    for j in range(4):
        lhs = jnp.concatenate(
            [act[:, i * 4 * half_rows + j * half_rows : i * 4 * half_rows + (j + 1) * half_rows] for i in range(columns)],
            axis=1,
        )
        down = down + mm(lhs, wb[:, LANE_FO + D * j : LANE_FO + D * (j + 1)])
    ob[0, my_slot] = (after_cross + down).astype(BF16)
    ag_out = ShortGather(place, block_view(ob.at[0]), block_bulk(ob.at[0]), short_sems, 1)

    at_holders(d_pairs)

    push_left((4,), 2, n2)
    push_left((3,), 1, sm)
    doh = jnp.concatenate([dobuf[s] for s in range(SLOTS)], axis=0)
    for g in range(3):
        sl = slice(256 * g, 256 * g + 256)
        kg = kvb[:, sl]
        vg = kvb[:, D + 256 * g : D + 256 * g + 256]
        q4 = stack(qh[:, sl])
        do4 = stack(doh[:, sl])
        lse_col = jnp.concatenate([dstat[n][:, 4 * g + h : 4 * g + h + 1] for h in range(4) for n in range(SLOTS)], axis=0)
        del_col = jnp.concatenate([dstat[n][:, 64 + 4 * g + h : 65 + 4 * g + h] for h in range(4) for n in range(SLOTS)], axis=0)
        s = mm_nt(q4, kg)
        p = jnp.where(allowed, jnp.exp(jnp.where(allowed, s - lse_col, 0.0)), 0.0)
        dp = mm_nt(do4, vg)
        ds = (p * (dp - del_col)).astype(BF16)
        kvg[:, D + 256 * g : D + 256 * g + 256] = mm_tn(p.astype(BF16), do4).astype(BF16)
        kvg[:, sl] = mm_tn(ds, q4).astype(BF16)
        dq = unstack(mm(ds, kg)) * scale
        for n in range(SLOTS):
            dqsend[n, :, sl] = dq[n * SUFFIX : (n + 1) * SUFFIX].astype(BF16)
    to_owners(dq_pairs)
    ag_n.step_three()
    across_n.start()
    def kp_step(i, carry):
        lane = pl.multiple_of(i * 256, 256)
        kp[:, pl.ds(lane, 256)] = mm_tn(memp[...], kvg[:, pl.ds(lane, 256)]).astype(BF16)
        return carry

    lax.fori_loop(0, 6, kp_step, 0)
    kr_item = pltpu.make_async_remote_copy(
        src_ref=kp.at[pl.ds(pl.multiple_of((1 - c) * half_rows, 128), half_rows)], dst_ref=kr,
        send_sem=ksend.at[2 * chips], recv_sem=krecv.at[chips], device_id=mate, device_id_type=MESH,
    )
    kr_item.start()

    across_o.relay()
    ag_out.step_one()
    at_owners(dq_pairs)
    push_left((5,), 3, cm)
    push_right(5, cross_low)
    kr_item.wait_recv()
    kc[...] = (
        kp[pl.ds(pl.multiple_of(c * half_rows, 128), half_rows)].astype(F32) + kr[...].astype(F32)
    ).astype(BF16)
    half_slabs = half_rows // SIDE

    def ky_copy(j):
        lanes = pl.ds(j * D, D)
        return pltpu.make_async_remote_copy(
            src_ref=kc.at[:, lanes], dst_ref=ky.at[:, lanes], send_sem=ksend.at[2 * chips + 1 + j],
            recv_sem=krecv.at[chips + 1 + j], device_id=(me, other), device_id_type=MESH,
        )

    def kx_copy(j):
        lanes = pl.ds(j * D, D)
        return pltpu.make_async_remote_copy(
            src_ref=kc.at[pl.ds(pl.multiple_of((1 - x) * half_slabs, 16), half_slabs), lanes], dst_ref=kx.at[:, lanes],
            send_sem=ksend.at[2 * chips + 3 + j], recv_sem=krecv.at[chips + 3 + j],
            device_id=(z * (SIDE * CORES) + (1 - x) * CORES + c, f), device_id_type=MESH,
        )

    @pl.when(c != f)
    def _():
        ky_copy(0).start()
        ky_copy(1).start()

    cqg = (dqbuf[0].astype(F32) + dqbuf[1].astype(F32) + dqbuf[2].astype(F32)).astype(BF16)
    n2_grad = mm_nt(cqg, wb[:, LANE_CQ : LANE_CQ + D])
    part, cross_gain_grad = norm_back(n2_grad, hat_two, rs_two, gain[1])
    self_res = cross_res + part
    self_low = self_res.astype(BF16)
    dmix = mm_nt(self_low, wb[:, LANE_SO : LANE_SO + D]).astype(BF16)
    dqs, dks, dvs = [], [], []
    for g in range(3):
        sl = slice(256 * g, 256 * g + 256)
        q4 = stack(qs[:, sl])
        do4 = stack(dmix[:, sl])
        p = self_p[g]
        dp = mm_nt(do4, v[:, sl])
        ds = (p * (dp - jnp.sum(p * dp, axis=-1, keepdims=True))).astype(BF16)
        dvs.append(mm_tn(p.astype(BF16), do4))
        dks.append(mm_tn(ds, q4))
        dqs.append(unstack(mm(ds, k[:, sl])) * scale)
    packed_grad = [jnp.concatenate(parts, axis=1).astype(BF16) for parts in (dqs, dks, dvs)]
    for j in range(3):
        push_right(j, packed_grad[j])
    push_right(4, cqg)
    push_right(3, self_low)

    n1_grad = jnp.zeros((SUFFIX, D), F32)
    for j in range(3):
        n1_grad = n1_grad + mm_nt(packed_grad[j], wb[:, D * j : D * (j + 1)])
    part, self_gain_grad = norm_back(n1_grad, hat_one, rs_one, gain[0])
    ob[1, my_slot] = (self_res + part).astype(BF16)
    ag_grad = ShortGather(place, block_view(ob.at[1]), block_bulk(ob.at[1]), short_sems, 2)
    gmine[0] = jnp.concatenate(
        [self_gain_grad, cross_gain_grad, ffn_gain_grad, jnp.zeros((5, D), F32)], axis=0
    )
    partners = (
        mate,
        (me, other),
        (z * (SIDE * CORES) + (1 - x) * CORES + c, f),
        ((z + 1 - 2 * lax.rem(z, 2)) * (SIDE * CORES) + x * CORES + c, f),
        (lax.rem(z + 2, RING) * (SIDE * CORES) + x * CORES + c, f),
    )

    def gain_copy(k):
        return pltpu.make_async_remote_copy(
            src_ref=gmine.at[k], dst_ref=gpeer.at[k], send_sem=gain_sem.at[0, k], recv_sem=gain_sem.at[1, k],
            device_id=partners[k], device_id_type=MESH,
        )

    def gain_step(k):
        gain_copy(k - 1).wait_recv()
        total = gmine[k - 1] + gpeer[k - 1]
        if k == len(partners):
            return total
        gmine[k] = total
        gain_copy(k).start()

    gain_copy(0).start()
    ag_grad.step_one()
    ag_out.step_two()

    ag_n.step_six()
    across_n.relay()
    across_o.wait()
    across_n.wait()

    rows_step = 128
    hidden = [col * 4 * half_rows + D * c for col in range(columns)]

    def ffn_rows(first, last):
        def one(i, carry):
            at = pl.ds(pl.multiple_of(i * rows_step, rows_step), rows_step)
            for col in range(columns):
                lane = pl.multiple_of(LANE_FI + hidden[col], 128)
                value, slope = gelu_parts(mm(nb[at], wb[:, pl.ds(lane, D)]))

                @pl.when(f == col)
                def _():
                    ab[at] = value.astype(BF16)

                back = []
                for t in range(CORES):
                    lane_o = pl.multiple_of(LANE_FO + D * (2 * c + t), 128)
                    back.append(mm_nt(olr[at], wb[col * half_rows : (col + 1) * half_rows, pl.ds(lane_o, D)]))
                hb[col, at] = (jnp.concatenate(back, axis=1) * slope).astype(BF16)
            return carry

        lax.fori_loop(first, last, one, 0)

    own_lanes = pl.ds(pl.multiple_of(f * half_rows, 128), half_rows)

    def ffn_in_sum(col):
        lane = pl.multiple_of(LANE_FI + hidden[col], 128)
        for part in range(0, D, PIECE):
            total = mm_tn(nb[:, own_lanes], hb[col, :, part : part + PIECE])
            gb[:, pl.ds(lane + part, PIECE)] = total.astype(BF16)

    def ffn_out_sum(t):
        lane = pl.multiple_of(LANE_FO + D * (2 * c + t), 128)
        for part in range(0, D, PIECE):
            total = mm_tn(ab[:, t * half_rows : (t + 1) * half_rows], olr[:, part : part + PIECE])
            gb[:, pl.ds(lane + part, PIECE)] = total.astype(BF16)

    f_items = []

    def to_mate(lane, width):
        ref = gb.at[:, pl.ds(pl.multiple_of(lane, 128), width)]
        item = pltpu.make_async_remote_copy(
            src_ref=ref, dst_ref=ref, send_sem=fsend.at[len(f_items)], recv_sem=frecv.at[len(f_items)],
            device_id=mate, device_id_type=MESH,
        )
        item.start()
        f_items.append(item)

    has_unit = (seat >= 1) & (seat <= UNIT_CHIPS)

    def unit_lane(n, cc):
        return PIECE * jnp.clip(n - 1, 0, UNIT_CHIPS - 1) + UNIT_CHIPS * PIECE * cc

    def unit_take(which, src, dst):
        def take(i, carry):
            @pl.when(i != me)
            def _():
                pltpu.make_async_remote_copy(
                    src_ref=src, dst_ref=dst(i), send_sem=usend.at[which, 0],
                    recv_sem=urecv.at[which, i], device_id=mate, device_id_type=MESH,
                ).wait_recv()

            return carry

        lax.fori_loop(0, ranks, take, 0)

    def left_lanes(core):
        return pl.ds(pl.multiple_of(core * PIECE, 128), PIECE)

    def left_copy(core):
        ref = rl.at[:, left_lanes(core)]
        return pltpu.make_async_remote_copy(
            src_ref=ref, dst_ref=ref, send_sem=ysend.at[1], recv_sem=yrecv.at[1], device_id=mate, device_id_type=MESH,
        )

    def unit_left(pred):
        @pl.when(pred)
        def _():
            unit_take(0, lb.at[0, :, pl.ds(0, PIECE)], lambda i: rl.at[rows_of(i), left_lanes(c)])
            left_copy(c).start()

    def unit_rows(n):
        return pl.ds(n * (half_rows // 2), half_rows // 2)

    def unit_copy(n):
        rows = unit_rows(n)
        return pltpu.make_async_remote_copy(
            src_ref=usend_b.at[rows], dst_ref=urecv_b.at[rows], send_sem=ysend.at[3 + n], recv_sem=yrecv.at[3 + n],
            device_id=(me, other), device_id_type=MESH,
        )

    def unit_sum(pred):
        @pl.when(pred)
        def _():
            unit_take(1, sb.at[0, 0], lambda i: rr.at[rows_of(i)])
            left_copy(1 - c).wait_recv()
            for col in range(columns):
                ug[col] = mm_tn(rl[:, col * half_rows : (col + 1) * half_rows], rr[...])
            usend_b[...] = ug[other].astype(BF16)
            for n in range(2):
                unit_copy(n).start()

    def unit_join(pred, n):
        @pl.when(pred)
        def _():
            unit_copy(n).wait_recv()
            rows = unit_rows(n)
            gb[rows, pl.ds(pl.multiple_of(unit_lane(seat, c), 128), PIECE)] = (
                ug[f, rows] + urecv_b[rows].astype(F32)
            ).astype(BF16)

    def has_block(zz, xx, cc):
        n = xx * RING + zz
        return (n >= 1) & (n <= UNIT_CHIPS)

    def unit_bulk(rows):
        width = UNIT_CHIPS * PIECE // SIDE
        return lambda cc, xx: gb.at[rows, pl.ds(pl.multiple_of(width * (SIDE * cc + xx), 128), width)]

    def gb_view(lane_of, rows):
        def view(zz, xx, cc):
            return gb.at[rows, pl.ds(pl.multiple_of(lane_of(xx * RING + zz, cc), 128), PIECE)]

        return view

    class UnitGather:
        def __init__(self):
            parts = [unit_rows(n) for n in range(2)]
            self.gathers = [
                Gather(place, gb_view(unit_lane, rows), unit_bulk(rows), sems, at, has_block)
                for at, rows in zip((2, 3), parts)
            ]

        def step(self, name):
            for gather in self.gathers:
                getattr(gather, name)()

    ag_u = UnitGather()

    k_items = []

    def k_copy(t, j):
        return pltpu.make_async_remote_copy(
            src_ref=ks.at[pl.ds(t * slab, slab), pl.ds(j * D, D)], dst_ref=cp.at[z],
            send_sem=ksend.at[t * CORES + j], recv_sem=krecv.at[z],
            device_id=(t * (SIDE * CORES) + x * CORES + j, f), device_id_type=MESH,
        )

    def k_over_x(j):
        lanes = pl.ds(j * D, D)

        @pl.when(c == f)
        def _():
            ky_copy(j).wait_recv()
            kc[:, lanes] = (kc[:, lanes].astype(F32) + ky[:, lanes].astype(F32)).astype(BF16)
            kx_copy(j).start()

    def k_on_line(j):
        lanes = pl.ds(j * D, D)

        @pl.when(c == f)
        def _():
            kx_copy(j).wait_recv()
            ks[:, lanes] = (
                kc[pl.ds(pl.multiple_of(x * half_slabs, 16), half_slabs), lanes].astype(F32) + kx[:, lanes].astype(F32)
            ).astype(BF16)

        for t in range(RING):
            here = (z == t) & (c == j)

            @pl.when((c == f) & here)
            def _():
                cp[z] = ks[t * slab : (t + 1) * slab, j * D : (j + 1) * D]

            @pl.when((c == f) & jnp.logical_not(here))
            def _():
                k_copy(t, j).start()

            k_items.append((t, j, here))

    k_over_x(0)
    ffn_rows(0, 2)
    gain_step(1)
    unit_left(has_unit)
    k_on_line(0)
    k_over_x(1)
    unit_sum(has_unit)
    ffn_rows(2, 4)
    gain_step(2)
    k_on_line(1)
    unit_join(has_unit, 0)
    ag_u.gathers[0].step_one()
    ffn_rows(4, 5)
    unit_join(has_unit, 1)
    ag_u.gathers[1].step_one()
    ffn_rows(5, 6)
    gain_step(3)

    def take_k(i, carry):
        @pl.when((i != z) | (c != f))
        def _():
            pltpu.make_async_remote_copy(
                src_ref=ks.at[pl.ds(0, slab), pl.ds(0, D)], dst_ref=cp.at[i], send_sem=ksend.at[0],
                recv_sem=krecv.at[i], device_id=mate, device_id_type=MESH,
            ).wait_recv()

        return carry

    lax.fori_loop(0, RING, take_k, 0)
    total = cp[0].astype(F32)
    for i in range(1, RING):
        total = total + cp[i].astype(F32)
    k_lane = pl.multiple_of(OUT_CKV + c * D, 128)
    gb[pl.ds(pl.multiple_of(x * half_slabs + z * slab, 16), slab), pl.ds(k_lane, D)] = total.astype(BF16)

    def kv_view(zz, xx, cc):
        row = pl.multiple_of(xx * half_slabs + zz * slab, 16)
        return gb.at[pl.ds(row, slab), pl.ds(pl.multiple_of(OUT_CKV + cc * D, 128), D)]

    ag_k = Gather(place, kv_view, lambda cc, xx: gb.at[pl.ds(pl.multiple_of(xx * half_slabs, 16), half_slabs), pl.ds(pl.multiple_of(OUT_CKV + cc * D, 128), D)], sems, 4)
    ag_k.step_one()

    def mg_step(i, carry):
        row = pl.multiple_of(i * 128, 128)
        memgrad_ref[pl.ds(row, 128)] = mm_nt(kvg[pl.ds(row, 128)], wb[:, LANE_CKV : LANE_CKV + 2 * D])
        return carry

    full = own_rows // 128
    lax.fori_loop(0, full, mg_step, 0)
    if own_rows % 128:
        tail = mm_nt(kvg[full * 128 : (full + 1) * 128], wb[:, LANE_CKV : LANE_CKV + 2 * D])
        memgrad_ref[full * 128 : own_rows] = tail[0 : own_rows - full * 128]


    ag_u.gathers[0].step_two()
    ffn_rows(6, 7)
    ag_u.gathers[1].step_two()
    ffn_rows(7, 8)
    ag_u.gathers[0].step_three()
    gain_step(4)
    ag_k.step_two()
    ffn_in_sum(0)
    to_mate(LANE_FI + hidden[0], D)
    ag_u.gathers[1].step_three()
    ag_grad.step_two()
    ag_out.step_three()
    ffn_in_sum(1)
    to_mate(LANE_FI + hidden[1], D)
    ag_u.gathers[0].step_four()
    ag_k.step_three()
    ffn_out_sum(0)
    ag_u.gathers[1].step_four()
    ffn_out_sum(1)
    to_mate(LANE_FO + CORES * D * c, CORES * D)
    ag_grad.step_three()
    ag_out.step_six()
    ag_u.gathers[0].step_five()
    ag_k.step_four()
    ag_u.gathers[1].step_five()
    for n, (lane, width) in enumerate(
        [(LANE_FI + col * 4 * half_rows + D * (1 - c), D) for col in range(columns)] + [(LANE_FO + CORES * D * (1 - c), CORES * D)]
    ):
        ref = gb.at[:, pl.ds(pl.multiple_of(lane, 128), width)]
        pltpu.make_async_remote_copy(
            src_ref=ref, dst_ref=ref, send_sem=fsend.at[n], recv_sem=frecv.at[n], device_id=mate, device_id_type=MESH,
        ).wait_recv()
    outs = []

    def write(lane, width):
        lanes = pl.ds(lane, width)
        item = pltpu.make_async_copy(gb.at[:, lanes], weights_out_ref.at[:, lanes], load_sem.at[len(outs)])
        item.start()
        outs.append(item)

    write(LANE_FI, 8 * D)
    ag_k.step_five()
    ag_grad.step_six()
    out_ref[...] = ob[0, out_slot].astype(F32)
    grad_ref[...] = ob[1, out_slot].astype(F32)
    gains_all = gain_step(5)
    own_gain = gains_all[:, 0:half_rows]
    for i in range(1, columns):
        own_gain = jnp.where(f == i, gains_all[:, i * half_rows : (i + 1) * half_rows], own_gain)
    gain_out_ref[...] = own_gain
    ag_u.step("step_six")
    write(0, OUT_CKV)
    ag_k.step_six()
    write(OUT_CKV, 2 * D)

    to_holders_sent(q_pairs)
    to_owners_sent(o_pairs)
    to_holders_sent(d_pairs)
    to_owners_sent(dq_pairs)
    for which, at, to, src, dst in unit_items:
        @pl.when(me != to)
        def _():
            pltpu.make_async_remote_copy(
                src_ref=src, dst_ref=dst, send_sem=usend.at[which, at],
                recv_sem=urecv.at[which, 0], device_id=(to, f), device_id_type=MESH,
            ).wait_send()
    @pl.when(has_unit)
    def _():
        for n in range(2):
            unit_copy(n).wait_send()
        left_copy(c).wait_send()

    for t, j, here in k_items:
        @pl.when((c == f) & jnp.logical_not(here))
        def _():
            k_copy(t, j).wait_send()

    @pl.when(c == f)
    def _():
        kx_copy(0).wait_send()
        kx_copy(1).wait_send()

    across_o.finish()
    across_n.finish()
    for item in f_items:
        item.wait_send()
    kr_item.wait_send()

    @pl.when(c != f)
    def _():
        ky_copy(0).wait_send()
        ky_copy(1).wait_send()

    for item in y_items:
        item.wait_send()
    tell_p.finish()
    for k in range(len(partners)):
        gain_copy(k).wait_send()
    for item in [ag_x, *spread, ag_c, ag_n, *ag_u.gathers, ag_out, ag_grad, ag_k]:
        item.finish()
    for item in outs:
        item.wait()


def fused_body(
    ranks, columns,
    decoder_in, memory, res_group, prefix_len, self_gain, self_qkv, self_out, cross_gain, cross_query,
    cross_kv, cross_out, ffn_gain, ffn_in, ffn_out, cotangent,
):
    half_rows = D // columns
    chips = ranks // CORES
    slab = half_rows // chips
    own_rows = memory.shape[1]
    padded = -(-own_rows // 128) * 128
    tokens = ranks * SUFFIX
    vm = pl.BlockSpec(memory_space=pltpu.VMEM)
    sm = pl.BlockSpec(memory_space=pltpu.SMEM)
    hbm = pl.BlockSpec(memory_space=pl.ANY)
    dma = pltpu.SemaphoreType.DMA
    scratch = [
        pltpu.VMEM((D, UNITS * D), BF16),
        pltpu.VMEM((half_rows, UNITS * D), BF16),
        pltpu.VMEM((tokens, D), BF16),
        pltpu.VMEM((tokens, PIECE), BF16),
        pltpu.VMEM((4, SUFFIX, D), BF16),
        pltpu.VMEM((UNIT_CHIPS, CORES, SUFFIX, PIECE), BF16),
        pltpu.VMEM((ranks, SUFFIX, D), F32),
        pltpu.VMEM((ranks, SUFFIX, D), BF16),
        pltpu.VMEM((columns * tokens, D), BF16),
        pltpu.VMEM((columns * tokens, D), BF16),
        pltpu.VMEM((2, ranks, SUFFIX, D), BF16),
        pltpu.VMEM((ranks, 8, 128), F32),
        pltpu.VMEM((columns, 16, 128), F32),
        pltpu.VMEM((padded, D), BF16),
        pltpu.VMEM((padded, 2 * D), BF16),
        pltpu.VMEM((padded, 2 * D), BF16),
        pltpu.VMEM((D, 2 * D), BF16),
        pltpu.VMEM((half_rows, 2 * D), BF16),
        pltpu.VMEM((half_rows, 2 * D), BF16),
        pltpu.VMEM((half_rows, 2 * D), BF16),
        pltpu.VMEM((RING, slab, D), BF16),
        pltpu.VMEM((half_rows // SIDE, 2 * D), BF16),
        pltpu.VMEM((half_rows // SIDE, 2 * D), BF16),
        pltpu.VMEM((columns, columns * tokens, D), BF16),
        pltpu.VMEM((columns * tokens, D), BF16),
        pltpu.VMEM((columns, half_rows, PIECE), F32),
        pltpu.VMEM((half_rows, PIECE), BF16),
        pltpu.VMEM((half_rows, PIECE), BF16),
        pltpu.VMEM((SUFFIX, D), BF16),
        pltpu.VMEM((SLOTS, SUFFIX, D), BF16),
        pltpu.VMEM((SLOTS, SUFFIX, D), BF16),
        pltpu.VMEM((SLOTS, SUFFIX, 128), F32),
        pltpu.VMEM((SLOTS, SUFFIX, D), BF16),
        pltpu.VMEM((SLOTS, SUFFIX, 128), F32),
        pltpu.VMEM((SUFFIX, D), BF16),
        pltpu.VMEM((SUFFIX, 128), F32),
        pltpu.VMEM((SLOTS, SUFFIX, D), BF16),
        pltpu.VMEM((SLOTS, SUFFIX, 128), F32),
        pltpu.VMEM((SLOTS, SUFFIX, D), BF16),
        pltpu.VMEM((SLOTS, SUFFIX, D), BF16),
        pltpu.VMEM((5, 8, D), F32),
        pltpu.VMEM((5, 8, D), F32),
        dma((10,)),
        dma((len(CHUNKS), 17)),
        dma((len(CHUNKS), 14)),
        dma((5, 17)),
        dma((5, 10)),
        dma((3, 9)),
        dma((3, 10)),
        dma((1, ranks)),
        dma((1, ranks)),
        dma((2, 5)),
        dma((2, 2)),
        dma((2, 2)),
        dma((3,)),
        dma((3,)),
        dma((5,)),
        dma((5,)),
        dma((6, SLOTS)),
        dma((6, SLOTS)),
        dma((2, CORES * UNIT_CHIPS)),
        dma((2, ranks)),
        dma((2 * chips + 5,)),
        dma((chips + 5,)),
    ]
    out, grad, memgrad, gain_grads, weight_grads = pl.pallas_call(
        partial(layer_kernel, ranks, columns),
        out_shape=(
            jax.ShapeDtypeStruct((SUFFIX, D), F32),
            jax.ShapeDtypeStruct((SUFFIX, D), F32),
            jax.ShapeDtypeStruct((own_rows, D), F32),
            jax.ShapeDtypeStruct((8, half_rows), F32),
            jax.ShapeDtypeStruct((half_rows, UNITS * D), BF16),
        ),
        in_specs=[vm, vm, vm, sm, sm, vm, vm, vm] + [hbm] * 7,
        out_specs=(vm, vm, vm, vm, hbm),
        scratch_shapes=scratch,
        compiler_params=pltpu.CompilerParams(
            collective_id=0, has_side_effects=True, vmem_limit_bytes=63 * 2**20
        ),
        name="layer",
    )(
        decoder_in[0], cotangent[0], memory[0], res_group, prefix_len, self_gain, cross_gain, ffn_gain,
        self_qkv, self_out, cross_query, cross_kv, cross_out, ffn_in, ffn_out,
    )

    return unpack(half_rows, columns, weight_grads, memgrad, out, grad, gain_grads)


SPLIT = ((0, 3), (3, 1), (4, 1), (OUT_CKV, 2 * D), (5, 1), (LANE_FI, 4 * D))
WHOLE = (OUT_CKV, LANE_FI)


def unpack_kernel(w_ref, m_ref, o_ref, g_ref, gains_ref, *refs):
    *weights, ffn_out_ref, mem_ref, out_ref, grad_ref, one_ref, two_ref, three_ref = refs
    for n, ref in enumerate((one_ref, two_ref, three_ref)):
        ref[...] = gains_ref[n : n + 1].reshape(ref.shape)
    for (low, width), ref in zip(SPLIT, weights):
        if low in WHOLE:
            ref[...] = w_ref[:, low : low + width].astype(F32)
            continue
        for n in range(width):
            for j in range(CORES):
                at = (UNIT_CHIPS * j + low + n) * PIECE
                to = (CORES * n + j) * PIECE
                ref[:, to : to + PIECE] = w_ref[:, at : at + PIECE].astype(F32)
    for j in range(4):
        ffn_out_ref[j] = w_ref[:, LANE_FO + D * j : LANE_FO + D * (j + 1)].astype(F32)
    mem_ref[:, 0, :] = m_ref[...]
    out_ref[...] = o_ref[...]
    grad_ref[...] = g_ref[...]


def unpack(half_rows, columns, weight_grads, memgrad, out, grad, gain_grads):
    steps = 2
    rows = half_rows // steps
    own_rows = memgrad.shape[0]
    mem_rows = -(-own_rows // (8 * steps)) * 8
    tokens = out.shape[0] // steps
    block = lambda height, width: pl.BlockSpec((height, width), lambda i: (i, 0))
    results = pl.pallas_call(
        unpack_kernel,
        grid=(steps,),
        out_shape=[jax.ShapeDtypeStruct((half_rows, width if low in WHOLE else width * D), F32) for low, width in SPLIT]
        + [
            jax.ShapeDtypeStruct((4, half_rows, D), F32),
            jax.ShapeDtypeStruct((own_rows, 1, D), F32),
            jax.ShapeDtypeStruct(out.shape, F32),
            jax.ShapeDtypeStruct(grad.shape, F32),
        ]
        + [jax.ShapeDtypeStruct((half_rows,), F32)] * 3,
        in_specs=[block(rows, UNITS * D), block(mem_rows, D), block(tokens, D), block(tokens, D), pl.BlockSpec(gain_grads.shape, lambda i: (0, 0))],
        out_specs=[block(rows, width if low in WHOLE else width * D) for low, width in SPLIT]
        + [
            pl.BlockSpec((4, rows, D), lambda i: (0, i, 0)),
            pl.BlockSpec((mem_rows, 1, D), lambda i: (i, 0, 0)),
            block(tokens, D),
            block(tokens, D),
        ]
        + [pl.BlockSpec((half_rows,), lambda i: (0,))] * 3,
        compiler_params=pltpu.CompilerParams(vmem_limit_bytes=63 * 2**20),
        name="unpack",
    )(weight_grads, memgrad, out, grad, gain_grads)
    qkv, so, cq, ckv, co, fi, fo, mem, out, grad, gain_one, gain_two, gain_three = results
    return (
        out[None], grad[None], mem.reshape(1, own_rows, D),
        gain_one, qkv, so, gain_two, cq, ckv, co, gain_three, fi, fo.reshape(4 * half_rows, D),
    )


def layer_norm(value, gain):
    mean = jnp.mean(value, axis=-1, keepdims=True)
    centred = value - mean
    variance = jnp.mean(centred * centred, axis=-1, keepdims=True)
    return centred * lax.rsqrt(variance + norm_eps) * gain


def product(left, right):
    return jnp.dot(left, right, preferred_element_type=jnp.float32)


def outer_sum(left, right):
    flat_left = left.reshape(-1, left.shape[-1])
    flat_right = right.reshape(-1, right.shape[-1])
    return lax.dot_general(
        flat_left, flat_right, (((0,), (0,)), ((), ())), preferred_element_type=jnp.float32
    )


def back_product(grad, weight):
    return lax.dot_general(
        grad, weight, (((grad.ndim - 1,), (1,)), ((), ())), preferred_element_type=jnp.float32
    )


def attend(query, keys, values, allowed, scale):
    scores = jnp.einsum("eqhd,ekhd->ehqk", query, keys, preferred_element_type=jnp.float32) * scale
    scores = jnp.where(allowed[:, None], scores, -1e30)
    top = jnp.max(scores, axis=-1, keepdims=True)
    weights = jnp.exp(scores - top)
    probs = weights / jnp.sum(weights, axis=-1, keepdims=True)
    mixed = jnp.einsum(
        "ehqk,ekhd->eqhd", probs.astype(jnp.bfloat16), values, preferred_element_type=jnp.float32
    )
    return (mixed.astype(jnp.bfloat16), probs)


def attend_back(grad_mixed, query, keys, values, probs, scale):
    probs_low = probs.astype(jnp.bfloat16)
    grad_values = jnp.einsum(
        "ehqk,eqhd->ekhd", probs_low, grad_mixed, preferred_element_type=jnp.float32
    )
    grad_probs = jnp.einsum(
        "eqhd,ekhd->ehqk", grad_mixed, values, preferred_element_type=jnp.float32
    )
    grad_scores = probs * (grad_probs - jnp.sum(probs * grad_probs, axis=-1, keepdims=True))
    grad_low = grad_scores.astype(jnp.bfloat16)
    grad_query = (
        jnp.einsum("ehqk,ekhd->eqhd", grad_low, keys, preferred_element_type=jnp.float32) * scale
    )
    grad_keys = (
        jnp.einsum("ehqk,eqhd->ekhd", grad_low, query, preferred_element_type=jnp.float32) * scale
    )
    return (grad_query, grad_keys, grad_values)


def window_layout(res_group, mem_col):
    small = 1 - res_group
    small_count = jnp.sum(small, axis=-1, keepdims=True)
    small_before = jnp.cumsum(small, axis=-1) - small
    large_before = jnp.cumsum(res_group, axis=-1) - res_group
    offset = jnp.where(
        res_group == 1, SLOT_S * small_count + SLOT_L * large_before, SLOT_S * small_before
    )
    start = jnp.minimum(offset, mem_col - SLOT_L)
    return (offset, start)


def take_windows(column, starts):
    return jax.vmap(lambda begin: lax.dynamic_slice_in_dim(column, begin, SLOT_L, 0))(starts)


def forward(decoder_rows, windows, cross_allowed, weights):
    (
        self_gain,
        self_qkv,
        self_out,
        cross_gain,
        cross_query,
        cross_kv,
        cross_out,
        ffn_gain,
        ffn_in,
        ffn_out,
    ) = weights
    count = decoder_rows.shape[0] // SUFFIX
    scale = HEAD_DIM ** (-0.5)
    row_index = lax.broadcasted_iota(jnp.int32, (SUFFIX, SUFFIX), 0)
    col_index = lax.broadcasted_iota(jnp.int32, (SUFFIX, SUFFIX), 1)
    causal = (row_index >= col_index)[None]
    resid = decoder_rows.reshape(count, SUFFIX, D)
    normed_one = layer_norm(resid, self_gain.astype(jnp.float32)).astype(jnp.bfloat16)
    packed = product(normed_one, self_qkv).astype(jnp.bfloat16)
    heads = packed.reshape(count, SUFFIX, 3, HEADS, HEAD_DIM)
    self_mixed, self_probs = attend(heads[:, :, 0], heads[:, :, 1], heads[:, :, 2], causal, scale)
    self_mixed = self_mixed.reshape(count, SUFFIX, D)
    after_self = resid + product(self_mixed, self_out)
    normed_two = layer_norm(after_self, cross_gain.astype(jnp.float32)).astype(jnp.bfloat16)
    cross_q = product(normed_two, cross_query).astype(jnp.bfloat16)
    window_kv = product(windows, cross_kv).astype(jnp.bfloat16)
    query_heads = cross_q.reshape(count, SUFFIX, HEADS, HEAD_DIM)
    kv_heads = window_kv.reshape(count, SLOT_L, 2, HEADS, HEAD_DIM)
    cross_mixed, cross_probs = attend(
        query_heads, kv_heads[:, :, 0], kv_heads[:, :, 1], cross_allowed, scale
    )
    cross_mixed = cross_mixed.reshape(count, SUFFIX, D)
    after_cross = after_self + product(cross_mixed, cross_out)
    normed_three = layer_norm(after_cross, ffn_gain.astype(jnp.float32)).astype(jnp.bfloat16)
    up = product(normed_three, ffn_in)
    act = jax.nn.gelu(up, approximate=True).astype(jnp.bfloat16)
    result = after_cross + product(act, ffn_out)
    return (
        resid,
        normed_one,
        packed,
        self_probs,
        self_mixed,
        after_self,
        normed_two,
        cross_q,
        window_kv,
        cross_probs,
        cross_mixed,
        after_cross,
        normed_three,
        up,
        act,
        result,
    )


def backward(grad_out, saved, weights):
    (
        self_gain,
        self_qkv,
        self_out,
        cross_gain,
        cross_query,
        cross_kv,
        cross_out,
        ffn_gain,
        ffn_in,
        ffn_out,
    ) = weights
    (
        resid,
        normed_one,
        packed,
        self_probs,
        self_mixed,
        after_self,
        normed_two,
        cross_q,
        window_kv,
        cross_probs,
        cross_mixed,
        after_cross,
        normed_three,
        up,
        act,
        result,
    ) = saved
    count = resid.shape[0]
    scale = HEAD_DIM ** (-0.5)
    grad_out = grad_out.reshape(count, SUFFIX, D)
    out_low = grad_out.astype(jnp.bfloat16)
    ffn_out_grad = outer_sum(act, out_low)
    act_grad = back_product(out_low, ffn_out)
    gelu_value, gelu_back = jax.vjp(partial(jax.nn.gelu, approximate=True), up)
    up_grad = gelu_back(act_grad)[0].astype(jnp.bfloat16)
    ffn_in_grad = outer_sum(normed_three, up_grad)
    normed_three_grad = back_product(up_grad, ffn_in)
    norm_value, norm_back = jax.vjp(layer_norm, after_cross, ffn_gain.astype(jnp.float32))
    resid_part, ffn_gain_grad = norm_back(normed_three_grad)
    cross_res_grad = grad_out + resid_part
    cross_low = cross_res_grad.astype(jnp.bfloat16)
    cross_out_grad = outer_sum(cross_mixed, cross_low)
    mixed_grad = (
        back_product(cross_low, cross_out)
        .astype(jnp.bfloat16)
        .reshape(count, SUFFIX, HEADS, HEAD_DIM)
    )
    query_heads = cross_q.reshape(count, SUFFIX, HEADS, HEAD_DIM)
    kv_heads = window_kv.reshape(count, SLOT_L, 2, HEADS, HEAD_DIM)
    query_grad, keys_grad, values_grad = attend_back(
        mixed_grad, query_heads, kv_heads[:, :, 0], kv_heads[:, :, 1], cross_probs, scale
    )
    cross_q_grad = query_grad.reshape(count, SUFFIX, D).astype(jnp.bfloat16)
    window_kv_grad = (
        jnp.stack((keys_grad, values_grad), axis=2)
        .reshape(count, SLOT_L, 2 * D)
        .astype(jnp.bfloat16)
    )
    cross_query_grad = outer_sum(normed_two, cross_q_grad)
    normed_two_grad = back_product(cross_q_grad, cross_query)
    norm_value, norm_back = jax.vjp(layer_norm, after_self, cross_gain.astype(jnp.float32))
    resid_part, cross_gain_grad = norm_back(normed_two_grad)
    self_res_grad = cross_res_grad + resid_part
    self_low = self_res_grad.astype(jnp.bfloat16)
    self_out_grad = outer_sum(self_mixed, self_low)
    mixed_grad = (
        back_product(self_low, self_out)
        .astype(jnp.bfloat16)
        .reshape(count, SUFFIX, HEADS, HEAD_DIM)
    )
    heads = packed.reshape(count, SUFFIX, 3, HEADS, HEAD_DIM)
    query_grad, keys_grad, values_grad = attend_back(
        mixed_grad, heads[:, :, 0], heads[:, :, 1], heads[:, :, 2], self_probs, scale
    )
    packed_grad = (
        jnp.stack((query_grad, keys_grad, values_grad), axis=2)
        .reshape(count, SUFFIX, 3 * D)
        .astype(jnp.bfloat16)
    )
    self_qkv_grad = outer_sum(normed_one, packed_grad)
    normed_one_grad = back_product(packed_grad, self_qkv)
    norm_value, norm_back = jax.vjp(layer_norm, resid, self_gain.astype(jnp.float32))
    resid_part, self_gain_grad = norm_back(normed_one_grad)
    decoder_grad = self_res_grad + resid_part
    weight_grads = (
        self_gain_grad,
        self_qkv_grad,
        self_out_grad,
        cross_gain_grad,
        cross_query_grad,
        cross_out_grad,
        ffn_gain_grad,
        ffn_in_grad,
        ffn_out_grad,
    )
    return (decoder_grad, window_kv_grad, weight_grads)


def make_placer(all_starts, lowest, own_rows):

    def place(total, piece, begin):

        def add_one(item, acc):
            relative = all_starts[item] - lowest
            inside = ((relative > -SLOT_L) & (relative < own_rows)).astype(jnp.float32)
            spot = jnp.clip(relative + SLOT_L, 0, own_rows + SLOT_L)
            current = lax.dynamic_slice_in_dim(acc, spot, SLOT_L, 0)
            added = current + piece[item].astype(jnp.float32) * inside
            return lax.dynamic_update_slice_in_dim(acc, added, spot, 0)

        return lax.fori_loop(0, piece.shape[0], add_one, total)

    return place


def body(
    decoder_in,
    memory,
    res_group,
    prefix_len,
    self_gain,
    self_qkv,
    self_out,
    cross_gain,
    cross_query,
    cross_kv,
    cross_out,
    ffn_gain,
    ffn_in,
    ffn_out,
    cotangent,
):
    count = prefix_len.shape[1]
    own_rows = memory.shape[1]
    mem_col = own_rows * lax.axis_size("dp")
    offset, start = window_layout(res_group, mem_col)
    all_starts = start[0]
    first = lax.axis_index("dp") * count
    own_offset = lax.dynamic_slice_in_dim(offset[0], first, count)
    own_start = lax.dynamic_slice_in_dim(all_starts, first, count)
    own_group = lax.dynamic_slice_in_dim(res_group[0], first, count)
    valid = jnp.where(own_group == 1, PATCH_L, PATCH_S) + prefix_len[0]
    positions = own_start[:, None] + jnp.arange(SLOT_L, dtype=jnp.int32)[None]
    cross_allowed = (
        (positions >= own_offset[:, None]) & (positions < (own_offset + valid)[:, None])
    )[:, None]
    weights = (
        lax.all_gather(self_gain, "fsdp", axis=0, tiled=True),
        lax.all_gather(self_qkv, "fsdp", axis=0, tiled=True),
        lax.all_gather(self_out, "fsdp", axis=0, tiled=True),
        lax.all_gather(cross_gain, "fsdp", axis=0, tiled=True),
        lax.all_gather(cross_query, "fsdp", axis=0, tiled=True),
        lax.all_gather(cross_kv, "fsdp", axis=0, tiled=True),
        lax.all_gather(cross_out, "fsdp", axis=0, tiled=True),
        lax.all_gather(ffn_gain, "fsdp", axis=0, tiled=True),
        lax.all_gather(ffn_in, "fsdp", axis=0, tiled=True),
        lax.all_gather(ffn_out, "fsdp", axis=0, tiled=True),
    )
    column = lax.all_gather(memory[0], "dp", axis=0, tiled=True)
    windows = take_windows(column, own_start)
    saved = forward(decoder_in[0], windows, cross_allowed, weights)
    decoder_out = saved[-1]
    weights = (
        lax.all_gather(self_gain, "fsdp", axis=0, tiled=True),
        lax.all_gather(self_qkv, "fsdp", axis=0, tiled=True),
        lax.all_gather(self_out, "fsdp", axis=0, tiled=True),
        lax.all_gather(cross_gain, "fsdp", axis=0, tiled=True),
        lax.all_gather(cross_query, "fsdp", axis=0, tiled=True),
        lax.all_gather(cross_kv, "fsdp", axis=0, tiled=True),
        lax.all_gather(cross_out, "fsdp", axis=0, tiled=True),
        lax.all_gather(ffn_gain, "fsdp", axis=0, tiled=True),
        lax.all_gather(ffn_in, "fsdp", axis=0, tiled=True),
        lax.all_gather(ffn_out, "fsdp", axis=0, tiled=True),
    )
    column = lax.all_gather(memory[0], "dp", axis=0, tiled=True)
    windows = take_windows(column, own_start)
    saved = forward(decoder_in[0], windows, cross_allowed, weights)
    whole_kv = weights[5]
    decoder_grad, window_kv_grad, local_grads = backward(cotangent[0], saved, weights)
    lowest = lax.axis_index("dp") * own_rows
    place = make_placer(all_starts, lowest, own_rows)
    empty = jnp.zeros((own_rows + 2 * SLOT_L, 2 * D), jnp.float32)
    summed = place(empty, lax.all_gather(window_kv_grad, "dp", axis=0, tiled=True), jnp.int32(0))
    own_kv_grad = summed[SLOT_L : SLOT_L + own_rows].astype(jnp.bfloat16)
    memory_grad = back_product(own_kv_grad, whole_kv)
    cross_kv_part = outer_sum(memory[0], own_kv_grad)
    grads = (
        local_grads[0],
        local_grads[1],
        local_grads[2],
        local_grads[3],
        local_grads[4],
        cross_kv_part,
        local_grads[5],
        local_grads[6],
        local_grads[7],
        local_grads[8],
    )
    shards = (
        lax.psum_scatter(
            grads[0].astype(jnp.bfloat16), "fsdp", scatter_dimension=0, tiled=True
        ).astype(jnp.float32),
        lax.psum_scatter(
            grads[1].astype(jnp.bfloat16), "fsdp", scatter_dimension=0, tiled=True
        ).astype(jnp.float32),
        lax.psum_scatter(
            grads[2].astype(jnp.bfloat16), "fsdp", scatter_dimension=0, tiled=True
        ).astype(jnp.float32),
        lax.psum_scatter(
            grads[3].astype(jnp.bfloat16), "fsdp", scatter_dimension=0, tiled=True
        ).astype(jnp.float32),
        lax.psum_scatter(
            grads[4].astype(jnp.bfloat16), "fsdp", scatter_dimension=0, tiled=True
        ).astype(jnp.float32),
        lax.psum_scatter(
            grads[5].astype(jnp.bfloat16), "fsdp", scatter_dimension=0, tiled=True
        ).astype(jnp.float32),
        lax.psum_scatter(
            grads[6].astype(jnp.bfloat16), "fsdp", scatter_dimension=0, tiled=True
        ).astype(jnp.float32),
        lax.psum_scatter(
            grads[7].astype(jnp.bfloat16), "fsdp", scatter_dimension=0, tiled=True
        ).astype(jnp.float32),
        lax.psum_scatter(
            grads[8].astype(jnp.bfloat16), "fsdp", scatter_dimension=0, tiled=True
        ).astype(jnp.float32),
        lax.psum_scatter(
            grads[9].astype(jnp.bfloat16), "fsdp", scatter_dimension=0, tiled=True
        ).astype(jnp.float32),
    )
    totals = (
        lax.psum(shards[0].astype(jnp.bfloat16), "dp").astype(jnp.float32),
        lax.psum(shards[1].astype(jnp.bfloat16), "dp").astype(jnp.float32),
        lax.psum(shards[2].astype(jnp.bfloat16), "dp").astype(jnp.float32),
        lax.psum(shards[3].astype(jnp.bfloat16), "dp").astype(jnp.float32),
        lax.psum(shards[4].astype(jnp.bfloat16), "dp").astype(jnp.float32),
        lax.psum(shards[5].astype(jnp.bfloat16), "dp").astype(jnp.float32),
        lax.psum(shards[6].astype(jnp.bfloat16), "dp").astype(jnp.float32),
        lax.psum(shards[7].astype(jnp.bfloat16), "dp").astype(jnp.float32),
        lax.psum(shards[8].astype(jnp.bfloat16), "dp").astype(jnp.float32),
        lax.psum(shards[9].astype(jnp.bfloat16), "dp").astype(jnp.float32),
    )
    return (
        decoder_out,
        decoder_grad,
        memory_grad[None],
        totals[0],
        totals[1],
        totals[2],
        totals[3],
        totals[4],
        totals[5],
        totals[6],
        totals[7],
        totals[8],
        totals[9],
    )


def choose(mesh):
    ranks, columns = mesh.shape["dp"], mesh.shape["fsdp"]
    slabs = (D // columns) % (16 * (ranks // CORES)) == 0
    if slabs and columns == 2 and ranks == RING * SIDE * CORES:
        return partial(fused_body, ranks, columns)
    return body


def solution(mesh):
    placed = (
        P("fsdp", "dp", None),
        P("fsdp", "dp", None),
        P("fsdp", None),
        P("fsdp", "dp"),
        P("fsdp"),
        P("fsdp", None),
        P("fsdp", None),
        P("fsdp"),
        P("fsdp", None),
        P("fsdp", None),
        P("fsdp", None),
        P("fsdp"),
        P("fsdp", None),
        P("fsdp", None),
        P("fsdp", "dp", None),
    )
    return jax.shard_map(
        choose(mesh),
        mesh=mesh,
        in_specs=placed,
        out_specs=(
            P("fsdp", "dp", None),
            P("fsdp", "dp", None),
            P("fsdp", "dp", None),
            P("fsdp"),
            P("fsdp", None),
            P("fsdp", None),
            P("fsdp"),
            P("fsdp", None),
            P("fsdp", None),
            P("fsdp", None),
            P("fsdp"),
            P("fsdp", None),
            P("fsdp", None),
        ),
        check_vma=False,
    )
```

```python
from functools import partial

import jax
import jax.numpy as jnp
from jax import lax
from jax.experimental import pallas as pl
from jax.experimental.pallas import tpu as pltpu
from jax.sharding import PartitionSpec as P

D = 768
HEADS = 12
HEAD_DIM = 64
SUFFIX = 32
PATCH_S = 196
PATCH_L = 576
SLOT_S = 228
SLOT_L = 608
RING = 4
SIDE = 2
CORES = 2
norm_eps = 1e-06
MESH = pl.DeviceIdType.MESH
F32 = jnp.float32
BF16 = jnp.bfloat16
NONE = -1e30


def mm(left, right):
    return jnp.dot(left, right, preferred_element_type=F32)


def mm_nt(left, right):
    return lax.dot_general(left, right, (((1,), (1,)), ((), ())), preferred_element_type=F32)


def mm_tn(left, right):
    return lax.dot_general(left, right, (((0,), (0,)), ((), ())), preferred_element_type=F32)


def normed(value):
    mean = jnp.mean(value, axis=-1, keepdims=True)
    centred = value - mean
    variance = jnp.mean(centred * centred, axis=-1, keepdims=True)
    scale = lax.rsqrt(variance + norm_eps)
    return centred * scale, scale


def norm_back(grad, hat, scale, gain):
    inner = grad * gain
    mean_one = jnp.mean(inner, axis=-1, keepdims=True)
    mean_two = jnp.mean(inner * hat, axis=-1, keepdims=True)
    gain_grad = jnp.sum(grad * hat, axis=0, keepdims=True)
    return scale * (inner - mean_one - hat * mean_two), gain_grad


def gelu_parts(up):
    inner = 0.7978845608 * (up + 0.044715 * up * up * up)
    tanh = jnp.tanh(inner)
    slope = 0.7978845608 * (1.0 + 3.0 * 0.044715 * up * up)
    value = 0.5 * up * (1.0 + tanh)
    grad = 0.5 * (1.0 + tanh) + 0.5 * up * (1.0 - tanh * tanh) * slope
    return value, grad


class Gather:
    def __init__(self, place, view, bulk, sems, at, has=None):
        self.z, self.x, self.c, self.f = place
        self.view, self.bulk = view, bulk
        self.send, self.recv = sems
        self.at = at
        self.has = has
        self.sent = []

    def place_at(self, k):
        return lax.rem(self.z + k + RING, RING)

    def copy(self, ref, target, into, index):
        z, x, c = target
        return pltpu.make_async_remote_copy(
            src_ref=ref,
            dst_ref=ref,
            send_sem=self.send.at[self.at, index],
            recv_sem=self.recv.at[self.at, into],
            device_id=(z * (SIDE * CORES) + x * CORES + c, self.f),
            device_id_type=MESH,
        )

    def holds(self, block, cond):
        return cond if self.has is None else cond & self.has(*block)

    def go(self, block, target, into, cond):
        item = self.copy(self.view(*block), target, into, len(self.sent))
        cond = self.holds(block, cond)
        pl.when(cond)(item.start)
        self.sent.append((cond, item))

    def wait(self, block, into, cond):
        item = self.copy(self.view(*block), (self.z, 1 - self.x, self.c), into, 0)
        pl.when(self.holds(block, cond))(item.wait_recv)

    def line(self, block, up, down, cond):
        z, x, c = self.z, self.x, self.c
        if up:
            self.go(block, (self.place_at(1), x, c), block[0], cond & (z < RING - 1))
        if down:
            self.go(block, (self.place_at(-1), x, c), block[0], cond & (z > 0))

    def across(self, block, cond):
        self.go(block, (self.z, 1 - self.x, self.c), RING + block[0], cond)

    def step_one(self):
        own = (self.z, self.x, self.c)
        self.line(own, True, True, self.z >= 0)
        self.across(own, self.z >= 0)

    def arrive(self, k):
        low, high = (self.place_at(-k), self.x, self.c), (self.place_at(k), self.x, self.c)
        self.wait(low, low[0], self.z >= k)
        self.line(low, True, False, self.z >= k)
        self.wait(high, high[0], self.z < RING - k)
        self.line(high, False, True, self.z < RING - k)
        self.across(low, self.z >= k)
        self.across(high, self.z < RING - k)

    def side(self, k):
        for at, cond in ((self.place_at(-k), self.z >= k), (self.place_at(k), self.z < RING - k))[: 1 if k == 0 else 2]:
            self.wait((at, 1 - self.x, self.c), RING + at, cond)

    def step_two(self):
        self.arrive(1)

    def step_three(self):
        self.arrive(2)
        self.side(0)
        self.side(1)

    def step_four(self):
        self.arrive(3)
        self.hand_over(0)
        self.side(2)

    def step_five(self):
        self.side(3)
        self.hand_over(1)

    def hand_over(self, n):
        item = self.copy(self.bulk(self.c, self.x + n * (1 - 2 * self.x)), (self.z, self.x, 1 - self.c), 2 * RING + n, len(self.sent))
        item.start()
        self.sent.append((self.z >= 0, item))

    def step_six(self):
        for n in range(2):
            ref = self.bulk(1 - self.c, self.x + n * (1 - 2 * self.x))
            self.copy(ref, (self.z, self.x, 1 - self.c), 2 * RING + n, 0).wait_recv()

    def finish(self):
        for cond, item in self.sent:
            pl.when(cond)(item.wait_send)


class ShortGather(Gather):
    def step_one(self):
        own = (self.z, self.x, self.c)
        for k in range(1, RING):
            self.go(own, (self.place_at(k), self.x, self.c), self.z, self.z >= 0)
        self.across(own, self.z >= 0)

    def step_two(self):
        for k in range(1, RING):
            block = (self.place_at(k), self.x, self.c)
            self.wait(block, block[0], self.z >= 0)
            self.across(block, self.z >= 0)
        self.hand_over(0)

    def step_three(self):
        for k in range(RING):
            at = self.place_at(k)
            self.wait((at, 1 - self.x, self.c), RING + at, self.z >= 0)
        self.hand_over(1)


class Spread(Gather):
    def __init__(self, place, theirs, mine, bulk, sems, at):
        super().__init__(place, theirs, bulk, sems, at)
        self.mine = mine
        z, x, c = self.z, self.x, self.c
        always, end = z >= 0, (z == 0) | (z == RING - 1)
        self.opposite = RING - 1 - z
        self.over = (
            ((z, x, c), None, always),
            ((z, 1 - x, c), None, always),
            ((self.opposite, x, c), 1, end),
            ((self.opposite, 1 - x, c), 1, end),
        )
        self.pushed = []

    def over_copy(self, n, view):
        block, part, cond = self.over[n]
        ref = view(*block, part)
        return pltpu.make_async_remote_copy(
            src_ref=ref, dst_ref=ref, send_sem=self.send.at[self.at, 13 + n], recv_sem=self.recv.at[self.at, 10 + n],
            device_id=(self.z * (SIDE * CORES) + self.x * CORES + self.c, 1 - self.f), device_id_type=MESH,
        )

    def push(self):
        for n in range(4):
            item, cond = self.over_copy(n, self.mine), self.over[n][2]
            pl.when(cond)(item.start)
            self.pushed.append((cond, item))

    def landed(self, n):
        pl.when(self.over[n][2])(self.over_copy(n, self.view).wait_recv)

    def step_one(self):
        always = self.z >= 0
        own = (self.z, self.x, self.c)
        self.landed(0)
        self.line(own, True, True, always)

    def step_three(self):
        z, x, c = self.z, self.x, self.c
        low, high = (self.place_at(-2), x, c), (self.place_at(2), x, c)
        self.wait(low, low[0], z >= 2)
        self.go((*low, 0), (self.place_at(1), x, c), low[0], z == RING - 2)
        self.wait(high, high[0], z < RING - 2)
        self.go((*high, 0), (self.place_at(-1), x, c), high[0], z == 1)
        self.across(low, z >= 2)
        self.across(high, z < RING - 2)
        self.side(1)

    def step_four(self):
        z, x, c = self.z, self.x, self.c
        end = (z == 0) | (z == RING - 1)
        block = (self.opposite, x, c, 0)
        self.wait(block, self.opposite, end)
        self.across(block, end)
        self.landed(2)
        self.hand_over(0)
        self.side(2)

    def step_five(self):
        z, x, c = self.z, self.x, self.c
        self.landed(1)
        self.landed(3)
        self.wait((self.opposite, 1 - x, c, 0), RING + self.opposite, (z == 0) | (z == RING - 1))
        self.hand_over(1)

    def finish(self):
        super().finish()
        for cond, item in self.pushed:
            pl.when(cond)(item.wait_send)


class Pieces:
    def __init__(self, count, own_rows):
        self.half = count // 2
        self.edge = self.half * SLOT_S
        self.rows = own_rows
        self.count = count

    def start(self, rank):
        return jnp.where(
            rank < self.half, SLOT_S * rank, self.edge + SLOT_L * (rank - self.half)
        )

    def size(self, rank):
        return jnp.where(rank < self.half, SLOT_S, SLOT_L)

    def rank_of(self, row):
        return jnp.where(
            row < self.edge,
            lax.div(row, SLOT_S),
            self.half + lax.div(jnp.maximum(row - self.edge, 0), SLOT_L),
        )

    def first_rank(self, device):
        return self.rank_of(device * self.rows)

    def last_rank(self, device):
        return self.rank_of(device * self.rows + self.rows - 1)

    def first_device(self, rank):
        return lax.div(self.start(rank), self.rows)

    def last_device(self, rank):
        return lax.div(self.start(rank) + self.size(rank) - 1, self.rows)


SLOTS = 3
UNITS = 16
LANE_QKV, LANE_SO, LANE_CQ, LANE_CKV, LANE_CO, LANE_FI, LANE_FO = 0, 2304, 3072, 3840, 5376, 6144, 9216
OUT_CO, OUT_CKV = 3840, 4608
CHUNKS = ((0, 2304), (2304, 1536), (3840, 1536), (5376, 3072), (8448, 2304), (10752, 1536))
LOADS_BY_CHUNK = ((0,), (1, 2), (3,), (4, 5), (6, 7), (8, 9))
PIECE = 384
UNIT_CHIPS = 6


def layer_kernel(
    ranks,
    columns,
    x_ref, cot_ref, mem_ref, res_ref, pre_ref, gain_one_ref, gain_two_ref, gain_three_ref,
    qkv_ref, so_ref, cq_ref, ckv_ref, co_ref, fi_ref, fo_ref,
    out_ref, grad_ref, memgrad_ref, gain_out_ref, weights_out_ref,
    wb, gb, rl, rr, lb, sb, xb, cb, nb, olr, ob, pb, gainb, memp, kvb, kvg, kp, kr, kc, ky, cp,
    kx, ks, hb, ab, ug, usend_b, urecv_b,
    cqb, qbuf, osend, ostat_send, obuf, ostat, dob, dstat_b, dobuf, dstat, dqsend, dqbuf, gmine, gpeer,
    load_sem, wsend, wrecv, gsend, grecv, ssend, srecv, bsend, brecv, gain_sem, asend, arecv, fsend, frecv, ysend, yrecv, psend, precv, usend, urecv,
    ksend, krecv,
):
    me = lax.axis_index("dp")
    f = lax.axis_index("fsdp")
    z = lax.div(me, SIDE * CORES)
    x = lax.rem(lax.div(me, CORES), SIDE)
    c = lax.rem(me, CORES)
    seat = x * RING + z
    chips = ranks // CORES
    place = (z, x, c, f)
    half_rows = D // columns
    slab = half_rows // chips
    own_rows = mem_ref.shape[0]
    padded = memp.shape[0]
    lay = Pieces(ranks, own_rows)
    other = 1 - f
    mate = (z * (SIDE * CORES) + x * CORES + (1 - c), f)
    everyone = ranks * columns
    lin = f * ranks + me

    loads = []

    def load(src, lane, width):
        item = pltpu.make_async_copy(
            src, wb.at[pl.ds(pl.multiple_of(f * half_rows, 128), half_rows), pl.ds(lane, width)],
            load_sem.at[len(loads)],
        )
        item.start()
        loads.append(item)

    load(qkv_ref, LANE_QKV, 3 * D)
    load(so_ref, LANE_SO, D)
    load(cq_ref, LANE_CQ, D)
    load(ckv_ref, LANE_CKV, 2 * D)
    load(co_ref, LANE_CO, D)
    load(fi_ref, LANE_FI, 4 * D)
    for j in range(4):
        load(fo_ref.at[pl.ds(j * half_rows, half_rows)], LANE_FO + D * j, D)

    for s in range(SLOTS):
        qbuf[s] = jnp.zeros_like(qbuf[s])
        obuf[s] = jnp.zeros_like(obuf[s])
        ostat[s] = jnp.where(lax.broadcasted_iota(jnp.int32, ostat.shape[1:], 1) < 64, NONE, 0.0)
        dobuf[s] = jnp.zeros_like(dobuf[s])
        dstat[s] = jnp.zeros_like(dstat[s])
        dqbuf[s] = jnp.zeros_like(dqbuf[s])

    def rows_of(device):
        return pl.ds(pl.multiple_of(device * SUFFIX, SUFFIX), SUFFIX)

    def slot_of(device):
        side = lax.rem(lax.div(device, CORES), SIDE)
        return lax.rem(device, CORES) * chips + side * RING + lax.div(device, SIDE * CORES)

    my_slot = slot_of(me)
    xb[my_slot] = x_ref[...]
    cb[my_slot] = cot_ref[...].astype(BF16)
    pb[my_slot] = jnp.full((8, 128), pre_ref[0, 0].astype(F32), F32)
    for n, ref in enumerate((gain_one_ref, gain_two_ref, gain_three_ref)):
        values = ref[...].astype(F32).reshape(1, half_rows)
        for j in range(half_rows // 128):
            at = n * (half_rows // 128) + j
            gainb[f, at : at + 1] = values[:, 128 * j : 128 * (j + 1)]

    barrier = pltpu.get_barrier_semaphore()

    def greet(i, carry):
        to = lax.rem(me + i, ranks)
        pl.semaphore_signal(barrier, inc=1, device_id=(to, f), device_id_type=MESH)
        return carry

    lax.fori_loop(1, ranks, greet, 0)
    pl.semaphore_signal(barrier, inc=1, device_id=(me, other), device_id_type=MESH)
    pl.semaphore_wait(barrier, ranks)

    y_items = []

    def push_y(src, dst, at):
        item = pltpu.make_async_remote_copy(
            src_ref=src, dst_ref=dst, send_sem=ysend.at[at], recv_sem=yrecv.at[at],
            device_id=(me, other), device_id_type=MESH,
        )
        item.start()
        y_items.append(item)
        return item

    class Tell:
        def __init__(self, ref, at):
            self.ref, self.at = ref, at

        def copy(self, source, index, to):
            return pltpu.make_async_remote_copy(
                src_ref=self.ref.at[slot_of(source)], dst_ref=self.ref.at[slot_of(source)], send_sem=bsend.at[self.at, index],
                recv_sem=brecv.at[self.at, source], device_id=(to, f), device_id_type=MESH,
            )

        def start(self):
            def one(i, carry):
                self.copy(me, i, lax.rem(me + i, ranks)).start()
                return carry

            lax.fori_loop(1, ranks, one, 0)

        def wait(self):
            def one(i, carry):
                source = lax.rem(me + i, ranks)
                self.copy(source, i, source).wait_recv()
                return carry

            lax.fori_loop(1, ranks, one, 0)

        def finish(self):
            def one(i, carry):
                self.copy(me, i, lax.rem(me + i, ranks)).wait_send()
                return carry

            lax.fori_loop(1, ranks, one, 0)

    def slab_view(first, width, rows_from):
        half = width // CORES

        cut = (half // 256) * 128

        def view(zz, xx, cc, part=None):
            low, size = {None: (0, half), 0: (0, half - cut), 1: (half - cut, cut)}[part]
            row = pl.multiple_of(rows_from * half_rows + (xx * RING + zz) * slab, 16)
            lane = pl.multiple_of(first + cc * half + low, 128)
            return wb.at[pl.ds(row, slab), pl.ds(lane, size)]

        return view

    def block_view(ref):
        def view(zz, xx, cc):
            return ref.at[cc * chips + xx * RING + zz]

        return view

    def block_bulk(ref):
        return lambda cc, xx: ref.at[pl.ds(cc * chips + xx * RING, RING)]

    def token_rows(col, cc, at):
        return pl.ds(pl.multiple_of(((col * CORES + cc) * chips + at) * SUFFIX, SUFFIX), SUFFIX)

    def token_view(ref):
        def view(zz, xx, cc):
            return ref.at[token_rows(f, cc, xx * RING + zz)]

        return view

    def token_bulk(ref):
        rows = RING * SUFFIX
        return lambda cc, xx: ref.at[pl.ds(pl.multiple_of(((f * CORES + cc) * SIDE + xx) * rows, rows), rows)]

    def chunk_bulk(first, width):
        half = width // CORES
        rows = RING * slab

        def bulk(cc, xx):
            row = pl.multiple_of(other * half_rows + xx * rows, 16)
            return wb.at[pl.ds(row, rows), pl.ds(pl.multiple_of(first + cc * half, 128), half)]

        return bulk

    plane = pl.ds(pl.multiple_of((f * CORES + c) * chips * SUFFIX, SUFFIX), chips * SUFFIX)
    plane_in = pl.ds(pl.multiple_of((other * CORES + c) * chips * SUFFIX, SUFFIX), chips * SUFFIX)
    plane_mate = pl.ds(pl.multiple_of((other * CORES + 1 - c) * chips * SUFFIX, SUFFIX), chips * SUFFIX)

    class Across:
        def __init__(self, ref, at):
            self.ref, self.at = ref, at

        def copy(self, rows, n, to):
            ref = self.ref.at[rows]
            return pltpu.make_async_remote_copy(
                src_ref=ref, dst_ref=ref, send_sem=asend.at[self.at, n], recv_sem=arecv.at[self.at, n],
                device_id=to, device_id_type=MESH,
            )

        def start(self):
            self.copy(plane, 0, (me, other)).start()

        def relay(self):
            self.copy(plane_in, 0, (me, other)).wait_recv()
            self.copy(plane_in, 1, mate).start()

        def wait(self):
            self.copy(plane_mate, 1, mate).wait_recv()

        def finish(self):
            self.copy(plane, 0, (me, other)).wait_send()
            self.copy(plane_in, 1, mate).wait_send()

    sems, short_sems = (gsend, grecv), (ssend, srecv)
    ag_x = Gather(place, block_view(xb), block_bulk(xb), sems, 0)
    ag_c = Gather(place, block_view(cb), block_bulk(cb), sems, 1)
    ag_n = ShortGather(place, token_view(nb), token_bulk(nb), short_sems, 0)
    tell_p = Tell(pb, 0)
    spread = [
        Spread(place, slab_view(first, width, other), slab_view(first, width, f), chunk_bulk(first, width), (wsend, wrecv), n)
        for n, (first, width) in enumerate(CHUNKS)
    ]

    def push_chunk(n):
        for i in LOADS_BY_CHUNK[n]:
            loads[i].wait()
        spread[n].push()

    ag_x.step_one()
    push_chunk(0)
    gain_item = push_y(gainb.at[f], gainb.at[f], 0)
    tell_p.start()
    push_chunk(1)

    def tick(n):
        for age, act in ((4, "step_five"), (3, "step_four"), (2, "step_three"), (1, "step_two"), (0, "step_one")):
            if 0 <= n - age < len(spread):
                getattr(spread[n - age], act)()
        if n + 2 < len(spread):
            push_chunk(n + 2)

    ag_x.step_two()
    tick(0)
    ag_x.step_three()
    tick(1)
    ag_x.step_four()
    tick(2)
    ag_x.step_five()
    ag_x.step_six()
    tick(3)
    gain_item.wait_recv()

    memp[0:own_rows] = mem_ref[...]
    memp[own_rows:padded] = jnp.zeros((padded - own_rows, D), BF16)

    positions = []
    before_large = jnp.int32(0)
    mine_rank = jnp.int32(0)
    for i in range(ranks):
        group = res_ref[0, i]
        spot = jnp.where(group == 1, lay.half + before_large, i - before_large)
        positions.append(spot)
        mine_rank = jnp.where(me == i, spot, mine_rank)
        before_large = before_large + group

    spots = [i // CORES % SIDE * RING + i // (SIDE * CORES) for i in range(ranks)]
    slots = [(i % CORES) * chips + spots[i] for i in range(ranks)]

    def example_of(rank):
        found = jnp.int32(0)
        for i in range(ranks):
            found = jnp.where(positions[i] == rank, slots[i], found)
        return found

    by_rank = [example_of(r) for r in range(ranks)]
    out_slot = jnp.int32(0)
    for i in range(ranks):
        out_slot = jnp.where(mine_rank == i, slots[i], out_slot)

    tiles = half_rows // 128
    gain = [
        jnp.concatenate([gainb[i, tiles * n + j : tiles * n + j + 1] for i in range(columns) for j in range(tiles)], axis=1)
        for n in range(3)
    ]

    mine = example_of(me)
    resid = xb[mine]
    hat_one, rs_one = normed(resid)
    n1 = (hat_one * gain[0]).astype(BF16)

    lanes = lax.broadcasted_iota(jnp.int32, (1, 256), 1)
    head_f32 = [(lax.div(lanes, HEAD_DIM) == h).astype(F32) for h in range(4)]
    head_b16 = [m.astype(BF16) for m in head_f32]

    def stack(value):
        return jnp.concatenate([value * m for m in head_b16], axis=0)

    def unstack(value):
        rows = value.shape[0] // 4
        total = value[0:rows] * head_f32[0]
        for h in range(1, 4):
            total = total + value[h * rows : (h + 1) * rows] * head_f32[h]
        return total

    tick(4)
    ag_c.step_one()
    spread[0].step_six()
    q = mm(n1, wb[:, 0:D]).astype(BF16)
    k = mm(n1, wb[:, D : 2 * D]).astype(BF16)
    v = mm(n1, wb[:, 2 * D : 3 * D]).astype(BF16)
    scale = HEAD_DIM**-0.5
    qs = (q.astype(F32) * scale).astype(BF16)
    row_at = lax.broadcasted_iota(jnp.int32, (SUFFIX, SUFFIX), 0)
    col_at = lax.broadcasted_iota(jnp.int32, (SUFFIX, SUFFIX), 1)
    causal = jnp.concatenate([(row_at >= col_at).astype(F32)] * 4, axis=0) > 0.0
    self_p = []
    mixed = []
    for g in range(3):
        sl = slice(256 * g, 256 * g + 256)
        s = mm_nt(stack(qs[:, sl]), k[:, sl])
        s = jnp.where(causal, s, NONE)
        e = jnp.exp(s - jnp.max(s, axis=-1, keepdims=True))
        p = e / jnp.sum(e, axis=-1, keepdims=True)
        self_p.append(p)
        mixed.append(unstack(mm(p.astype(BF16), v[:, sl])))
    sm = jnp.concatenate(mixed, axis=1).astype(BF16)

    tick(5)
    ag_c.step_two()
    spread[1].step_six()
    after_self = resid + mm(sm, wb[:, LANE_SO : LANE_SO + D])
    hat_two, rs_two = normed(after_self)
    n2 = (hat_two * gain[1]).astype(BF16)
    cq = mm(n2, wb[:, LANE_CQ : LANE_CQ + D]).astype(BF16)
    cqb[...] = cq

    my_first, my_last = lay.first_device(me), lay.last_device(me)
    held_first, held_last = lay.first_rank(me), lay.last_rank(me)

    def piece_copy(src, dst, at, sent, landed, target):
        return pltpu.make_async_remote_copy(
            src_ref=src, dst_ref=dst, send_sem=psend.at[at, sent], recv_sem=precv.at[at, landed],
            device_id=(target, f), device_id_type=MESH,
        )

    def to_holders(pairs):
        for i in range(SLOTS):
            target = my_first + i
            slot = me - lay.first_rank(target)
            there = target <= my_last

            @pl.when(there & (target == me))
            def _():
                for src, dst, at in pairs:
                    dst[slot] = src[...]

            @pl.when(there & (target != me))
            def _():
                for src, dst, at in pairs:
                    piece_copy(src, dst.at[slot], at, i, slot, target).start()

    def to_holders_sent(pairs):
        for i in range(SLOTS):
            target = my_first + i

            @pl.when((target <= my_last) & (target != me))
            def _():
                for src, dst, at in pairs:
                    piece_copy(src, dst.at[0], at, i, 0, target).wait_send()

    def at_holders(pairs):
        for s in range(SLOTS):
            rank = held_first + s

            @pl.when((rank <= held_last) & (rank != me))
            def _():
                for src, dst, at in pairs:
                    piece_copy(src, dst.at[s], at, 0, s, rank).wait_recv()

    def to_owners(pairs):
        for s in range(SLOTS):
            rank = held_first + s
            index = me - lay.first_device(rank)
            there = rank <= held_last

            @pl.when(there & (rank == me))
            def _():
                for src, dst, at in pairs:
                    dst[index] = src[s]

            @pl.when(there & (rank != me))
            def _():
                for src, dst, at in pairs:
                    piece_copy(src.at[s], dst.at[index], at, s, index, rank).start()

    def to_owners_sent(pairs):
        for s in range(SLOTS):
            rank = held_first + s

            @pl.when((rank <= held_last) & (rank != me))
            def _():
                for src, dst, at in pairs:
                    piece_copy(src.at[s], dst.at[0], at, s, 0, rank).wait_send()

    def at_owners(pairs):
        for i in range(SLOTS):
            target = my_first + i

            @pl.when((target <= my_last) & (target != me))
            def _():
                for src, dst, at in pairs:
                    piece_copy(src.at[0], dst.at[i], at, 0, i, target).wait_recv()

    q_pairs = [(cqb, qbuf, 0)]
    o_pairs = [(osend, obuf, 1), (ostat_send, ostat, 2)]
    d_pairs = [(dob, dobuf, 3), (dstat_b, dstat, 4)]
    dq_pairs = [(dqsend, dqbuf, 5)]

    to_holders(q_pairs)

    tick(6)
    ag_c.step_three()
    spread[2].step_six()


    def kv_step(i, carry):
        lane = pl.multiple_of(i * 256, 256)
        kvb[:, pl.ds(lane, 256)] = mm(memp[...], wb[:, pl.ds(LANE_CKV + lane, 256)]).astype(BF16)
        return carry

    lax.fori_loop(0, 6, kv_step, 0)

    tell_p.wait()
    lane_f = lax.broadcasted_iota(jnp.int32, (SUFFIX, padded), 1).astype(F32)
    allowed = []
    for s in range(SLOTS):
        rank = held_first + s
        ok = rank <= held_last
        example = example_of(jnp.minimum(rank, ranks - 1))
        prefix = pb[example][0:1, 0:1]
        low = (lay.start(rank) - me * own_rows).astype(F32)
        patches = jnp.where(rank < lay.half, PATCH_S, PATCH_L).astype(F32)
        high = jnp.minimum(low + patches + prefix, jnp.float32(own_rows))
        high = jnp.where(ok, high, jnp.float32(-1.0))
        allowed.append(((lane_f >= low) & (lane_f < high)).astype(F32))
    allowed = jnp.concatenate(allowed * 4, axis=0) > 0.0

    at_holders(q_pairs)
    qh = jnp.concatenate([qbuf[s] for s in range(SLOTS)], axis=0)
    qh = (qh.astype(F32) * scale).astype(BF16)
    lane_c = lax.broadcasted_iota(jnp.int32, (SUFFIX, 128), 1)
    def swap(tile):
        return jnp.concatenate([tile[:, 64:], tile[:, :64]], axis=1)

    top_c = [jnp.zeros((SUFFIX, 128), F32) for _ in range(SLOTS)]
    sum_c = [jnp.zeros((SUFFIX, 128), F32) for _ in range(SLOTS)]
    for g in range(3):
        sl = slice(256 * g, 256 * g + 256)
        s = mm_nt(stack(qh[:, sl]), kvb[:, sl])
        s = jnp.where(allowed, s, NONE)
        top = jnp.max(s, axis=-1, keepdims=True)
        e = jnp.where(allowed, jnp.exp(s - top), 0.0)
        total = jnp.sum(e, axis=-1, keepdims=True)
        o = mm(e.astype(BF16), kvb[:, D + 256 * g : D + 256 * g + 256])
        o = o * jnp.where(total > 0.0, 1.0 / jnp.where(total > 0.0, total, 1.0), 0.0)
        o = unstack(o).astype(BF16)
        for n in range(SLOTS):
            osend[n, :, sl] = o[n * SUFFIX : (n + 1) * SUFFIX]
            for h in range(4):
                at = h * SLOTS * SUFFIX + n * SUFFIX
                hit = lane_c == 4 * g + h
                top_c[n] = jnp.where(hit, top[at : at + SUFFIX], top_c[n])
                sum_c[n] = jnp.where(hit, total[at : at + SUFFIX], sum_c[n])
    for n in range(SLOTS):
        ostat_send[n] = jnp.where(lane_c < 64, top_c[n], swap(sum_c[n]))
    to_owners(o_pairs)

    tick(7)
    ag_c.step_four()
    at_owners(o_pairs)
    spread[3].step_six()

    def expand(compact):
        low = lane_c < HEAD_DIM
        return jnp.concatenate(
            [jnp.where(low, compact[:, 2 * t : 2 * t + 1], compact[:, 2 * t + 1 : 2 * t + 2]) for t in range(6)],
            axis=1,
        )

    tops = [ostat[i] for i in range(SLOTS)]
    top_all = jnp.maximum(jnp.maximum(tops[0], tops[1]), tops[2])
    shares = [jnp.where(lane_c < 64, swap(tops[i]) * jnp.exp(tops[i] - top_all), 0.0) for i in range(SLOTS)]
    whole = shares[0] + shares[1] + shares[2]
    whole = jnp.where(whole > 0.0, whole, 1.0)
    lse = top_all + jnp.log(whole)
    cross = jnp.zeros((SUFFIX, D), F32)
    for i in range(SLOTS):
        cross = cross + expand(shares[i] / whole) * obuf[i].astype(F32)
    cm = cross.astype(BF16)

    after_cross = after_self + mm(cm, wb[:, LANE_CO : LANE_CO + D])
    hat_three, rs_three = normed(after_cross)
    n3 = (hat_three * gain[2]).astype(BF16)
    nb[token_rows(f, c, seat)] = n3
    ag_n.step_one()

    tick(8)
    ag_c.step_five()
    tick(9)
    spread[4].step_six()
    acts, slopes = [], []
    for j in range(4):
        value, slope = gelu_parts(mm(n3, wb[:, LANE_FI + D * j : LANE_FI + D * (j + 1)]))
        acts.append(value.astype(BF16))
        slopes.append(slope)
    act = jnp.concatenate(acts, axis=1)
    ag_c.step_six()
    for r in range(ranks):
        olr[token_rows(f, r % CORES, spots[r])] = cb[by_rank[r]]
    across_o = Across(olr, 0)
    across_n = Across(nb, 1)
    across_o.start()
    spread[5].step_six()
    unit_items = []

    def unit_device(unit, j):
        at = unit + 1
        return at % RING * (SIDE * CORES) + at // RING * CORES + j

    def push_part(which, at, to, src, dst):
        @pl.when(me == to)
        def _():
            dst[...] = src[...]

        @pl.when(me != to)
        def _():
            pltpu.make_async_remote_copy(
                src_ref=src, dst_ref=dst, send_sem=usend.at[which, at],
                recv_sem=urecv.at[which, me], device_id=(to, f), device_id_type=MESH,
            ).start()

        unit_items.append((which, at, to, src, dst))

    def push_left(units, at, left):
        lb[at] = left
        for unit in units:
            for j in range(CORES):
                lanes = pl.ds(j * PIECE, PIECE)
                push_part(0, CORES * unit + j, unit_device(unit, j), lb.at[at, :, lanes], rl.at[rows_of(me), lanes])

    def push_right(unit, right):
        for j in range(CORES):
            sb[unit, j] = right[:, j * PIECE : (j + 1) * PIECE]
            push_part(1, CORES * unit + j, unit_device(unit, j), sb.at[unit, j], rr.at[rows_of(me)])

    out_low = cb[mine]
    cot = out_low.astype(F32)
    hidden_grad = [mm_nt(out_low, wb[:, LANE_FO + D * j : LANE_FO + D * (j + 1)]) for j in range(4)]

    def by_hidden(j):
        parts = []
        for t in range(D // half_rows):
            at = D * j + t * half_rows
            col, unit = at // (4 * half_rows), (at % (4 * half_rows)) // half_rows
            parts.append(hidden_grad[unit][:, col * half_rows : (col + 1) * half_rows])
        return jnp.concatenate(parts, axis=1)

    n3_grad = jnp.zeros((SUFFIX, D), F32)
    for j in range(4):
        part = (by_hidden(j) * slopes[j]).astype(BF16)
        n3_grad = n3_grad + mm_nt(part, wb[:, LANE_FI + D * j : LANE_FI + D * (j + 1)])

    ag_n.step_two()
    part, ffn_gain_grad = norm_back(n3_grad, hat_three, rs_three, gain[2])
    cross_res = cot + part
    cross_low = cross_res.astype(BF16)
    d_mixed = mm_nt(cross_low, wb[:, LANE_CO : LANE_CO + D]).astype(BF16)
    dob[...] = d_mixed
    prod = d_mixed.astype(F32) * cross
    delta = jnp.zeros((SUFFIX, 128), F32)
    for t in range(6):
        tile = prod[:, 128 * t : 128 * (t + 1)]
        left = jnp.sum(jnp.where(lane_c < HEAD_DIM, tile, 0.0), axis=-1, keepdims=True)
        right = jnp.sum(jnp.where(lane_c < HEAD_DIM, 0.0, tile), axis=-1, keepdims=True)
        delta = jnp.where(lane_c == 2 * t, left, delta)
        delta = jnp.where(lane_c == 2 * t + 1, right, delta)
    dstat_b[...] = jnp.where(lane_c < 64, lse, swap(delta))
    to_holders(d_pairs)
    push_left((0, 1, 2), 0, n1)
    down = jnp.zeros((SUFFIX, D), F32)
    for j in range(4):
        lhs = jnp.concatenate(
            [act[:, i * 4 * half_rows + j * half_rows : i * 4 * half_rows + (j + 1) * half_rows] for i in range(columns)],
            axis=1,
        )
        down = down + mm(lhs, wb[:, LANE_FO + D * j : LANE_FO + D * (j + 1)])
    ob[0, my_slot] = (after_cross + down).astype(BF16)
    ag_out = ShortGather(place, block_view(ob.at[0]), block_bulk(ob.at[0]), short_sems, 1)

    at_holders(d_pairs)

    push_left((4,), 2, n2)
    push_left((3,), 1, sm)
    doh = jnp.concatenate([dobuf[s] for s in range(SLOTS)], axis=0)
    for g in range(3):
        sl = slice(256 * g, 256 * g + 256)
        kg = kvb[:, sl]
        vg = kvb[:, D + 256 * g : D + 256 * g + 256]
        q4 = stack(qh[:, sl])
        do4 = stack(doh[:, sl])
        lse_col = jnp.concatenate([dstat[n][:, 4 * g + h : 4 * g + h + 1] for h in range(4) for n in range(SLOTS)], axis=0)
        del_col = jnp.concatenate([dstat[n][:, 64 + 4 * g + h : 65 + 4 * g + h] for h in range(4) for n in range(SLOTS)], axis=0)
        s = mm_nt(q4, kg)
        p = jnp.where(allowed, jnp.exp(jnp.where(allowed, s - lse_col, 0.0)), 0.0)
        dp = mm_nt(do4, vg)
        ds = (p * (dp - del_col)).astype(BF16)
        kvg[:, D + 256 * g : D + 256 * g + 256] = mm_tn(p.astype(BF16), do4).astype(BF16)
        kvg[:, sl] = mm_tn(ds, q4).astype(BF16)
        dq = unstack(mm(ds, kg)) * scale
        for n in range(SLOTS):
            dqsend[n, :, sl] = dq[n * SUFFIX : (n + 1) * SUFFIX].astype(BF16)
    to_owners(dq_pairs)
    ag_n.step_three()
    across_n.start()
    def kp_step(i, carry):
        lane = pl.multiple_of(i * 256, 256)
        kp[:, pl.ds(lane, 256)] = mm_tn(memp[...], kvg[:, pl.ds(lane, 256)]).astype(BF16)
        return carry

    lax.fori_loop(0, 6, kp_step, 0)
    kr_item = pltpu.make_async_remote_copy(
        src_ref=kp.at[pl.ds(pl.multiple_of((1 - c) * half_rows, 128), half_rows)], dst_ref=kr,
        send_sem=ksend.at[2 * chips], recv_sem=krecv.at[chips], device_id=mate, device_id_type=MESH,
    )
    kr_item.start()

    across_o.relay()
    ag_out.step_one()
    at_owners(dq_pairs)
    push_left((5,), 3, cm)
    push_right(5, cross_low)
    kr_item.wait_recv()
    kc[...] = (
        kp[pl.ds(pl.multiple_of(c * half_rows, 128), half_rows)].astype(F32) + kr[...].astype(F32)
    ).astype(BF16)
    half_slabs = half_rows // SIDE

    def ky_copy(j):
        lanes = pl.ds(j * D, D)
        return pltpu.make_async_remote_copy(
            src_ref=kc.at[:, lanes], dst_ref=ky.at[:, lanes], send_sem=ksend.at[2 * chips + 1 + j],
            recv_sem=krecv.at[chips + 1 + j], device_id=(me, other), device_id_type=MESH,
        )

    def kx_copy(j):
        lanes = pl.ds(j * D, D)
        return pltpu.make_async_remote_copy(
            src_ref=kc.at[pl.ds(pl.multiple_of((1 - x) * half_slabs, 16), half_slabs), lanes], dst_ref=kx.at[:, lanes],
            send_sem=ksend.at[2 * chips + 3 + j], recv_sem=krecv.at[chips + 3 + j],
            device_id=(z * (SIDE * CORES) + (1 - x) * CORES + c, f), device_id_type=MESH,
        )

    @pl.when(c != f)
    def _():
        ky_copy(0).start()
        ky_copy(1).start()

    cqg = (dqbuf[0].astype(F32) + dqbuf[1].astype(F32) + dqbuf[2].astype(F32)).astype(BF16)
    n2_grad = mm_nt(cqg, wb[:, LANE_CQ : LANE_CQ + D])
    part, cross_gain_grad = norm_back(n2_grad, hat_two, rs_two, gain[1])
    self_res = cross_res + part
    self_low = self_res.astype(BF16)
    dmix = mm_nt(self_low, wb[:, LANE_SO : LANE_SO + D]).astype(BF16)
    dqs, dks, dvs = [], [], []
    for g in range(3):
        sl = slice(256 * g, 256 * g + 256)
        q4 = stack(qs[:, sl])
        do4 = stack(dmix[:, sl])
        p = self_p[g]
        dp = mm_nt(do4, v[:, sl])
        ds = (p * (dp - jnp.sum(p * dp, axis=-1, keepdims=True))).astype(BF16)
        dvs.append(mm_tn(p.astype(BF16), do4))
        dks.append(mm_tn(ds, q4))
        dqs.append(unstack(mm(ds, k[:, sl])) * scale)
    packed_grad = [jnp.concatenate(parts, axis=1).astype(BF16) for parts in (dqs, dks, dvs)]
    for j in range(3):
        push_right(j, packed_grad[j])
    push_right(4, cqg)
    push_right(3, self_low)

    n1_grad = jnp.zeros((SUFFIX, D), F32)
    for j in range(3):
        n1_grad = n1_grad + mm_nt(packed_grad[j], wb[:, D * j : D * (j + 1)])
    part, self_gain_grad = norm_back(n1_grad, hat_one, rs_one, gain[0])
    ob[1, my_slot] = (self_res + part).astype(BF16)
    ag_grad = ShortGather(place, block_view(ob.at[1]), block_bulk(ob.at[1]), short_sems, 2)
    gmine[0] = jnp.concatenate(
        [self_gain_grad, cross_gain_grad, ffn_gain_grad, jnp.zeros((5, D), F32)], axis=0
    )
    partners = (
        mate,
        (me, other),
        (z * (SIDE * CORES) + (1 - x) * CORES + c, f),
        ((z + 1 - 2 * lax.rem(z, 2)) * (SIDE * CORES) + x * CORES + c, f),
        (lax.rem(z + 2, RING) * (SIDE * CORES) + x * CORES + c, f),
    )

    def gain_copy(k):
        return pltpu.make_async_remote_copy(
            src_ref=gmine.at[k], dst_ref=gpeer.at[k], send_sem=gain_sem.at[0, k], recv_sem=gain_sem.at[1, k],
            device_id=partners[k], device_id_type=MESH,
        )

    def gain_step(k):
        gain_copy(k - 1).wait_recv()
        total = gmine[k - 1] + gpeer[k - 1]
        if k == len(partners):
            return total
        gmine[k] = total
        gain_copy(k).start()

    gain_copy(0).start()
    ag_grad.step_one()
    ag_out.step_two()

    ag_n.step_six()
    across_n.relay()
    across_o.wait()
    across_n.wait()

    rows_step = 128
    hidden = [col * 4 * half_rows + D * c for col in range(columns)]

    def ffn_rows(first, last):
        def one(i, carry):
            at = pl.ds(pl.multiple_of(i * rows_step, rows_step), rows_step)
            for col in range(columns):
                lane = pl.multiple_of(LANE_FI + hidden[col], 128)
                value, slope = gelu_parts(mm(nb[at], wb[:, pl.ds(lane, D)]))

                @pl.when(f == col)
                def _():
                    ab[at] = value.astype(BF16)

                back = []
                for t in range(CORES):
                    lane_o = pl.multiple_of(LANE_FO + D * (2 * c + t), 128)
                    back.append(mm_nt(olr[at], wb[col * half_rows : (col + 1) * half_rows, pl.ds(lane_o, D)]))
                hb[col, at] = (jnp.concatenate(back, axis=1) * slope).astype(BF16)
            return carry

        lax.fori_loop(first, last, one, 0)

    own_lanes = pl.ds(pl.multiple_of(f * half_rows, 128), half_rows)

    def ffn_in_sum(col):
        lane = pl.multiple_of(LANE_FI + hidden[col], 128)
        for part in range(0, D, PIECE):
            total = mm_tn(nb[:, own_lanes], hb[col, :, part : part + PIECE])
            gb[:, pl.ds(lane + part, PIECE)] = total.astype(BF16)

    def ffn_out_sum(t):
        lane = pl.multiple_of(LANE_FO + D * (2 * c + t), 128)
        for part in range(0, D, PIECE):
            total = mm_tn(ab[:, t * half_rows : (t + 1) * half_rows], olr[:, part : part + PIECE])
            gb[:, pl.ds(lane + part, PIECE)] = total.astype(BF16)

    f_items = []

    def to_mate(lane, width):
        ref = gb.at[:, pl.ds(pl.multiple_of(lane, 128), width)]
        item = pltpu.make_async_remote_copy(
            src_ref=ref, dst_ref=ref, send_sem=fsend.at[len(f_items)], recv_sem=frecv.at[len(f_items)],
            device_id=mate, device_id_type=MESH,
        )
        item.start()
        f_items.append(item)

    has_unit = (seat >= 1) & (seat <= UNIT_CHIPS)

    def unit_lane(n, cc):
        return PIECE * jnp.clip(n - 1, 0, UNIT_CHIPS - 1) + UNIT_CHIPS * PIECE * cc

    def unit_take(which, src, dst):
        def take(i, carry):
            @pl.when(i != me)
            def _():
                pltpu.make_async_remote_copy(
                    src_ref=src, dst_ref=dst(i), send_sem=usend.at[which, 0],
                    recv_sem=urecv.at[which, i], device_id=mate, device_id_type=MESH,
                ).wait_recv()

            return carry

        lax.fori_loop(0, ranks, take, 0)

    def left_lanes(core):
        return pl.ds(pl.multiple_of(core * PIECE, 128), PIECE)

    def left_copy(core):
        ref = rl.at[:, left_lanes(core)]
        return pltpu.make_async_remote_copy(
            src_ref=ref, dst_ref=ref, send_sem=ysend.at[1], recv_sem=yrecv.at[1], device_id=mate, device_id_type=MESH,
        )

    def unit_left(pred):
        @pl.when(pred)
        def _():
            unit_take(0, lb.at[0, :, pl.ds(0, PIECE)], lambda i: rl.at[rows_of(i), left_lanes(c)])
            left_copy(c).start()

    def unit_rows(n):
        return pl.ds(n * (half_rows // 2), half_rows // 2)

    def unit_copy(n):
        rows = unit_rows(n)
        return pltpu.make_async_remote_copy(
            src_ref=usend_b.at[rows], dst_ref=urecv_b.at[rows], send_sem=ysend.at[3 + n], recv_sem=yrecv.at[3 + n],
            device_id=(me, other), device_id_type=MESH,
        )

    def unit_sum(pred):
        @pl.when(pred)
        def _():
            unit_take(1, sb.at[0, 0], lambda i: rr.at[rows_of(i)])
            left_copy(1 - c).wait_recv()
            for col in range(columns):
                ug[col] = mm_tn(rl[:, col * half_rows : (col + 1) * half_rows], rr[...])
            usend_b[...] = ug[other].astype(BF16)
            for n in range(2):
                unit_copy(n).start()

    def unit_join(pred, n):
        @pl.when(pred)
        def _():
            unit_copy(n).wait_recv()
            rows = unit_rows(n)
            gb[rows, pl.ds(pl.multiple_of(unit_lane(seat, c), 128), PIECE)] = (
                ug[f, rows] + urecv_b[rows].astype(F32)
            ).astype(BF16)

    def has_block(zz, xx, cc):
        n = xx * RING + zz
        return (n >= 1) & (n <= UNIT_CHIPS)

    def unit_bulk(rows):
        width = UNIT_CHIPS * PIECE // SIDE
        return lambda cc, xx: gb.at[rows, pl.ds(pl.multiple_of(width * (SIDE * cc + xx), 128), width)]

    def gb_view(lane_of, rows):
        def view(zz, xx, cc):
            return gb.at[rows, pl.ds(pl.multiple_of(lane_of(xx * RING + zz, cc), 128), PIECE)]

        return view

    class UnitGather:
        def __init__(self):
            parts = [unit_rows(n) for n in range(2)]
            self.gathers = [
                Gather(place, gb_view(unit_lane, rows), unit_bulk(rows), (wsend, grecv), at, has_block)
                for at, rows in zip((2, 3), parts)
            ]

        def step(self, name):
            for gather in self.gathers:
                getattr(gather, name)()

    ag_u = UnitGather()

    k_items = []

    def k_copy(t, j):
        return pltpu.make_async_remote_copy(
            src_ref=ks.at[pl.ds(t * slab, slab), pl.ds(j * D, D)], dst_ref=cp.at[z],
            send_sem=ksend.at[t * CORES + j], recv_sem=krecv.at[z],
            device_id=(t * (SIDE * CORES) + x * CORES + j, f), device_id_type=MESH,
        )

    def k_over_x(j):
        lanes = pl.ds(j * D, D)

        @pl.when(c == f)
        def _():
            ky_copy(j).wait_recv()
            kc[:, lanes] = (kc[:, lanes].astype(F32) + ky[:, lanes].astype(F32)).astype(BF16)
            kx_copy(j).start()

    def k_on_line(j):
        lanes = pl.ds(j * D, D)

        @pl.when(c == f)
        def _():
            kx_copy(j).wait_recv()
            ks[:, lanes] = (
                kc[pl.ds(pl.multiple_of(x * half_slabs, 16), half_slabs), lanes].astype(F32) + kx[:, lanes].astype(F32)
            ).astype(BF16)

        for t in range(RING):
            here = (z == t) & (c == j)

            @pl.when((c == f) & here)
            def _():
                cp[z] = ks[t * slab : (t + 1) * slab, j * D : (j + 1) * D]

            @pl.when((c == f) & jnp.logical_not(here))
            def _():
                k_copy(t, j).start()

            k_items.append((t, j, here))

    for item in spread:
        item.finish()
    k_over_x(0)
    ffn_rows(0, 2)
    gain_step(1)
    unit_left(has_unit)
    k_on_line(0)
    k_over_x(1)
    unit_sum(has_unit)
    ffn_rows(2, 4)
    gain_step(2)
    k_on_line(1)
    unit_join(has_unit, 0)
    ag_u.gathers[0].step_one()
    ffn_rows(4, 5)
    unit_join(has_unit, 1)
    ag_u.gathers[1].step_one()
    ffn_rows(5, 6)
    gain_step(3)

    def take_k(i, carry):
        @pl.when((i != z) | (c != f))
        def _():
            pltpu.make_async_remote_copy(
                src_ref=ks.at[pl.ds(0, slab), pl.ds(0, D)], dst_ref=cp.at[i], send_sem=ksend.at[0],
                recv_sem=krecv.at[i], device_id=mate, device_id_type=MESH,
            ).wait_recv()

        return carry

    lax.fori_loop(0, RING, take_k, 0)
    total = cp[0].astype(F32)
    for i in range(1, RING):
        total = total + cp[i].astype(F32)
    k_lane = pl.multiple_of(OUT_CKV + c * D, 128)
    gb[pl.ds(pl.multiple_of(x * half_slabs + z * slab, 16), slab), pl.ds(k_lane, D)] = total.astype(BF16)

    def kv_view(zz, xx, cc):
        row = pl.multiple_of(xx * half_slabs + zz * slab, 16)
        return gb.at[pl.ds(row, slab), pl.ds(pl.multiple_of(OUT_CKV + cc * D, 128), D)]

    ag_k = Gather(place, kv_view, lambda cc, xx: gb.at[pl.ds(pl.multiple_of(xx * half_slabs, 16), half_slabs), pl.ds(pl.multiple_of(OUT_CKV + cc * D, 128), D)], (wsend, grecv), 4)
    ag_k.step_one()

    def mg_step(i, carry):
        row = pl.multiple_of(i * 128, 128)
        memgrad_ref[pl.ds(row, 128)] = mm_nt(kvg[pl.ds(row, 128)], wb[:, LANE_CKV : LANE_CKV + 2 * D])
        return carry

    full = own_rows // 128
    lax.fori_loop(0, full, mg_step, 0)
    if own_rows % 128:
        tail = mm_nt(kvg[full * 128 : (full + 1) * 128], wb[:, LANE_CKV : LANE_CKV + 2 * D])
        memgrad_ref[full * 128 : own_rows] = tail[0 : own_rows - full * 128]


    ag_u.gathers[0].step_two()
    ffn_rows(6, 7)
    ag_u.gathers[1].step_two()
    ffn_rows(7, 8)
    ag_u.gathers[0].step_three()
    gain_step(4)
    ag_k.step_two()
    ffn_in_sum(0)
    to_mate(LANE_FI + hidden[0], D)
    ag_u.gathers[1].step_three()
    ag_grad.step_two()
    ag_out.step_three()
    ffn_in_sum(1)
    to_mate(LANE_FI + hidden[1], D)
    ag_u.gathers[0].step_four()
    ag_k.step_three()
    ffn_out_sum(0)
    ag_u.gathers[1].step_four()
    ffn_out_sum(1)
    to_mate(LANE_FO + CORES * D * c, CORES * D)
    ag_grad.step_three()
    ag_out.step_six()
    ag_u.gathers[0].step_five()
    ag_k.step_four()
    ag_u.gathers[1].step_five()
    for n, (lane, width) in enumerate(
        [(LANE_FI + col * 4 * half_rows + D * (1 - c), D) for col in range(columns)] + [(LANE_FO + CORES * D * (1 - c), CORES * D)]
    ):
        ref = gb.at[:, pl.ds(pl.multiple_of(lane, 128), width)]
        pltpu.make_async_remote_copy(
            src_ref=ref, dst_ref=ref, send_sem=fsend.at[n], recv_sem=frecv.at[n], device_id=mate, device_id_type=MESH,
        ).wait_recv()
    outs = []

    def write(lane, width):
        lanes = pl.ds(lane, width)
        item = pltpu.make_async_copy(gb.at[:, lanes], weights_out_ref.at[:, lanes], load_sem.at[len(outs)])
        item.start()
        outs.append(item)

    write(LANE_FI, 8 * D)
    ag_k.step_five()
    ag_grad.step_six()
    out_ref[...] = ob[0, out_slot].astype(F32)
    grad_ref[...] = ob[1, out_slot].astype(F32)
    gains_all = gain_step(5)
    own_gain = gains_all[:, 0:half_rows]
    for i in range(1, columns):
        own_gain = jnp.where(f == i, gains_all[:, i * half_rows : (i + 1) * half_rows], own_gain)
    gain_out_ref[...] = own_gain
    ag_u.step("step_six")
    write(0, OUT_CKV)
    ag_k.step_six()
    write(OUT_CKV, 2 * D)

    to_holders_sent(q_pairs)
    to_owners_sent(o_pairs)
    to_holders_sent(d_pairs)
    to_owners_sent(dq_pairs)
    for which, at, to, src, dst in unit_items:
        @pl.when(me != to)
        def _():
            pltpu.make_async_remote_copy(
                src_ref=src, dst_ref=dst, send_sem=usend.at[which, at],
                recv_sem=urecv.at[which, 0], device_id=(to, f), device_id_type=MESH,
            ).wait_send()
    @pl.when(has_unit)
    def _():
        for n in range(2):
            unit_copy(n).wait_send()
        left_copy(c).wait_send()

    for t, j, here in k_items:
        @pl.when((c == f) & jnp.logical_not(here))
        def _():
            k_copy(t, j).wait_send()

    @pl.when(c == f)
    def _():
        kx_copy(0).wait_send()
        kx_copy(1).wait_send()

    across_o.finish()
    across_n.finish()
    for item in f_items:
        item.wait_send()
    kr_item.wait_send()

    @pl.when(c != f)
    def _():
        ky_copy(0).wait_send()
        ky_copy(1).wait_send()

    for item in y_items:
        item.wait_send()
    tell_p.finish()
    for k in range(len(partners)):
        gain_copy(k).wait_send()
    for item in [ag_x, ag_c, ag_n, *ag_u.gathers, ag_out, ag_grad, ag_k]:
        item.finish()
    for item in outs:
        item.wait()


def fused_body(
    ranks, columns,
    decoder_in, memory, res_group, prefix_len, self_gain, self_qkv, self_out, cross_gain, cross_query,
    cross_kv, cross_out, ffn_gain, ffn_in, ffn_out, cotangent,
):
    half_rows = D // columns
    chips = ranks // CORES
    slab = half_rows // chips
    own_rows = memory.shape[1]
    padded = -(-own_rows // 128) * 128
    tokens = ranks * SUFFIX
    vm = pl.BlockSpec(memory_space=pltpu.VMEM)
    sm = pl.BlockSpec(memory_space=pltpu.SMEM)
    hbm = pl.BlockSpec(memory_space=pl.ANY)
    dma = pltpu.SemaphoreType.DMA
    scratch = [
        pltpu.VMEM((D, UNITS * D), BF16),
        pltpu.VMEM((half_rows, UNITS * D), BF16),
        pltpu.VMEM((tokens, D), BF16),
        pltpu.VMEM((tokens, PIECE), BF16),
        pltpu.VMEM((4, SUFFIX, D), BF16),
        pltpu.VMEM((UNIT_CHIPS, CORES, SUFFIX, PIECE), BF16),
        pltpu.VMEM((ranks, SUFFIX, D), F32),
        pltpu.VMEM((ranks, SUFFIX, D), BF16),
        pltpu.VMEM((columns * tokens, D), BF16),
        pltpu.VMEM((columns * tokens, D), BF16),
        pltpu.VMEM((2, ranks, SUFFIX, D), BF16),
        pltpu.VMEM((ranks, 8, 128), F32),
        pltpu.VMEM((columns, 16, 128), F32),
        pltpu.VMEM((padded, D), BF16),
        pltpu.VMEM((padded, 2 * D), BF16),
        pltpu.VMEM((padded, 2 * D), BF16),
        pltpu.VMEM((D, 2 * D), BF16),
        pltpu.VMEM((half_rows, 2 * D), BF16),
        pltpu.VMEM((half_rows, 2 * D), BF16),
        pltpu.VMEM((half_rows, 2 * D), BF16),
        pltpu.VMEM((RING, slab, D), BF16),
        pltpu.VMEM((half_rows // SIDE, 2 * D), BF16),
        pltpu.VMEM((half_rows // SIDE, 2 * D), BF16),
        pltpu.VMEM((columns, columns * tokens, D), BF16),
        pltpu.VMEM((columns * tokens, D), BF16),
        pltpu.VMEM((columns, half_rows, PIECE), F32),
        pltpu.VMEM((half_rows, PIECE), BF16),
        pltpu.VMEM((half_rows, PIECE), BF16),
        pltpu.VMEM((SUFFIX, D), BF16),
        pltpu.VMEM((SLOTS, SUFFIX, D), BF16),
        pltpu.VMEM((SLOTS, SUFFIX, D), BF16),
        pltpu.VMEM((SLOTS, SUFFIX, 128), F32),
        pltpu.VMEM((SLOTS, SUFFIX, D), BF16),
        pltpu.VMEM((SLOTS, SUFFIX, 128), F32),
        pltpu.VMEM((SUFFIX, D), BF16),
        pltpu.VMEM((SUFFIX, 128), F32),
        pltpu.VMEM((SLOTS, SUFFIX, D), BF16),
        pltpu.VMEM((SLOTS, SUFFIX, 128), F32),
        pltpu.VMEM((SLOTS, SUFFIX, D), BF16),
        pltpu.VMEM((SLOTS, SUFFIX, D), BF16),
        pltpu.VMEM((5, 8, D), F32),
        pltpu.VMEM((5, 8, D), F32),
        dma((10,)),
        dma((len(CHUNKS), 17)),
        dma((len(CHUNKS), 14)),
        dma((2, 17)),
        dma((5, 10)),
        dma((3, 9)),
        dma((3, 10)),
        dma((1, ranks)),
        dma((1, ranks)),
        dma((2, 5)),
        dma((2, 2)),
        dma((2, 2)),
        dma((3,)),
        dma((3,)),
        dma((5,)),
        dma((5,)),
        dma((6, SLOTS)),
        dma((6, SLOTS)),
        dma((2, CORES * UNIT_CHIPS)),
        dma((2, ranks)),
        dma((2 * chips + 5,)),
        dma((chips + 5,)),
    ]
    out, grad, memgrad, gain_grads, weight_grads = pl.pallas_call(
        partial(layer_kernel, ranks, columns),
        out_shape=(
            jax.ShapeDtypeStruct((SUFFIX, D), F32),
            jax.ShapeDtypeStruct((SUFFIX, D), F32),
            jax.ShapeDtypeStruct((own_rows, D), F32),
            jax.ShapeDtypeStruct((8, half_rows), F32),
            jax.ShapeDtypeStruct((half_rows, UNITS * D), BF16),
        ),
        in_specs=[vm, vm, vm, sm, sm, vm, vm, vm] + [hbm] * 7,
        out_specs=(vm, vm, vm, vm, hbm),
        scratch_shapes=scratch,
        compiler_params=pltpu.CompilerParams(
            collective_id=0, has_side_effects=True, vmem_limit_bytes=63 * 2**20
        ),
        name="layer",
    )(
        decoder_in[0], cotangent[0], memory[0], res_group, prefix_len, self_gain, cross_gain, ffn_gain,
        self_qkv, self_out, cross_query, cross_kv, cross_out, ffn_in, ffn_out,
    )

    return unpack(half_rows, columns, weight_grads, memgrad, out, grad, gain_grads)


SPLIT = ((0, 3), (3, 1), (4, 1), (OUT_CKV, 2 * D), (5, 1), (LANE_FI, 4 * D))
WHOLE = (OUT_CKV, LANE_FI)


def unpack_kernel(w_ref, m_ref, o_ref, g_ref, gains_ref, *refs):
    *weights, ffn_out_ref, mem_ref, out_ref, grad_ref, one_ref, two_ref, three_ref = refs
    for n, ref in enumerate((one_ref, two_ref, three_ref)):
        ref[...] = gains_ref[n : n + 1].reshape(ref.shape)
    for (low, width), ref in zip(SPLIT, weights):
        if low in WHOLE:
            ref[...] = w_ref[:, low : low + width].astype(F32)
            continue
        for n in range(width):
            for j in range(CORES):
                at = (UNIT_CHIPS * j + low + n) * PIECE
                to = (CORES * n + j) * PIECE
                ref[:, to : to + PIECE] = w_ref[:, at : at + PIECE].astype(F32)
    for j in range(4):
        ffn_out_ref[j] = w_ref[:, LANE_FO + D * j : LANE_FO + D * (j + 1)].astype(F32)
    mem_ref[:, 0, :] = m_ref[...]
    out_ref[...] = o_ref[...]
    grad_ref[...] = g_ref[...]


def unpack(half_rows, columns, weight_grads, memgrad, out, grad, gain_grads):
    steps = 2
    rows = half_rows // steps
    own_rows = memgrad.shape[0]
    mem_rows = -(-own_rows // (8 * steps)) * 8
    tokens = out.shape[0] // steps
    block = lambda height, width: pl.BlockSpec((height, width), lambda i: (i, 0))
    results = pl.pallas_call(
        unpack_kernel,
        grid=(steps,),
        out_shape=[jax.ShapeDtypeStruct((half_rows, width if low in WHOLE else width * D), F32) for low, width in SPLIT]
        + [
            jax.ShapeDtypeStruct((4, half_rows, D), F32),
            jax.ShapeDtypeStruct((own_rows, 1, D), F32),
            jax.ShapeDtypeStruct(out.shape, F32),
            jax.ShapeDtypeStruct(grad.shape, F32),
        ]
        + [jax.ShapeDtypeStruct((half_rows,), F32)] * 3,
        in_specs=[block(rows, UNITS * D), block(mem_rows, D), block(tokens, D), block(tokens, D), pl.BlockSpec(gain_grads.shape, lambda i: (0, 0))],
        out_specs=[block(rows, width if low in WHOLE else width * D) for low, width in SPLIT]
        + [
            pl.BlockSpec((4, rows, D), lambda i: (0, i, 0)),
            pl.BlockSpec((mem_rows, 1, D), lambda i: (i, 0, 0)),
            block(tokens, D),
            block(tokens, D),
        ]
        + [pl.BlockSpec((half_rows,), lambda i: (0,))] * 3,
        compiler_params=pltpu.CompilerParams(vmem_limit_bytes=63 * 2**20),
        name="unpack",
    )(weight_grads, memgrad, out, grad, gain_grads)
    qkv, so, cq, ckv, co, fi, fo, mem, out, grad, gain_one, gain_two, gain_three = results
    return (
        out[None], grad[None], mem.reshape(1, own_rows, D),
        gain_one, qkv, so, gain_two, cq, ckv, co, gain_three, fi, fo.reshape(4 * half_rows, D),
    )


def layer_norm(value, gain):
    mean = jnp.mean(value, axis=-1, keepdims=True)
    centred = value - mean
    variance = jnp.mean(centred * centred, axis=-1, keepdims=True)
    return centred * lax.rsqrt(variance + norm_eps) * gain


def product(left, right):
    return jnp.dot(left, right, preferred_element_type=jnp.float32)


def outer_sum(left, right):
    flat_left = left.reshape(-1, left.shape[-1])
    flat_right = right.reshape(-1, right.shape[-1])
    return lax.dot_general(
        flat_left, flat_right, (((0,), (0,)), ((), ())), preferred_element_type=jnp.float32
    )


def back_product(grad, weight):
    return lax.dot_general(
        grad, weight, (((grad.ndim - 1,), (1,)), ((), ())), preferred_element_type=jnp.float32
    )


def attend(query, keys, values, allowed, scale):
    scores = jnp.einsum("eqhd,ekhd->ehqk", query, keys, preferred_element_type=jnp.float32) * scale
    scores = jnp.where(allowed[:, None], scores, -1e30)
    top = jnp.max(scores, axis=-1, keepdims=True)
    weights = jnp.exp(scores - top)
    probs = weights / jnp.sum(weights, axis=-1, keepdims=True)
    mixed = jnp.einsum(
        "ehqk,ekhd->eqhd", probs.astype(jnp.bfloat16), values, preferred_element_type=jnp.float32
    )
    return (mixed.astype(jnp.bfloat16), probs)


def attend_back(grad_mixed, query, keys, values, probs, scale):
    probs_low = probs.astype(jnp.bfloat16)
    grad_values = jnp.einsum(
        "ehqk,eqhd->ekhd", probs_low, grad_mixed, preferred_element_type=jnp.float32
    )
    grad_probs = jnp.einsum(
        "eqhd,ekhd->ehqk", grad_mixed, values, preferred_element_type=jnp.float32
    )
    grad_scores = probs * (grad_probs - jnp.sum(probs * grad_probs, axis=-1, keepdims=True))
    grad_low = grad_scores.astype(jnp.bfloat16)
    grad_query = (
        jnp.einsum("ehqk,ekhd->eqhd", grad_low, keys, preferred_element_type=jnp.float32) * scale
    )
    grad_keys = (
        jnp.einsum("ehqk,eqhd->ekhd", grad_low, query, preferred_element_type=jnp.float32) * scale
    )
    return (grad_query, grad_keys, grad_values)


def window_layout(res_group, mem_col):
    small = 1 - res_group
    small_count = jnp.sum(small, axis=-1, keepdims=True)
    small_before = jnp.cumsum(small, axis=-1) - small
    large_before = jnp.cumsum(res_group, axis=-1) - res_group
    offset = jnp.where(
        res_group == 1, SLOT_S * small_count + SLOT_L * large_before, SLOT_S * small_before
    )
    start = jnp.minimum(offset, mem_col - SLOT_L)
    return (offset, start)


def take_windows(column, starts):
    return jax.vmap(lambda begin: lax.dynamic_slice_in_dim(column, begin, SLOT_L, 0))(starts)


def forward(decoder_rows, windows, cross_allowed, weights):
    (
        self_gain,
        self_qkv,
        self_out,
        cross_gain,
        cross_query,
        cross_kv,
        cross_out,
        ffn_gain,
        ffn_in,
        ffn_out,
    ) = weights
    count = decoder_rows.shape[0] // SUFFIX
    scale = HEAD_DIM ** (-0.5)
    row_index = lax.broadcasted_iota(jnp.int32, (SUFFIX, SUFFIX), 0)
    col_index = lax.broadcasted_iota(jnp.int32, (SUFFIX, SUFFIX), 1)
    causal = (row_index >= col_index)[None]
    resid = decoder_rows.reshape(count, SUFFIX, D)
    normed_one = layer_norm(resid, self_gain.astype(jnp.float32)).astype(jnp.bfloat16)
    packed = product(normed_one, self_qkv).astype(jnp.bfloat16)
    heads = packed.reshape(count, SUFFIX, 3, HEADS, HEAD_DIM)
    self_mixed, self_probs = attend(heads[:, :, 0], heads[:, :, 1], heads[:, :, 2], causal, scale)
    self_mixed = self_mixed.reshape(count, SUFFIX, D)
    after_self = resid + product(self_mixed, self_out)
    normed_two = layer_norm(after_self, cross_gain.astype(jnp.float32)).astype(jnp.bfloat16)
    cross_q = product(normed_two, cross_query).astype(jnp.bfloat16)
    window_kv = product(windows, cross_kv).astype(jnp.bfloat16)
    query_heads = cross_q.reshape(count, SUFFIX, HEADS, HEAD_DIM)
    kv_heads = window_kv.reshape(count, SLOT_L, 2, HEADS, HEAD_DIM)
    cross_mixed, cross_probs = attend(
        query_heads, kv_heads[:, :, 0], kv_heads[:, :, 1], cross_allowed, scale
    )
    cross_mixed = cross_mixed.reshape(count, SUFFIX, D)
    after_cross = after_self + product(cross_mixed, cross_out)
    normed_three = layer_norm(after_cross, ffn_gain.astype(jnp.float32)).astype(jnp.bfloat16)
    up = product(normed_three, ffn_in)
    act = jax.nn.gelu(up, approximate=True).astype(jnp.bfloat16)
    result = after_cross + product(act, ffn_out)
    return (
        resid,
        normed_one,
        packed,
        self_probs,
        self_mixed,
        after_self,
        normed_two,
        cross_q,
        window_kv,
        cross_probs,
        cross_mixed,
        after_cross,
        normed_three,
        up,
        act,
        result,
    )


def backward(grad_out, saved, weights):
    (
        self_gain,
        self_qkv,
        self_out,
        cross_gain,
        cross_query,
        cross_kv,
        cross_out,
        ffn_gain,
        ffn_in,
        ffn_out,
    ) = weights
    (
        resid,
        normed_one,
        packed,
        self_probs,
        self_mixed,
        after_self,
        normed_two,
        cross_q,
        window_kv,
        cross_probs,
        cross_mixed,
        after_cross,
        normed_three,
        up,
        act,
        result,
    ) = saved
    count = resid.shape[0]
    scale = HEAD_DIM ** (-0.5)
    grad_out = grad_out.reshape(count, SUFFIX, D)
    out_low = grad_out.astype(jnp.bfloat16)
    ffn_out_grad = outer_sum(act, out_low)
    act_grad = back_product(out_low, ffn_out)
    gelu_value, gelu_back = jax.vjp(partial(jax.nn.gelu, approximate=True), up)
    up_grad = gelu_back(act_grad)[0].astype(jnp.bfloat16)
    ffn_in_grad = outer_sum(normed_three, up_grad)
    normed_three_grad = back_product(up_grad, ffn_in)
    norm_value, norm_back = jax.vjp(layer_norm, after_cross, ffn_gain.astype(jnp.float32))
    resid_part, ffn_gain_grad = norm_back(normed_three_grad)
    cross_res_grad = grad_out + resid_part
    cross_low = cross_res_grad.astype(jnp.bfloat16)
    cross_out_grad = outer_sum(cross_mixed, cross_low)
    mixed_grad = (
        back_product(cross_low, cross_out)
        .astype(jnp.bfloat16)
        .reshape(count, SUFFIX, HEADS, HEAD_DIM)
    )
    query_heads = cross_q.reshape(count, SUFFIX, HEADS, HEAD_DIM)
    kv_heads = window_kv.reshape(count, SLOT_L, 2, HEADS, HEAD_DIM)
    query_grad, keys_grad, values_grad = attend_back(
        mixed_grad, query_heads, kv_heads[:, :, 0], kv_heads[:, :, 1], cross_probs, scale
    )
    cross_q_grad = query_grad.reshape(count, SUFFIX, D).astype(jnp.bfloat16)
    window_kv_grad = (
        jnp.stack((keys_grad, values_grad), axis=2)
        .reshape(count, SLOT_L, 2 * D)
        .astype(jnp.bfloat16)
    )
    cross_query_grad = outer_sum(normed_two, cross_q_grad)
    normed_two_grad = back_product(cross_q_grad, cross_query)
    norm_value, norm_back = jax.vjp(layer_norm, after_self, cross_gain.astype(jnp.float32))
    resid_part, cross_gain_grad = norm_back(normed_two_grad)
    self_res_grad = cross_res_grad + resid_part
    self_low = self_res_grad.astype(jnp.bfloat16)
    self_out_grad = outer_sum(self_mixed, self_low)
    mixed_grad = (
        back_product(self_low, self_out)
        .astype(jnp.bfloat16)
        .reshape(count, SUFFIX, HEADS, HEAD_DIM)
    )
    heads = packed.reshape(count, SUFFIX, 3, HEADS, HEAD_DIM)
    query_grad, keys_grad, values_grad = attend_back(
        mixed_grad, heads[:, :, 0], heads[:, :, 1], heads[:, :, 2], self_probs, scale
    )
    packed_grad = (
        jnp.stack((query_grad, keys_grad, values_grad), axis=2)
        .reshape(count, SUFFIX, 3 * D)
        .astype(jnp.bfloat16)
    )
    self_qkv_grad = outer_sum(normed_one, packed_grad)
    normed_one_grad = back_product(packed_grad, self_qkv)
    norm_value, norm_back = jax.vjp(layer_norm, resid, self_gain.astype(jnp.float32))
    resid_part, self_gain_grad = norm_back(normed_one_grad)
    decoder_grad = self_res_grad + resid_part
    weight_grads = (
        self_gain_grad,
        self_qkv_grad,
        self_out_grad,
        cross_gain_grad,
        cross_query_grad,
        cross_out_grad,
        ffn_gain_grad,
        ffn_in_grad,
        ffn_out_grad,
    )
    return (decoder_grad, window_kv_grad, weight_grads)


def make_placer(all_starts, lowest, own_rows):

    def place(total, piece, begin):

        def add_one(item, acc):
            relative = all_starts[item] - lowest
            inside = ((relative > -SLOT_L) & (relative < own_rows)).astype(jnp.float32)
            spot = jnp.clip(relative + SLOT_L, 0, own_rows + SLOT_L)
            current = lax.dynamic_slice_in_dim(acc, spot, SLOT_L, 0)
            added = current + piece[item].astype(jnp.float32) * inside
            return lax.dynamic_update_slice_in_dim(acc, added, spot, 0)

        return lax.fori_loop(0, piece.shape[0], add_one, total)

    return place


def body(
    decoder_in,
    memory,
    res_group,
    prefix_len,
    self_gain,
    self_qkv,
    self_out,
    cross_gain,
    cross_query,
    cross_kv,
    cross_out,
    ffn_gain,
    ffn_in,
    ffn_out,
    cotangent,
):
    count = prefix_len.shape[1]
    own_rows = memory.shape[1]
    mem_col = own_rows * lax.axis_size("dp")
    offset, start = window_layout(res_group, mem_col)
    all_starts = start[0]
    first = lax.axis_index("dp") * count
    own_offset = lax.dynamic_slice_in_dim(offset[0], first, count)
    own_start = lax.dynamic_slice_in_dim(all_starts, first, count)
    own_group = lax.dynamic_slice_in_dim(res_group[0], first, count)
    valid = jnp.where(own_group == 1, PATCH_L, PATCH_S) + prefix_len[0]
    positions = own_start[:, None] + jnp.arange(SLOT_L, dtype=jnp.int32)[None]
    cross_allowed = (
        (positions >= own_offset[:, None]) & (positions < (own_offset + valid)[:, None])
    )[:, None]
    weights = (
        lax.all_gather(self_gain, "fsdp", axis=0, tiled=True),
        lax.all_gather(self_qkv, "fsdp", axis=0, tiled=True),
        lax.all_gather(self_out, "fsdp", axis=0, tiled=True),
        lax.all_gather(cross_gain, "fsdp", axis=0, tiled=True),
        lax.all_gather(cross_query, "fsdp", axis=0, tiled=True),
        lax.all_gather(cross_kv, "fsdp", axis=0, tiled=True),
        lax.all_gather(cross_out, "fsdp", axis=0, tiled=True),
        lax.all_gather(ffn_gain, "fsdp", axis=0, tiled=True),
        lax.all_gather(ffn_in, "fsdp", axis=0, tiled=True),
        lax.all_gather(ffn_out, "fsdp", axis=0, tiled=True),
    )
    column = lax.all_gather(memory[0], "dp", axis=0, tiled=True)
    windows = take_windows(column, own_start)
    saved = forward(decoder_in[0], windows, cross_allowed, weights)
    decoder_out = saved[-1]
    weights = (
        lax.all_gather(self_gain, "fsdp", axis=0, tiled=True),
        lax.all_gather(self_qkv, "fsdp", axis=0, tiled=True),
        lax.all_gather(self_out, "fsdp", axis=0, tiled=True),
        lax.all_gather(cross_gain, "fsdp", axis=0, tiled=True),
        lax.all_gather(cross_query, "fsdp", axis=0, tiled=True),
        lax.all_gather(cross_kv, "fsdp", axis=0, tiled=True),
        lax.all_gather(cross_out, "fsdp", axis=0, tiled=True),
        lax.all_gather(ffn_gain, "fsdp", axis=0, tiled=True),
        lax.all_gather(ffn_in, "fsdp", axis=0, tiled=True),
        lax.all_gather(ffn_out, "fsdp", axis=0, tiled=True),
    )
    column = lax.all_gather(memory[0], "dp", axis=0, tiled=True)
    windows = take_windows(column, own_start)
    saved = forward(decoder_in[0], windows, cross_allowed, weights)
    whole_kv = weights[5]
    decoder_grad, window_kv_grad, local_grads = backward(cotangent[0], saved, weights)
    lowest = lax.axis_index("dp") * own_rows
    place = make_placer(all_starts, lowest, own_rows)
    empty = jnp.zeros((own_rows + 2 * SLOT_L, 2 * D), jnp.float32)
    summed = place(empty, lax.all_gather(window_kv_grad, "dp", axis=0, tiled=True), jnp.int32(0))
    own_kv_grad = summed[SLOT_L : SLOT_L + own_rows].astype(jnp.bfloat16)
    memory_grad = back_product(own_kv_grad, whole_kv)
    cross_kv_part = outer_sum(memory[0], own_kv_grad)
    grads = (
        local_grads[0],
        local_grads[1],
        local_grads[2],
        local_grads[3],
        local_grads[4],
        cross_kv_part,
        local_grads[5],
        local_grads[6],
        local_grads[7],
        local_grads[8],
    )
    shards = (
        lax.psum_scatter(
            grads[0].astype(jnp.bfloat16), "fsdp", scatter_dimension=0, tiled=True
        ).astype(jnp.float32),
        lax.psum_scatter(
            grads[1].astype(jnp.bfloat16), "fsdp", scatter_dimension=0, tiled=True
        ).astype(jnp.float32),
        lax.psum_scatter(
            grads[2].astype(jnp.bfloat16), "fsdp", scatter_dimension=0, tiled=True
        ).astype(jnp.float32),
        lax.psum_scatter(
            grads[3].astype(jnp.bfloat16), "fsdp", scatter_dimension=0, tiled=True
        ).astype(jnp.float32),
        lax.psum_scatter(
            grads[4].astype(jnp.bfloat16), "fsdp", scatter_dimension=0, tiled=True
        ).astype(jnp.float32),
        lax.psum_scatter(
            grads[5].astype(jnp.bfloat16), "fsdp", scatter_dimension=0, tiled=True
        ).astype(jnp.float32),
        lax.psum_scatter(
            grads[6].astype(jnp.bfloat16), "fsdp", scatter_dimension=0, tiled=True
        ).astype(jnp.float32),
        lax.psum_scatter(
            grads[7].astype(jnp.bfloat16), "fsdp", scatter_dimension=0, tiled=True
        ).astype(jnp.float32),
        lax.psum_scatter(
            grads[8].astype(jnp.bfloat16), "fsdp", scatter_dimension=0, tiled=True
        ).astype(jnp.float32),
        lax.psum_scatter(
            grads[9].astype(jnp.bfloat16), "fsdp", scatter_dimension=0, tiled=True
        ).astype(jnp.float32),
    )
    totals = (
        lax.psum(shards[0].astype(jnp.bfloat16), "dp").astype(jnp.float32),
        lax.psum(shards[1].astype(jnp.bfloat16), "dp").astype(jnp.float32),
        lax.psum(shards[2].astype(jnp.bfloat16), "dp").astype(jnp.float32),
        lax.psum(shards[3].astype(jnp.bfloat16), "dp").astype(jnp.float32),
        lax.psum(shards[4].astype(jnp.bfloat16), "dp").astype(jnp.float32),
        lax.psum(shards[5].astype(jnp.bfloat16), "dp").astype(jnp.float32),
        lax.psum(shards[6].astype(jnp.bfloat16), "dp").astype(jnp.float32),
        lax.psum(shards[7].astype(jnp.bfloat16), "dp").astype(jnp.float32),
        lax.psum(shards[8].astype(jnp.bfloat16), "dp").astype(jnp.float32),
        lax.psum(shards[9].astype(jnp.bfloat16), "dp").astype(jnp.float32),
    )
    return (
        decoder_out,
        decoder_grad,
        memory_grad[None],
        totals[0],
        totals[1],
        totals[2],
        totals[3],
        totals[4],
        totals[5],
        totals[6],
        totals[7],
        totals[8],
        totals[9],
    )


def choose(mesh):
    ranks, columns = mesh.shape["dp"], mesh.shape["fsdp"]
    slabs = (D // columns) % (16 * (ranks // CORES)) == 0
    if slabs and columns == 2 and ranks == RING * SIDE * CORES:
        return partial(fused_body, ranks, columns)
    return body


def solution(mesh):
    placed = (
        P("fsdp", "dp", None),
        P("fsdp", "dp", None),
        P("fsdp", None),
        P("fsdp", "dp"),
        P("fsdp"),
        P("fsdp", None),
        P("fsdp", None),
        P("fsdp"),
        P("fsdp", None),
        P("fsdp", None),
        P("fsdp", None),
        P("fsdp"),
        P("fsdp", None),
        P("fsdp", None),
        P("fsdp", "dp", None),
    )
    return jax.shard_map(
        choose(mesh),
        mesh=mesh,
        in_specs=placed,
        out_specs=(
            P("fsdp", "dp", None),
            P("fsdp", "dp", None),
            P("fsdp", "dp", None),
            P("fsdp"),
            P("fsdp", None),
            P("fsdp", None),
            P("fsdp"),
            P("fsdp", None),
            P("fsdp", None),
            P("fsdp", None),
            P("fsdp"),
            P("fsdp", None),
            P("fsdp", None),
        ),
        check_vma=False,
    )
```
